32 devices in a mesh: pipe: 8 (over z, x), tensor: 4 (over y, core).
Axes of the slice: x: 2, y: 2, z: 4, core: 2. Of those that a mesh axis runs over, the one named last changes fastest.
Arguments:
- inputs: bfloat16 [2, 4, 32, 3584], replicated
- cotangent: bfloat16 [2, 4, 32, 3584], replicated, may hold values from -0.59765625 to 0.59765625
- section_weights: bfloat16 [8, 2, 3, 3584, 1024], P('pipe', None, None, None, 'tensor'), as said below
- section_gains: float32 [8, 2, 3584], P('pipe'), as said below
Outputs:
- section_grads: bfloat16 [8, 3, 3584, 1024], P('pipe', None, None, 'tensor')
The draws below stay inside these ranges and needn't reach their ends.
Inputs may be any that keep to these rules, and one draw needn't show every extreme that they name: section_weights[r * 4 + k, 1] is an exact copy of section_weights[r * 4 + 3 - k, 0] for every r and k, and section_weights[r * 4 + k] is the same for every r. section_gains[r * 4 + k, 1] is an exact copy of section_gains[r * 4 + 3 - k, 0] for every r and k, and section_gains[r * 4 + k] is the same for every r.
All inputs are finite; a program needn't handle non-finite values.
Results may differ from the reference program's by a relative error of at most 0.035.
Values may be sent and summed in bfloat16 or wider, within the bound.
No kernel may reach another device: no remote copies, remote signals or barrier semaphores. Data moves between devices by JAX's collectives and lax.ppermute only.
A program may use at most 128 MiB of HBM per device.

```python
import math
import jax
import jax.numpy as jnp
from jax import lax

D = 3584
FFW = 1024
TOK = 32
MB_DIR = 2
REPL = 2
MB = 4
LAYERS = 4
N_TENSOR = 4


def draw_inputs(key, part):
    key = jax.random.fold_in(key, 9)
    row_key, value_key = jax.random.split(key, 2)
    rows_scale = jnp.exp(jax.random.uniform(row_key, (REPL, MB, TOK, 1), jnp.float32, math.log(0.3), math.log(3.0)))
    values = jax.random.normal(value_key, (REPL, MB, TOK, D), jnp.float32)
    return (values * rows_scale).astype(jnp.bfloat16)


def draw_section_weights(key, part):
    key = jax.random.fold_in(key, 5)
    spread = jnp.array([D ** (-0.5), D ** (-0.5), FFW ** (-0.5)], jnp.float32).reshape(1, 3, 1, 1)
    samples = jax.random.normal(key, (LAYERS, 3, D, FFW), jnp.float32)
    samples = (samples * spread).astype(jnp.bfloat16)
    paired = jnp.stack([samples, samples[::-1]], axis=1)
    return jnp.concatenate([paired] * REPL, axis=0)


def draw_section_gains(key, part):
    key = jax.random.fold_in(key, 7)
    low_end = math.log(0.5)
    high_end = math.log(2.0)
    samples = jnp.exp(jax.random.uniform(key, (LAYERS, D), jnp.float32, low_end, high_end))
    paired = jnp.stack([samples, samples[::-1]], axis=1)
    return jnp.concatenate([paired] * REPL, axis=0)


def centred(own_key, extent, scale, bound, held_as=jnp.bfloat16):
    values = scale * jax.random.normal(own_key, extent, jnp.float32)
    return jnp.clip(values, min=-bound, max=bound).astype(held_as)


def setup_inputs(seed: int = 0) -> dict:
    keys = jax.random.split(jax.random.key(seed), 5)
    inputs = draw_inputs(jax.random.fold_in(keys[4], 71), 0)
    cotangent = centred(keys[1], (REPL, MB, TOK, D), 0.1, 0.59765625)
    section_weights = draw_section_weights(jax.random.fold_in(keys[4], 71), 0)
    section_gains = draw_section_gains(jax.random.fold_in(keys[4], 71), 0)
    return {"inputs": inputs, "cotangent": cotangent, "section_weights": section_weights, "section_gains": section_gains}


EPS = 1e-06

def norm_parts(layer_in, gain_row):
    widened = layer_in.astype(jnp.float32)
    root_mean = jnp.sqrt(lax.optimization_barrier(jnp.mean(widened * widened, axis=-1, keepdims=True)) + EPS)
    unit_rows = widened / root_mean
    normed = (unit_rows * gain_row).astype(jnp.bfloat16)
    return (unit_rows, root_mean, normed)

def contract_last(left_op, right_op):
    return lax.dot_general(left_op, right_op, (((1,), (1,)), ((), ())), preferred_element_type=jnp.float32)

def contract_first(left_op, right_op):
    return lax.dot_general(left_op, right_op, (((0,), (0,)), ((), ())), preferred_element_type=jnp.float32)

def weight_terms(normed, active, d_gate, d_upper, upstream):
    return jnp.stack([contract_first(normed, d_gate), contract_first(normed, d_upper), contract_first(upstream, active)])

def block_sum(operands):
    narrow = FFW // N_TENSOR
    running = jnp.zeros((operands[0][0].shape[0], operands[0][1].shape[0]), jnp.float32)
    for segment in range(N_TENSOR):
        offset = segment * narrow
        partial_value = jnp.zeros_like(running)
        for left_op, right_op in operands:
            partial_value = partial_value + contract_last(left_op[:, offset:offset + narrow], right_op[:, offset:offset + narrow])
        rounded = lax.optimization_barrier(partial_value.astype(jnp.bfloat16))
        running = running + rounded.astype(jnp.float32)
    return running

def replica_grads(inputs, cotangent, section_weights, section_gains):
    layer_in = inputs.reshape(-1, D)
    retained = []
    for layer_idx in range(LAYERS):
        retained.append(layer_in)
        weights = section_weights[layer_idx, 0]
        unit_rows, root_mean, normed = norm_parts(layer_in, section_gains[layer_idx, 0])
        gate_pre = jnp.dot(normed, weights[0], preferred_element_type=jnp.float32)
        upper = jnp.dot(normed, weights[1], preferred_element_type=jnp.float32)
        active = (gate_pre * jax.nn.sigmoid(gate_pre) * upper).astype(jnp.bfloat16)
        layer_in = (layer_in.astype(jnp.float32) + block_sum([(active, weights[2])])).astype(jnp.bfloat16)
    upstream = cotangent.reshape(-1, D)
    boundary = MB_DIR * TOK
    gradient_list = []
    for layer_idx in reversed(range(LAYERS)):
        weights = section_weights[layer_idx, 0]
        gain_row = section_gains[layer_idx, 0]
        unit_rows, root_mean, normed = norm_parts(retained[layer_idx], gain_row)
        gate_pre = jnp.dot(normed, weights[0], preferred_element_type=jnp.float32)
        upper = jnp.dot(normed, weights[1], preferred_element_type=jnp.float32)
        sig_gate = jax.nn.sigmoid(gate_pre)
        smooth = gate_pre * sig_gate
        active = (smooth * upper).astype(jnp.bfloat16)
        d_active = jnp.dot(upstream, weights[2], preferred_element_type=jnp.float32)
        d_gate = (d_active * upper * (sig_gate * (1.0 + gate_pre * (1.0 - sig_gate)))).astype(jnp.bfloat16)
        d_upper = (d_active * smooth).astype(jnp.bfloat16)
        summed = block_sum([(d_gate, weights[0]), (d_upper, weights[1])])
        first_sum = weight_terms(normed[:boundary], active[:boundary], d_gate[:boundary], d_upper[:boundary], upstream[:boundary])
        second_sum = weight_terms(normed[boundary:], active[boundary:], d_gate[boundary:], d_upper[boundary:], upstream[boundary:])
        first_sum = lax.optimization_barrier(first_sum.astype(jnp.bfloat16))
        second_sum = lax.optimization_barrier(second_sum.astype(jnp.bfloat16))
        gradient_list.append((first_sum.astype(jnp.float32) + second_sum.astype(jnp.float32)).astype(jnp.bfloat16))
        d_unit = summed * gain_row
        d_state = (d_unit - unit_rows * lax.optimization_barrier(jnp.mean(d_unit * unit_rows, axis=-1, keepdims=True))) / root_mean
        upstream = (upstream.astype(jnp.float32) + d_state).astype(jnp.bfloat16)
    return jnp.stack(gradient_list[::-1])

def reference(inputs, cotangent, section_weights, section_gains):
    total = jnp.zeros((LAYERS, 3, D, FFW), jnp.float32)
    for replica in range(REPL):
        lower = replica * LAYERS
        grads = replica_grads(inputs[replica], cotangent[replica], section_weights[lower:lower + LAYERS], section_gains[lower:lower + LAYERS])
        total = total + lax.optimization_barrier(grads).astype(jnp.float32)
    combined = total.astype(jnp.bfloat16)
    return jnp.concatenate([combined] * REPL, axis=0)
```

```python
import functools

import jax
import jax.numpy as jnp
from jax import lax
from jax.experimental import pallas as pl
from jax.experimental.pallas import tpu as pltpu
from jax.sharding import PartitionSpec as P

REPL = 2
EPS = 1e-06
BF = jnp.bfloat16
F32 = jnp.float32


def chunk_of(features):
    for size in (512, 256, 128):
        if features % size == 0:
            return size
    return features


def norm_rows(rows, gain_row):
    widened = rows.astype(F32)
    root = jnp.sqrt(jnp.mean(widened * widened, axis=-1, keepdims=True) + EPS)
    unit = widened / root
    return unit, root, (unit * gain_row).astype(BF)


def dot_last(left, right):
    return lax.dot_general(left, right, (((1,), (1,)), ((), ())), preferred_element_type=F32)


def dot_first(left, right):
    return lax.dot_general(left, right, (((0,), (0,)), ((), ())), preferred_element_type=F32)


def weight_copies(which, w_ref, w_buf, sems, order, size):
    features = w_buf.shape[1]
    copies = {}
    for matrix in order:
        for k in range(features // size):
            rows = pl.ds(k * size, size)
            copies[matrix, k] = pltpu.make_async_copy(
                w_ref.at[which, matrix, rows], w_buf.at[matrix, rows], sems.at[matrix, k]
            )
    return copies


def start_pairs(copies, first, second, count):
    for k in range(count):
        for matrix in (first, second):
            copies[matrix, k].start()


def gate_upper(copies, w_buf, normed, size):
    count = w_buf.shape[1] // size
    gate = upper = None
    for k in range(count):
        cols = pl.ds(k * size, size)
        copies[0, k].wait()
        copies[1, k].wait()
        block = normed[:, cols]
        gate_k = jnp.dot(block, w_buf[0, cols], preferred_element_type=F32)
        upper_k = jnp.dot(block, w_buf[1, cols], preferred_element_type=F32)
        gate = gate_k if gate is None else gate + gate_k
        upper = upper_k if upper is None else upper + upper_k
    return gate, upper


def fill_normed(xm_ref, xo_ref, gain, normed):
    half = xm_ref.shape[0]
    normed[:half] = norm_rows(xm_ref[...], gain)[2]
    normed[half:] = norm_rows(xo_ref[...], gain)[2]


def forward_kernel(
    which_ref, xm_ref, xo_ref, gain_ref, w_ref, pm_ref, po_ref, gate_ref, upper_ref, w_buf, normed, sems
):
    which = which_ref[0]
    features = w_buf.shape[1]
    size = chunk_of(features)
    count = features // size
    half = xm_ref.shape[0]
    copies = weight_copies(which, w_ref, w_buf, sems, (0, 1, 2), size)
    start_pairs(copies, 0, 1, count)
    for k in range(count):
        copies[2, k].start()
    fill_normed(xm_ref, xo_ref, gain_ref[which], normed)
    gate, upper = gate_upper(copies, w_buf, normed, size)
    gate_ref[...] = gate
    upper_ref[...] = upper
    active = (gate * jax.nn.sigmoid(gate) * upper).astype(BF)
    for k in range(count):
        cols = pl.ds(k * size, size)
        copies[2, k].wait()
        part = dot_last(active, w_buf[2, cols]).astype(BF)
        pm_ref[:, cols] = part[:half]
        po_ref[:, cols] = part[half:]


def backward_kernel(
    recompute, which_ref, um_ref, uo_ref, a_ref, b_ref, gain_ref, w_ref, pm_ref, po_ref, w_buf, normed, sems
):
    which = which_ref[0]
    features = w_buf.shape[1]
    size = chunk_of(features)
    count = features // size
    half = um_ref.shape[0]
    copies = weight_copies(which, w_ref, w_buf, sems, (0, 1, 2), size)
    for k in range(count):
        copies[2, k].start()
    start_pairs(copies, 0, 1, count)
    d_active = None
    for k in range(count):
        cols = pl.ds(k * size, size)
        copies[2, k].wait()
        block = jnp.concatenate([um_ref[:, cols], uo_ref[:, cols]], axis=0)
        part = jnp.dot(block, w_buf[2, cols], preferred_element_type=F32)
        d_active = part if d_active is None else d_active + part
    if recompute:
        fill_normed(a_ref, b_ref, gain_ref[which], normed)
        gate, upper = gate_upper(copies, w_buf, normed, size)
    else:
        gate, upper = a_ref[...], b_ref[...]
    sig = jax.nn.sigmoid(gate)
    d_gate = (d_active * upper * (sig * (1.0 + gate * (1.0 - sig)))).astype(BF)
    d_upper = (d_active * (gate * sig)).astype(BF)
    for k in range(count):
        cols = pl.ds(k * size, size)
        if not recompute:
            copies[0, k].wait()
            copies[1, k].wait()
        part = (dot_last(d_gate, w_buf[0, cols]) + dot_last(d_upper, w_buf[1, cols])).astype(BF)
        pm_ref[:, cols] = part[:half]
        po_ref[:, cols] = part[half:]


def layer_scratch(rows, features, narrow):
    count = features // chunk_of(features)
    return [
        pltpu.VMEM((3, features, narrow), BF),
        pltpu.VMEM((rows, features), BF),
        pltpu.SemaphoreType.DMA((3, count)),
    ]


SMEM_SPEC = pl.BlockSpec(memory_space=pltpu.SMEM)
VMEM_SPEC = pl.BlockSpec(memory_space=pltpu.VMEM)
ANY_SPEC = pl.BlockSpec(memory_space=pl.ANY)
VMEM_LIMIT = 32 * 1024 * 1024


def cost(rows, features, narrow):
    return pl.CostEstimate(
        flops=6 * rows * features * narrow, bytes_accessed=6 * features * narrow, transcendentals=rows * narrow
    )


def forward_layer(which, xm, xo, gains, weights):
    half, features = xm.shape
    narrow = weights.shape[-1]
    return pl.pallas_call(
        forward_kernel,
        out_shape=[
            jax.ShapeDtypeStruct((half, features), BF),
            jax.ShapeDtypeStruct((half, features), BF),
            jax.ShapeDtypeStruct((2 * half, narrow), F32),
            jax.ShapeDtypeStruct((2 * half, narrow), F32),
        ],
        in_specs=[SMEM_SPEC, VMEM_SPEC, VMEM_SPEC, VMEM_SPEC, ANY_SPEC],
        out_specs=[VMEM_SPEC] * 4,
        scratch_shapes=layer_scratch(2 * half, features, narrow),
        cost_estimate=cost(2 * half, features, narrow),
        compiler_params=pltpu.CompilerParams(vmem_limit_bytes=VMEM_LIMIT),
        name="forward_layer",
    )(which, xm, xo, gains, weights)


def backward_layer(which, um, uo, a, b, gains, weights, recompute):
    half, features = um.shape
    narrow = weights.shape[-1]
    return pl.pallas_call(
        functools.partial(backward_kernel, recompute),
        out_shape=[
            jax.ShapeDtypeStruct((half, features), BF),
            jax.ShapeDtypeStruct((half, features), BF),
        ],
        in_specs=[SMEM_SPEC, VMEM_SPEC, VMEM_SPEC, VMEM_SPEC, VMEM_SPEC, VMEM_SPEC, ANY_SPEC],
        out_specs=[VMEM_SPEC] * 2,
        scratch_shapes=layer_scratch(2 * half, features, narrow),
        cost_estimate=cost(2 * half, features, narrow),
        compiler_params=pltpu.CompilerParams(vmem_limit_bytes=VMEM_LIMIT),
        name="backward_layer_full" if recompute else "backward_layer",
    )(which, um, uo, a, b, gains, weights)


def body(inputs, cotangent, section_weights, section_gains):
    sections = lax.axis_size("pipe") // REPL
    ranks = lax.axis_size("tensor")
    chips = ranks // 2
    pipe = lax.axis_index("pipe")
    tensor = lax.axis_index("tensor")
    position = pipe % sections
    replica = pipe // sections
    middle = sections // 2
    near = position < middle
    kind = jnp.where(near, position, sections - 1 - position)
    core = tensor % 2
    chip = tensor // 2
    weights = section_weights[0]
    gains = section_gains[0][:, None, :]
    rows, features = inputs.shape[2:]
    group = rows // 2
    early = jnp.where(near, 0, 1).astype(jnp.int32).reshape(1)
    late = 1 - early

    core_swap = [(i, i ^ 1) for i in range(ranks)]
    chip_swap = [(i, (i + 2) % ranks) for i in range(ranks)]

    def swap_core(block):
        return lax.ppermute(block, "tensor", core_swap)

    def hop(block, source, target, turn, other):
        pairs = []
        for copy in range(REPL):
            for side in range(2):
                start = source if side == 0 else sections - 1 - source
                end_side = side ^ turn
                end = target if end_side == 0 else sections - 1 - target
                for rank in range(ranks):
                    end_rank = (rank + 2) % ranks if other else rank
                    pairs.append(
                        ((copy * sections + start) * ranks + rank, (copy * sections + end) * ranks + end_rank)
                    )
        return lax.ppermute(block, ("pipe", "tensor"), pairs)

    def transition(part_mine, part_other, finish, source, target):
        received = swap_core(part_other)
        summed = part_mine.astype(F32) + received.astype(F32)
        held = finish(summed)
        if source == target:
            pieces = held, lax.ppermute(held, "tensor", chip_swap)
            mine = (pieces[0].astype(F32) + pieces[1].astype(F32)).astype(BF)
        else:
            arrived = []
            for turn in range(2):
                block = held[turn * group : (turn + 1) * group]
                straight = hop(block, source, target, turn, False)
                crossed = hop(block, source, target, turn, True)
                arrived.append((straight.astype(F32) + crossed.astype(F32)).astype(BF))
            mine = jnp.concatenate(arrived, axis=0)
        return mine, swap_core(mine)

    def class_gather(mine):
        quarter = lax.dynamic_slice_in_dim(mine, chip * group, group, 0)
        groups = []
        for c in range(middle):
            members = []
            for copy in range(REPL):
                for place in (c, sections - 1 - c):
                    for rank in range(ranks):
                        members.append((copy * sections + place) * ranks + rank)
            groups.append(members)
        return lax.all_gather(quarter, ("pipe", "tensor"), axis_index_groups=groups, tiled=True)

    def first_rows(array):
        base = jnp.where(near, 0, 2)
        block = array[replica]
        return (
            lax.dynamic_index_in_dim(block, base + core, 0, keepdims=False),
            lax.dynamic_index_in_dim(block, base + 1 - core, 0, keepdims=False),
        )

    def whole_rows(array):
        parts = array.reshape(REPL, 2, 2, chips, group, features).swapaxes(2, 3)
        return parts.reshape(-1, features)

    def kind_of(step):
        return min(step, sections - 1 - step)

    def pick(step, new, old):
        if old is None:
            return new
        live = kind == kind_of(step)
        return jax.tree.map(lambda a, b: jnp.where(live, a, b), new, old)

    mine, other = first_rows(inputs)
    states = [None, None]
    gates = [None, None]
    for step in range(sections):
        side = 0 if step < middle else 1
        which = late if side else early
        states[side] = pick(step, (mine, other), states[side])
        if step == sections - 1:
            break
        part_mine, part_other, gate, upper = forward_layer(which, mine, other, gains, weights)
        gates[side] = pick(step, (gate, upper), gates[side])
        residual = jnp.where(chip == 0, mine.astype(F32), 0.0)
        mine, other = transition(
            part_mine, part_other, lambda summed: (summed + residual).astype(BF), kind_of(step), kind_of(step + 1)
        )
    gathered_early = class_gather(states[0][0])
    gathered_late = class_gather(states[1][0])

    up_mine, up_other = first_rows(cotangent)
    ups = [None, None]
    for step in range(sections - 1, -1, -1):
        side = 0 if step < middle else 1
        which = late if side else early
        ups[side] = pick(step, (up_mine, up_other), ups[side])
        if step == 0:
            break
        if step == sections - 1:
            first, second = states[side]
        else:
            first, second = gates[side]
        part_mine, part_other = backward_layer(
            which, up_mine, up_other, first, second, gains, weights, step == sections - 1
        )
        gain_row = jnp.where(which[0] == 0, gains[0], gains[1])
        unit, root, _ = norm_rows(states[side][0], gain_row)
        upward = jnp.where(chip == 0, up_mine.astype(F32), 0.0)

        def finish(summed):
            d_unit = summed * gain_row
            d_state = (d_unit - unit * jnp.mean(d_unit * unit, axis=-1, keepdims=True)) / root
            return (upward + d_state).astype(BF)

        up_mine, up_other = transition(part_mine, part_other, finish, kind_of(step), kind_of(step - 1))
    gathered_up_late = class_gather(ups[1][0])
    gathered_up_early = class_gather(ups[0][0])

    outer = kind == 0
    own_early = jnp.where(outer, whole_rows(inputs), gathered_early)
    own_up_late = jnp.where(outer, whole_rows(cotangent), gathered_up_late)
    state = jnp.where(near, own_early, gathered_late)
    upstream = jnp.where(near, gathered_up_early, own_up_late)
    normed = norm_rows(state, gains[0])[2]
    gate = jnp.dot(normed, weights[0, 0], preferred_element_type=F32)
    upper = jnp.dot(normed, weights[0, 1], preferred_element_type=F32)
    sig = jax.nn.sigmoid(gate)
    smooth = gate * sig
    active = (smooth * upper).astype(BF)
    d_active = jnp.dot(upstream, weights[0, 2], preferred_element_type=F32)
    d_gate = (d_active * upper * (sig * (1.0 + gate * (1.0 - sig)))).astype(BF)
    d_upper = (d_active * smooth).astype(BF)
    return jnp.stack(
        [dot_first(normed, d_gate), dot_first(normed, d_upper), dot_first(upstream, active)]
    ).astype(BF)[None]


def solution(mesh):
    return jax.shard_map(
        body,
        mesh=mesh,
        in_specs=(P(), P(), P("pipe", None, None, None, "tensor"), P("pipe", None, None)),
        out_specs=P("pipe", None, None, "tensor"),
        check_vma=False,
    )
```

```python
import functools

import jax
import jax.numpy as jnp
from jax import lax
from jax.experimental import pallas as pl
from jax.experimental.pallas import tpu as pltpu
from jax.sharding import PartitionSpec as P

REPL = 2
EPS = 1e-06
BF = jnp.bfloat16
F32 = jnp.float32
SMEM_SPEC = pl.BlockSpec(memory_space=pltpu.SMEM)
VMEM_SPEC = pl.BlockSpec(memory_space=pltpu.VMEM)
ANY_SPEC = pl.BlockSpec(memory_space=pl.ANY)
PARAMS = pltpu.CompilerParams(vmem_limit_bytes=32 * 1024 * 1024)


def chunk_of(features):
    for size in (512, 256, 128):
        if features % size == 0:
            return size
    return features


def norm_rows(rows, gain_row):
    widened = rows.astype(F32)
    root = jnp.sqrt(jnp.mean(widened * widened, axis=-1, keepdims=True) + EPS)
    unit = widened / root
    return unit, root, (unit * gain_row).astype(BF)


def dot(left, right):
    return jnp.dot(left, right, preferred_element_type=F32)


def dot_last(left, right):
    return lax.dot_general(left, right, (((1,), (1,)), ((), ())), preferred_element_type=F32)


def dot_first(left, right):
    return lax.dot_general(left, right, (((0,), (0,)), ((), ())), preferred_element_type=F32)


def weight_copies(which, w_ref, w_buf, sems, size):
    features = w_buf.shape[1]
    copies = {}
    for matrix in range(3):
        for k in range(features // size):
            rows = pl.ds(k * size, size)
            copies[matrix, k] = pltpu.make_async_copy(
                w_ref.at[which, matrix, rows], w_buf.at[matrix, rows], sems.at[matrix, k]
            )
    return copies


def fill_normed(xm_ref, xo_ref, gain, normed):
    half = xm_ref.shape[0]
    normed[:half] = norm_rows(xm_ref[...], gain)[2]
    normed[half:] = norm_rows(xo_ref[...], gain)[2]


def gate_upper(copies, w_buf, normed, size):
    gate = upper = None
    for k in range(w_buf.shape[1] // size):
        cols = pl.ds(k * size, size)
        if copies:
            copies[0, k].wait()
            copies[1, k].wait()
        block = normed[:, cols]
        gate_k = dot(block, w_buf[0, cols])
        upper_k = dot(block, w_buf[1, cols])
        gate = gate_k if gate is None else gate + gate_k
        upper = upper_k if upper is None else upper + upper_k
    return gate, upper


def forward_math(copies, xm_ref, xo_ref, gain_ref, w_buf, pm_ref, po_ref, gate_ref, upper_ref, normed):
    size = chunk_of(w_buf.shape[1])
    half = xm_ref.shape[0]
    fill_normed(xm_ref, xo_ref, gain_ref[...], normed)
    gate, upper = gate_upper(copies, w_buf, normed, size)
    gate_ref[...] = gate
    upper_ref[...] = upper
    active = (gate * jax.nn.sigmoid(gate) * upper).astype(BF)
    for k in range(w_buf.shape[1] // size):
        cols = pl.ds(k * size, size)
        if copies:
            copies[2, k].wait()
        part = dot_last(active, w_buf[2, cols]).astype(BF)
        pm_ref[:, cols] = part[:half]
        po_ref[:, cols] = part[half:]


def first_kernel(
    which_ref, xm_ref, xo_ref, gain_ref, w_ref, pm_ref, po_ref, gate_ref, upper_ref, w_buf, normed, sems
):
    size = chunk_of(w_buf.shape[1])
    copies = weight_copies(which_ref[0], w_ref, w_buf, sems, size)
    for group in ((0, 1), (2,)):
        for k in range(w_buf.shape[1] // size):
            for matrix in group:
                copies[matrix, k].start()
    forward_math(copies, xm_ref, xo_ref, gain_ref, w_buf, pm_ref, po_ref, gate_ref, upper_ref, normed)


def forward_kernel(xm_ref, xo_ref, gain_ref, w_buf, pm_ref, po_ref, gate_ref, upper_ref, normed):
    forward_math(None, xm_ref, xo_ref, gain_ref, w_buf, pm_ref, po_ref, gate_ref, upper_ref, normed)


def load_kernel(which_ref, w_ref, w_buf, sems):
    size = w_buf.shape[1]
    copies = weight_copies(which_ref[0], w_ref, w_buf, sems, size)
    for copy in copies.values():
        copy.start()
    for copy in copies.values():
        copy.wait()


def backward_kernel(recompute, um_ref, uo_ref, a_ref, b_ref, gain_ref, w_buf, pm_ref, po_ref, normed):
    features = w_buf.shape[1]
    size = chunk_of(features)
    count = features // size
    half = um_ref.shape[0]
    d_active = None
    for k in range(count):
        cols = pl.ds(k * size, size)
        block = jnp.concatenate([um_ref[:, cols], uo_ref[:, cols]], axis=0)
        part = dot(block, w_buf[2, cols])
        d_active = part if d_active is None else d_active + part
    if recompute:
        fill_normed(a_ref, b_ref, gain_ref[...], normed)
        gate, upper = gate_upper(None, w_buf, normed, size)
    else:
        gate, upper = a_ref[...], b_ref[...]
    sig = jax.nn.sigmoid(gate)
    d_gate = (d_active * upper * (sig * (1.0 + gate * (1.0 - sig)))).astype(BF)
    d_upper = (d_active * (gate * sig)).astype(BF)
    for k in range(count):
        cols = pl.ds(k * size, size)
        part = (dot_last(d_gate, w_buf[0, cols]) + dot_last(d_upper, w_buf[1, cols])).astype(BF)
        pm_ref[:, cols] = part[:half]
        po_ref[:, cols] = part[half:]


def own_first_kernel(x_ref, gain_ref, w_ref, turned_ref, left_ref, right_ref, active_ref, w_buf, normed, sems):
    features = w_buf.shape[1]
    size = chunk_of(features)
    count = features // size
    copies = {}
    for k in range(count):
        rows = pl.ds(k * size, size)
        for matrix in range(2):
            copies[matrix, k] = pltpu.make_async_copy(
                w_ref.at[0, matrix, rows], w_buf.at[matrix, rows], sems.at[matrix, k]
            )
            copies[matrix, k].start()
    gain = gain_ref[...]
    pieces, half = x_ref.shape[:2]
    for piece in range(pieces):
        normed[piece * half : (piece + 1) * half] = norm_rows(x_ref[piece], gain)[2]
    gate, upper = gate_upper(copies, w_buf, normed, size)
    sig = jax.nn.sigmoid(gate)
    smooth = gate * sig
    left_ref[...] = upper * (sig * (1.0 + gate * (1.0 - sig)))
    right_ref[...] = smooth
    active_ref[...] = (smooth * upper).astype(BF)
    for k in range(count):
        cols = pl.ds(k * size, size)
        turned_ref[cols] = normed[:, cols].T


def own_last_kernel(near_ref, u_ref, turned_ref, left_ref, right_ref, active_ref, early_ref, late_ref, out_ref, d_act, out_buf, sems):
    features = turned_ref.shape[0]
    size = chunk_of(features)
    count = features // size
    pieces, half = u_ref.shape[:2]

    def upstream(cols):
        return jnp.concatenate([u_ref[piece, :, cols] for piece in range(pieces)], axis=0)

    def fill(w_ref):
        total = None
        for k in range(count):
            cols = pl.ds(k * size, size)
            part = dot(upstream(cols), w_ref[2, cols])
            total = part if total is None else total + part
        d_act[...] = total

    @pl.when(near_ref[0] == 1)
    def _():
        fill(early_ref)

    @pl.when(near_ref[0] == 0)
    def _():
        fill(late_ref)

    copies = []

    def send(matrix, k):
        rows = pl.ds(k * size, size)
        copy = pltpu.make_async_copy(out_buf.at[matrix, rows], out_ref.at[0, matrix, rows], sems.at[matrix, k])
        copy.start()
        copies.append(copy)

    active = active_ref[...]
    d_active = d_act[...]
    d_gate = (d_active * left_ref[...]).astype(BF)
    d_upper = (d_active * right_ref[...]).astype(BF)
    for k in range(count):
        cols = pl.ds(k * size, size)
        turned = turned_ref[cols]
        out_buf[0, cols] = dot(turned, d_gate).astype(BF)
        send(0, k)
        out_buf[1, cols] = dot(turned, d_upper).astype(BF)
        send(1, k)
        out_buf[2, cols] = dot_first(upstream(cols), active).astype(BF)
        send(2, k)
    for copy in copies:
        copy.wait()


def cost(flops, moved):
    return pl.CostEstimate(flops=flops, bytes_accessed=moved, transcendentals=0)


def layer_outputs(half, features, narrow):
    return [jax.ShapeDtypeStruct((half, features), BF)] * 2 + [jax.ShapeDtypeStruct((2 * half, narrow), F32)] * 2


def first_layer(which, xm, xo, gain, weights):
    half, features = xm.shape
    narrow = weights.shape[-1]
    return pl.pallas_call(
        first_kernel,
        out_shape=layer_outputs(half, features, narrow) + [pltpu.VMEM((3, features, narrow), BF)],
        in_specs=[SMEM_SPEC, VMEM_SPEC, VMEM_SPEC, VMEM_SPEC, ANY_SPEC],
        out_specs=[VMEM_SPEC] * 5,
        scratch_shapes=[
            pltpu.VMEM((2 * half, features), BF),
            pltpu.SemaphoreType.DMA((3, features // chunk_of(features))),
        ],
        cost_estimate=cost(12 * half * features * narrow, 6 * features * narrow),
        compiler_params=PARAMS,
        name="first_layer",
    )(which, xm, xo, gain, weights)


def load_weights(which, weights):
    features, narrow = weights.shape[-2:]
    return pl.pallas_call(
        load_kernel,
        out_shape=pltpu.VMEM((3, features, narrow), BF),
        in_specs=[SMEM_SPEC, ANY_SPEC],
        out_specs=VMEM_SPEC,
        scratch_shapes=[pltpu.SemaphoreType.DMA((3, 1))],
        cost_estimate=cost(0, 6 * features * narrow),
        compiler_params=PARAMS,
        name="load_weights",
    )(which, weights)


def forward_layer(xm, xo, gain, held):
    half, features = xm.shape
    narrow = held.shape[-1]
    return pl.pallas_call(
        forward_kernel,
        out_shape=layer_outputs(half, features, narrow),
        in_specs=[VMEM_SPEC] * 4,
        out_specs=[VMEM_SPEC] * 4,
        scratch_shapes=[pltpu.VMEM((2 * half, features), BF)],
        cost_estimate=cost(12 * half * features * narrow, 6 * features * narrow),
        compiler_params=PARAMS,
        name="forward_layer",
    )(xm, xo, gain, held)


def backward_layer(um, uo, a, b, gain, held, recompute):
    half, features = um.shape
    narrow = held.shape[-1]
    return pl.pallas_call(
        functools.partial(backward_kernel, recompute),
        out_shape=[jax.ShapeDtypeStruct((half, features), BF)] * 2,
        in_specs=[VMEM_SPEC] * 6,
        out_specs=[VMEM_SPEC] * 2,
        scratch_shapes=[pltpu.VMEM((2 * half, features), BF)],
        cost_estimate=cost(12 * half * features * narrow, 6 * features * narrow),
        compiler_params=PARAMS,
        name="backward_full" if recompute else "backward_layer",
    )(um, uo, a, b, gain, held)


def own_first(pieces, gain, weights):
    count, half, features = pieces.shape
    narrow = weights.shape[-1]
    rows = count * half
    return pl.pallas_call(
        own_first_kernel,
        out_shape=[
            jax.ShapeDtypeStruct((features, rows), BF),
            jax.ShapeDtypeStruct((rows, narrow), F32),
            jax.ShapeDtypeStruct((rows, narrow), F32),
            jax.ShapeDtypeStruct((rows, narrow), BF),
        ],
        in_specs=[VMEM_SPEC, VMEM_SPEC, ANY_SPEC],
        out_specs=[VMEM_SPEC] * 4,
        scratch_shapes=[
            pltpu.VMEM((2, features, narrow), BF),
            pltpu.VMEM((rows, features), BF),
            pltpu.SemaphoreType.DMA((2, features // chunk_of(features))),
        ],
        cost_estimate=cost(4 * rows * features * narrow, 8 * features * narrow),
        compiler_params=PARAMS,
        name="own_first",
    )(pieces, gain, weights)


def own_last(near, pieces, turned, left, right, active, early, late):
    count, half, features = pieces.shape
    narrow = left.shape[-1]
    rows = count * half
    return pl.pallas_call(
        own_last_kernel,
        out_shape=jax.ShapeDtypeStruct((1, 3, features, narrow), BF),
        in_specs=[SMEM_SPEC] + [VMEM_SPEC] * 7,
        out_specs=ANY_SPEC,
        scratch_shapes=[
            pltpu.VMEM((rows, narrow), F32),
            pltpu.VMEM((3, features, narrow), BF),
            pltpu.SemaphoreType.DMA((3, features // chunk_of(features))),
        ],
        cost_estimate=cost(8 * rows * features * narrow, 8 * features * narrow),
        compiler_params=PARAMS,
        name="own_last",
    )(near, pieces, turned, left, right, active, early, late)


def body(inputs, cotangent, section_weights, section_gains):
    sections = lax.axis_size("pipe") // REPL
    ranks = lax.axis_size("tensor")
    pipe = lax.axis_index("pipe")
    tensor = lax.axis_index("tensor")
    position = pipe % sections
    replica = pipe // sections
    middle = sections // 2
    near = position < middle
    side = jnp.where(near, 0, 1)
    kind = jnp.where(near, position, sections - 1 - position)
    outer = kind == 0
    core = tensor % 2
    chip = tensor // 2
    weights = section_weights[0]
    own_gain = section_gains[0, 0][None]
    far_gain = section_gains[0, 1][None]
    gain_rows = (jnp.where(near, own_gain, far_gain), jnp.where(near, far_gain, own_gain))
    rows, features = inputs.shape[2:]
    group = rows // 2
    early = side.astype(jnp.int32).reshape(1)
    late = 1 - early
    core_swap = [(i, i ^ 1) for i in range(ranks)]
    chip_swap = [(i, (i + 2) % ranks) for i in range(ranks)]

    def swap_core(block):
        return lax.ppermute(block, "tensor", core_swap)

    def place(copy, end, c, rank):
        spot = c if end == 0 else sections - 1 - c
        return (copy * sections + spot) * ranks + rank

    def hop(block, source, target, turn, other):
        pairs = []
        for copy in range(REPL):
            for end in range(2):
                for rank in range(ranks):
                    arrival = (rank + 2) % ranks if other else rank
                    pairs.append((place(copy, end, source, rank), place(copy, end ^ turn, target, arrival)))
        return lax.ppermute(block, ("pipe", "tensor"), pairs)

    def exchange(payload, turn, across, wanted):
        pairs = []
        for copy in range(REPL):
            for end in range(2):
                for c in range(middle):
                    if not wanted(c, end):
                        continue
                    for rank in range(ranks):
                        pairs.append(
                            (place((copy + across) % REPL, end ^ turn, c, rank), place(copy, end, c, rank))
                        )
        return lax.ppermute(payload, ("pipe", "tensor"), pairs)

    def collect(early_rows, late_rows, wanted):
        same = jnp.where(near, early_rows, late_rows)
        opposite = jnp.where(near, late_rows, early_rows)
        arrived = [
            exchange(opposite, 1, 0, wanted),
            exchange(same, 0, 1, wanted),
            exchange(opposite, 1, 1, wanted),
        ]
        arrived = jnp.stack(arrived)
        return arrived, swap_core(arrived)

    def transition(part_mine, part_other, finish, source, target):
        received = swap_core(part_other)
        held = finish(part_mine.astype(F32) + received.astype(F32))
        if source == target:
            crossed = lax.ppermute(held, "tensor", chip_swap)
            mine = (held.astype(F32) + crossed.astype(F32)).astype(BF)
        else:
            blocks = [held[:group], held[group:]]
            straight = [hop(blocks[turn], source, target, turn, False) for turn in range(2)]
            crossed = [hop(blocks[turn], source, target, turn, True) for turn in range(2)]
            mine = jnp.concatenate(straight, axis=0).astype(F32) + jnp.concatenate(crossed, axis=0).astype(F32)
            mine = mine.astype(BF)
        return mine, swap_core(mine)

    def first_rows(array):
        block = array[replica]
        return (
            lax.dynamic_index_in_dim(block, 2 * side + core, 0, keepdims=False),
            lax.dynamic_index_in_dim(block, 2 * side + 1 - core, 0, keepdims=False),
        )

    def all_rows(array):
        flat = array.reshape(-1, rows, features)
        out = []
        for batch in (core, 1 - core):
            for across, turn in ((0, 0), (0, 1), (1, 0), (1, 1)):
                copy = (replica + across) % REPL
                out.append((copy * 2 + (side ^ turn)) * 2 + batch)
        order = [0, 4, 1, 2, 3, 5, 6, 7]
        return jnp.stack([lax.dynamic_index_in_dim(flat, out[i], 0, keepdims=False) for i in order])

    def kind_of(step):
        return min(step, sections - 1 - step)

    def pick(step, new, old):
        if old is None:
            return new
        live = kind == kind_of(step)
        return jax.tree.map(lambda a, b: jnp.where(live, a, b), new, old)

    mine, other = first_rows(inputs)
    states = [None, None]
    gates = [None, None]
    held = [None, load_weights(late, weights)]
    for step in range(sections - 1):
        part = 0 if step < middle else 1
        states[part] = pick(step, (mine, other), states[part])
        if step == 0:
            part_mine, part_other, gate, upper, held[0] = first_layer(early, mine, other, gain_rows[0], weights)
        else:
            part_mine, part_other, gate, upper = forward_layer(mine, other, gain_rows[part], held[part])
        gates[part] = pick(step, (gate, upper), gates[part])
        residual = jnp.where(chip == 0, mine.astype(F32), 0.0)
        mine, other = transition(
            part_mine, part_other, lambda summed: (summed + residual).astype(BF), kind_of(step), kind_of(step + 1)
        )
    states[1] = pick(sections - 1, (mine, other), states[1])

    up_mine, up_other = first_rows(cotangent)
    ups = [None, None]
    arrived_states = collect(states[0][0], states[1][0], lambda c, end: c > 0 or end == 1)
    for step in range(sections - 1, 0, -1):
        part = 0 if step < middle else 1
        ups[part] = pick(step, (up_mine, up_other), ups[part])
        if step == 1:
            arrived_ups = collect(ups[0][0], ups[1][0], lambda c, end: c > 0)
        last = step == sections - 1
        first, second = states[part] if last else gates[part]
        part_mine, part_other = backward_layer(
            up_mine, up_other, first, second, gain_rows[part], held[part], last
        )
        unit, root, _ = norm_rows(states[part][0], gain_rows[part])
        upward = jnp.where(chip == 0, up_mine.astype(F32), 0.0)

        def finish(summed):
            d_unit = summed * gain_rows[part]
            d_state = (d_unit - unit * jnp.mean(d_unit * unit, axis=-1, keepdims=True)) / root
            return (upward + d_state).astype(BF)

        up_mine, up_other = transition(part_mine, part_other, finish, kind_of(step), kind_of(step - 1))
    ups[0] = pick(0, (up_mine, up_other), ups[0])

    def lay(own, arrived):
        return jnp.concatenate([jnp.stack(own), arrived[0], arrived[1]], axis=0)

    own_state = [jnp.where(near, a, b) for a, b in zip(*states)]
    state = jnp.where(outer & near, all_rows(inputs), lay(own_state, arrived_states))
    turned, left, right, active = own_first(state, own_gain, weights)
    final_ups = collect(ups[0][0], ups[0][0], lambda c, end: c == 0 and end == 0)
    own_up = [jnp.where(near, a, b) for a, b in zip(*ups)]
    arrived = [jnp.where(outer, a, b) for a, b in zip(final_ups, arrived_ups)]
    upstream = jnp.where(outer & ~near, all_rows(cotangent), lay(own_up, arrived))
    is_near = near.astype(jnp.int32).reshape(1)
    return own_last(is_near, upstream, turned, left, right, active, held[0], held[1])


def solution(mesh):
    return jax.shard_map(
        body,
        mesh=mesh,
        in_specs=(P(), P(), P("pipe", None, None, None, "tensor"), P("pipe", None, None)),
        out_specs=P("pipe", None, None, "tensor"),
        check_vma=False,
    )
```

```python
import functools

import jax
import jax.numpy as jnp
from jax import lax
from jax.experimental import pallas as pl
from jax.experimental.pallas import tpu as pltpu
from jax.sharding import PartitionSpec as P

REPL = 2
EPS = 1e-06
BF = jnp.bfloat16
F32 = jnp.float32
SMEM_SPEC = pl.BlockSpec(memory_space=pltpu.SMEM)
VMEM_SPEC = pl.BlockSpec(memory_space=pltpu.VMEM)
HBM_SPEC = pl.BlockSpec(memory_space=pltpu.HBM)
PARAMS = pltpu.CompilerParams(vmem_limit_bytes=16 * 1024 * 1024)


def chunk_of(features):
    for size in (512, 256, 128):
        if features % size == 0:
            return size
    return features


def norm_rows(rows, gain_row):
    widened = rows.astype(F32)
    root = jnp.sqrt(jnp.mean(widened * widened, axis=-1, keepdims=True) + EPS)
    unit = widened / root
    return unit, root, (unit * gain_row).astype(BF)


def dot(left, right):
    return jnp.dot(left, right, preferred_element_type=F32)


def dot_last(left, right):
    return lax.dot_general(left, right, (((1,), (1,)), ((), ())), preferred_element_type=F32)


def dot_first(left, right):
    return lax.dot_general(left, right, (((0,), (0,)), ((), ())), preferred_element_type=F32)


def weight_copies(which, w_ref, w_buf, sems, size):
    features = w_buf.shape[1]
    copies = {}
    for matrix in range(3):
        for k in range(features // size):
            rows = pl.ds(k * size, size)
            copies[matrix, k] = pltpu.make_async_copy(
                w_ref.at[which, matrix, rows], w_buf.at[matrix, rows], sems.at[matrix, k]
            )
    return copies


def fill_normed(xm_ref, xo_ref, gain, normed):
    half = xm_ref.shape[0]
    normed[:half] = norm_rows(xm_ref[...], gain)[2]
    normed[half:] = norm_rows(xo_ref[...], gain)[2]


def gate_upper(copies, w_buf, normed, size):
    gate = upper = None
    for k in range(w_buf.shape[1] // size):
        cols = pl.ds(k * size, size)
        if copies:
            copies[0, k].wait()
            copies[1, k].wait()
        block = normed[:, cols]
        gate_k = dot(block, w_buf[0, cols])
        upper_k = dot(block, w_buf[1, cols])
        gate = gate_k if gate is None else gate + gate_k
        upper = upper_k if upper is None else upper + upper_k
    return gate, upper


def forward_math(copies, xm_ref, xo_ref, gain_ref, w_buf, pm_ref, po_ref, gate_ref, upper_ref, normed):
    size = chunk_of(w_buf.shape[1])
    half = xm_ref.shape[0]
    fill_normed(xm_ref, xo_ref, gain_ref[...], normed)
    gate, upper = gate_upper(copies, w_buf, normed, size)
    gate_ref[...] = gate
    upper_ref[...] = upper
    active = (gate * jax.nn.sigmoid(gate) * upper).astype(BF)
    for k in range(w_buf.shape[1] // size):
        cols = pl.ds(k * size, size)
        if copies:
            copies[2, k].wait()
        part = dot_last(active, w_buf[2, cols]).astype(BF)
        pm_ref[:, cols] = part[:half]
        po_ref[:, cols] = part[half:]


def first_kernel(
    which_ref, spots_ref, rows_ref, gain_ref, w_ref, pm_ref, po_ref, gate_ref, upper_ref, w_buf, xm_ref, xo_ref, normed, sems, row_sems
):
    size = chunk_of(w_buf.shape[1])
    which = which_ref[0]
    moves = [
        pltpu.make_async_copy(rows_ref.at[spots_ref[i]], ref, row_sems.at[i]) for i, ref in enumerate((xm_ref, xo_ref))
    ]
    for move in moves:
        move.start()
    copies = weight_copies(which, w_ref, w_buf, sems, size)
    for group in ((0, 1), (2,)):
        for k in range(w_buf.shape[1] // size):
            for matrix in group:
                copies[matrix, k].start()
    for move in moves:
        move.wait()
    gain = gain_ref.at[which]
    forward_math(copies, xm_ref, xo_ref, gain, w_buf, pm_ref, po_ref, gate_ref, upper_ref, normed)


def forward_kernel(xm_ref, xo_ref, gain_ref, w_buf, pm_ref, po_ref, gate_ref, upper_ref, normed):
    forward_math(None, xm_ref, xo_ref, gain_ref, w_buf, pm_ref, po_ref, gate_ref, upper_ref, normed)


def load_kernel(which_ref, spots_ref, rows_ref, cot_ref, w_ref, w_buf, xs_ref, us_ref, sems, row_sems):
    copies = list(weight_copies(which_ref[0], w_ref, w_buf, sems, w_buf.shape[1]).values())
    for i in range(xs_ref.shape[0]):
        spot = spots_ref[i]
        copies.append(pltpu.make_async_copy(cot_ref.at[spot], us_ref.at[i], row_sems.at[0, i]))
        copies.append(pltpu.make_async_copy(rows_ref.at[spot], xs_ref.at[i], row_sems.at[1, i]))
    for copy in copies:
        copy.start()
    for copy in copies:
        copy.wait()


def backward_kernel(recompute, um_ref, uo_ref, a_ref, b_ref, gain_ref, w_buf, pm_ref, po_ref, normed):
    features = w_buf.shape[1]
    size = chunk_of(features)
    count = features // size
    half = um_ref.shape[0]
    d_active = None
    for k in range(count):
        cols = pl.ds(k * size, size)
        block = jnp.concatenate([um_ref[:, cols], uo_ref[:, cols]], axis=0)
        part = dot(block, w_buf[2, cols])
        d_active = part if d_active is None else d_active + part
    if recompute:
        fill_normed(a_ref, b_ref, gain_ref[...], normed)
        gate, upper = gate_upper(None, w_buf, normed, size)
    else:
        gate, upper = a_ref[...], b_ref[...]
    sig = jax.nn.sigmoid(gate)
    d_gate = (d_active * upper * (sig * (1.0 + gate * (1.0 - sig)))).astype(BF)
    d_upper = (d_active * (gate * sig)).astype(BF)
    for k in range(count):
        cols = pl.ds(k * size, size)
        part = (dot_last(d_gate, w_buf[0, cols]) + dot_last(d_upper, w_buf[1, cols])).astype(BF)
        pm_ref[:, cols] = part[:half]
        po_ref[:, cols] = part[half:]


def own_first_kernel(x_ref, gain_ref, w_ref, turned_ref, left_ref, right_ref, active_ref, w_buf, normed, sems):
    features = w_buf.shape[1]
    size = chunk_of(features)
    count = features // size
    copies = {}
    for k in range(count):
        rows = pl.ds(k * size, size)
        for matrix in range(2):
            copies[matrix, k] = pltpu.make_async_copy(
                w_ref.at[0, matrix, rows], w_buf.at[matrix, rows], sems.at[matrix, k]
            )
            copies[matrix, k].start()
    gain = gain_ref[...]
    pieces, half = x_ref.shape[:2]
    for piece in range(pieces):
        normed[piece * half : (piece + 1) * half] = norm_rows(x_ref[piece], gain)[2]
    gate, upper = gate_upper(copies, w_buf, normed, size)
    sig = jax.nn.sigmoid(gate)
    smooth = gate * sig
    left_ref[...] = upper * (sig * (1.0 + gate * (1.0 - sig)))
    right_ref[...] = smooth
    active_ref[...] = (smooth * upper).astype(BF)
    for k in range(count):
        cols = pl.ds(k * size, size)
        turned_ref[cols] = normed[:, cols].T


def own_last_kernel(near_ref, u_ref, turned_ref, left_ref, right_ref, active_ref, early_ref, late_ref, out_ref, d_act, out_buf, sems):
    features = turned_ref.shape[0]
    size = chunk_of(features)
    count = features // size
    pieces, half = u_ref.shape[:2]

    def upstream(cols):
        return jnp.concatenate([u_ref[piece, :, cols] for piece in range(pieces)], axis=0)

    def fill(w_ref):
        total = None
        for k in range(count):
            cols = pl.ds(k * size, size)
            part = dot(upstream(cols), w_ref[2, cols])
            total = part if total is None else total + part
        d_act[...] = total

    @pl.when(near_ref[0] == 1)
    def _():
        fill(early_ref)

    @pl.when(near_ref[0] == 0)
    def _():
        fill(late_ref)

    copies = []

    def send(matrix, k):
        rows = pl.ds(k * size, size)
        copy = pltpu.make_async_copy(out_buf.at[matrix, rows], out_ref.at[0, matrix, rows], sems.at[matrix, k])
        copy.start()
        copies.append(copy)

    active = active_ref[...]
    d_active = d_act[...]
    d_gate = (d_active * left_ref[...]).astype(BF)
    d_upper = (d_active * right_ref[...]).astype(BF)
    for k in range(count):
        cols = pl.ds(k * size, size)
        turned = turned_ref[cols]
        out_buf[0, cols] = dot(turned, d_gate).astype(BF)
        send(0, k)
        out_buf[1, cols] = dot(turned, d_upper).astype(BF)
        send(1, k)
        out_buf[2, cols] = dot_first(upstream(cols), active).astype(BF)
        send(2, k)
    for copy in copies:
        copy.wait()


def cost(flops, moved):
    return pl.CostEstimate(flops=flops, bytes_accessed=moved, transcendentals=0)


def layer_outputs(half, features, narrow):
    return [jax.ShapeDtypeStruct((half, features), BF)] * 2 + [jax.ShapeDtypeStruct((2 * half, narrow), F32)] * 2


def first_layer(which, spots, blocks, gains, weights):
    half, features = blocks.shape[1:]
    narrow = weights.shape[-1]
    rows = jax.ShapeDtypeStruct((half, features), BF)
    return pl.pallas_call(
        first_kernel,
        out_shape=layer_outputs(half, features, narrow) + [pltpu.VMEM((3, features, narrow), BF), rows, rows],
        in_specs=[SMEM_SPEC, SMEM_SPEC, HBM_SPEC, VMEM_SPEC, HBM_SPEC],
        out_specs=[VMEM_SPEC] * 7,
        scratch_shapes=[
            pltpu.VMEM((2 * half, features), BF),
            pltpu.SemaphoreType.DMA((3, features // chunk_of(features))),
            pltpu.SemaphoreType.DMA((2,)),
        ],
        cost_estimate=cost(12 * half * features * narrow, 6 * features * narrow),
        compiler_params=PARAMS,
        name="first_layer",
    )(which, spots, blocks, gains, weights)


def load_late(which, spots, blocks, cot_blocks, weights):
    features, narrow = weights.shape[-2:]
    rows = jax.ShapeDtypeStruct((spots.shape[0],) + blocks.shape[1:], BF)
    return pl.pallas_call(
        load_kernel,
        out_shape=[pltpu.VMEM((3, features, narrow), BF), rows, rows],
        in_specs=[SMEM_SPEC, SMEM_SPEC, HBM_SPEC, HBM_SPEC, HBM_SPEC],
        out_specs=[VMEM_SPEC] * 3,
        scratch_shapes=[pltpu.SemaphoreType.DMA((3, 1)), pltpu.SemaphoreType.DMA((2, spots.shape[0]))],
        cost_estimate=cost(0, 10 * features * narrow),
        compiler_params=PARAMS,
        name="load_late",
    )(which, spots, blocks, cot_blocks, weights)


def forward_layer(xm, xo, gain, held):
    half, features = xm.shape
    narrow = held.shape[-1]
    return pl.pallas_call(
        forward_kernel,
        out_shape=layer_outputs(half, features, narrow),
        in_specs=[VMEM_SPEC] * 4,
        out_specs=[VMEM_SPEC] * 4,
        scratch_shapes=[pltpu.VMEM((2 * half, features), BF)],
        cost_estimate=cost(12 * half * features * narrow, 6 * features * narrow),
        compiler_params=PARAMS,
        name="forward_layer",
    )(xm, xo, gain, held)


def backward_layer(um, uo, a, b, gain, held, recompute):
    half, features = um.shape
    narrow = held.shape[-1]
    return pl.pallas_call(
        functools.partial(backward_kernel, recompute),
        out_shape=[jax.ShapeDtypeStruct((half, features), BF)] * 2,
        in_specs=[VMEM_SPEC] * 6,
        out_specs=[VMEM_SPEC] * 2,
        scratch_shapes=[pltpu.VMEM((2 * half, features), BF)],
        cost_estimate=cost(12 * half * features * narrow, 6 * features * narrow),
        compiler_params=PARAMS,
        name="backward_full" if recompute else "backward_layer",
    )(um, uo, a, b, gain, held)


def own_first(pieces, gain, weights):
    count, half, features = pieces.shape
    narrow = weights.shape[-1]
    rows = count * half
    return pl.pallas_call(
        own_first_kernel,
        out_shape=[
            jax.ShapeDtypeStruct((features, rows), BF),
            jax.ShapeDtypeStruct((rows, narrow), F32),
            jax.ShapeDtypeStruct((rows, narrow), F32),
            jax.ShapeDtypeStruct((rows, narrow), BF),
        ],
        in_specs=[VMEM_SPEC, VMEM_SPEC, HBM_SPEC],
        out_specs=[VMEM_SPEC] * 4,
        scratch_shapes=[
            pltpu.VMEM((2, features, narrow), BF),
            pltpu.VMEM((rows, features), BF),
            pltpu.SemaphoreType.DMA((2, features // chunk_of(features))),
        ],
        cost_estimate=cost(4 * rows * features * narrow, 8 * features * narrow),
        compiler_params=PARAMS,
        name="own_first",
    )(pieces, gain, weights)


def own_last(near, pieces, turned, left, right, active, early, late):
    count, half, features = pieces.shape
    narrow = left.shape[-1]
    rows = count * half
    return pl.pallas_call(
        own_last_kernel,
        out_shape=jax.ShapeDtypeStruct((1, 3, features, narrow), BF),
        in_specs=[SMEM_SPEC] + [VMEM_SPEC] * 7,
        out_specs=HBM_SPEC,
        scratch_shapes=[
            pltpu.VMEM((rows, narrow), F32),
            pltpu.VMEM((3, features, narrow), BF),
            pltpu.SemaphoreType.DMA((3, features // chunk_of(features))),
        ],
        cost_estimate=cost(8 * rows * features * narrow, 8 * features * narrow),
        compiler_params=PARAMS,
        name="own_last",
    )(near, pieces, turned, left, right, active, early, late)


def body(inputs, cotangent, section_weights, section_gains):
    sections = lax.axis_size("pipe") // REPL
    ranks = lax.axis_size("tensor")
    pipe = lax.axis_index("pipe")
    tensor = lax.axis_index("tensor")
    position = pipe % sections
    replica = pipe // sections
    middle = sections // 2
    near = position < middle
    side = jnp.where(near, 0, 1)
    kind = jnp.where(near, position, sections - 1 - position)
    outer = kind == 0
    core = tensor % 2
    chip = tensor // 2
    weights = pltpu.with_memory_space_constraint(section_weights[0], pltpu.HBM)
    own_gain = section_gains[0, 0][None]
    far_gain = section_gains[0, 1][None]
    gain_rows = (jnp.where(near, own_gain, far_gain), jnp.where(near, far_gain, own_gain))
    rows, features = inputs.shape[2:]
    group = rows // 2
    early = side.astype(jnp.int32).reshape(1)
    late = 1 - early
    core_swap = [(i, i ^ 1) for i in range(ranks)]
    chip_swap = [(i, (i + 2) % ranks) for i in range(ranks)]

    def swap_core(block):
        return lax.ppermute(block, "tensor", core_swap)

    def place(copy, end, c, rank):
        spot = c if end == 0 else sections - 1 - c
        return (copy * sections + spot) * ranks + rank

    def hop(block, source, target, turn, other):
        pairs = []
        for copy in range(REPL):
            for end in range(2):
                for rank in range(ranks):
                    arrival = (rank + 2) % ranks if other else rank
                    pairs.append((place(copy, end, source, rank), place(copy, end ^ turn, target, arrival)))
        return lax.ppermute(block, ("pipe", "tensor"), pairs)

    def exchange(payload, turn, across, wanted):
        pairs = []
        for copy in range(REPL):
            for end in range(2):
                for c in range(middle):
                    if not wanted(c, end):
                        continue
                    for rank in range(ranks):
                        pairs.append(
                            (place((copy + across) % REPL, end ^ turn, c, rank), place(copy, end, c, rank))
                        )
        return lax.ppermute(payload, ("pipe", "tensor"), pairs)

    def collect(early_rows, late_rows, wanted):
        same = jnp.where(near, early_rows, late_rows)
        opposite = jnp.where(near, late_rows, early_rows)
        return [
            exchange(opposite, 1, 0, wanted),
            exchange(same, 0, 1, wanted),
            exchange(opposite, 1, 1, wanted),
        ]

    def both_cores(arrived):
        arrived = jnp.stack(arrived)
        return arrived, swap_core(arrived)

    def transition(part_mine, part_other, finish, source, target, beside, during=()):
        received = swap_core(part_other)
        held = finish(part_mine.astype(F32) + received.astype(F32))
        round_result = None
        if source == target:
            held, payload, during = lax.optimization_barrier((held, beside[0], during))
            crossed = lax.ppermute(held, "tensor", chip_swap)
            mine = (held.astype(F32) + crossed.astype(F32)).astype(BF)
            round_result = collect(*payload, beside[1])
            other, round_result = lax.optimization_barrier((swap_core(mine), round_result))
        else:
            blocks = [held[:group], held[group:]]
            straight = [hop(blocks[turn], source, target, turn, False) for turn in range(2)]
            crossed = [hop(blocks[turn], source, target, turn, True) for turn in range(2)]
            straight, crossed, during = lax.optimization_barrier((straight, crossed, during))
            mine = jnp.concatenate(straight, axis=0).astype(F32) + jnp.concatenate(crossed, axis=0).astype(F32)
            mine = mine.astype(BF)
            other = swap_core(mine)
        return mine, other, round_result, during

    def all_spots():
        spots = []
        for batch in (core, 1 - core):
            for across, turn in ((0, 0), (0, 1), (1, 0), (1, 1)):
                copy = (replica + across) % REPL
                spots.append((copy * 2 + (side ^ turn)) * 2 + batch)
        return jnp.stack([spots[i] for i in (0, 4, 1, 2, 3, 5, 6, 7)]).astype(jnp.int32)

    def kind_of(step):
        return min(step, sections - 1 - step)

    def pick(step, new, old):
        if old is None:
            return new
        live = kind == kind_of(step)
        return jax.tree.map(lambda a, b: jnp.where(live, a, b), new, old)

    def lay(own, arrived):
        return jnp.concatenate([jnp.stack(own), arrived[0], arrived[1]], axis=0)

    spots = all_spots()
    blocks = pltpu.with_memory_space_constraint(inputs.reshape(-1, rows, features), pltpu.HBM)
    cot_blocks = pltpu.with_memory_space_constraint(cotangent.reshape(-1, rows, features), pltpu.HBM)
    gains = section_gains[0][:, None]
    states = [None, None]
    gates = [None, None]
    held = [None, None]
    *outputs, held[0], mine, other = first_layer(early, spots[:2], blocks, gains, weights)
    loaded = load_late(late, spots, blocks, cot_blocks, weights)
    for step in range(sections - 1):
        part = 0 if step < middle else 1
        states[part] = pick(step, (mine, other), states[part])
        if step > 0:
            outputs = forward_layer(mine, other, gain_rows[part], held[part])
        part_mine, part_other, gate, upper = outputs
        gates[part] = pick(step, (gate, upper), gates[part])
        residual = jnp.where(chip == 0, mine.astype(F32), 0.0)
        mine, other, arrived, during = transition(
            part_mine,
            part_other,
            lambda summed: (summed + residual).astype(BF),
            kind_of(step),
            kind_of(step + 1),
            ((states[0][0], states[0][0]), lambda c, end: c > 0 and end == 0),
            loaded if step == 0 else (),
        )
        if step == 0:
            held[1], input_rows, cot_rows = during
        if arrived:
            arrived_early = both_cores(arrived)
    states[1] = pick(sections - 1, (mine, other), states[1])
    arrived_late = both_cores(collect(states[1][0], states[1][0], lambda c, end: c > 0 and end == 1))

    up_mine, up_other = cot_rows[0], cot_rows[1]
    ups = [None, None]
    for step in range(sections - 1, 0, -1):
        part = 0 if step < middle else 1
        ups[part] = pick(step, (up_mine, up_other), ups[part])
        last = step == sections - 1
        first, second = states[part] if last else gates[part]
        part_mine, part_other = backward_layer(
            up_mine, up_other, first, second, gain_rows[part], held[part], last
        )
        unit, root, _ = norm_rows(states[part][0], gain_rows[part])
        upward = jnp.where(chip == 0, up_mine.astype(F32), 0.0)

        def finish(summed):
            d_unit = summed * gain_rows[part]
            d_state = (d_unit - unit * jnp.mean(d_unit * unit, axis=-1, keepdims=True)) / root
            return (upward + d_state).astype(BF)

        mixed = jnp.where(outer, states[1][0], ups[1][0])
        during = ()
        if step == middle:
            during = arrived_late
        if step == 1:
            own_state = [jnp.where(near, a, b) for a, b in zip(*states)]
            arrived_own = [
                jnp.where(near, a, jnp.where(outer, c, b))
                for a, b, c in zip(arrived_early, arrived_late, arrived_mixed)
            ]
            state = jnp.where(outer & near, input_rows, lay(own_state, arrived_own))
            during = own_first(state, own_gain, weights)
        up_mine, up_other, arrived, during = transition(
            part_mine,
            part_other,
            finish,
            kind_of(step),
            kind_of(step - 1),
            ((mixed, mixed), lambda c, end: end == 1),
            during,
        )
        if step == middle:
            arrived_late = during
            arrived_mixed = both_cores(arrived)
    turned, left, right, active = during
    ups[0] = pick(0, (up_mine, up_other), ups[0])

    final_ups = both_cores(collect(ups[0][0], ups[0][0], lambda c, end: end == 0))
    own_up = [jnp.where(near, a, b) for a, b in zip(*ups)]
    arrived = [jnp.where(near, a, b) for a, b in zip(final_ups, arrived_mixed)]
    upstream = jnp.where(outer & ~near, cot_rows, lay(own_up, arrived))
    is_near = near.astype(jnp.int32).reshape(1)
    return own_last(is_near, upstream, turned, left, right, active, held[0], held[1])


def solution(mesh):
    return jax.shard_map(
        body,
        mesh=mesh,
        in_specs=(P(), P(), P("pipe", None, None, None, "tensor"), P("pipe", None, None)),
        out_specs=P("pipe", None, None, "tensor"),
        check_vma=False,
    )
```

```python
import functools

import jax
import jax.numpy as jnp
from jax import lax
from jax.experimental import pallas as pl
from jax.experimental.pallas import tpu as pltpu
from jax.sharding import PartitionSpec as P

REPL = 2
EPS = 1e-06
BF = jnp.bfloat16
F32 = jnp.float32
SMEM_SPEC = pl.BlockSpec(memory_space=pltpu.SMEM)
VMEM_SPEC = pl.BlockSpec(memory_space=pltpu.VMEM)
HBM_SPEC = pl.BlockSpec(memory_space=pltpu.HBM)
MIB = 1024 * 1024
NEAR, OUTER, FIRST_CHIP, KIND, OWN, TOP, BOTTOM = 1, 2, 3, 4, 5, 13, 21


def chunk_of(features):
    for size in (512, 256, 128):
        if features % size == 0:
            return size
    return features


def norm_rows(rows, gain_row):
    widened = rows.astype(F32)
    root = jnp.sqrt(jnp.mean(widened * widened, axis=-1, keepdims=True) + EPS)
    unit = widened / root
    return unit, root, (unit * gain_row).astype(BF)


def dot(left, right):
    return jnp.dot(left, right, preferred_element_type=F32)


def dot_last(left, right):
    return lax.dot_general(left, right, (((1,), (1,)), ((), ())), preferred_element_type=F32)


def dot_first(left, right):
    return lax.dot_general(left, right, (((0,), (0,)), ((), ())), preferred_element_type=F32)


def gain_at(flags_ref, gains_ref, part):
    first = flags_ref[NEAR] == 1 - part
    return jnp.where(first, gains_ref[0:1], gains_ref[1:2])


def own_index(flags_ref, part):
    return jnp.where(flags_ref[NEAR] == 1 - part, 0, 1)


def choose(condition, first, second):
    return jnp.where(condition, first, second)


def weight_copies(which, w_ref, w_buf, sems, size):
    features = w_buf.shape[1]
    copies = {}
    for matrix in range(3):
        for k in range(features // size):
            rows = pl.ds(k * size, size)
            copies[matrix, k] = pltpu.make_async_copy(
                w_ref.at[which, matrix, rows], w_buf.at[matrix, rows], sems.at[matrix, k]
            )
    return copies


def fill_normed(xm_ref, xo_ref, gain, normed):
    half = xm_ref.shape[0]
    normed[:half] = norm_rows(xm_ref[...], gain)[2]
    normed[half:] = norm_rows(xo_ref[...], gain)[2]


def gate_upper(copies, w_buf, normed, size):
    gate = upper = None
    for k in range(w_buf.shape[1] // size):
        cols = pl.ds(k * size, size)
        if copies:
            copies[0, k].wait()
            copies[1, k].wait()
        block = normed[:, cols]
        gate_k = dot(block, w_buf[0, cols])
        upper_k = dot(block, w_buf[1, cols])
        gate = gate_k if gate is None else gate + gate_k
        upper = upper_k if upper is None else upper + upper_k
    return gate, upper


def forward_math(copies, xm_ref, xo_ref, gain, w_buf, pm_ref, po_ref, normed):
    size = chunk_of(w_buf.shape[1])
    half = xm_ref.shape[0]
    fill_normed(xm_ref, xo_ref, gain, normed)
    gate, upper = gate_upper(copies, w_buf, normed, size)
    active = (gate * jax.nn.sigmoid(gate) * upper).astype(BF)
    for k in range(w_buf.shape[1] // size):
        cols = pl.ds(k * size, size)
        if copies:
            copies[2, k].wait()
        part = dot_last(active, w_buf[2, cols]).astype(BF)
        pm_ref[:, cols] = part[:half]
        po_ref[:, cols] = part[half:]
    return gate, upper


def first_kernel(
    flags_ref, rows_ref, gains_ref, w_ref, pm_ref, po_ref, gate_ref, upper_ref, w_buf, xm_ref, xo_ref, normed, sems, row_sems
):
    size = chunk_of(w_buf.shape[1])
    moves = [
        pltpu.make_async_copy(rows_ref.at[flags_ref[OWN + i]], ref, row_sems.at[i])
        for i, ref in enumerate((xm_ref, xo_ref))
    ]
    for move in moves:
        move.start()
    copies = weight_copies(own_index(flags_ref, 0), w_ref, w_buf, sems, size)
    for group in ((0, 1), (2,)):
        for k in range(w_buf.shape[1] // size):
            for matrix in group:
                copies[matrix, k].start()
    for move in moves:
        move.wait()
    gain = gain_at(flags_ref, gains_ref, 0)
    gate_ref[...], upper_ref[...] = forward_math(copies, xm_ref, xo_ref, gain, w_buf, pm_ref, po_ref, normed)


def load_kernel(flags_ref, rows_ref, cot_ref, w_ref, w_buf, xs_ref, us_ref, um_ref, uo_ref, sems, row_sems):
    copies = list(weight_copies(own_index(flags_ref, 1), w_ref, w_buf, sems, w_buf.shape[1]).values())
    pieces, rows = xs_ref.shape[:2]
    group = rows // 2
    for i in range(pieces):
        spot = flags_ref[OWN + i]
        copies.append(pltpu.make_async_copy(cot_ref.at[spot], us_ref.at[i], row_sems.at[0, i]))
        for half, base in enumerate((TOP, BOTTOM)):
            part = pl.ds(half * group, group)
            copies.append(
                pltpu.make_async_copy(
                    rows_ref.at[flags_ref[base + i], part], xs_ref.at[i, part], row_sems.at[1 + half, i]
                )
            )
    for i, ref in enumerate((um_ref, uo_ref)):
        copies.append(pltpu.make_async_copy(cot_ref.at[flags_ref[OWN + i]], ref, row_sems.at[3, i]))
    for copy in copies:
        copy.start()
    for copy in copies:
        copy.wait()


def forward_kernel(part, live, flags_ref, xm_ref, xo_ref, gains_ref, w_buf, *refs):
    *old, pm_ref, po_ref, gate_ref, upper_ref, xms_ref, xos_ref, normed = refs
    gain = gain_at(flags_ref, gains_ref, part)
    gate, upper = forward_math(None, xm_ref, xo_ref, gain, w_buf, pm_ref, po_ref, normed)
    found = (gate, upper, xm_ref[...], xo_ref[...])
    outs = (gate_ref, upper_ref, xms_ref, xos_ref)
    if old:
        is_live = flags_ref[KIND] == live
        found = [choose(is_live, a, b[...]) for a, b in zip(found, old)]
    for out, value in zip(outs, found):
        out[...] = value


def backward_math(um_ref, uo_ref, gate_of, w_buf, pm_ref, po_ref):
    size = chunk_of(w_buf.shape[1])
    count = w_buf.shape[1] // size
    half = um_ref.shape[0]
    d_active = None
    for k in range(count):
        cols = pl.ds(k * size, size)
        block = jnp.concatenate([um_ref[:, cols], uo_ref[:, cols]], axis=0)
        part = dot(block, w_buf[2, cols])
        d_active = part if d_active is None else d_active + part
    gate, upper = gate_of()
    sig = jax.nn.sigmoid(gate)
    d_gate = (d_active * upper * (sig * (1.0 + gate * (1.0 - sig)))).astype(BF)
    d_upper = (d_active * (gate * sig)).astype(BF)
    for k in range(count):
        cols = pl.ds(k * size, size)
        part = (dot_last(d_gate, w_buf[0, cols]) + dot_last(d_upper, w_buf[1, cols])).astype(BF)
        pm_ref[:, cols] = part[:half]
        po_ref[:, cols] = part[half:]


def turn_kernel(
    flags_ref, um_ref, uo_ref, xm_ref, xo_ref, early_ref, oldm_ref, oldo_ref, gains_ref, w_buf,
    pm_ref, po_ref, latem_ref, lateo_ref, same_ref, opposite_ref, normed
):
    gain = gain_at(flags_ref, gains_ref, 1)

    def gate_of():
        fill_normed(xm_ref, xo_ref, gain, normed)
        return gate_upper(None, w_buf, normed, chunk_of(w_buf.shape[1]))

    backward_math(um_ref, uo_ref, gate_of, w_buf, pm_ref, po_ref)
    is_outer = flags_ref[OUTER] == 1
    is_near = flags_ref[NEAR] == 1
    late = choose(is_outer, xm_ref[...], oldm_ref[...])
    latem_ref[...] = late
    lateo_ref[...] = choose(is_outer, xo_ref[...], oldo_ref[...])
    same_ref[...] = choose(is_near, early_ref[...], late)
    opposite_ref[...] = choose(is_near, late, early_ref[...])


def backward_kernel(live, has_old, has_mixed, flags_ref, um_ref, uo_ref, gate_ref, upper_ref, w_buf, *refs):
    refs = list(refs)
    old = [refs.pop(0) for _ in range(2)] if has_old else []
    late = refs.pop(0) if has_mixed else None
    pm_ref, po_ref, ums_ref, uos_ref = refs[:4]
    backward_math(um_ref, uo_ref, lambda: (gate_ref[...], upper_ref[...]), w_buf, pm_ref, po_ref)
    found = [um_ref[...], uo_ref[...]]
    if old:
        is_live = flags_ref[KIND] == live
        found = [choose(is_live, a, b[...]) for a, b in zip(found, old)]
    ums_ref[...], uos_ref[...] = found
    if has_mixed:
        refs[4][...] = choose(flags_ref[OUTER] == 1, late[...], found[0])


def hold_kernel(part, backward, flags_ref, pm_ref, recv_ref, base_ref, *refs):
    summed = pm_ref[...].astype(F32) + recv_ref[...].astype(F32)
    if backward:
        state_ref, gains_ref, *outs = refs
        gain = gain_at(flags_ref, gains_ref, part)
        unit, root, _ = norm_rows(state_ref[...], gain)
        d_unit = summed * gain
        summed = (d_unit - unit * jnp.mean(d_unit * unit, axis=-1, keepdims=True)) / root
    else:
        outs = refs
    base = jnp.where(flags_ref[FIRST_CHIP] == 1, base_ref[...].astype(F32), 0.0)
    value = (summed + base).astype(BF)
    rows = value.shape[0] // len(outs)
    for i, out in enumerate(outs):
        out[...] = value[i * rows : (i + 1) * rows]


def sum_kernel(*refs):
    *terms, out = refs
    count = len(terms) // 2
    rows = out.shape[0] // count
    for i in range(count):
        total = terms[i][...].astype(F32) + terms[count + i][...].astype(F32)
        out[i * rows : (i + 1) * rows] = total.astype(BF)


def own_first_kernel(
    flags_ref, xs_ref, em_ref, eo_ref, lm_ref, lo_ref, p0, p1, p2, p3, p4, p5, q0, q1, q2, q3, q4, q5, gains_ref, w_ref,
    turned_ref, left_ref, right_ref, active_ref, w_buf, normed, sems
):
    features = w_buf.shape[1]
    size = chunk_of(features)
    count = features // size
    copies = {}
    for k in range(count):
        rows = pl.ds(k * size, size)
        for matrix in range(2):
            copies[matrix, k] = pltpu.make_async_copy(
                w_ref.at[0, matrix, rows], w_buf.at[matrix, rows], sems.at[matrix, k]
            )
            copies[matrix, k].start()
    gain = gains_ref[0:1]
    pieces, half = xs_ref.shape[:2]
    is_near = flags_ref[NEAR] == 1
    is_outer = flags_ref[OUTER] == 1
    inputs_used = jnp.logical_and(is_near, is_outer)

    def put(piece, rows):
        normed[piece * half : (piece + 1) * half] = norm_rows(rows, gain)[2]

    @pl.when(inputs_used)
    def _():
        for piece in range(pieces):
            put(piece, xs_ref[piece])

    @pl.when(jnp.logical_not(inputs_used))
    def _():
        put(0, choose(is_near, em_ref[...], lm_ref[...]))
        put(1, choose(is_near, eo_ref[...], lo_ref[...]))
        for i, (p, q) in enumerate(zip((p0, p1, p2, p3, p4, p5), (q0, q1, q2, q3, q4, q5))):
            put(2 + i, choose(is_outer, q[...], p[...]))

    gate, upper = gate_upper(copies, w_buf, normed, size)
    sig = jax.nn.sigmoid(gate)
    smooth = gate * sig
    left_ref[...] = upper * (sig * (1.0 + gate * (1.0 - sig)))
    right_ref[...] = smooth
    active_ref[...] = (smooth * upper).astype(BF)
    for k in range(count):
        cols = pl.ds(k * size, size)
        turned_ref[cols] = normed[:, cols].T


def own_last_kernel(flags_ref, us_ref, *refs):
    refs = list(refs)

    def take(count):
        return [refs.pop(0) for _ in range(count)]

    direct, early, late, r_in, q_in = take(8), take(2), take(2), take(6), take(6)
    turned_ref, left_ref, right_ref, active_ref, early_ref, late_ref = take(6)
    out_ref, u_buf, d_act, out_buf, sems = take(5)
    features = turned_ref.shape[0]
    size = chunk_of(features)
    count = features // size
    pieces, half = us_ref.shape[:2]
    is_near = flags_ref[NEAR] == 1
    is_outer = flags_ref[OUTER] == 1

    def fill(sources, w_ref):
        for i in range(pieces):
            u_buf[i * half : (i + 1) * half] = sources[i][...]
        total = None
        for k in range(count):
            cols = pl.ds(k * size, size)
            part = dot(u_buf[:, cols], w_ref[2, cols])
            total = part if total is None else total + part
        d_act[...] = total

    cases = (
        (True, True, direct, early_ref),
        (True, False, [us_ref.at[i] for i in range(pieces)], late_ref),
        (False, True, early + r_in, early_ref),
        (False, False, late + q_in, late_ref),
    )
    for outer, near, sources, w_ref in cases:

        @pl.when(jnp.logical_and(is_outer == outer, is_near == near))
        def _(sources=sources, w_ref=w_ref):
            fill(sources, w_ref)

    copies = []

    def send(matrix, k):
        rows = pl.ds(k * size, size)
        copy = pltpu.make_async_copy(out_buf.at[matrix, rows], out_ref.at[0, matrix, rows], sems.at[matrix, k])
        copy.start()
        copies.append(copy)

    active = active_ref[...]
    d_active = d_act[...]
    for k in range(count):
        cols = pl.ds(k * size, size)
        out_buf[2, cols] = dot_first(u_buf[:, cols], active).astype(BF)
        send(2, k)
    d_gate = (d_active * left_ref[...]).astype(BF)
    d_upper = (d_active * right_ref[...]).astype(BF)
    for k in range(count):
        cols = pl.ds(k * size, size)
        turned = turned_ref[cols]
        out_buf[0, cols] = dot(turned, d_gate).astype(BF)
        send(0, k)
        out_buf[1, cols] = dot(turned, d_upper).astype(BF)
        send(1, k)
    for copy in copies:
        copy.wait()


def call(kernel, name, operands, outs, scratch, limit, flops, moved, hbm=(), out_hbm=False):
    specs = [SMEM_SPEC] + [HBM_SPEC if i + 1 in hbm else VMEM_SPEC for i in range(len(operands) - 1)]
    out_spec = HBM_SPEC if out_hbm else VMEM_SPEC
    return pl.pallas_call(
        kernel,
        out_shape=outs,
        in_specs=specs,
        out_specs=[out_spec] * len(outs),
        scratch_shapes=scratch,
        cost_estimate=pl.CostEstimate(flops=flops, bytes_accessed=moved, transcendentals=0),
        compiler_params=pltpu.CompilerParams(vmem_limit_bytes=limit * MIB),
        name=name,
    )(*operands)


def body(inputs, cotangent, section_weights, section_gains):
    sections = lax.axis_size("pipe") // REPL
    ranks = lax.axis_size("tensor")
    pipe = lax.axis_index("pipe")
    tensor = lax.axis_index("tensor")
    position = pipe % sections
    replica = pipe // sections
    middle = sections // 2
    near = position < middle
    side = jnp.where(near, 0, 1)
    kind = jnp.where(near, position, sections - 1 - position)
    core = tensor % 2
    chip = tensor // 2
    rows, features = inputs.shape[2:]
    narrow = section_weights.shape[-1]
    group = rows // 2
    chunks = features // chunk_of(features)
    weights = pltpu.with_memory_space_constraint(section_weights[0], pltpu.HBM)
    blocks = pltpu.with_memory_space_constraint(inputs.reshape(-1, rows, features), pltpu.HBM)
    cot_blocks = pltpu.with_memory_space_constraint(cotangent.reshape(-1, rows, features), pltpu.HBM)
    gains = section_gains[0]
    core_swap = [(i, i ^ 1) for i in range(ranks)]
    chip_swap = [(i, (i + 2) % ranks) for i in range(ranks)]

    def spot(across, end, batch):
        return (((replica + across) % REPL) * 2 + end) * 2 + batch

    pairs = ((0, 0), (0, 1), (1, 0), (1, 1))
    own = [spot(across, side ^ turn, batch) for batch in (core, 1 - core) for across, turn in pairs]
    own = [own[i] for i in (0, 4, 1, 2, 3, 5, 6, 7)]
    top = [spot(across, end, batch) for batch in (core, 1 - core) for across, end in pairs]
    bottom = [spot(across, 1 - end, batch) for batch in (core, 1 - core) for across, end in pairs]
    flags = [side, near, kind == 0, chip == 0, kind] + own + top + bottom
    flags = jnp.stack([jnp.asarray(flag).astype(jnp.int32) for flag in flags])

    def swap_core(block):
        return lax.ppermute(block, "tensor", core_swap)

    def swap_chip(block):
        return lax.ppermute(block, "tensor", chip_swap)

    def place(copy, end, c, rank):
        at = c if end == 0 else sections - 1 - c
        return (copy * sections + at) * ranks + rank

    def send(block, route):
        moves = []
        for copy in range(REPL):
            for end in range(2):
                for c in range(middle):
                    source = route(copy, end, c)
                    if source is None:
                        continue
                    for rank in range(ranks):
                        came = (rank + 2) % ranks if source[3] else rank
                        moves.append((place(*source[:3], came), place(copy, end, c, rank)))
        return lax.ppermute(block, ("pipe", "tensor"), moves)

    def hop(block, source, target, turn, other):
        return send(block, lambda copy, end, c: (copy, end ^ turn, source, other) if c == target else None)

    def collect(same, opposite, wanted):
        def part(payload, turn, across):
            return send(
                payload,
                lambda copy, end, c: ((copy + across) % REPL, end ^ turn, c, False) if wanted(c, end) else None,
            )

        return [part(opposite, 1, 0), part(same, 0, 1), part(opposite, 1, 1)]

    def with_other_core(arrived):
        return arrived + [swap_core(block) for block in arrived]

    def shape(*extent, dtype=BF):
        return jax.ShapeDtypeStruct(extent, dtype)

    row = shape(rows, features)
    piece = shape(group, features)
    pieces = shape(4 * REPL, rows, features)
    gate_shape = shape(2 * rows, narrow, dtype=F32)
    held_shape = pltpu.VMEM((3, features, narrow), BF)
    normed_scratch = pltpu.VMEM((2 * rows, features), BF)
    layer_flops = 12 * rows * features * narrow
    layer_bytes = 6 * features * narrow
    row_bytes = 2 * rows * features

    def layer(kernel, name, operands, outs):
        return call(kernel, name, operands, outs, [normed_scratch], 8, layer_flops, layer_bytes)

    def hold(part, backward, split, operands):
        outs = [piece, piece] if split else [row]
        kernel = functools.partial(hold_kernel, part, backward)
        return call(kernel, "hold", [flags] + operands, outs, [], 4, 0, 4 * row_bytes)

    def total(terms):
        return pl.pallas_call(
            sum_kernel,
            out_shape=row,
            in_specs=[VMEM_SPEC] * len(terms),
            out_specs=VMEM_SPEC,
            cost_estimate=pl.CostEstimate(flops=0, bytes_accessed=3 * row_bytes, transcendentals=0),
            compiler_params=pltpu.CompilerParams(vmem_limit_bytes=4 * MIB),
            name="total",
        )(*terms)

    def kind_of(step):
        return min(step, sections - 1 - step)

    def across(held, source, target, during):
        straight = [hop(held[turn], source, target, turn, False) for turn in range(2)]
        crossed = [hop(held[turn], source, target, turn, True) for turn in range(2)]
        straight, crossed, during = lax.optimization_barrier((straight, crossed, during))
        mine = total(straight + crossed)
        return mine, swap_core(mine), during

    pm, po, gate, upper, held_early, mine, other = call(
        first_kernel,
        "first_layer",
        [flags, blocks, gains, weights],
        [row, row, gate_shape, gate_shape, held_shape, row, row],
        [normed_scratch, pltpu.SemaphoreType.DMA((3, chunks)), pltpu.SemaphoreType.DMA((2,))],
        8,
        layer_flops,
        layer_bytes,
        hbm=(1, 3),
    )
    saved = [(gate, upper, mine, other), None]
    loaded = call(
        load_kernel,
        "load_late",
        [flags, blocks, cot_blocks, weights],
        [held_shape, pieces, pieces, row, row],
        [pltpu.SemaphoreType.DMA((3, 1)), pltpu.SemaphoreType.DMA((4, 4 * REPL))],
        4,
        0,
        2 * layer_bytes,
        hbm=(1, 2, 3),
    )
    for step in range(sections - 1):
        part = 0 if step < middle else 1
        if step > 0:
            old = list(saved[part] or ())
            pm, po, *saved[part] = layer(
                functools.partial(forward_kernel, part, kind_of(step)),
                "forward_layer",
                [flags, mine, other, gains, held_late if part else held_early] + old,
                [row, row, gate_shape, gate_shape, row, row],
            )
        same_kind = step == middle - 1
        held = hold(part, False, not same_kind, [pm, swap_core(po), mine])
        if same_kind:
            mine = total([held[0], swap_chip(held[0])])
            other = swap_core(mine)
        else:
            mine, other, during = across(held, kind_of(step), kind_of(step + 1), loaded if step == 0 else ())
        if step == 0:
            held_late, input_rows, cot_rows, up_mine, up_other = during

    early_rows = saved[0][2:]
    gates = [saved[0][:2], saved[1][:2]]
    pm, po, late_mine, late_other, same, opposite = layer(
        turn_kernel,
        "turn_layer",
        [flags, up_mine, up_other, mine, other, early_rows[0], *saved[1][2:], gains, held_late],
        [row] * 6,
    )
    state_mine = [early_rows[0], late_mine]
    ups = [None, (up_mine, up_other)]
    for step in range(sections - 1, 0, -1):
        part = 0 if step < middle else 1
        if step < sections - 1:
            old = list(ups[part] or ())
            mixes = [late_mine] if step == middle else []
            pm, po, *kept = layer(
                functools.partial(backward_kernel, kind_of(step), bool(old), bool(mixes)),
                "backward_layer",
                [flags, up_mine, up_other, *gates[part], held_late if part else held_early] + old + mixes,
                [row] * (5 if mixes else 4),
            )
            ups[part] = kept[:2]
            if mixes:
                mixed = kept[2]
        local = step == middle or step == 1
        operands = [pm, swap_core(po), up_mine, state_mine[part], gains]
        held = hold(part, True, not local, operands)
        if step == middle:
            block, mixed = lax.optimization_barrier((held[0], mixed))
            up_mine = total([block, swap_chip(block)])
            q_arrived = collect(mixed, mixed, lambda c, end: end == 1)
            up_other, p_arrived = lax.optimization_barrier((swap_core(up_mine), p_arrived))
        elif step > 1:
            up_mine, up_other, _ = across(held, kind_of(step), kind_of(step - 1), ())
            if step == middle + 1:
                up_mine, same, opposite = lax.optimization_barrier((up_mine, same, opposite))
                p_arrived = collect(same, opposite, lambda c, end: c > 0)
        else:
            block, turned_up = lax.optimization_barrier((held[0], ups[0][0]))
            mine = total([block, swap_chip(block)])
            r_arrived = collect(turned_up, turned_up, lambda c, end: c > 0 and end == 0)
            mine, q_arrived = lax.optimization_barrier((mine, q_arrived))
    straight = [
        send(
            mine,
            lambda copy, end, c, shift=shift, source=source: (
                ((copy + shift) % REPL, source, 1, False) if c == 0 and end == 0 else None
            ),
        )
        for shift, source in pairs
    ]
    p_all = with_other_core(p_arrived)
    q_all = with_other_core(q_arrived)
    own_rows = 4 * REPL * rows
    prepared = call(
        own_first_kernel,
        "own_first",
        [flags, input_rows, *early_rows, late_mine, late_other, *p_all, *q_all, gains, weights],
        [
            shape(features, own_rows),
            shape(own_rows, narrow, dtype=F32),
            shape(own_rows, narrow, dtype=F32),
            shape(own_rows, narrow),
        ],
        [
            pltpu.VMEM((2, features, narrow), BF),
            pltpu.VMEM((own_rows, features), BF),
            pltpu.SemaphoreType.DMA((2, chunks)),
        ],
        12,
        4 * own_rows * features * narrow,
        8 * features * narrow,
        hbm=(19,),
    )
    straight, prepared = lax.optimization_barrier((straight, prepared))
    return call(
        own_last_kernel,
        "own_last",
        [flags, cot_rows, *with_other_core(straight), *ups[0], *ups[1], *with_other_core(r_arrived), *q_all]
        + [*prepared, held_early, held_late],
        [shape(1, 3, features, narrow)],
        [
            pltpu.VMEM((own_rows, features), BF),
            pltpu.VMEM((own_rows, narrow), F32),
            pltpu.VMEM((3, features, narrow), BF),
            pltpu.SemaphoreType.DMA((3, chunks)),
        ],
        16,
        8 * own_rows * features * narrow,
        8 * features * narrow,
        out_hbm=True,
    )[0]


def solution(mesh):
    return jax.shard_map(
        body,
        mesh=mesh,
        in_specs=(P(), P(), P("pipe", None, None, None, "tensor"), P("pipe", None, None)),
        out_specs=P("pipe", None, None, "tensor"),
        check_vma=False,
    )
```

```python
import functools

import jax
import jax.numpy as jnp
from jax import lax
from jax.experimental import pallas as pl
from jax.experimental.pallas import tpu as pltpu
from jax.sharding import PartitionSpec as P

REPL = 2
EPS = 1e-06
BF = jnp.bfloat16
F32 = jnp.float32
SMEM_SPEC = pl.BlockSpec(memory_space=pltpu.SMEM)
VMEM_SPEC = pl.BlockSpec(memory_space=pltpu.VMEM)
HBM_SPEC = pl.BlockSpec(memory_space=pltpu.HBM)
MIB = 1024 * 1024
NEAR, OUTER, FIRST_CHIP, KIND, OWN, TOP, BOTTOM = 1, 2, 3, 4, 5, 13, 21


def chunk_of(features):
    for size in (512, 256, 128):
        if features % size == 0:
            return size
    return features


def norm_rows(rows, gain_row):
    widened = rows.astype(F32)
    root = jnp.sqrt(jnp.mean(widened * widened, axis=-1, keepdims=True) + EPS)
    unit = widened / root
    return unit, root, (unit * gain_row).astype(BF)


def dot(left, right):
    return jnp.dot(left, right, preferred_element_type=F32)


def dot_last(left, right):
    return lax.dot_general(left, right, (((1,), (1,)), ((), ())), preferred_element_type=F32)


def dot_first(left, right):
    return lax.dot_general(left, right, (((0,), (0,)), ((), ())), preferred_element_type=F32)


def is_set(flags_ref, index, value=1):
    if len(flags_ref.shape) == 1:
        return flags_ref[index] == value
    return flags_ref[index : index + 1, 0:1] == value


def gain_at(flags_ref, gains_ref, part):
    return jnp.where(is_set(flags_ref, NEAR, 1 - part), gains_ref[0:1], gains_ref[1:2])


def own_index(flags_ref, part):
    return jnp.where(flags_ref[NEAR] == 1 - part, 0, 1)


def choose(condition, first, second):
    kept = first.dtype
    return jnp.where(condition, first.astype(F32), second.astype(F32)).astype(kept)


def weight_copies(which, w_ref, w_buf, sems, size):
    features = w_buf.shape[1]
    copies = {}
    for matrix in range(3):
        for k in range(features // size):
            rows = pl.ds(k * size, size)
            copies[matrix, k] = pltpu.make_async_copy(
                w_ref.at[which, matrix, rows], w_buf.at[matrix, rows], sems.at[matrix, k]
            )
    return copies


def fill_normed(xm_ref, xo_ref, gain, normed):
    half = xm_ref.shape[0]
    normed[:half] = norm_rows(xm_ref[...], gain)[2]
    normed[half:] = norm_rows(xo_ref[...], gain)[2]


def gate_upper(copies, w_buf, normed, size):
    gate = upper = None
    for k in range(w_buf.shape[1] // size):
        cols = pl.ds(k * size, size)
        if copies:
            copies[0, k].wait()
            copies[1, k].wait()
        block = normed[:, cols]
        gate_k = dot(block, w_buf[0, cols])
        upper_k = dot(block, w_buf[1, cols])
        gate = gate_k if gate is None else gate + gate_k
        upper = upper_k if upper is None else upper + upper_k
    return gate, upper


def forward_math(copies, xm_ref, xo_ref, gain, w_buf, pm_ref, po_ref, normed):
    size = chunk_of(w_buf.shape[1])
    half = xm_ref.shape[0]
    fill_normed(xm_ref, xo_ref, gain, normed)
    gate, upper = gate_upper(copies, w_buf, normed, size)
    active = (gate * jax.nn.sigmoid(gate) * upper).astype(BF)
    for k in range(w_buf.shape[1] // size):
        cols = pl.ds(k * size, size)
        if copies:
            copies[2, k].wait()
        part = dot_last(active, w_buf[2, cols]).astype(BF)
        pm_ref[:, cols] = part[:half]
        po_ref[:, cols] = part[half:]
    return gate, upper


def first_kernel(
    flags_ref, rows_ref, gains_ref, w_ref,
    pm_ref, po_ref, gate_ref, upper_ref, w_buf, xm_ref, xo_ref, marks_ref, normed, gains_buf, sems, row_sems
):
    size = chunk_of(w_buf.shape[1])
    moves = [
        pltpu.make_async_copy(rows_ref.at[flags_ref[OWN + i]], ref, row_sems.at[i])
        for i, ref in enumerate((xm_ref, xo_ref))
    ]
    moves.append(pltpu.make_async_copy(gains_ref, gains_buf, row_sems.at[2]))
    for move in moves:
        move.start()
    for i in range(marks_ref.shape[0]):
        marks_ref[i : i + 1] = jnp.full((1, marks_ref.shape[1]), flags_ref[i], jnp.int32)
    for move in moves:
        move.wait()
    copies = weight_copies(own_index(flags_ref, 0), w_ref, w_buf, sems, size)
    for group in ((0, 1), (2,)):
        for k in range(w_buf.shape[1] // size):
            for matrix in group:
                copies[matrix, k].start()
    gain = gain_at(flags_ref, gains_buf, 0)
    gate_ref[...], upper_ref[...] = forward_math(copies, xm_ref, xo_ref, gain, w_buf, pm_ref, po_ref, normed)


def load_kernel(flags_ref, rows_ref, cot_ref, w_ref, w_buf, xs_ref, us_ref, um_ref, uo_ref, sems, row_sems):
    copies = list(weight_copies(own_index(flags_ref, 1), w_ref, w_buf, sems, w_buf.shape[1]).values())
    pieces, rows = xs_ref.shape[:2]
    group = rows // 2
    for i in range(pieces):
        spot = flags_ref[OWN + i]
        copies.append(pltpu.make_async_copy(cot_ref.at[spot], us_ref.at[i], row_sems.at[0, i]))
        for half, base in enumerate((TOP, BOTTOM)):
            part = pl.ds(half * group, group)
            copies.append(
                pltpu.make_async_copy(
                    rows_ref.at[flags_ref[base + i], part], xs_ref.at[i, part], row_sems.at[1 + half, i]
                )
            )
    for i, ref in enumerate((um_ref, uo_ref)):
        copies.append(pltpu.make_async_copy(cot_ref.at[flags_ref[OWN + i]], ref, row_sems.at[3, i]))
    for copy in copies:
        copy.start()
    for copy in copies:
        copy.wait()


def forward_kernel(part, live, flags_ref, xm_ref, xo_ref, gains_ref, w_buf, *refs):
    *old, pm_ref, po_ref, gate_ref, upper_ref, xms_ref, xos_ref, normed = refs
    gain = gain_at(flags_ref, gains_ref, part)
    gate, upper = forward_math(None, xm_ref, xo_ref, gain, w_buf, pm_ref, po_ref, normed)
    found = (gate, upper, xm_ref[...], xo_ref[...])
    outs = (gate_ref, upper_ref, xms_ref, xos_ref)
    if old:
        is_live = is_set(flags_ref, KIND, live)
        found = [choose(is_live, a, b[...]) for a, b in zip(found, old)]
    for out, value in zip(outs, found):
        out[...] = value


def active_gradient(um_ref, uo_ref, w_buf):
    size = chunk_of(w_buf.shape[1])
    d_active = None
    for k in range(w_buf.shape[1] // size):
        cols = pl.ds(k * size, size)
        block = jnp.concatenate([um_ref[:, cols], uo_ref[:, cols]], axis=0)
        part = dot(block, w_buf[2, cols])
        d_active = part if d_active is None else d_active + part
    return d_active


def backward_math(d_active, gate, upper, w_buf, pm_ref, po_ref):
    size = chunk_of(w_buf.shape[1])
    half = pm_ref.shape[0]
    sig = jax.nn.sigmoid(gate)
    d_gate = (d_active * upper * (sig * (1.0 + gate * (1.0 - sig)))).astype(BF)
    d_upper = (d_active * (gate * sig)).astype(BF)
    for k in range(w_buf.shape[1] // size):
        cols = pl.ds(k * size, size)
        part = (dot_last(d_gate, w_buf[0, cols]) + dot_last(d_upper, w_buf[1, cols])).astype(BF)
        pm_ref[:, cols] = part[:half]
        po_ref[:, cols] = part[half:]


def cotangent_kernel(um_ref, uo_ref, w_buf, d_ref):
    d_ref[...] = active_gradient(um_ref, uo_ref, w_buf)


def turn_kernel(
    flags_ref, d_ref, xm_ref, xo_ref, oldm_ref, oldo_ref, gains_ref, w_buf, pm_ref, po_ref, latem_ref, lateo_ref, normed
):
    fill_normed(xm_ref, xo_ref, gain_at(flags_ref, gains_ref, 1), normed)
    gate, upper = gate_upper(None, w_buf, normed, chunk_of(w_buf.shape[1]))
    backward_math(d_ref[...], gate, upper, w_buf, pm_ref, po_ref)
    is_outer = is_set(flags_ref, OUTER)
    latem_ref[...] = choose(is_outer, xm_ref[...], oldm_ref[...])
    lateo_ref[...] = choose(is_outer, xo_ref[...], oldo_ref[...])


def backward_kernel(live, has_old, has_late, flags_ref, um_ref, uo_ref, gate_ref, upper_ref, w_buf, *refs):
    refs = list(refs)
    old = [refs.pop(0) for _ in range(2)] if has_old else []
    late = refs.pop(0) if has_late else None
    pm_ref, po_ref, ums_ref, uos_ref = refs[:4]
    backward_math(active_gradient(um_ref, uo_ref, w_buf), gate_ref[...], upper_ref[...], w_buf, pm_ref, po_ref)
    found = [um_ref[...], uo_ref[...]]
    if old:
        is_live = is_set(flags_ref, KIND, live)
        found = [choose(is_live, a, b[...]) for a, b in zip(found, old)]
    ums_ref[...], uos_ref[...] = found
    if has_late:
        is_near = is_set(flags_ref, NEAR)
        refs[4][...] = choose(is_near, found[0], late[...])
        refs[5][...] = choose(is_near, late[...], found[0])


def hold_kernel(part, backward, flags_ref, pm_ref, recv_ref, base_ref, *refs):
    summed = pm_ref[...].astype(F32) + recv_ref[...].astype(F32)
    if backward:
        state_ref, gains_ref, *outs = refs
        gain = gain_at(flags_ref, gains_ref, part)
        unit, root, _ = norm_rows(state_ref[...], gain)
        d_unit = summed * gain
        summed = (d_unit - unit * jnp.mean(d_unit * unit, axis=-1, keepdims=True)) / root
    else:
        outs = refs
    base = jnp.where(is_set(flags_ref, FIRST_CHIP), base_ref[...].astype(F32), 0.0)
    value = (summed + base).astype(BF)
    rows = value.shape[0] // len(outs)
    for i, out in enumerate(outs):
        out[...] = value[i * rows : (i + 1) * rows]


def sum_kernel(*refs):
    *terms, out = refs
    count = len(terms) // 2
    rows = out.shape[0] // count
    for i in range(count):
        total = terms[i][...].astype(F32) + terms[count + i][...].astype(F32)
        out[i * rows : (i + 1) * rows] = total.astype(BF)


def own_first_kernel(
    flags_ref, xs_ref, em_ref, eo_ref, lm_ref, lo_ref, p0, p1, p2, p3, p4, p5, q0, q1, q2, q3, q4, q5, gains_ref, w_ref,
    turned_ref, left_ref, right_ref, active_ref, w_buf, normed, sems
):
    features = w_buf.shape[1]
    size = chunk_of(features)
    count = features // size
    copies = {}
    for k in range(count):
        rows = pl.ds(k * size, size)
        for matrix in range(2):
            copies[matrix, k] = pltpu.make_async_copy(
                w_ref.at[0, matrix, rows], w_buf.at[matrix, rows], sems.at[matrix, k]
            )
            copies[matrix, k].start()
    gain = gains_ref[0:1]
    pieces, half = xs_ref.shape[:2]
    is_near = flags_ref[NEAR] == 1
    is_outer = flags_ref[OUTER] == 1
    inputs_used = jnp.logical_and(is_near, is_outer)

    def put(piece, rows):
        normed[piece * half : (piece + 1) * half] = norm_rows(rows, gain)[2]

    @pl.when(inputs_used)
    def _():
        for piece in range(pieces):
            put(piece, xs_ref[piece])

    @pl.when(jnp.logical_and(is_near, jnp.logical_not(is_outer)))
    def _():
        for i, ref in enumerate((em_ref, eo_ref, p0, p1, p2, p3, p4, p5)):
            put(i, ref[...])

    @pl.when(jnp.logical_not(is_near))
    def _():
        for i, ref in enumerate((lm_ref, lo_ref, q0, q1, q2, q3, q4, q5)):
            put(i, ref[...])

    gate, upper = gate_upper(copies, w_buf, normed, size)
    sig = jax.nn.sigmoid(gate)
    smooth = gate * sig
    left_ref[...] = upper * (sig * (1.0 + gate * (1.0 - sig)))
    right_ref[...] = smooth
    active_ref[...] = (smooth * upper).astype(BF)
    for k in range(count):
        cols = pl.ds(k * size, size)
        turned_ref[cols] = normed[:, cols].T


def own_last_kernel(flags_ref, us_ref, *refs):
    refs = list(refs)

    def take(count):
        return [refs.pop(0) for _ in range(count)]

    direct, early, late, arrived = take(8), take(2), take(2), take(6)
    turned_ref, left_ref, right_ref, active_ref, early_ref, late_ref = take(6)
    out_ref, u_buf, d_act, out_buf, sems = take(5)
    features = turned_ref.shape[0]
    size = chunk_of(features)
    count = features // size
    pieces, half = us_ref.shape[:2]
    is_near = flags_ref[NEAR] == 1
    is_outer = flags_ref[OUTER] == 1

    def fill(sources, w_ref):
        for i in range(pieces):
            u_buf[i * half : (i + 1) * half] = sources[i][...]
        total = None
        for k in range(count):
            cols = pl.ds(k * size, size)
            part = dot(u_buf[:, cols], w_ref[2, cols])
            total = part if total is None else total + part
        d_act[...] = total

    cases = (
        (True, True, direct, early_ref),
        (True, False, [us_ref.at[i] for i in range(pieces)], late_ref),
        (False, True, early + arrived, early_ref),
        (False, False, late + arrived, late_ref),
    )
    for outer, near, sources, w_ref in cases:

        @pl.when(jnp.logical_and(is_outer == outer, is_near == near))
        def _(sources=sources, w_ref=w_ref):
            fill(sources, w_ref)

    copies = []

    def send(matrix, k):
        rows = pl.ds(k * size, size)
        copy = pltpu.make_async_copy(out_buf.at[matrix, rows], out_ref.at[0, matrix, rows], sems.at[matrix, k])
        copy.start()
        copies.append(copy)

    active = active_ref[...]
    d_active = d_act[...]
    for k in range(count):
        cols = pl.ds(k * size, size)
        out_buf[2, cols] = dot_first(u_buf[:, cols], active).astype(BF)
        send(2, k)
    d_gate = (d_active * left_ref[...]).astype(BF)
    d_upper = (d_active * right_ref[...]).astype(BF)
    for k in range(count):
        cols = pl.ds(k * size, size)
        turned = turned_ref[cols]
        out_buf[0, cols] = dot(turned, d_gate).astype(BF)
        send(0, k)
        out_buf[1, cols] = dot(turned, d_upper).astype(BF)
        send(1, k)
    for copy in copies:
        copy.wait()


def call(kernel, name, operands, outs, scratch, limit, flops, moved, hbm=(), out_hbm=False, smem=(0,)):
    specs = [
        SMEM_SPEC if i in smem else HBM_SPEC if i in hbm else VMEM_SPEC for i in range(len(operands))
    ]
    out_spec = HBM_SPEC if out_hbm else VMEM_SPEC
    results = pl.pallas_call(
        kernel,
        out_shape=outs,
        in_specs=specs,
        out_specs=[out_spec] * len(outs),
        scratch_shapes=scratch,
        cost_estimate=pl.CostEstimate(flops=flops, bytes_accessed=moved, transcendentals=0),
        compiler_params=pltpu.CompilerParams(vmem_limit_bytes=limit * MIB),
        name=name,
    )(*operands)
    return list(results)


def body(inputs, cotangent, section_weights, section_gains):
    sections = lax.axis_size("pipe") // REPL
    ranks = lax.axis_size("tensor")
    pipe = lax.axis_index("pipe")
    tensor = lax.axis_index("tensor")
    position = pipe % sections
    replica = pipe // sections
    middle = sections // 2
    near = position < middle
    side = jnp.where(near, 0, 1)
    kind = jnp.where(near, position, sections - 1 - position)
    core = tensor % 2
    chip = tensor // 2
    rows, features = inputs.shape[2:]
    narrow = section_weights.shape[-1]
    group = rows // 2
    chunks = features // chunk_of(features)
    weights = pltpu.with_memory_space_constraint(section_weights[0], pltpu.HBM)
    blocks = pltpu.with_memory_space_constraint(inputs.reshape(-1, rows, features), pltpu.HBM)
    cot_blocks = pltpu.with_memory_space_constraint(cotangent.reshape(-1, rows, features), pltpu.HBM)
    gains = section_gains[0]
    core_swap = [(i, i ^ 1) for i in range(ranks)]
    chip_swap = [(i, (i + 2) % ranks) for i in range(ranks)]

    def spot(across, end, batch):
        return (((replica + across) % REPL) * 2 + end) * 2 + batch

    pairs = ((0, 0), (0, 1), (1, 0), (1, 1))
    own = [spot(across, side ^ turn, batch) for batch in (core, 1 - core) for across, turn in pairs]
    own = [own[i] for i in (0, 4, 1, 2, 3, 5, 6, 7)]
    top = [spot(across, end, batch) for batch in (core, 1 - core) for across, end in pairs]
    bottom = [spot(across, 1 - end, batch) for batch in (core, 1 - core) for across, end in pairs]
    flags = [side, near, kind == 0, chip == 0, kind] + own + top + bottom
    flags = jnp.stack([jnp.asarray(flag).astype(jnp.int32) for flag in flags])

    def swap_core(block):
        return lax.ppermute(block, "tensor", core_swap)

    def swap_chip(block):
        return lax.ppermute(block, "tensor", chip_swap)

    def place(copy, end, c, rank):
        at = c if end == 0 else sections - 1 - c
        return (copy * sections + at) * ranks + rank

    def send(block, route):
        moves = []
        for copy in range(REPL):
            for end in range(2):
                for c in range(middle):
                    source = route(copy, end, c)
                    if source is None:
                        continue
                    for rank in range(ranks):
                        came = (rank + 2) % ranks if source[3] else rank
                        moves.append((place(*source[:3], came), place(copy, end, c, rank)))
        return lax.ppermute(block, ("pipe", "tensor"), moves)

    def hop(block, source, target, turn, other):
        return send(block, lambda copy, end, c: (copy, end ^ turn, source, other) if c == target else None)

    def collect(same, opposite, wanted):
        def part(payload, turn, across):
            return send(
                payload,
                lambda copy, end, c: ((copy + across) % REPL, end ^ turn, c, False) if wanted(c, end) else None,
            )

        return [part(opposite, 1, 0), part(same, 0, 1), part(opposite, 1, 1)]

    def with_other_core(arrived):
        return arrived + [swap_core(block) for block in arrived]

    def shape(*extent, dtype=BF):
        return jax.ShapeDtypeStruct(extent, dtype)

    row = shape(rows, features)
    piece = shape(group, features)
    pieces = shape(4 * REPL, rows, features)
    gate_shape = shape(2 * rows, narrow, dtype=F32)
    held_shape = pltpu.VMEM((3, features, narrow), BF)
    normed_scratch = pltpu.VMEM((2 * rows, features), BF)
    layer_flops = 12 * rows * features * narrow
    layer_bytes = 6 * features * narrow
    row_bytes = 2 * rows * features

    def layer(kernel, name, operands, outs):
        return call(kernel, name, operands, outs, [normed_scratch], 8, layer_flops, layer_bytes, smem=())

    def hold(part, backward, split, operands):
        outs = [piece, piece] if split else [row]
        kernel = functools.partial(hold_kernel, part, backward)
        return call(kernel, "hold", [marks] + operands, outs, [], 4, 0, 4 * row_bytes, smem=())

    def total(terms):
        return call(sum_kernel, "total", terms, [row], [], 4, 0, 3 * row_bytes, smem=())[0]

    def kind_of(step):
        return min(step, sections - 1 - step)

    def across(held, source, target, during):
        straight = [hop(held[turn], source, target, turn, False) for turn in range(2)]
        crossed = [hop(held[turn], source, target, turn, True) for turn in range(2)]
        straight, crossed, during = lax.optimization_barrier((straight, crossed, during))
        mine = total(straight + crossed)
        return mine, swap_core(mine), during

    pm, po, gate, upper, held_early, mine, other, marks = call(
        first_kernel,
        "first_layer",
        [flags, blocks, pltpu.with_memory_space_constraint(gains, pltpu.HBM), weights],
        [row, row, gate_shape, gate_shape, held_shape, row, row, shape(8, 128, dtype=jnp.int32)],
        [
            normed_scratch,
            pltpu.VMEM(gains.shape, F32),
            pltpu.SemaphoreType.DMA((3, chunks)),
            pltpu.SemaphoreType.DMA((3,)),
        ],
        8,
        layer_flops,
        layer_bytes,
        hbm=(1, 2, 3),
    )
    saved = [(gate, upper, mine, other), None]
    loaded = call(
        load_kernel,
        "load_late",
        [flags, blocks, cot_blocks, weights],
        [held_shape, pieces, pieces, row, row],
        [pltpu.SemaphoreType.DMA((3, 1)), pltpu.SemaphoreType.DMA((4, 4 * REPL))],
        4,
        0,
        2 * layer_bytes,
        hbm=(1, 2, 3),
    )
    for step in range(sections - 1):
        part = 0 if step < middle else 1
        if step > 0:
            old = list(saved[part] or ())
            pm, po, *saved[part] = layer(
                functools.partial(forward_kernel, part, kind_of(step)),
                "forward_layer",
                [marks, mine, other, gains, held_late if part else held_early] + old,
                [row, row, gate_shape, gate_shape, row, row],
            )
        same_kind = step == middle - 1
        held = hold(part, False, not same_kind, [pm, swap_core(po), mine])
        during = ()
        if step == 0:
            during = loaded
        if step == middle:
            during = call(
                cotangent_kernel,
                "cotangent",
                [up_mine, up_other, held_late],
                [gate_shape],
                [],
                4,
                layer_flops // 3,
                layer_bytes // 3,
                smem=(),
            ) + with_other_core(early_arrived)
        if same_kind:
            block, early_mine = lax.optimization_barrier((held[0], saved[0][2]))
            mine = total([block, swap_chip(block)])
            early_arrived = collect(early_mine, early_mine, lambda c, end: c > 0 and end == 0)
            other, early_arrived = lax.optimization_barrier((swap_core(mine), early_arrived))
        else:
            mine, other, during = across(held, kind_of(step), kind_of(step + 1), during)
        if step == 0:
            held_late, input_rows, cot_rows, up_mine, up_other = during
        if step == middle:
            d_active, *early_arrived = during

    early_rows = saved[0][2:]
    gates = [saved[0][:2], saved[1][:2]]
    pm, po, late_mine, late_other = layer(
        turn_kernel,
        "turn_layer",
        [marks, d_active, mine, other, *saved[1][2:], gains, held_late],
        [row] * 4,
    )
    state_mine = [early_rows[0], late_mine]
    ups = [None, (up_mine, up_other)]
    own_rows = 4 * REPL * rows
    for step in range(sections - 1, 0, -1):
        part = 0 if step < middle else 1
        if step < sections - 1:
            old = list(ups[part] or ())
            extra = [ups[1][0]] if step == 1 else []
            pm, po, *kept = layer(
                functools.partial(backward_kernel, kind_of(step), bool(old), bool(extra)),
                "backward_layer",
                [marks, up_mine, up_other, *gates[part], held_late if part else held_early] + old + extra,
                [row] * (6 if extra else 4),
            )
            ups[part] = kept[:2]
        local = step == middle or step == 1
        operands = [pm, swap_core(po), up_mine, state_mine[part], gains]
        held = hold(part, True, not local, operands)
        if step == 1:
            prepared = call(
                own_first_kernel,
                "own_first",
                [flags, input_rows, *early_rows, late_mine, late_other, *early_arrived]
                + with_other_core(late_arrived)
                + [gains, weights],
                [
                    shape(features, own_rows),
                    shape(own_rows, narrow, dtype=F32),
                    shape(own_rows, narrow, dtype=F32),
                    shape(own_rows, narrow),
                ],
                [
                    pltpu.VMEM((2, features, narrow), BF),
                    pltpu.VMEM((own_rows, features), BF),
                    pltpu.SemaphoreType.DMA((2, chunks)),
                ],
                12,
                4 * own_rows * features * narrow,
                8 * features * narrow,
                hbm=(19,),
            )
            block, same, opposite = lax.optimization_barrier((held[0], *kept[2:]))
            crossed, prepared = lax.optimization_barrier((swap_chip(block), prepared))
            mine = total([block, crossed])
            up_arrived = collect(same, opposite, lambda c, end: c > 0)
        elif step == middle:
            block, late = lax.optimization_barrier((held[0], late_mine))
            up_mine = total([block, swap_chip(block)])
            late_arrived = collect(late, late, lambda c, end: end == 1)
            up_other, late_arrived = lax.optimization_barrier((swap_core(up_mine), late_arrived))
        else:
            up_mine, up_other, _ = across(held, kind_of(step), kind_of(step - 1), ())
    straight = [
        send(
            mine,
            lambda copy, end, c, shift=shift, source=source: (
                ((copy + shift) % REPL, source, 1, False) if c == 0 and end == 0 else None
            ),
        )
        for shift, source in pairs
    ]
    return call(
        own_last_kernel,
        "own_last",
        [flags, cot_rows, *with_other_core(straight), *ups[0], *ups[1], *with_other_core(up_arrived)]
        + [*prepared, held_early, held_late],
        [shape(1, 3, features, narrow)],
        [
            pltpu.VMEM((own_rows, features), BF),
            pltpu.VMEM((own_rows, narrow), F32),
            pltpu.VMEM((3, features, narrow), BF),
            pltpu.SemaphoreType.DMA((3, chunks)),
        ],
        16,
        8 * own_rows * features * narrow,
        8 * features * narrow,
        out_hbm=True,
    )[0]


def solution(mesh):
    return jax.shard_map(
        body,
        mesh=mesh,
        in_specs=(P(), P(), P("pipe", None, None, None, "tensor"), P("pipe", None, None)),
        out_specs=P("pipe", None, None, "tensor"),
        check_vma=False,
    )
```

```python
import functools

import jax
import jax.numpy as jnp
from jax import lax
from jax.experimental import pallas as pl
from jax.experimental.pallas import tpu as pltpu
from jax.sharding import PartitionSpec as P

REPL = 2
EPS = 1e-06
BF = jnp.bfloat16
F32 = jnp.float32
SMEM_SPEC = pl.BlockSpec(memory_space=pltpu.SMEM)
VMEM_SPEC = pl.BlockSpec(memory_space=pltpu.VMEM)
HBM_SPEC = pl.BlockSpec(memory_space=pltpu.HBM)
MIB = 1024 * 1024
NEAR, OUTER, FIRST_CHIP, KIND, OWN, STATE_ROWS, UP_ROWS = 1, 2, 3, 4, 5, 7, 23


def chunk_of(features):
    for size in (512, 256, 128):
        if features % size == 0:
            return size
    return features


def norm_rows(rows, gain_row):
    widened = rows.astype(F32)
    root = jnp.sqrt(jnp.mean(widened * widened, axis=-1, keepdims=True) + EPS)
    unit = widened / root
    return unit, root, (unit * gain_row).astype(BF)


def dot(left, right):
    return jnp.dot(left, right, preferred_element_type=F32)


def dot_last(left, right):
    return lax.dot_general(left, right, (((1,), (1,)), ((), ())), preferred_element_type=F32)


def dot_first(left, right):
    return lax.dot_general(left, right, (((0,), (0,)), ((), ())), preferred_element_type=F32)


def is_set(flags_ref, index, value=1):
    if len(flags_ref.shape) == 1:
        return flags_ref[index] == value
    return flags_ref[index : index + 1, 0:1] == value


def gain_at(flags_ref, gains_ref, part):
    return jnp.where(is_set(flags_ref, NEAR, 1 - part), gains_ref[0:1], gains_ref[1:2])


def own_index(flags_ref, part):
    return jnp.where(flags_ref[NEAR] == 1 - part, 0, 1)


def choose(condition, first, second):
    kept = first.dtype
    return jnp.where(condition, first.astype(F32), second.astype(F32)).astype(kept)


def weight_copies(which, w_ref, w_buf, sems, size):
    features = w_buf.shape[1]
    copies = {}
    for matrix in range(3):
        for k in range(features // size):
            rows = pl.ds(k * size, size)
            copies[matrix, k] = pltpu.make_async_copy(
                w_ref.at[which, matrix, rows], w_buf.at[matrix, rows], sems.at[matrix, k]
            )
    return copies


def fill_normed(xm_ref, xo_ref, gain, normed):
    half = xm_ref.shape[0]
    normed[:half] = norm_rows(xm_ref[...], gain)[2]
    normed[half:] = norm_rows(xo_ref[...], gain)[2]


def gate_upper(copies, w_buf, normed, size):
    gate = upper = None
    for k in range(w_buf.shape[1] // size):
        cols = pl.ds(k * size, size)
        if copies:
            copies[0, k].wait()
            copies[1, k].wait()
        block = normed[:, cols]
        gate_k = dot(block, w_buf[0, cols])
        upper_k = dot(block, w_buf[1, cols])
        gate = gate_k if gate is None else gate + gate_k
        upper = upper_k if upper is None else upper + upper_k
    return gate, upper


def forward_math(copies, xm_ref, xo_ref, gain, w_buf, pm_ref, po_ref, normed):
    size = chunk_of(w_buf.shape[1])
    half = xm_ref.shape[0]
    fill_normed(xm_ref, xo_ref, gain, normed)
    gate, upper = gate_upper(copies, w_buf, normed, size)
    active = (gate * jax.nn.sigmoid(gate) * upper).astype(BF)
    for k in range(w_buf.shape[1] // size):
        cols = pl.ds(k * size, size)
        if copies:
            copies[2, k].wait()
        part = dot_last(active, w_buf[2, cols]).astype(BF)
        pm_ref[:, cols] = part[:half]
        po_ref[:, cols] = part[half:]
    return gate, upper


def first_kernel(
    flags_ref, rows_ref, gains_ref, w_ref,
    pm_ref, po_ref, gate_ref, upper_ref, w_buf, xm_ref, xo_ref, marks_ref, normed, gains_buf, sems, row_sems
):
    size = chunk_of(w_buf.shape[1])
    moves = [
        pltpu.make_async_copy(rows_ref.at[flags_ref[OWN + i]], ref, row_sems.at[i])
        for i, ref in enumerate((xm_ref, xo_ref))
    ]
    moves.append(pltpu.make_async_copy(gains_ref, gains_buf, row_sems.at[2]))
    for move in moves:
        move.start()
    for i in range(marks_ref.shape[0]):
        marks_ref[i : i + 1] = jnp.full((1, marks_ref.shape[1]), flags_ref[i], jnp.int32)
    for move in moves:
        move.wait()
    copies = weight_copies(own_index(flags_ref, 0), w_ref, w_buf, sems, size)
    for group in ((0, 1), (2,)):
        for k in range(w_buf.shape[1] // size):
            for matrix in group:
                copies[matrix, k].start()
    gain = gain_at(flags_ref, gains_buf, 0)
    gate_ref[...], upper_ref[...] = forward_math(copies, xm_ref, xo_ref, gain, w_buf, pm_ref, po_ref, normed)


def load_kernel(flags_ref, rows_ref, cot_ref, w_ref, w_buf, xs_ref, us_ref, um_ref, uo_ref, sems, row_sems):
    copies = list(weight_copies(own_index(flags_ref, 1), w_ref, w_buf, sems, w_buf.shape[1]).values())
    group = rows_ref.shape[1]
    count = xs_ref.shape[0] // group
    for i in range(count):
        part = pl.ds(i * group, group)
        copies.append(
            pltpu.make_async_copy(rows_ref.at[flags_ref[STATE_ROWS + i]], xs_ref.at[part], row_sems.at[0, i])
        )
        copies.append(pltpu.make_async_copy(cot_ref.at[flags_ref[UP_ROWS + i]], us_ref.at[part], row_sems.at[1, i]))
    for i, ref in enumerate((um_ref, uo_ref)):
        for half in range(2):
            copies.append(
                pltpu.make_async_copy(
                    cot_ref.at[2 * flags_ref[OWN + i] + half],
                    ref.at[pl.ds(half * group, group)],
                    row_sems.at[2 + half, i],
                )
            )
    for copy in copies:
        copy.start()
    for copy in copies:
        copy.wait()


def pick_kernel(marks_ref, *refs):
    count = len(refs) // 2
    for source, out in zip(refs[:count], refs[count:]):
        rows = out.shape[0]
        out[...] = choose(is_set(marks_ref, FIRST_CHIP), source[:rows], source[rows:])


def stack_kernel(*refs):
    *sources, out = refs
    rows = sources[0].shape[0]
    for i, source in enumerate(sources):
        out[i * rows : (i + 1) * rows] = source[...]


def forward_kernel(part, live, flags_ref, xm_ref, xo_ref, gains_ref, w_buf, *refs):
    *old, pm_ref, po_ref, gate_ref, upper_ref, xms_ref, xos_ref, normed = refs
    gain = gain_at(flags_ref, gains_ref, part)
    gate, upper = forward_math(None, xm_ref, xo_ref, gain, w_buf, pm_ref, po_ref, normed)
    found = (gate, upper, xm_ref[...], xo_ref[...])
    outs = (gate_ref, upper_ref, xms_ref, xos_ref)
    if old:
        is_live = is_set(flags_ref, KIND, live)
        found = [choose(is_live, a, b[...]) for a, b in zip(found, old)]
    for out, value in zip(outs, found):
        out[...] = value


def active_gradient(um_ref, uo_ref, w_buf):
    size = chunk_of(w_buf.shape[1])
    d_active = None
    for k in range(w_buf.shape[1] // size):
        cols = pl.ds(k * size, size)
        block = jnp.concatenate([um_ref[:, cols], uo_ref[:, cols]], axis=0)
        part = dot(block, w_buf[2, cols])
        d_active = part if d_active is None else d_active + part
    return d_active


def backward_math(d_active, gate, upper, w_buf, pm_ref, po_ref):
    size = chunk_of(w_buf.shape[1])
    half = pm_ref.shape[0]
    sig = jax.nn.sigmoid(gate)
    d_gate = (d_active * upper * (sig * (1.0 + gate * (1.0 - sig)))).astype(BF)
    d_upper = (d_active * (gate * sig)).astype(BF)
    for k in range(w_buf.shape[1] // size):
        cols = pl.ds(k * size, size)
        part = (dot_last(d_gate, w_buf[0, cols]) + dot_last(d_upper, w_buf[1, cols])).astype(BF)
        pm_ref[:, cols] = part[:half]
        po_ref[:, cols] = part[half:]


def cotangent_kernel(um_ref, uo_ref, w_buf, d_ref):
    d_ref[...] = active_gradient(um_ref, uo_ref, w_buf)


def turn_kernel(
    flags_ref, d_ref, xm_ref, xo_ref, oldm_ref, oldo_ref, gains_ref, w_buf, pm_ref, po_ref, latem_ref, lateo_ref, normed
):
    fill_normed(xm_ref, xo_ref, gain_at(flags_ref, gains_ref, 1), normed)
    gate, upper = gate_upper(None, w_buf, normed, chunk_of(w_buf.shape[1]))
    backward_math(d_ref[...], gate, upper, w_buf, pm_ref, po_ref)
    is_outer = is_set(flags_ref, OUTER)
    latem_ref[...] = choose(is_outer, xm_ref[...], oldm_ref[...])
    lateo_ref[...] = choose(is_outer, xo_ref[...], oldo_ref[...])


def backward_kernel(live, has_old, has_late, flags_ref, um_ref, uo_ref, gate_ref, upper_ref, w_buf, *refs):
    refs = list(refs)
    old = [refs.pop(0) for _ in range(2)] if has_old else []
    late = refs.pop(0) if has_late else None
    pm_ref, po_ref, ums_ref, uos_ref = refs[:4]
    backward_math(active_gradient(um_ref, uo_ref, w_buf), gate_ref[...], upper_ref[...], w_buf, pm_ref, po_ref)
    found = [um_ref[...], uo_ref[...]]
    if old:
        is_live = is_set(flags_ref, KIND, live)
        found = [choose(is_live, a, b[...]) for a, b in zip(found, old)]
    ums_ref[...], uos_ref[...] = found
    if has_late:
        is_near = is_set(flags_ref, NEAR)
        refs[4][...] = choose(is_near, found[0], late[...])
        refs[5][...] = choose(is_near, late[...], found[0])


def hold_kernel(part, backward, flags_ref, pm_ref, recv_ref, base_ref, *refs):
    summed = pm_ref[...].astype(F32) + recv_ref[...].astype(F32)
    if backward:
        state_ref, gains_ref, *outs = refs
        gain = gain_at(flags_ref, gains_ref, part)
        unit, root, _ = norm_rows(state_ref[...], gain)
        d_unit = summed * gain
        summed = (d_unit - unit * jnp.mean(d_unit * unit, axis=-1, keepdims=True)) / root
    else:
        outs = refs
    base = jnp.where(is_set(flags_ref, FIRST_CHIP), base_ref[...].astype(F32), 0.0)
    value = (summed + base).astype(BF)
    rows = value.shape[0] // len(outs)
    for i, out in enumerate(outs):
        out[...] = value[i * rows : (i + 1) * rows]


def sum_kernel(*refs):
    *terms, out = refs
    count = len(terms) // 2
    rows = out.shape[0] // count
    for i in range(count):
        total = terms[i][...].astype(F32) + terms[count + i][...].astype(F32)
        out[i * rows : (i + 1) * rows] = total.astype(BF)


def fill_rows(target, sources, change=None):
    start = 0
    for source in sources:
        rows = source[...]
        target[start : start + rows.shape[0]] = change(rows) if change else rows
        start += rows.shape[0]


def pieces_of(ref, rows):
    return [ref.at[pl.ds(i * rows, rows)] for i in range(ref.shape[0] // rows)]


def own_first_kernel(flags_ref, xs_ref, *refs):
    refs = list(refs)

    def take(count):
        return [refs.pop(0) for _ in range(count)]

    early, late, early_arrived, late_arrived = take(2), take(2), take(4), take(4)
    gains_ref, w_ref, turned_ref, left_ref, right_ref, active_ref, w_buf, normed, sems = take(9)
    features = w_buf.shape[1]
    size = chunk_of(features)
    count = features // size
    copies = {}
    for k in range(count):
        rows = pl.ds(k * size, size)
        for matrix in range(2):
            copies[matrix, k] = pltpu.make_async_copy(
                w_ref.at[0, matrix, rows], w_buf.at[matrix, rows], sems.at[matrix, k]
            )
            copies[matrix, k].start()
    gain = gains_ref[0:1]
    half = early[0].shape[0]
    is_near = flags_ref[NEAR] == 1
    is_outer = flags_ref[OUTER] == 1

    def fill(sources):
        fill_rows(normed, sources, lambda rows: norm_rows(rows, gain)[2])

    @pl.when(jnp.logical_and(is_near, is_outer))
    def _():
        fill(pieces_of(xs_ref, half))

    @pl.when(jnp.logical_and(is_near, jnp.logical_not(is_outer)))
    def _():
        fill(early + early_arrived)

    @pl.when(jnp.logical_not(is_near))
    def _():
        fill(late + late_arrived)

    gate, upper = gate_upper(copies, w_buf, normed, size)
    sig = jax.nn.sigmoid(gate)
    smooth = gate * sig
    left_ref[...] = upper * (sig * (1.0 + gate * (1.0 - sig)))
    right_ref[...] = smooth
    active_ref[...] = (smooth * upper).astype(BF)
    for k in range(count):
        cols = pl.ds(k * size, size)
        turned_ref[cols] = normed[:, cols].T


def own_last_kernel(flags_ref, us_ref, *refs):
    refs = list(refs)

    def take(count):
        return [refs.pop(0) for _ in range(count)]

    direct, early, late, arrived = take(8), take(2), take(2), take(4)
    turned_ref, left_ref, right_ref, active_ref, early_ref, late_ref = take(6)
    out_ref, u_buf, d_act, out_buf, sems = take(5)
    features = turned_ref.shape[0]
    size = chunk_of(features)
    count = features // size
    is_near = flags_ref[NEAR] == 1
    is_outer = flags_ref[OUTER] == 1

    def fill(sources, w_ref):
        fill_rows(u_buf, sources)
        total = None
        for k in range(count):
            cols = pl.ds(k * size, size)
            part = dot(u_buf[:, cols], w_ref[2, cols])
            total = part if total is None else total + part
        d_act[...] = total

    cases = (
        (True, True, direct, early_ref),
        (True, False, [us_ref], late_ref),
        (False, True, early + arrived, early_ref),
        (False, False, late + arrived, late_ref),
    )
    for outer, near, sources, w_ref in cases:

        @pl.when(jnp.logical_and(is_outer == outer, is_near == near))
        def _(sources=sources, w_ref=w_ref):
            fill(sources, w_ref)

    copies = []

    def send(matrix, k):
        rows = pl.ds(k * size, size)
        copy = pltpu.make_async_copy(out_buf.at[matrix, rows], out_ref.at[0, matrix, rows], sems.at[matrix, k])
        copy.start()
        copies.append(copy)

    active = active_ref[...]
    d_active = d_act[...]
    for k in range(count):
        cols = pl.ds(k * size, size)
        out_buf[2, cols] = dot_first(u_buf[:, cols], active).astype(BF)
        send(2, k)
    d_gate = (d_active * left_ref[...]).astype(BF)
    d_upper = (d_active * right_ref[...]).astype(BF)
    for k in range(count):
        cols = pl.ds(k * size, size)
        turned = turned_ref[cols]
        out_buf[0, cols] = dot(turned, d_gate).astype(BF)
        send(0, k)
        out_buf[1, cols] = dot(turned, d_upper).astype(BF)
        send(1, k)
    for copy in copies:
        copy.wait()


def call(kernel, name, operands, outs, scratch, limit, flops, moved, hbm=(), out_hbm=False, smem=(0,)):
    specs = [
        SMEM_SPEC if i in smem else HBM_SPEC if i in hbm else VMEM_SPEC for i in range(len(operands))
    ]
    out_spec = HBM_SPEC if out_hbm else VMEM_SPEC
    results = pl.pallas_call(
        kernel,
        out_shape=outs,
        in_specs=specs,
        out_specs=[out_spec] * len(outs),
        scratch_shapes=scratch,
        cost_estimate=pl.CostEstimate(flops=flops, bytes_accessed=moved, transcendentals=0),
        compiler_params=pltpu.CompilerParams(vmem_limit_bytes=limit * MIB),
        name=name,
    )(*operands)
    return list(results)


def body(inputs, cotangent, section_weights, section_gains):
    sections = lax.axis_size("pipe") // REPL
    ranks = lax.axis_size("tensor")
    pipe = lax.axis_index("pipe")
    tensor = lax.axis_index("tensor")
    position = pipe % sections
    replica = pipe // sections
    middle = sections // 2
    near = position < middle
    side = jnp.where(near, 0, 1)
    kind = jnp.where(near, position, sections - 1 - position)
    core = tensor % 2
    chip = tensor // 2
    rows, features = inputs.shape[2:]
    narrow = section_weights.shape[-1]
    group = rows // 2
    chunks = features // chunk_of(features)
    weights = pltpu.with_memory_space_constraint(section_weights[0], pltpu.HBM)
    blocks = pltpu.with_memory_space_constraint(inputs.reshape(-1, rows, features), pltpu.HBM)
    half_blocks = pltpu.with_memory_space_constraint(inputs.reshape(-1, group, features), pltpu.HBM)
    cot_half_blocks = pltpu.with_memory_space_constraint(cotangent.reshape(-1, group, features), pltpu.HBM)
    gains = section_gains[0]
    core_swap = [(i, i ^ 1) for i in range(ranks)]
    chip_swap = [(i, (i + 2) % ranks) for i in range(ranks)]

    def spot(across, end, batch):
        return (((replica + across) % REPL) * 2 + end) * 2 + batch

    pairs = ((0, 0), (0, 1), (1, 0), (1, 1))
    own = [spot(0, side, batch) for batch in (core, 1 - core)]
    state_rows = []
    up_rows = [2 * at + half for at in own for half in range(2)]
    for batch in (core, 1 - core):
        for across, end in pairs:
            state_rows += [2 * spot(across, end, batch), 2 * spot(across, 1 - end, batch) + 1]
        for half in (chip, 1 - chip):
            up_rows += [2 * spot(across, side ^ turn, batch) + half for across, turn in pairs[1:]]
    flags = [side, near, kind == 0, chip == 0, kind] + own + state_rows + up_rows
    flags = jnp.stack([jnp.asarray(flag).astype(jnp.int32) for flag in flags])

    def swap_core(block):
        return lax.ppermute(block, "tensor", core_swap)

    def swap_chip(block):
        return lax.ppermute(block, "tensor", chip_swap)

    def place(copy, end, c, rank):
        at = c if end == 0 else sections - 1 - c
        return (copy * sections + at) * ranks + rank

    def send(block, route):
        moves = []
        for copy in range(REPL):
            for end in range(2):
                for c in range(middle):
                    source = route(copy, end, c)
                    if source is None:
                        continue
                    for rank in range(ranks):
                        came = (rank + 2) % ranks if source[3] else rank
                        moves.append((place(*source[:3], came), place(copy, end, c, rank)))
        return lax.ppermute(block, ("pipe", "tensor"), moves)

    def hop(block, source, target, turn, other):
        return send(block, lambda copy, end, c: (copy, end ^ turn, source, other) if c == target else None)

    def collect(same, opposite, wanted):
        def part(payload, turn, across):
            return send(
                payload,
                lambda copy, end, c: ((copy + across) % REPL, end ^ turn, c, False) if wanted(c, end) else None,
            )

        return [part(opposite, 1, 0), part(same, 0, 1), part(opposite, 1, 1)]

    def with_other_core(arrived):
        return arrived + [swap_core(block) for block in arrived]

    def picked(blocks):
        return call(pick_kernel, "pick", [marks, *blocks], [piece] * len(blocks), [], 4, 0, 0, smem=())

    def spread(arrived):
        mine = call(stack_kernel, "stack", arrived, [shape(len(arrived) * group, features)], [], 4, 0, 0, smem=())[0]
        return with_other_core([mine, swap_chip(mine)])

    def shape(*extent, dtype=BF):
        return jax.ShapeDtypeStruct(extent, dtype)

    row = shape(rows, features)
    piece = shape(group, features)
    all_rows = shape(4 * REPL * rows, features)
    gate_shape = shape(2 * rows, narrow, dtype=F32)
    held_shape = pltpu.VMEM((3, features, narrow), BF)
    normed_scratch = pltpu.VMEM((2 * rows, features), BF)
    layer_flops = 12 * rows * features * narrow
    layer_bytes = 6 * features * narrow
    row_bytes = 2 * rows * features

    def layer(kernel, name, operands, outs):
        return call(kernel, name, operands, outs, [normed_scratch], 8, layer_flops, layer_bytes, smem=())

    def hold(part, backward, split, operands):
        outs = [piece, piece] if split else [row]
        kernel = functools.partial(hold_kernel, part, backward)
        return call(kernel, "hold", [marks] + operands, outs, [], 4, 0, 4 * row_bytes, smem=())

    def total(terms):
        return call(sum_kernel, "total", terms, [row], [], 4, 0, 3 * row_bytes, smem=())[0]

    def kind_of(step):
        return min(step, sections - 1 - step)

    def across(held, source, target, during):
        straight = [hop(held[turn], source, target, turn, False) for turn in range(2)]
        crossed = [hop(held[turn], source, target, turn, True) for turn in range(2)]
        straight, crossed, during = lax.optimization_barrier((straight, crossed, during))
        mine = total(straight + crossed)
        return mine, swap_core(mine), during

    pm, po, gate, upper, held_early, mine, other, marks = call(
        first_kernel,
        "first_layer",
        [flags, blocks, pltpu.with_memory_space_constraint(gains, pltpu.HBM), weights],
        [row, row, gate_shape, gate_shape, held_shape, row, row, shape(8, 128, dtype=jnp.int32)],
        [
            normed_scratch,
            pltpu.VMEM(gains.shape, F32),
            pltpu.SemaphoreType.DMA((3, chunks)),
            pltpu.SemaphoreType.DMA((3,)),
        ],
        8,
        layer_flops,
        layer_bytes,
        hbm=(1, 2, 3),
    )
    saved = [(gate, upper, mine, other), None]
    loaded = call(
        load_kernel,
        "load_late",
        [flags, half_blocks, cot_half_blocks, weights],
        [held_shape, all_rows, all_rows, row, row],
        [pltpu.SemaphoreType.DMA((3, 1)), pltpu.SemaphoreType.DMA((4, 8 * REPL))],
        4,
        0,
        2 * layer_bytes,
        hbm=(1, 2, 3),
    )
    for step in range(sections - 1):
        part = 0 if step < middle else 1
        if step > 0:
            old = list(saved[part] or ())
            pm, po, *saved[part] = layer(
                functools.partial(forward_kernel, part, kind_of(step)),
                "forward_layer",
                [marks, mine, other, gains, held_late if part else held_early] + old,
                [row, row, gate_shape, gate_shape, row, row],
            )
        same_kind = step == middle - 1
        held = hold(part, False, not same_kind, [pm, swap_core(po), mine])
        during = ()
        if step == 0:
            during = loaded
        if step == middle:
            during = call(
                cotangent_kernel,
                "cotangent",
                [up_mine, up_other, held_late],
                [gate_shape],
                [],
                4,
                layer_flops // 3,
                layer_bytes // 3,
                smem=(),
            ) + spread(early_arrived)
        if same_kind:
            block, early_mine = lax.optimization_barrier((held[0], saved[0][2]))
            early_part = picked([early_mine])[0]
            early_arrived = collect(early_part, early_part, lambda c, end: c > 0 and end == 0)
            crossed, early_arrived = lax.optimization_barrier((swap_chip(block), early_arrived))
            mine = total([block, crossed])
            other = swap_core(mine)
        else:
            mine, other, during = across(held, kind_of(step), kind_of(step + 1), during)
        if step == 0:
            held_late, input_rows, cot_rows, up_mine, up_other = during
        if step == middle:
            d_active, *early_arrived = during

    early_rows = saved[0][2:]
    gates = [saved[0][:2], saved[1][:2]]
    pm, po, late_mine, late_other = layer(
        turn_kernel,
        "turn_layer",
        [marks, d_active, mine, other, *saved[1][2:], gains, held_late],
        [row] * 4,
    )
    state_mine = [early_rows[0], late_mine]
    ups = [None, (up_mine, up_other)]
    own_rows = 4 * REPL * rows
    for step in range(sections - 1, 0, -1):
        part = 0 if step < middle else 1
        if step < sections - 1:
            old = list(ups[part] or ())
            extra = [ups[1][0]] if step == 1 else []
            pm, po, *kept = layer(
                functools.partial(backward_kernel, kind_of(step), bool(old), bool(extra)),
                "backward_layer",
                [marks, up_mine, up_other, *gates[part], held_late if part else held_early] + old + extra,
                [row] * (6 if extra else 4),
            )
            ups[part] = kept[:2]
        local = step == middle or step == 1
        operands = [pm, swap_core(po), up_mine, state_mine[part], gains]
        held = hold(part, True, not local, operands)
        if step == 1:
            prepared = call(
                own_first_kernel,
                "own_first",
                [flags, input_rows, *early_rows, late_mine, late_other, *early_arrived]
                + spread(late_arrived)
                + [gains, weights],
                [
                    shape(features, own_rows),
                    shape(own_rows, narrow, dtype=F32),
                    shape(own_rows, narrow, dtype=F32),
                    shape(own_rows, narrow),
                ],
                [
                    pltpu.VMEM((2, features, narrow), BF),
                    pltpu.VMEM((own_rows, features), BF),
                    pltpu.SemaphoreType.DMA((2, chunks)),
                ],
                12,
                4 * own_rows * features * narrow,
                8 * features * narrow,
                hbm=(15,),
            )
            block, same, opposite = lax.optimization_barrier((held[0], *kept[2:]))
            up_arrived = collect(*picked([same, opposite]), lambda c, end: c > 0)
            mine, up_arrived = lax.optimization_barrier((total([block, swap_chip(block)]), up_arrived))
        elif step == middle:
            block, late = lax.optimization_barrier((held[0], late_mine))
            late_part = picked([late])[0]
            late_arrived = collect(late_part, late_part, lambda c, end: end == 1)
            crossed, late_arrived = lax.optimization_barrier((swap_chip(block), late_arrived))
            up_mine = total([block, crossed])
            up_other = swap_core(up_mine)
        else:
            up_mine, up_other, _ = across(held, kind_of(step), kind_of(step - 1), ())
    straight = [
        send(
            mine,
            lambda copy, end, c, shift=shift, source=source: (
                ((copy + shift) % REPL, source, 1, False) if c == 0 and end == 0 else None
            ),
        )
        for shift, source in pairs
    ]
    straight, prepared = lax.optimization_barrier((straight, prepared))
    return call(
        own_last_kernel,
        "own_last",
        [flags, cot_rows, *with_other_core(straight), *ups[0], *ups[1], *spread(up_arrived)]
        + [*prepared, held_early, held_late],
        [shape(1, 3, features, narrow)],
        [
            pltpu.VMEM((own_rows, features), BF),
            pltpu.VMEM((own_rows, narrow), F32),
            pltpu.VMEM((3, features, narrow), BF),
            pltpu.SemaphoreType.DMA((3, chunks)),
        ],
        16,
        8 * own_rows * features * narrow,
        8 * features * narrow,
        out_hbm=True,
    )[0]


def solution(mesh):
    return jax.shard_map(
        body,
        mesh=mesh,
        in_specs=(P(), P(), P("pipe", None, None, None, "tensor"), P("pipe", None, None)),
        out_specs=P("pipe", None, None, "tensor"),
        check_vma=False,
    )
```

```python
import functools

import jax
import jax.numpy as jnp
from jax import lax
from jax.experimental import pallas as pl
from jax.experimental.pallas import tpu as pltpu
from jax.sharding import PartitionSpec as P

REPL = 2
EPS = 1e-06
BF = jnp.bfloat16
F32 = jnp.float32
SMEM_SPEC = pl.BlockSpec(memory_space=pltpu.SMEM)
VMEM_SPEC = pl.BlockSpec(memory_space=pltpu.VMEM)
HBM_SPEC = pl.BlockSpec(memory_space=pltpu.HBM)
MIB = 1024 * 1024
NEAR, OUTER, FIRST_CHIP, KIND, PLACE, OWN, TOP, BOTTOM = 1, 2, 3, 4, 5, 6, 8, 16


def chunk_of(features):
    for size in (512, 256, 128):
        if features % size == 0:
            return size
    return features


def norm_rows(rows, gain_row):
    widened = rows.astype(F32)
    root = jnp.sqrt(jnp.mean(widened * widened, axis=-1, keepdims=True) + EPS)
    unit = widened / root
    return unit, root, (unit * gain_row).astype(BF)


def dot(left, right):
    return jnp.dot(left, right, preferred_element_type=F32)


def dot_last(left, right):
    return lax.dot_general(left, right, (((1,), (1,)), ((), ())), preferred_element_type=F32)


def dot_first(left, right):
    return lax.dot_general(left, right, (((0,), (0,)), ((), ())), preferred_element_type=F32)


def is_set(flags_ref, index, value=1):
    if len(flags_ref.shape) == 1:
        return flags_ref[index] == value
    return flags_ref[index : index + 1, 0:1] == value


def gain_at(flags_ref, gains_ref, part):
    return jnp.where(is_set(flags_ref, NEAR, 1 - part), gains_ref[0:1], gains_ref[1:2])


def own_index(flags_ref, part):
    return jnp.where(flags_ref[NEAR] == 1 - part, 0, 1)


def choose(condition, first, second):
    kept = first.dtype
    return jnp.where(condition, first.astype(F32), second.astype(F32)).astype(kept)


def weight_copies(which, w_ref, w_buf, sems, size):
    features = w_buf.shape[1]
    copies = {}
    for matrix in range(3):
        for k in range(features // size):
            rows = pl.ds(k * size, size)
            copies[matrix, k] = pltpu.make_async_copy(
                w_ref.at[which, matrix, rows], w_buf.at[matrix, rows], sems.at[matrix, k]
            )
    return copies


def fill_normed(xm_ref, xo_ref, gain, normed):
    half = xm_ref.shape[0]
    normed[:half] = norm_rows(xm_ref[...], gain)[2]
    normed[half:] = norm_rows(xo_ref[...], gain)[2]


def gate_upper(copies, w_buf, normed, size):
    gate = upper = None
    for k in range(w_buf.shape[1] // size):
        cols = pl.ds(k * size, size)
        if copies:
            copies[0, k].wait()
            copies[1, k].wait()
        block = normed[:, cols]
        gate_k = dot(block, w_buf[0, cols])
        upper_k = dot(block, w_buf[1, cols])
        gate = gate_k if gate is None else gate + gate_k
        upper = upper_k if upper is None else upper + upper_k
    return gate, upper


def forward_math(copies, xm_ref, xo_ref, gain, w_buf, pm_ref, po_ref, normed):
    size = chunk_of(w_buf.shape[1])
    half = xm_ref.shape[0]
    fill_normed(xm_ref, xo_ref, gain, normed)
    gate, upper = gate_upper(copies, w_buf, normed, size)
    active = (gate * jax.nn.sigmoid(gate) * upper).astype(BF)
    for k in range(w_buf.shape[1] // size):
        cols = pl.ds(k * size, size)
        if copies:
            copies[2, k].wait()
        part = dot_last(active, w_buf[2, cols]).astype(BF)
        pm_ref[:, cols] = part[:half]
        po_ref[:, cols] = part[half:]
    return gate, upper


def first_kernel(
    flags_ref, rows_ref, gains_ref, w_ref,
    pm_ref, po_ref, gate_ref, upper_ref, w_buf, xm_ref, xo_ref, marks_ref, normed, gains_buf, sems, row_sems
):
    size = chunk_of(w_buf.shape[1])
    moves = [
        pltpu.make_async_copy(rows_ref.at[flags_ref[OWN + i]], ref, row_sems.at[i])
        for i, ref in enumerate((xm_ref, xo_ref))
    ]
    moves.append(pltpu.make_async_copy(gains_ref, gains_buf, row_sems.at[2]))
    for move in moves:
        move.start()
    for i in range(marks_ref.shape[0]):
        marks_ref[i : i + 1] = jnp.full((1, marks_ref.shape[1]), flags_ref[i], jnp.int32)
    for move in moves:
        move.wait()
    copies = weight_copies(own_index(flags_ref, 0), w_ref, w_buf, sems, size)
    for group in ((0, 1), (2,)):
        for k in range(w_buf.shape[1] // size):
            for matrix in group:
                copies[matrix, k].start()
    gain = gain_at(flags_ref, gains_buf, 0)
    gate_ref[...], upper_ref[...] = forward_math(copies, xm_ref, xo_ref, gain, w_buf, pm_ref, po_ref, normed)


def load_kernel(flags_ref, rows_ref, cot_ref, w_ref, w_buf, xs_ref, us_ref, um_ref, uo_ref, sems, row_sems):
    copies = list(weight_copies(own_index(flags_ref, 1), w_ref, w_buf, sems, w_buf.shape[1]).values())
    pieces, rows = xs_ref.shape[:2]
    group = rows // 2
    for i in range(pieces):
        copies.append(pltpu.make_async_copy(cot_ref.at[i], us_ref.at[i], row_sems.at[0, i]))
        for half, base in enumerate((TOP, BOTTOM)):
            part = pl.ds(half * group, group)
            copies.append(
                pltpu.make_async_copy(
                    rows_ref.at[flags_ref[base + i], part], xs_ref.at[i, part], row_sems.at[1 + half, i]
                )
            )
    for i, ref in enumerate((um_ref, uo_ref)):
        copies.append(pltpu.make_async_copy(cot_ref.at[flags_ref[OWN + i]], ref, row_sems.at[3, i]))
    for copy in copies:
        copy.start()
    for copy in copies:
        copy.wait()


def forward_kernel(part, live, flags_ref, xm_ref, xo_ref, gains_ref, w_buf, *refs):
    *old, pm_ref, po_ref, gate_ref, upper_ref, xms_ref, xos_ref, normed = refs
    gain = gain_at(flags_ref, gains_ref, part)
    gate, upper = forward_math(None, xm_ref, xo_ref, gain, w_buf, pm_ref, po_ref, normed)
    found = (gate, upper, xm_ref[...], xo_ref[...])
    outs = (gate_ref, upper_ref, xms_ref, xos_ref)
    if old:
        is_live = is_set(flags_ref, KIND, live)
        found = [choose(is_live, a, b[...]) for a, b in zip(found, old)]
    for out, value in zip(outs, found):
        out[...] = value


def active_gradient(um_ref, uo_ref, w_buf):
    size = chunk_of(w_buf.shape[1])
    d_active = None
    for k in range(w_buf.shape[1] // size):
        cols = pl.ds(k * size, size)
        block = jnp.concatenate([um_ref[:, cols], uo_ref[:, cols]], axis=0)
        part = dot(block, w_buf[2, cols])
        d_active = part if d_active is None else d_active + part
    return d_active


def backward_math(d_active, gate, upper, w_buf, pm_ref, po_ref):
    size = chunk_of(w_buf.shape[1])
    half = pm_ref.shape[0]
    sig = jax.nn.sigmoid(gate)
    d_gate = (d_active * upper * (sig * (1.0 + gate * (1.0 - sig)))).astype(BF)
    d_upper = (d_active * (gate * sig)).astype(BF)
    for k in range(w_buf.shape[1] // size):
        cols = pl.ds(k * size, size)
        part = (dot_last(d_gate, w_buf[0, cols]) + dot_last(d_upper, w_buf[1, cols])).astype(BF)
        pm_ref[:, cols] = part[:half]
        po_ref[:, cols] = part[half:]


def cotangent_kernel(um_ref, uo_ref, w_buf, d_ref):
    d_ref[...] = active_gradient(um_ref, uo_ref, w_buf)


def turn_kernel(
    flags_ref, d_ref, xm_ref, xo_ref, oldm_ref, oldo_ref, gains_ref, w_buf, pm_ref, po_ref, latem_ref, lateo_ref, normed
):
    fill_normed(xm_ref, xo_ref, gain_at(flags_ref, gains_ref, 1), normed)
    gate, upper = gate_upper(None, w_buf, normed, chunk_of(w_buf.shape[1]))
    backward_math(d_ref[...], gate, upper, w_buf, pm_ref, po_ref)
    is_outer = is_set(flags_ref, OUTER)
    latem_ref[...] = choose(is_outer, xm_ref[...], oldm_ref[...])
    lateo_ref[...] = choose(is_outer, xo_ref[...], oldo_ref[...])


def backward_kernel(live, has_old, has_late, flags_ref, um_ref, uo_ref, gate_ref, upper_ref, w_buf, *refs):
    refs = list(refs)
    old = [refs.pop(0) for _ in range(2)] if has_old else []
    late = refs.pop(0) if has_late else None
    pm_ref, po_ref, ums_ref, uos_ref = refs[:4]
    backward_math(active_gradient(um_ref, uo_ref, w_buf), gate_ref[...], upper_ref[...], w_buf, pm_ref, po_ref)
    found = [um_ref[...], uo_ref[...]]
    if old:
        is_live = is_set(flags_ref, KIND, live)
        found = [choose(is_live, a, b[...]) for a, b in zip(found, old)]
    ums_ref[...], uos_ref[...] = found
    if has_late:
        is_near = is_set(flags_ref, NEAR)
        refs[4][...] = choose(is_near, found[0], late[...])
        refs[5][...] = choose(is_near, late[...], found[0])


def hold_kernel(part, backward, flags_ref, pm_ref, recv_ref, base_ref, *refs):
    summed = pm_ref[...].astype(F32) + recv_ref[...].astype(F32)
    if backward:
        state_ref, gains_ref, *outs = refs
        gain = gain_at(flags_ref, gains_ref, part)
        unit, root, _ = norm_rows(state_ref[...], gain)
        d_unit = summed * gain
        summed = (d_unit - unit * jnp.mean(d_unit * unit, axis=-1, keepdims=True)) / root
    else:
        outs = refs
    base = jnp.where(is_set(flags_ref, FIRST_CHIP), base_ref[...].astype(F32), 0.0)
    value = (summed + base).astype(BF)
    rows = value.shape[0] // len(outs)
    for i, out in enumerate(outs):
        out[...] = value[i * rows : (i + 1) * rows]


def sum_kernel(*refs):
    *terms, out = refs
    count = len(terms) // 2
    rows = out.shape[0] // count
    for i in range(count):
        total = terms[i][...].astype(F32) + terms[count + i][...].astype(F32)
        out[i * rows : (i + 1) * rows] = total.astype(BF)


def own_first_kernel(
    flags_ref, xs_ref, early_ref, late_ref, gains_ref, w_ref,
    turned_ref, left_ref, right_ref, active_ref, w_buf, normed, sems
):
    features = w_buf.shape[1]
    size = chunk_of(features)
    count = features // size
    copies = {}
    for k in range(count):
        rows = pl.ds(k * size, size)
        for matrix in range(2):
            copies[matrix, k] = pltpu.make_async_copy(
                w_ref.at[0, matrix, rows], w_buf.at[matrix, rows], sems.at[matrix, k]
            )
            copies[matrix, k].start()
    gain = gains_ref[0:1]
    pieces, half = xs_ref.shape[:2]
    is_near = flags_ref[NEAR] == 1
    is_outer = flags_ref[OUTER] == 1
    inputs_used = jnp.logical_and(is_near, is_outer)

    def put(piece, rows):
        normed[piece * half : (piece + 1) * half] = norm_rows(rows, gain)[2]

    def fill(sources):
        for i, source in enumerate(sources):
            put(i, source[...])

    def blocks(ref):
        return [ref.at[pl.ds(i * half, half)] for i in range(pieces)]

    @pl.when(inputs_used)
    def _():
        fill([xs_ref.at[i] for i in range(pieces)])

    @pl.when(jnp.logical_and(is_near, jnp.logical_not(is_outer)))
    def _():
        fill(blocks(early_ref))

    @pl.when(jnp.logical_not(is_near))
    def _():
        fill(blocks(late_ref))

    gate, upper = gate_upper(copies, w_buf, normed, size)
    sig = jax.nn.sigmoid(gate)
    smooth = gate * sig
    left_ref[...] = upper * (sig * (1.0 + gate * (1.0 - sig)))
    right_ref[...] = smooth
    active_ref[...] = (smooth * upper).astype(BF)
    for k in range(count):
        cols = pl.ds(k * size, size)
        turned_ref[cols] = normed[:, cols].T


def own_last_kernel(flags_ref, us_ref, *refs):
    refs = list(refs)

    def take(count):
        return [refs.pop(0) for _ in range(count)]

    direct, early, late, arrived = take(8), take(2), take(2), take(6)
    turned_ref, left_ref, right_ref, active_ref, early_ref, late_ref = take(6)
    out_ref, u_buf, d_act, out_buf, sems = take(5)
    features = turned_ref.shape[0]
    size = chunk_of(features)
    count = features // size
    pieces, half = us_ref.shape[:2]
    is_near = flags_ref[NEAR] == 1
    is_outer = flags_ref[OUTER] == 1

    place = flags_ref[PLACE]

    def fill(sources, w_ref, turned):
        for i in range(pieces):
            lane = i % (pieces // 2)
            if turned:
                at = 2 * jnp.bitwise_xor(place, lane) + jnp.bitwise_xor(flags_ref[OWN] % 2, i // (pieces // 2))
                u_buf[pl.ds(pl.multiple_of(at * half, half), half)] = sources[i][...]
            else:
                u_buf[i * half : (i + 1) * half] = sources[i][...]
        total = None
        for k in range(count):
            cols = pl.ds(k * size, size)
            part = dot(u_buf[:, cols], w_ref[2, cols])
            total = part if total is None else total + part
        d_act[...] = total

    cases = (
        (True, True, direct, early_ref, False),
        (True, False, [us_ref.at[i] for i in range(pieces)], late_ref, False),
        (False, True, early[:1] + arrived[:3] + early[1:] + arrived[3:], early_ref, True),
        (False, False, late[:1] + arrived[:3] + late[1:] + arrived[3:], late_ref, True),
    )
    for outer, near, sources, w_ref, turned in cases:

        @pl.when(jnp.logical_and(is_outer == outer, is_near == near))
        def _(sources=sources, w_ref=w_ref, turned=turned):
            fill(sources, w_ref, turned)

    copies = []

    def send(matrix, k):
        rows = pl.ds(k * size, size)
        copy = pltpu.make_async_copy(out_buf.at[matrix, rows], out_ref.at[0, matrix, rows], sems.at[matrix, k])
        copy.start()
        copies.append(copy)

    active = active_ref[...]
    d_active = d_act[...]
    for k in range(count):
        cols = pl.ds(k * size, size)
        out_buf[2, cols] = dot_first(u_buf[:, cols], active).astype(BF)
        send(2, k)
    d_gate = (d_active * left_ref[...]).astype(BF)
    d_upper = (d_active * right_ref[...]).astype(BF)
    for k in range(count):
        cols = pl.ds(k * size, size)
        turned = turned_ref[cols]
        out_buf[0, cols] = dot(turned, d_gate).astype(BF)
        send(0, k)
        out_buf[1, cols] = dot(turned, d_upper).astype(BF)
        send(1, k)
    for copy in copies:
        copy.wait()


def call(kernel, name, operands, outs, scratch, limit, flops, moved, hbm=(), out_hbm=False, smem=(0,)):
    specs = [
        SMEM_SPEC if i in smem else HBM_SPEC if i in hbm else VMEM_SPEC for i in range(len(operands))
    ]
    out_spec = HBM_SPEC if out_hbm else VMEM_SPEC
    results = pl.pallas_call(
        kernel,
        out_shape=outs,
        in_specs=specs,
        out_specs=[out_spec] * len(outs),
        scratch_shapes=scratch,
        cost_estimate=pl.CostEstimate(flops=flops, bytes_accessed=moved, transcendentals=0),
        compiler_params=pltpu.CompilerParams(vmem_limit_bytes=limit * MIB),
        name=name,
    )(*operands)
    return list(results)


def body(inputs, cotangent, section_weights, section_gains):
    sections = lax.axis_size("pipe") // REPL
    ranks = lax.axis_size("tensor")
    pipe = lax.axis_index("pipe")
    tensor = lax.axis_index("tensor")
    position = pipe % sections
    replica = pipe // sections
    middle = sections // 2
    near = position < middle
    side = jnp.where(near, 0, 1)
    kind = jnp.where(near, position, sections - 1 - position)
    core = tensor % 2
    chip = tensor // 2
    rows, features = inputs.shape[2:]
    narrow = section_weights.shape[-1]
    group = rows // 2
    chunks = features // chunk_of(features)
    weights = pltpu.with_memory_space_constraint(section_weights[0], pltpu.HBM)
    blocks = pltpu.with_memory_space_constraint(inputs.reshape(-1, rows, features), pltpu.HBM)
    cot_blocks = pltpu.with_memory_space_constraint(cotangent.reshape(-1, rows, features), pltpu.HBM)
    gains = section_gains[0]
    core_swap = [(i, i ^ 1) for i in range(ranks)]
    chip_swap = [(i, (i + 2) % ranks) for i in range(ranks)]

    def spot(across, end, batch):
        return (((replica + across) % REPL) * 2 + end) * 2 + batch

    pairs = ((0, 0), (0, 1), (1, 0), (1, 1))
    own = [spot(0, side, batch) for batch in (core, 1 - core)]
    top = [spot(across, end, batch) for batch in (core, 1 - core) for across, end in pairs]
    bottom = [spot(across, 1 - end, batch) for batch in (core, 1 - core) for across, end in pairs]
    flags = [side, near, kind == 0, chip == 0, kind, 2 * replica + side] + own + top + bottom
    flags = jnp.stack([jnp.asarray(flag).astype(jnp.int32) for flag in flags])

    def swap_core(block):
        return lax.ppermute(block, "tensor", core_swap)

    def swap_chip(block):
        return lax.ppermute(block, "tensor", chip_swap)

    def place(copy, end, c, rank):
        at = c if end == 0 else sections - 1 - c
        return (copy * sections + at) * ranks + rank

    def send(block, route):
        moves = []
        for copy in range(REPL):
            for end in range(2):
                for c in range(middle):
                    source = route(copy, end, c)
                    if source is None:
                        continue
                    for rank in range(ranks):
                        came = (rank + 2) % ranks if source[3] else rank
                        moves.append((place(*source[:3], came), place(copy, end, c, rank)))
        return lax.ppermute(block, ("pipe", "tensor"), moves)

    def hop(block, source, target, turn, other):
        return send(block, lambda copy, end, c: (copy, end ^ turn, source, other) if c == target else None)

    def collect(same, opposite, wanted):
        def part(payload, turn, across):
            return send(
                payload,
                lambda copy, end, c: ((copy + across) % REPL, end ^ turn, c, False) if wanted(c, end) else None,
            )

        return [part(opposite, 1, 0), part(same, 0, 1), part(opposite, 1, 1)]

    def gather(block):
        groups = []
        for c in range(middle):
            for first in range(0, ranks, 2):
                ends = [(copy, end) for copy in range(REPL) for end in range(2)]
                groups.append([place(copy, end, c, first + i) for copy, end in ends for i in range(2)])
        return lax.all_gather(block, ("pipe", "tensor"), axis_index_groups=groups, tiled=True)

    def with_other_core(arrived):
        return arrived + [swap_core(block) for block in arrived]

    def shape(*extent, dtype=BF):
        return jax.ShapeDtypeStruct(extent, dtype)

    row = shape(rows, features)
    piece = shape(group, features)
    pieces = shape(4 * REPL, rows, features)
    gate_shape = shape(2 * rows, narrow, dtype=F32)
    held_shape = pltpu.VMEM((3, features, narrow), BF)
    normed_scratch = pltpu.VMEM((2 * rows, features), BF)
    layer_flops = 12 * rows * features * narrow
    layer_bytes = 6 * features * narrow
    row_bytes = 2 * rows * features

    def layer(kernel, name, operands, outs):
        return call(kernel, name, operands, outs, [normed_scratch], 8, layer_flops, layer_bytes, smem=())

    def hold(part, backward, split, operands):
        outs = [piece, piece] if split else [row]
        kernel = functools.partial(hold_kernel, part, backward)
        return call(kernel, "hold", [marks] + operands, outs, [], 4, 0, 4 * row_bytes, smem=())

    def total(terms):
        return call(sum_kernel, "total", terms, [row], [], 4, 0, 3 * row_bytes, smem=())[0]

    def kind_of(step):
        return min(step, sections - 1 - step)

    def across(held, source, target, during):
        straight = [hop(held[turn], source, target, turn, False) for turn in range(2)]
        crossed = [hop(held[turn], source, target, turn, True) for turn in range(2)]
        straight, crossed, during = lax.optimization_barrier((straight, crossed, during))
        mine = total(straight + crossed)
        return mine, swap_core(mine), during

    pm, po, gate, upper, held_early, mine, other, marks = call(
        first_kernel,
        "first_layer",
        [flags, blocks, pltpu.with_memory_space_constraint(gains, pltpu.HBM), weights],
        [row, row, gate_shape, gate_shape, held_shape, row, row, shape(8, 128, dtype=jnp.int32)],
        [
            normed_scratch,
            pltpu.VMEM(gains.shape, F32),
            pltpu.SemaphoreType.DMA((3, chunks)),
            pltpu.SemaphoreType.DMA((3,)),
        ],
        8,
        layer_flops,
        layer_bytes,
        hbm=(1, 2, 3),
    )
    saved = [(gate, upper, mine, other), None]
    loaded = call(
        load_kernel,
        "load_late",
        [flags, blocks, cot_blocks, weights],
        [held_shape, pieces, pieces, row, row],
        [pltpu.SemaphoreType.DMA((3, 1)), pltpu.SemaphoreType.DMA((4, 4 * REPL))],
        4,
        0,
        2 * layer_bytes,
        hbm=(1, 2, 3),
    )
    for step in range(sections - 1):
        part = 0 if step < middle else 1
        if step > 0:
            old = list(saved[part] or ())
            pm, po, *saved[part] = layer(
                functools.partial(forward_kernel, part, kind_of(step)),
                "forward_layer",
                [marks, mine, other, gains, held_late if part else held_early] + old,
                [row, row, gate_shape, gate_shape, row, row],
            )
        same_kind = step == middle - 1
        held = hold(part, False, not same_kind, [pm, swap_core(po), mine])
        during = ()
        if step == 0:
            during = loaded
        if step == middle:
            during = call(
                cotangent_kernel,
                "cotangent",
                [up_mine, up_other, held_late],
                [gate_shape],
                [],
                4,
                layer_flops // 3,
                layer_bytes // 3,
                smem=(),
            )
        if same_kind:
            mine = total([held[0], swap_chip(held[0])])
            early_arrived = gather(saved[0][2])
            other = swap_core(mine)
        else:
            mine, other, during = across(held, kind_of(step), kind_of(step + 1), during)
        if step == 0:
            held_late, input_rows, cot_rows, up_mine, up_other = during
        if step == middle:
            (d_active,) = during

    early_rows = saved[0][2:]
    gates = [saved[0][:2], saved[1][:2]]
    pm, po, late_mine, late_other = layer(
        turn_kernel,
        "turn_layer",
        [marks, d_active, mine, other, *saved[1][2:], gains, held_late],
        [row] * 4,
    )
    state_mine = [early_rows[0], late_mine]
    late_arrived = gather(late_mine)
    ups = [None, (up_mine, up_other)]
    own_rows = 4 * REPL * rows
    for step in range(sections - 1, 0, -1):
        part = 0 if step < middle else 1
        if step < sections - 1:
            old = list(ups[part] or ())
            extra = [ups[1][0]] if step == 1 else []
            pm, po, *kept = layer(
                functools.partial(backward_kernel, kind_of(step), bool(old), bool(extra)),
                "backward_layer",
                [marks, up_mine, up_other, *gates[part], held_late if part else held_early] + old + extra,
                [row] * (6 if extra else 4),
            )
            ups[part] = kept[:2]
        local = step == middle or step == 1
        operands = [pm, swap_core(po), up_mine, state_mine[part], gains]
        held = hold(part, True, not local, operands)
        if step == 1:
            prepared = call(
                own_first_kernel,
                "own_first",
                [flags, input_rows, early_arrived, late_arrived, gains, weights],
                [
                    shape(features, own_rows),
                    shape(own_rows, narrow, dtype=F32),
                    shape(own_rows, narrow, dtype=F32),
                    shape(own_rows, narrow),
                ],
                [
                    pltpu.VMEM((2, features, narrow), BF),
                    pltpu.VMEM((own_rows, features), BF),
                    pltpu.SemaphoreType.DMA((2, chunks)),
                ],
                12,
                4 * own_rows * features * narrow,
                8 * features * narrow,
                hbm=(5,),
            )
            mine, same, opposite = lax.optimization_barrier((total([held[0], swap_chip(held[0])]), *kept[2:]))
            up_arrived = collect(same, opposite, lambda c, end: c > 0)
        elif step == middle:
            up_mine = total([held[0], swap_chip(held[0])])
            up_other = swap_core(up_mine)
        else:
            up_mine, up_other, _ = across(held, kind_of(step), kind_of(step - 1), ())
    straight = [
        send(
            mine,
            lambda copy, end, c, shift=shift, source=source: (
                ((copy + shift) % REPL, source, 1, False) if c == 0 and end == 0 else None
            ),
        )
        for shift, source in pairs
    ]
    straight, prepared = lax.optimization_barrier((straight, prepared))
    return call(
        own_last_kernel,
        "own_last",
        [flags, cot_rows, *with_other_core(straight), *ups[0], *ups[1], *with_other_core(up_arrived)]
        + [*prepared, held_early, held_late],
        [shape(1, 3, features, narrow)],
        [
            pltpu.VMEM((own_rows, features), BF),
            pltpu.VMEM((own_rows, narrow), F32),
            pltpu.VMEM((3, features, narrow), BF),
            pltpu.SemaphoreType.DMA((3, chunks)),
        ],
        16,
        8 * own_rows * features * narrow,
        8 * features * narrow,
        out_hbm=True,
    )[0]


def solution(mesh):
    return jax.shard_map(
        body,
        mesh=mesh,
        in_specs=(P(), P(), P("pipe", None, None, None, "tensor"), P("pipe", None, None)),
        out_specs=P("pipe", None, None, "tensor"),
        check_vma=False,
    )
```

```python
import functools

import jax
import jax.numpy as jnp
from jax import lax
from jax.experimental import pallas as pl
from jax.experimental.pallas import tpu as pltpu
from jax.sharding import PartitionSpec as P

REPL = 2
EPS = 1e-06
BF = jnp.bfloat16
F32 = jnp.float32
SMEM_SPEC = pl.BlockSpec(memory_space=pltpu.SMEM)
VMEM_SPEC = pl.BlockSpec(memory_space=pltpu.VMEM)
HBM_SPEC = pl.BlockSpec(memory_space=pltpu.HBM)
MIB = 1024 * 1024
NEAR, OUTER, FIRST_CHIP, KIND, OWN, STATE = 1, 2, 3, 4, 5, 13


def chunk_of(features):
    for size in (512, 256, 128):
        if features % size == 0:
            return size
    return features


def norm_rows(rows, gain_row):
    widened = rows.astype(F32)
    root = jnp.sqrt(jnp.mean(widened * widened, axis=-1, keepdims=True) + EPS)
    unit = widened / root
    return unit, root, (unit * gain_row).astype(BF)


def dot(left, right):
    return jnp.dot(left, right, preferred_element_type=F32)


def dot_last(left, right):
    return lax.dot_general(left, right, (((1,), (1,)), ((), ())), preferred_element_type=F32)


def dot_first(left, right):
    return lax.dot_general(left, right, (((0,), (0,)), ((), ())), preferred_element_type=F32)


def is_set(flags_ref, index, value=1):
    if len(flags_ref.shape) == 1:
        return flags_ref[index] == value
    return flags_ref[index : index + 1, 0:1] == value


def gain_at(flags_ref, gains_ref, part):
    return jnp.where(is_set(flags_ref, NEAR, 1 - part), gains_ref[0:1], gains_ref[1:2])


def own_index(flags_ref, part):
    return jnp.where(flags_ref[NEAR] == 1 - part, 0, 1)


def choose(condition, first, second):
    kept = first.dtype
    return jnp.where(condition, first.astype(F32), second.astype(F32)).astype(kept)


def weight_copies(which, w_ref, w_buf, sems, size):
    features = w_buf.shape[1]
    copies = {}
    for matrix in range(3):
        for k in range(features // size):
            rows = pl.ds(k * size, size)
            copies[matrix, k] = pltpu.make_async_copy(
                w_ref.at[which, matrix, rows], w_buf.at[matrix, rows], sems.at[matrix, k]
            )
    return copies


def fill_normed(xm_ref, xo_ref, gain, normed):
    half = xm_ref.shape[0]
    normed[:half] = norm_rows(xm_ref[...], gain)[2]
    normed[half:] = norm_rows(xo_ref[...], gain)[2]


def gate_upper(copies, w_buf, normed, size):
    gate = upper = None
    for k in range(w_buf.shape[1] // size):
        cols = pl.ds(k * size, size)
        if copies:
            copies[0, k].wait()
            copies[1, k].wait()
        block = normed[:, cols]
        gate_k = dot(block, w_buf[0, cols])
        upper_k = dot(block, w_buf[1, cols])
        gate = gate_k if gate is None else gate + gate_k
        upper = upper_k if upper is None else upper + upper_k
    return gate, upper


def forward_math(copies, xm_ref, xo_ref, gain, w_buf, pm_ref, po_ref, normed):
    size = chunk_of(w_buf.shape[1])
    half = xm_ref.shape[0]
    fill_normed(xm_ref, xo_ref, gain, normed)
    gate, upper = gate_upper(copies, w_buf, normed, size)
    active = (gate * jax.nn.sigmoid(gate) * upper).astype(BF)
    for k in range(w_buf.shape[1] // size):
        cols = pl.ds(k * size, size)
        if copies:
            copies[2, k].wait()
        part = dot_last(active, w_buf[2, cols]).astype(BF)
        pm_ref[:, cols] = part[:half]
        po_ref[:, cols] = part[half:]
    return gate, upper


def first_kernel(
    flags_ref, rows_ref, gains_ref, w_ref,
    pm_ref, po_ref, gate_ref, upper_ref, w_buf, xm_ref, xo_ref, marks_ref, normed, gains_buf, sems, row_sems
):
    size = chunk_of(w_buf.shape[1])
    moves = [
        pltpu.make_async_copy(rows_ref.at[flags_ref[OWN + i]], ref, row_sems.at[i])
        for i, ref in enumerate((xm_ref, xo_ref))
    ]
    moves.append(pltpu.make_async_copy(gains_ref, gains_buf, row_sems.at[2]))
    for move in moves:
        move.start()
    for i in range(marks_ref.shape[0]):
        marks_ref[i : i + 1] = jnp.full((1, marks_ref.shape[1]), flags_ref[i], jnp.int32)
    for move in moves:
        move.wait()
    copies = weight_copies(own_index(flags_ref, 0), w_ref, w_buf, sems, size)
    for group in ((0, 1), (2,)):
        for k in range(w_buf.shape[1] // size):
            for matrix in group:
                copies[matrix, k].start()
    gain = gain_at(flags_ref, gains_buf, 0)
    gate_ref[...], upper_ref[...] = forward_math(copies, xm_ref, xo_ref, gain, w_buf, pm_ref, po_ref, normed)


def load_kernel(flags_ref, rows_ref, cot_ref, w_ref, w_buf, xs_ref, us_ref, um_ref, uo_ref, sems, row_sems):
    copies = list(weight_copies(own_index(flags_ref, 1), w_ref, w_buf, sems, w_buf.shape[1]).values())
    for i in range(xs_ref.shape[0]):
        copies.append(pltpu.make_async_copy(cot_ref.at[flags_ref[OWN + i]], us_ref.at[i], row_sems.at[0, i]))
        copies.append(pltpu.make_async_copy(rows_ref.at[flags_ref[STATE + i]], xs_ref.at[i], row_sems.at[1, i]))
    for i, ref in enumerate((um_ref, uo_ref)):
        copies.append(pltpu.make_async_copy(cot_ref.at[flags_ref[OWN + i]], ref, row_sems.at[2, i]))
    for copy in copies:
        copy.start()
    for copy in copies:
        copy.wait()


def forward_kernel(part, live, flags_ref, xm_ref, xo_ref, gains_ref, w_buf, *refs):
    *old, pm_ref, po_ref, gate_ref, upper_ref, xms_ref, xos_ref, normed = refs
    gain = gain_at(flags_ref, gains_ref, part)
    gate, upper = forward_math(None, xm_ref, xo_ref, gain, w_buf, pm_ref, po_ref, normed)
    found = (gate, upper, xm_ref[...], xo_ref[...])
    outs = (gate_ref, upper_ref, xms_ref, xos_ref)
    if old:
        is_live = is_set(flags_ref, KIND, live)
        found = [choose(is_live, a, b[...]) for a, b in zip(found, old)]
    for out, value in zip(outs, found):
        out[...] = value


def active_gradient(um_ref, uo_ref, w_buf):
    size = chunk_of(w_buf.shape[1])
    d_active = None
    for k in range(w_buf.shape[1] // size):
        cols = pl.ds(k * size, size)
        block = jnp.concatenate([um_ref[:, cols], uo_ref[:, cols]], axis=0)
        part = dot(block, w_buf[2, cols])
        d_active = part if d_active is None else d_active + part
    return d_active


def backward_math(d_active, gate, upper, w_buf, pm_ref, po_ref):
    size = chunk_of(w_buf.shape[1])
    half = pm_ref.shape[0]
    sig = jax.nn.sigmoid(gate)
    d_gate = (d_active * upper * (sig * (1.0 + gate * (1.0 - sig)))).astype(BF)
    d_upper = (d_active * (gate * sig)).astype(BF)
    for k in range(w_buf.shape[1] // size):
        cols = pl.ds(k * size, size)
        part = (dot_last(d_gate, w_buf[0, cols]) + dot_last(d_upper, w_buf[1, cols])).astype(BF)
        pm_ref[:, cols] = part[:half]
        po_ref[:, cols] = part[half:]


def cotangent_kernel(um_ref, uo_ref, w_buf, d_ref):
    d_ref[...] = active_gradient(um_ref, uo_ref, w_buf)


def turn_kernel(
    flags_ref, d_ref, xm_ref, xo_ref, oldm_ref, oldo_ref, gains_ref, w_buf, pm_ref, po_ref, latem_ref, lateo_ref, normed
):
    fill_normed(xm_ref, xo_ref, gain_at(flags_ref, gains_ref, 1), normed)
    gate, upper = gate_upper(None, w_buf, normed, chunk_of(w_buf.shape[1]))
    backward_math(d_ref[...], gate, upper, w_buf, pm_ref, po_ref)
    is_outer = is_set(flags_ref, OUTER)
    latem_ref[...] = choose(is_outer, xm_ref[...], oldm_ref[...])
    lateo_ref[...] = choose(is_outer, xo_ref[...], oldo_ref[...])


def backward_kernel(live, has_old, has_late, flags_ref, um_ref, uo_ref, gate_ref, upper_ref, w_buf, *refs):
    refs = list(refs)
    old = [refs.pop(0) for _ in range(2)] if has_old else []
    late = refs.pop(0) if has_late else None
    pm_ref, po_ref, ums_ref, uos_ref = refs[:4]
    backward_math(active_gradient(um_ref, uo_ref, w_buf), gate_ref[...], upper_ref[...], w_buf, pm_ref, po_ref)
    found = [um_ref[...], uo_ref[...]]
    if old:
        is_live = is_set(flags_ref, KIND, live)
        found = [choose(is_live, a, b[...]) for a, b in zip(found, old)]
    ums_ref[...], uos_ref[...] = found
    if has_late:
        is_near = is_set(flags_ref, NEAR)
        refs[4][...] = choose(is_near, found[0], late[...])
        refs[5][...] = choose(is_near, late[...], found[0])


def hold_kernel(part, backward, flags_ref, pm_ref, recv_ref, base_ref, *refs):
    summed = pm_ref[...].astype(F32) + recv_ref[...].astype(F32)
    if backward:
        state_ref, gains_ref, *outs = refs
        gain = gain_at(flags_ref, gains_ref, part)
        unit, root, _ = norm_rows(state_ref[...], gain)
        d_unit = summed * gain
        summed = (d_unit - unit * jnp.mean(d_unit * unit, axis=-1, keepdims=True)) / root
    else:
        outs = refs
    base = jnp.where(is_set(flags_ref, FIRST_CHIP), base_ref[...].astype(F32), 0.0)
    (out,) = outs
    out[...] = (summed + base).astype(BF)


def sum_kernel(first_ref, second_ref, out_ref):
    out_ref[...] = (first_ref[...].astype(F32) + second_ref[...].astype(F32)).astype(BF)


def own_first_kernel(
    flags_ref, xs_ref, em_ref, eo_ref, lm_ref, lo_ref, p0, p1, p2, p3, p4, p5, q0, q1, q2, q3, q4, q5, gains_ref, w_ref,
    turned_ref, left_ref, right_ref, active_ref, w_buf, normed, sems
):
    features = w_buf.shape[1]
    size = chunk_of(features)
    count = features // size
    copies = {}
    for k in range(count):
        rows = pl.ds(k * size, size)
        for matrix in range(2):
            copies[matrix, k] = pltpu.make_async_copy(
                w_ref.at[0, matrix, rows], w_buf.at[matrix, rows], sems.at[matrix, k]
            )
            copies[matrix, k].start()
    gain = gains_ref[0:1]
    pieces, half = xs_ref.shape[:2]
    is_near = flags_ref[NEAR] == 1
    is_outer = flags_ref[OUTER] == 1
    inputs_used = jnp.logical_and(is_near, is_outer)

    def put(piece, rows):
        normed[piece * half : (piece + 1) * half] = norm_rows(rows, gain)[2]

    @pl.when(inputs_used)
    def _():
        for piece in range(pieces):
            put(piece, xs_ref[piece])

    @pl.when(jnp.logical_and(is_near, jnp.logical_not(is_outer)))
    def _():
        for i, ref in enumerate((em_ref, eo_ref, p0, p1, p2, p3, p4, p5)):
            put(i, ref[...])

    @pl.when(jnp.logical_not(is_near))
    def _():
        for i, ref in enumerate((lm_ref, lo_ref, q0, q1, q2, q3, q4, q5)):
            put(i, ref[...])

    gate, upper = gate_upper(copies, w_buf, normed, size)
    sig = jax.nn.sigmoid(gate)
    smooth = gate * sig
    left_ref[...] = upper * (sig * (1.0 + gate * (1.0 - sig)))
    right_ref[...] = smooth
    active_ref[...] = (smooth * upper).astype(BF)
    for k in range(count):
        cols = pl.ds(k * size, size)
        turned_ref[cols] = normed[:, cols].T


def own_last_kernel(flags_ref, us_ref, *refs):
    refs = list(refs)

    def take(count):
        return [refs.pop(0) for _ in range(count)]

    direct, early, late, arrived = take(8), take(2), take(2), take(6)
    turned_ref, left_ref, right_ref, active_ref, early_ref, late_ref = take(6)
    out_ref, u_buf, d_act, out_buf, sems = take(5)
    features = turned_ref.shape[0]
    size = chunk_of(features)
    count = features // size
    pieces, half = us_ref.shape[:2]
    is_near = flags_ref[NEAR] == 1
    is_outer = flags_ref[OUTER] == 1

    def fill(sources, w_ref):
        for i in range(pieces):
            u_buf[i * half : (i + 1) * half] = sources[i][...]
        total = None
        for k in range(count):
            cols = pl.ds(k * size, size)
            part = dot(u_buf[:, cols], w_ref[2, cols])
            total = part if total is None else total + part
        d_act[...] = total

    cases = (
        (True, True, direct, early_ref),
        (True, False, [us_ref.at[i] for i in range(pieces)], late_ref),
        (False, True, early + arrived, early_ref),
        (False, False, late + arrived, late_ref),
    )
    for outer, near, sources, w_ref in cases:

        @pl.when(jnp.logical_and(is_outer == outer, is_near == near))
        def _(sources=sources, w_ref=w_ref):
            fill(sources, w_ref)

    copies = []

    def send(matrix, k):
        rows = pl.ds(k * size, size)
        copy = pltpu.make_async_copy(out_buf.at[matrix, rows], out_ref.at[0, matrix, rows], sems.at[matrix, k])
        copy.start()
        copies.append(copy)

    active = active_ref[...]
    d_active = d_act[...]
    for k in range(count):
        cols = pl.ds(k * size, size)
        out_buf[2, cols] = dot_first(u_buf[:, cols], active).astype(BF)
        send(2, k)
    d_gate = (d_active * left_ref[...]).astype(BF)
    d_upper = (d_active * right_ref[...]).astype(BF)
    for k in range(count):
        cols = pl.ds(k * size, size)
        turned = turned_ref[cols]
        out_buf[0, cols] = dot(turned, d_gate).astype(BF)
        send(0, k)
        out_buf[1, cols] = dot(turned, d_upper).astype(BF)
        send(1, k)
    for copy in copies:
        copy.wait()


def call(kernel, name, operands, outs, scratch, limit, flops, moved, hbm=(), out_hbm=False, smem=(0,)):
    specs = [
        SMEM_SPEC if i in smem else HBM_SPEC if i in hbm else VMEM_SPEC for i in range(len(operands))
    ]
    out_spec = HBM_SPEC if out_hbm else VMEM_SPEC
    results = pl.pallas_call(
        kernel,
        out_shape=outs,
        in_specs=specs,
        out_specs=[out_spec] * len(outs),
        scratch_shapes=scratch,
        cost_estimate=pl.CostEstimate(flops=flops, bytes_accessed=moved, transcendentals=0),
        compiler_params=pltpu.CompilerParams(vmem_limit_bytes=limit * MIB),
        name=name,
    )(*operands)
    return list(results)


def body(inputs, cotangent, section_weights, section_gains):
    sections = lax.axis_size("pipe") // REPL
    ranks = lax.axis_size("tensor")
    pipe = lax.axis_index("pipe")
    tensor = lax.axis_index("tensor")
    position = pipe % sections
    replica = pipe // sections
    middle = sections // 2
    near = position < middle
    side = jnp.where(near, 0, 1)
    kind = jnp.where(near, position, sections - 1 - position)
    core = tensor % 2
    chip = tensor // 2
    rows, features = inputs.shape[2:]
    narrow = section_weights.shape[-1]
    chunks = features // chunk_of(features)
    weights = pltpu.with_memory_space_constraint(section_weights[0], pltpu.HBM)
    blocks = pltpu.with_memory_space_constraint(inputs.reshape(-1, rows, features), pltpu.HBM)
    cot_blocks = pltpu.with_memory_space_constraint(cotangent.reshape(-1, rows, features), pltpu.HBM)
    gains = section_gains[0]
    core_swap = [(i, i ^ 1) for i in range(ranks)]
    chip_swap = [(i, (i + 2) % ranks) for i in range(ranks)]

    def spot(across, end, batch):
        return (((replica + across) % REPL) * 2 + end) * 2 + batch

    pairs = ((0, 0), (0, 1), (1, 0), (1, 1))
    pairs_of = ((1, 0), (0, 1), (1, 1))
    own = [spot(across, side ^ turn, batch) for batch in (core, 1 - core) for across, turn in pairs]
    own = [own[i] for i in (0, 4, 1, 2, 3, 5, 6, 7)]
    state = [spot(across, end, batch) for batch in (core, 1 - core) for across, end in pairs]
    flags = [side, near, kind == 0, chip == 0, kind] + own + state
    flags = jnp.stack([jnp.asarray(flag).astype(jnp.int32) for flag in flags])

    def swap_core(block):
        return lax.ppermute(block, "tensor", core_swap)

    def swap_chip(block):
        return lax.ppermute(block, "tensor", chip_swap)

    def place(copy, end, c, rank):
        at = c if end == 0 else sections - 1 - c
        return (copy * sections + at) * ranks + rank

    def send(block, route):
        moves = []
        for copy in range(REPL):
            for end in range(2):
                for c in range(middle):
                    source = route(copy, end, c)
                    if source is None:
                        continue
                    for rank in range(ranks):
                        came = (rank + 2) % ranks if source[3] else rank
                        moves.append((place(*source[:3], came), place(copy, end, c, rank)))
        return lax.ppermute(block, ("pipe", "tensor"), moves)

    def hop(block, source, target, other):
        return send(block, lambda copy, end, c: (copy, end, source, other) if c == target else None)

    def flow(payload, which, wanted):
        turn, shift = pairs_of[which]

        def route(copy, end, c):
            return ((copy + shift) % REPL, end ^ turn, c, False) if wanted(c, end) else None

        return send(payload, route)

    def with_other_core(arrived):
        return arrived + [swap_core(block) for block in arrived]

    def shape(*extent, dtype=BF):
        return jax.ShapeDtypeStruct(extent, dtype)

    row = shape(rows, features)
    pieces = shape(4 * REPL, rows, features)
    gate_shape = shape(2 * rows, narrow, dtype=F32)
    held_shape = pltpu.VMEM((3, features, narrow), BF)
    normed_scratch = pltpu.VMEM((2 * rows, features), BF)
    layer_flops = 12 * rows * features * narrow
    layer_bytes = 6 * features * narrow
    row_bytes = 2 * rows * features

    def layer(kernel, name, operands, outs):
        return call(kernel, name, operands, outs, [normed_scratch], 8, layer_flops, layer_bytes, smem=())

    def hold(part, backward, operands):
        kernel = functools.partial(hold_kernel, part, backward)
        return call(kernel, "hold", [marks] + operands, [row], [], 4, 0, 4 * row_bytes, smem=())[0]

    def total(terms):
        return call(sum_kernel, "total", terms, [row], [], 4, 0, 3 * row_bytes, smem=())[0]

    def kind_of(step):
        return min(step, sections - 1 - step)

    def across(held, source, target, during):
        straight, crossed = hop(held, source, target, False), hop(held, source, target, True)
        straight, crossed, during = lax.optimization_barrier((straight, crossed, during))
        mine = total([straight, crossed])
        return mine, swap_core(mine), during

    def near_early(c, end):
        return c > 0 and end == 0

    def far(c, end):
        return end == 1

    def middle_class(c, end):
        return c > 0

    pm, po, gate, upper, held_early, mine, other, marks = call(
        first_kernel,
        "first_layer",
        [flags, blocks, pltpu.with_memory_space_constraint(gains, pltpu.HBM), weights],
        [row, row, gate_shape, gate_shape, held_shape, row, row, shape(8, 128, dtype=jnp.int32)],
        [
            normed_scratch,
            pltpu.VMEM(gains.shape, F32),
            pltpu.SemaphoreType.DMA((3, chunks)),
            pltpu.SemaphoreType.DMA((3,)),
        ],
        8,
        layer_flops,
        layer_bytes,
        hbm=(1, 2, 3),
    )
    saved = [(gate, upper, mine, other), None]
    loaded = call(
        load_kernel,
        "load_late",
        [flags, blocks, cot_blocks, weights],
        [held_shape, pieces, pieces, row, row],
        [pltpu.SemaphoreType.DMA((3, 1)), pltpu.SemaphoreType.DMA((3, 4 * REPL))],
        4,
        0,
        2 * layer_bytes,
        hbm=(1, 2, 3),
    )
    for step in range(sections - 1):
        part = 0 if step < middle else 1
        if step > 0:
            old = list(saved[part] or ())
            pm, po, *saved[part] = layer(
                functools.partial(forward_kernel, part, kind_of(step)),
                "forward_layer",
                [marks, mine, other, gains, held_late if part else held_early] + old,
                [row, row, gate_shape, gate_shape, row, row],
            )
        held = hold(part, False, [pm, swap_core(po), mine])
        during = ()
        if step == 0:
            during = loaded
        if step == middle:
            held, early_mine = lax.optimization_barrier((held, early_mine))
            during = call(
                cotangent_kernel,
                "cotangent",
                [up_mine, up_other, held_late],
                [gate_shape],
                [],
                4,
                layer_flops // 3,
                layer_bytes // 3,
                smem=(),
            ) + [flow(early_mine, which, near_early) for which in (1, 2)]
        if step == middle - 1:
            held, early_mine = lax.optimization_barrier((held, saved[0][2]))
            crossed = swap_chip(held)
            crossed, first_flow = lax.optimization_barrier((crossed, flow(early_mine, 0, near_early)))
            mine = total([held, crossed])
            other = swap_core(mine)
        else:
            mine, other, during = across(held, kind_of(step), kind_of(step + 1), during)
        if step == 0:
            held_late, input_rows, cot_rows, up_mine, up_other = during
        if step == middle:
            d_active, *later_flows = during
            early_arrived = [first_flow] + later_flows

    early_rows = saved[0][2:]
    gates = [saved[0][:2], saved[1][:2]]
    pm, po, late_mine, late_other = layer(
        turn_kernel,
        "turn_layer",
        [marks, d_active, mine, other, *saved[1][2:], gains, held_late],
        [row] * 4,
    )
    state_mine = [early_rows[0], late_mine]
    ups = [None, (up_mine, up_other)]
    own_rows = 4 * REPL * rows
    for step in range(sections - 1, 0, -1):
        part = 0 if step < middle else 1
        if step < sections - 1:
            old = list(ups[part] or ())
            extra = [ups[1][0]] if step == 1 else []
            pm, po, *kept = layer(
                functools.partial(backward_kernel, kind_of(step), bool(old), bool(extra)),
                "backward_layer",
                [marks, up_mine, up_other, *gates[part], held_late if part else held_early] + old + extra,
                [row] * (6 if extra else 4),
            )
            ups[part] = kept[:2]
        held = hold(part, True, [pm, swap_core(po), up_mine, state_mine[part], gains])
        if step == 1:
            prepared = call(
                own_first_kernel,
                "own_first",
                [flags, input_rows, *early_rows, late_mine, late_other, *early_arrived]
                + with_other_core(late_arrived)
                + [gains, weights],
                [
                    shape(features, own_rows),
                    shape(own_rows, narrow, dtype=F32),
                    shape(own_rows, narrow, dtype=F32),
                    shape(own_rows, narrow),
                ],
                [
                    pltpu.VMEM((2, features, narrow), BF),
                    pltpu.VMEM((own_rows, features), BF),
                    pltpu.SemaphoreType.DMA((2, chunks)),
                ],
                12,
                4 * own_rows * features * narrow,
                8 * features * narrow,
                hbm=(19,),
            )
            held, same, opposite = lax.optimization_barrier((held, *kept[2:]))
            crossed, prepared = lax.optimization_barrier((swap_chip(held), prepared))
            mine = total([held, crossed])
            up_arrived = [flow((opposite, same, opposite)[which], which, middle_class) for which in range(3)]
        elif step == middle:
            held, late = lax.optimization_barrier((held, late))
            crossed = swap_chip(held)
            crossed, last_flow = lax.optimization_barrier((crossed, flow(late, 0, far)))
            late_arrived = [last_flow] + late_flows
            up_mine = total([held, crossed])
            up_other = swap_core(up_mine)
        else:
            during = ()
            if step == sections - 1:
                held, late = lax.optimization_barrier((held, late_mine))
                during = [flow(late, which, far) for which in (1, 2)], with_other_core(early_arrived)
            up_mine, up_other, during = across(held, kind_of(step), kind_of(step - 1), during)
            if step == sections - 1:
                late_flows, early_arrived = during
    straight = [
        send(
            mine,
            lambda copy, end, c, shift=shift, source=source: (
                ((copy + shift) % REPL, source, 1, False) if c == 0 and end == 0 else None
            ),
        )
        for shift, source in pairs
    ]
    return call(
        own_last_kernel,
        "own_last",
        [flags, cot_rows, *with_other_core(straight), *ups[0], *ups[1], *with_other_core(up_arrived)]
        + [*prepared, held_early, held_late],
        [shape(1, 3, features, narrow)],
        [
            pltpu.VMEM((own_rows, features), BF),
            pltpu.VMEM((own_rows, narrow), F32),
            pltpu.VMEM((3, features, narrow), BF),
            pltpu.SemaphoreType.DMA((3, chunks)),
        ],
        16,
        8 * own_rows * features * narrow,
        8 * features * narrow,
        out_hbm=True,
    )[0]


def solution(mesh):
    return jax.shard_map(
        body,
        mesh=mesh,
        in_specs=(P(), P(), P("pipe", None, None, None, "tensor"), P("pipe", None, None)),
        out_specs=P("pipe", None, None, "tensor"),
        check_vma=False,
    )
```

```python
import functools

import jax
import jax.numpy as jnp
from jax import lax
from jax.experimental import pallas as pl
from jax.experimental.pallas import tpu as pltpu
from jax.sharding import PartitionSpec as P

REPL = 2
EPS = 1e-06
BF = jnp.bfloat16
F32 = jnp.float32
SMEM_SPEC = pl.BlockSpec(memory_space=pltpu.SMEM)
VMEM_SPEC = pl.BlockSpec(memory_space=pltpu.VMEM)
HBM_SPEC = pl.BlockSpec(memory_space=pltpu.HBM)
MIB = 1024 * 1024
NEAR, OUTER, FIRST_CHIP, KIND, OWN, STATE = 1, 2, 3, 4, 5, 13


def chunk_of(features):
    for size in (512, 256, 128):
        if features % size == 0:
            return size
    return features


def norm_rows(rows, gain_row):
    widened = rows.astype(F32)
    root = jnp.sqrt(jnp.mean(widened * widened, axis=-1, keepdims=True) + EPS)
    unit = widened / root
    return unit, root, (unit * gain_row).astype(BF)


def dot(left, right):
    return jnp.dot(left, right, preferred_element_type=F32)


def dot_last(left, right):
    return lax.dot_general(left, right, (((1,), (1,)), ((), ())), preferred_element_type=F32)


def dot_first(left, right):
    return lax.dot_general(left, right, (((0,), (0,)), ((), ())), preferred_element_type=F32)


def is_set(flags_ref, index, value=1):
    if len(flags_ref.shape) == 1:
        return flags_ref[index] == value
    return flags_ref[index : index + 1, 0:1] == value


def gain_at(flags_ref, gains_ref, part):
    return jnp.where(is_set(flags_ref, NEAR, 1 - part), gains_ref[0:1], gains_ref[1:2])


def own_index(flags_ref, part):
    return jnp.where(flags_ref[NEAR] == 1 - part, 0, 1)


def choose(condition, first, second):
    kept = first.dtype
    return jnp.where(condition, first.astype(F32), second.astype(F32)).astype(kept)


def weight_copies(which, w_ref, w_buf, sems, size):
    features = w_buf.shape[1]
    copies = {}
    for matrix in range(3):
        for k in range(features // size):
            rows = pl.ds(k * size, size)
            copies[matrix, k] = pltpu.make_async_copy(
                w_ref.at[which, matrix, rows], w_buf.at[matrix, rows], sems.at[matrix, k]
            )
    return copies


def fill_normed(xm_ref, xo_ref, gain, normed):
    half = xm_ref.shape[0]
    normed[:half] = norm_rows(xm_ref[...], gain)[2]
    normed[half:] = norm_rows(xo_ref[...], gain)[2]


def gate_upper(copies, w_buf, normed, size):
    gate = upper = None
    for k in range(w_buf.shape[1] // size):
        cols = pl.ds(k * size, size)
        if copies:
            copies[0, k].wait()
            copies[1, k].wait()
        block = normed[:, cols]
        gate_k = dot(block, w_buf[0, cols])
        upper_k = dot(block, w_buf[1, cols])
        gate = gate_k if gate is None else gate + gate_k
        upper = upper_k if upper is None else upper + upper_k
    return gate, upper


def forward_math(copies, xm_ref, xo_ref, gain, w_buf, pm_ref, po_ref, normed):
    size = chunk_of(w_buf.shape[1])
    half = xm_ref.shape[0]
    fill_normed(xm_ref, xo_ref, gain, normed)
    gate, upper = gate_upper(copies, w_buf, normed, size)
    active = (gate * jax.nn.sigmoid(gate) * upper).astype(BF)
    for k in range(w_buf.shape[1] // size):
        cols = pl.ds(k * size, size)
        if copies:
            copies[2, k].wait()
        part = dot_last(active, w_buf[2, cols]).astype(BF)
        pm_ref[:, cols] = part[:half]
        po_ref[:, cols] = part[half:]
    return gate, upper


def first_kernel(
    flags_ref, rows_ref, gains_ref, w_ref,
    pm_ref, po_ref, gate_ref, upper_ref, w_buf, xm_ref, xo_ref, marks_ref, normed, gains_buf, sems, row_sems
):
    size = chunk_of(w_buf.shape[1])
    moves = [
        pltpu.make_async_copy(rows_ref.at[flags_ref[OWN + i]], ref, row_sems.at[i])
        for i, ref in enumerate((xm_ref, xo_ref))
    ]
    moves.append(pltpu.make_async_copy(gains_ref, gains_buf, row_sems.at[2]))
    for move in moves:
        move.start()
    for i in range(marks_ref.shape[0]):
        marks_ref[i : i + 1] = jnp.full((1, marks_ref.shape[1]), flags_ref[i], jnp.int32)
    for move in moves:
        move.wait()
    copies = weight_copies(own_index(flags_ref, 0), w_ref, w_buf, sems, size)
    for group in ((0, 1), (2,)):
        for k in range(w_buf.shape[1] // size):
            for matrix in group:
                copies[matrix, k].start()
    gain = gain_at(flags_ref, gains_buf, 0)
    gate_ref[...], upper_ref[...] = forward_math(copies, xm_ref, xo_ref, gain, w_buf, pm_ref, po_ref, normed)


def load_kernel(flags_ref, rows_ref, cot_ref, w_ref, w_buf, xs_ref, us_ref, um_ref, uo_ref, sems, row_sems):
    copies = list(weight_copies(own_index(flags_ref, 1), w_ref, w_buf, sems, w_buf.shape[1]).values())
    for i in range(xs_ref.shape[0]):
        copies.append(pltpu.make_async_copy(cot_ref.at[flags_ref[OWN + i]], us_ref.at[i], row_sems.at[0, i]))
        copies.append(pltpu.make_async_copy(rows_ref.at[flags_ref[STATE + i]], xs_ref.at[i], row_sems.at[1, i]))
    for i, ref in enumerate((um_ref, uo_ref)):
        copies.append(pltpu.make_async_copy(cot_ref.at[flags_ref[OWN + i]], ref, row_sems.at[2, i]))
    for copy in copies:
        copy.start()
    for copy in copies:
        copy.wait()


def forward_kernel(part, live, flags_ref, xm_ref, xo_ref, gains_ref, w_buf, *refs):
    *old, pm_ref, po_ref, gate_ref, upper_ref, xms_ref, xos_ref, normed = refs
    gain = gain_at(flags_ref, gains_ref, part)
    gate, upper = forward_math(None, xm_ref, xo_ref, gain, w_buf, pm_ref, po_ref, normed)
    found = (gate, upper, xm_ref[...], xo_ref[...])
    outs = (gate_ref, upper_ref, xms_ref, xos_ref)
    if old:
        is_live = is_set(flags_ref, KIND, live)
        found = [choose(is_live, a, b[...]) for a, b in zip(found, old)]
    for out, value in zip(outs, found):
        out[...] = value


def active_gradient(um_ref, uo_ref, w_buf):
    size = chunk_of(w_buf.shape[1])
    d_active = None
    for k in range(w_buf.shape[1] // size):
        cols = pl.ds(k * size, size)
        block = jnp.concatenate([um_ref[:, cols], uo_ref[:, cols]], axis=0)
        part = dot(block, w_buf[2, cols])
        d_active = part if d_active is None else d_active + part
    return d_active


def backward_math(d_active, gate, upper, w_buf, pm_ref, po_ref):
    size = chunk_of(w_buf.shape[1])
    half = pm_ref.shape[0]
    sig = jax.nn.sigmoid(gate)
    d_gate = (d_active * upper * (sig * (1.0 + gate * (1.0 - sig)))).astype(BF)
    d_upper = (d_active * (gate * sig)).astype(BF)
    for k in range(w_buf.shape[1] // size):
        cols = pl.ds(k * size, size)
        part = (dot_last(d_gate, w_buf[0, cols]) + dot_last(d_upper, w_buf[1, cols])).astype(BF)
        pm_ref[:, cols] = part[:half]
        po_ref[:, cols] = part[half:]


def cotangent_kernel(um_ref, uo_ref, w_buf, d_ref):
    d_ref[...] = active_gradient(um_ref, uo_ref, w_buf)


def turn_kernel(
    flags_ref, d_ref, xm_ref, xo_ref, oldm_ref, oldo_ref, gains_ref, w_buf, pm_ref, po_ref, latem_ref, lateo_ref, normed
):
    fill_normed(xm_ref, xo_ref, gain_at(flags_ref, gains_ref, 1), normed)
    gate, upper = gate_upper(None, w_buf, normed, chunk_of(w_buf.shape[1]))
    backward_math(d_ref[...], gate, upper, w_buf, pm_ref, po_ref)
    is_outer = is_set(flags_ref, OUTER)
    latem_ref[...] = choose(is_outer, xm_ref[...], oldm_ref[...])
    lateo_ref[...] = choose(is_outer, xo_ref[...], oldo_ref[...])


def backward_kernel(live, has_old, has_late, flags_ref, um_ref, uo_ref, gate_ref, upper_ref, w_buf, *refs):
    refs = list(refs)
    old = [refs.pop(0) for _ in range(2)] if has_old else []
    late = refs.pop(0) if has_late else None
    pm_ref, po_ref, ums_ref, uos_ref = refs[:4]
    backward_math(active_gradient(um_ref, uo_ref, w_buf), gate_ref[...], upper_ref[...], w_buf, pm_ref, po_ref)
    found = [um_ref[...], uo_ref[...]]
    if old:
        is_live = is_set(flags_ref, KIND, live)
        found = [choose(is_live, a, b[...]) for a, b in zip(found, old)]
    ums_ref[...], uos_ref[...] = found
    if has_late:
        is_near = is_set(flags_ref, NEAR)
        refs[4][...] = choose(is_near, found[0], late[...])
        refs[5][...] = choose(is_near, late[...], found[0])


def hold_kernel(part, backward, flags_ref, pm_ref, recv_ref, base_ref, *refs):
    summed = pm_ref[...].astype(F32) + recv_ref[...].astype(F32)
    if backward:
        state_ref, gains_ref, *outs = refs
        gain = gain_at(flags_ref, gains_ref, part)
        unit, root, _ = norm_rows(state_ref[...], gain)
        d_unit = summed * gain
        summed = (d_unit - unit * jnp.mean(d_unit * unit, axis=-1, keepdims=True)) / root
    else:
        outs = refs
    base = jnp.where(is_set(flags_ref, FIRST_CHIP), base_ref[...].astype(F32), 0.0)
    (out,) = outs
    out[...] = (summed + base).astype(BF)


def sum_kernel(first_ref, second_ref, out_ref):
    out_ref[...] = (first_ref[...].astype(F32) + second_ref[...].astype(F32)).astype(BF)


def own_first_kernel(
    flags_ref, xs_ref, em_ref, eo_ref, lm_ref, lo_ref, p0, p1, p2, p3, p4, p5, q0, q1, q2, q3, q4, q5, gains_ref, w_ref,
    turned_ref, left_ref, right_ref, active_ref, w_buf, normed, sems
):
    features = w_buf.shape[1]
    size = chunk_of(features)
    count = features // size
    copies = {}
    for k in range(count):
        rows = pl.ds(k * size, size)
        for matrix in range(2):
            copies[matrix, k] = pltpu.make_async_copy(
                w_ref.at[0, matrix, rows], w_buf.at[matrix, rows], sems.at[matrix, k]
            )
            copies[matrix, k].start()
    gain = gains_ref[0:1]
    pieces, half = xs_ref.shape[:2]
    is_near = flags_ref[NEAR] == 1
    is_outer = flags_ref[OUTER] == 1
    inputs_used = jnp.logical_and(is_near, is_outer)

    def put(piece, rows):
        normed[piece * half : (piece + 1) * half] = norm_rows(rows, gain)[2]

    @pl.when(inputs_used)
    def _():
        for piece in range(pieces):
            put(piece, xs_ref[piece])

    @pl.when(jnp.logical_and(is_near, jnp.logical_not(is_outer)))
    def _():
        for i, ref in enumerate((em_ref, eo_ref, p0, p1, p2, p3, p4, p5)):
            put(i, ref[...])

    @pl.when(jnp.logical_not(is_near))
    def _():
        for i, ref in enumerate((lm_ref, lo_ref, q0, q1, q2, q3, q4, q5)):
            put(i, ref[...])

    gate, upper = gate_upper(copies, w_buf, normed, size)
    sig = jax.nn.sigmoid(gate)
    smooth = gate * sig
    left_ref[...] = upper * (sig * (1.0 + gate * (1.0 - sig)))
    right_ref[...] = smooth
    active_ref[...] = (smooth * upper).astype(BF)
    for k in range(count):
        cols = pl.ds(k * size, size)
        turned_ref[cols] = normed[:, cols].T


def own_last_kernel(flags_ref, us_ref, *refs):
    refs = list(refs)

    def take(count):
        return [refs.pop(0) for _ in range(count)]

    direct, early, late, arrived = take(8), take(2), take(2), take(6)
    turned_ref, left_ref, right_ref, active_ref, early_ref, late_ref = take(6)
    out_ref, u_buf, d_act, out_buf, sems = take(5)
    features = turned_ref.shape[0]
    size = chunk_of(features)
    count = features // size
    pieces, half = us_ref.shape[:2]
    is_near = flags_ref[NEAR] == 1
    is_outer = flags_ref[OUTER] == 1

    def fill(sources, w_ref):
        for i in range(pieces):
            u_buf[i * half : (i + 1) * half] = sources[i][...]
        total = None
        for k in range(count):
            cols = pl.ds(k * size, size)
            part = dot(u_buf[:, cols], w_ref[2, cols])
            total = part if total is None else total + part
        d_act[...] = total

    cases = (
        (True, True, direct, early_ref),
        (True, False, [us_ref.at[i] for i in range(pieces)], late_ref),
        (False, True, early + arrived, early_ref),
        (False, False, late + arrived, late_ref),
    )
    for outer, near, sources, w_ref in cases:

        @pl.when(jnp.logical_and(is_outer == outer, is_near == near))
        def _(sources=sources, w_ref=w_ref):
            fill(sources, w_ref)

    copies = []

    def send(matrix, k):
        rows = pl.ds(k * size, size)
        copy = pltpu.make_async_copy(out_buf.at[matrix, rows], out_ref.at[0, matrix, rows], sems.at[matrix, k])
        copy.start()
        copies.append(copy)

    active = active_ref[...]
    d_active = d_act[...]
    for k in range(count):
        cols = pl.ds(k * size, size)
        out_buf[2, cols] = dot_first(u_buf[:, cols], active).astype(BF)
        send(2, k)
    d_gate = (d_active * left_ref[...]).astype(BF)
    d_upper = (d_active * right_ref[...]).astype(BF)
    for k in range(count):
        cols = pl.ds(k * size, size)
        turned = turned_ref[cols]
        out_buf[0, cols] = dot(turned, d_gate).astype(BF)
        send(0, k)
        out_buf[1, cols] = dot(turned, d_upper).astype(BF)
        send(1, k)
    for copy in copies:
        copy.wait()


def call(kernel, name, operands, outs, scratch, limit, flops, moved, hbm=(), out_hbm=False, smem=(0,)):
    specs = [
        SMEM_SPEC if i in smem else HBM_SPEC if i in hbm else VMEM_SPEC for i in range(len(operands))
    ]
    out_spec = HBM_SPEC if out_hbm else VMEM_SPEC
    results = pl.pallas_call(
        kernel,
        out_shape=outs,
        in_specs=specs,
        out_specs=[out_spec] * len(outs),
        scratch_shapes=scratch,
        cost_estimate=pl.CostEstimate(flops=flops, bytes_accessed=moved, transcendentals=0),
        compiler_params=pltpu.CompilerParams(vmem_limit_bytes=limit * MIB),
        name=name,
    )(*operands)
    return list(results)


def body(inputs, cotangent, section_weights, section_gains):
    sections = lax.axis_size("pipe") // REPL
    ranks = lax.axis_size("tensor")
    pipe = lax.axis_index("pipe")
    tensor = lax.axis_index("tensor")
    position = pipe % sections
    replica = pipe // sections
    middle = sections // 2
    near = position < middle
    side = jnp.where(near, 0, 1)
    kind = jnp.where(near, position, sections - 1 - position)
    core = tensor % 2
    chip = tensor // 2
    rows, features = inputs.shape[2:]
    narrow = section_weights.shape[-1]
    chunks = features // chunk_of(features)
    weights = pltpu.with_memory_space_constraint(section_weights[0], pltpu.HBM)
    blocks = pltpu.with_memory_space_constraint(inputs.reshape(-1, rows, features), pltpu.HBM)
    cot_blocks = pltpu.with_memory_space_constraint(cotangent.reshape(-1, rows, features), pltpu.HBM)
    gains = section_gains[0]
    core_swap = [(i, i ^ 1) for i in range(ranks)]
    chip_swap = [(i, (i + 2) % ranks) for i in range(ranks)]

    def spot(across, end, batch):
        return (((replica + across) % REPL) * 2 + end) * 2 + batch

    pairs = ((0, 0), (0, 1), (1, 0), (1, 1))
    pairs_of = ((1, 0), (0, 1), (1, 1))
    own = [spot(across, side ^ turn, batch) for batch in (core, 1 - core) for across, turn in pairs]
    own = [own[i] for i in (0, 4, 1, 2, 3, 5, 6, 7)]
    state = [spot(across, end, batch) for batch in (core, 1 - core) for across, end in pairs]
    flags = [side, near, kind == 0, chip == 0, kind] + own + state
    flags = jnp.stack([jnp.asarray(flag).astype(jnp.int32) for flag in flags])

    def swap_core(block):
        return lax.ppermute(block, "tensor", core_swap)

    def swap_chip(block):
        return lax.ppermute(block, "tensor", chip_swap)

    def place(copy, end, c, rank):
        at = c if end == 0 else sections - 1 - c
        return (copy * sections + at) * ranks + rank

    def send(block, route):
        moves = []
        for copy in range(REPL):
            for end in range(2):
                for c in range(middle):
                    source = route(copy, end, c)
                    if source is None:
                        continue
                    for rank in range(ranks):
                        came = (rank + 2) % ranks if source[3] else rank
                        moves.append((place(*source[:3], came), place(copy, end, c, rank)))
        return lax.ppermute(block, ("pipe", "tensor"), moves)

    def hop(block, source, target, other):
        return send(block, lambda copy, end, c: (copy, end, source, other) if c == target else None)

    def flow(payload, which, wanted):
        turn, shift = pairs_of[which]

        def route(copy, end, c):
            return ((copy + shift) % REPL, end ^ turn, c, False) if wanted(c, end) else None

        return send(payload, route)

    def with_other_core(arrived):
        return arrived + [swap_core(block) for block in arrived]

    def shape(*extent, dtype=BF):
        return jax.ShapeDtypeStruct(extent, dtype)

    row = shape(rows, features)
    pieces = shape(4 * REPL, rows, features)
    gate_shape = shape(2 * rows, narrow, dtype=F32)
    held_shape = pltpu.VMEM((3, features, narrow), BF)
    normed_scratch = pltpu.VMEM((2 * rows, features), BF)
    layer_flops = 12 * rows * features * narrow
    layer_bytes = 6 * features * narrow
    row_bytes = 2 * rows * features

    def layer(kernel, name, operands, outs):
        return call(kernel, name, operands, outs, [normed_scratch], 8, layer_flops, layer_bytes, smem=())

    def hold(part, backward, operands):
        kernel = functools.partial(hold_kernel, part, backward)
        return call(kernel, "hold", [marks] + operands, [row], [], 4, 0, 4 * row_bytes, smem=())[0]

    def total(terms):
        return call(sum_kernel, "total", terms, [row], [], 4, 0, 3 * row_bytes, smem=())[0]

    def kind_of(step):
        return min(step, sections - 1 - step)

    def across(held, source, target, during, flows=()):
        straight, crossed = hop(held, source, target, False), hop(held, source, target, True)
        straight, crossed, during = lax.optimization_barrier((straight, crossed, during))
        mine = total([straight, crossed])
        other, flows = lax.optimization_barrier((swap_core(mine), flows))
        return mine, other, during, flows

    def near_early(c, end):
        return c > 0 and end == 0

    def far(c, end):
        return end == 1

    def middle_class(c, end):
        return c > 0

    pm, po, gate, upper, held_early, mine, other, marks = call(
        first_kernel,
        "first_layer",
        [flags, blocks, pltpu.with_memory_space_constraint(gains, pltpu.HBM), weights],
        [row, row, gate_shape, gate_shape, held_shape, row, row, shape(8, 128, dtype=jnp.int32)],
        [
            normed_scratch,
            pltpu.VMEM(gains.shape, F32),
            pltpu.SemaphoreType.DMA((3, chunks)),
            pltpu.SemaphoreType.DMA((3,)),
        ],
        8,
        layer_flops,
        layer_bytes,
        hbm=(1, 2, 3),
    )
    saved = [(gate, upper, mine, other), None]
    loaded = call(
        load_kernel,
        "load_late",
        [flags, blocks, cot_blocks, weights],
        [held_shape, pieces, pieces, row, row],
        [pltpu.SemaphoreType.DMA((3, 1)), pltpu.SemaphoreType.DMA((3, 4 * REPL))],
        4,
        0,
        2 * layer_bytes,
        hbm=(1, 2, 3),
    )
    for step in range(sections - 1):
        part = 0 if step < middle else 1
        if step > 0:
            old = list(saved[part] or ())
            pm, po, *saved[part] = layer(
                functools.partial(forward_kernel, part, kind_of(step)),
                "forward_layer",
                [marks, mine, other, gains, held_late if part else held_early] + old,
                [row, row, gate_shape, gate_shape, row, row],
            )
        held = hold(part, False, [pm, swap_core(po), mine])
        during = flows = ()
        if step == 0:
            during = loaded
        if step == middle:
            held, early_mine = lax.optimization_barrier((held, early_mine))
            during = call(
                cotangent_kernel,
                "cotangent",
                [up_mine, up_other, held_late],
                [gate_shape],
                [],
                4,
                layer_flops // 3,
                layer_bytes // 3,
                smem=(),
            )
            held, first_flow = lax.optimization_barrier((held, first_flow))
            flows = [flow(payload, 1, near_early) for payload in (early_mine, first_flow)]
        if step == middle - 1:
            held, early_mine = lax.optimization_barrier((held, saved[0][2]))
            crossed = swap_chip(held)
            crossed, first_flow = lax.optimization_barrier((crossed, flow(early_mine, 0, near_early)))
            mine = total([held, crossed])
            other = swap_core(mine)
        else:
            mine, other, during, flows = across(held, kind_of(step), kind_of(step + 1), during, flows)
        if step == 0:
            held_late, input_rows, cot_rows, up_mine, up_other = during
        if step == middle:
            (d_active,) = during
            early_arrived = [first_flow] + list(flows)

    early_rows = saved[0][2:]
    gates = [saved[0][:2], saved[1][:2]]
    pm, po, late_mine, late_other = layer(
        turn_kernel,
        "turn_layer",
        [marks, d_active, mine, other, *saved[1][2:], gains, held_late],
        [row] * 4,
    )
    state_mine = [early_rows[0], late_mine]
    ups = [None, (up_mine, up_other)]
    own_rows = 4 * REPL * rows
    for step in range(sections - 1, 0, -1):
        part = 0 if step < middle else 1
        if step < sections - 1:
            old = list(ups[part] or ())
            extra = [ups[1][0]] if step == 1 else []
            pm, po, *kept = layer(
                functools.partial(backward_kernel, kind_of(step), bool(old), bool(extra)),
                "backward_layer",
                [marks, up_mine, up_other, *gates[part], held_late if part else held_early] + old + extra,
                [row] * (6 if extra else 4),
            )
            ups[part] = kept[:2]
        held = hold(part, True, [pm, swap_core(po), up_mine, state_mine[part], gains])
        if step == 1:
            prepared = call(
                own_first_kernel,
                "own_first",
                [flags, input_rows, *early_rows, late_mine, late_other, *early_arrived]
                + with_other_core(late_arrived)
                + [gains, weights],
                [
                    shape(features, own_rows),
                    shape(own_rows, narrow, dtype=F32),
                    shape(own_rows, narrow, dtype=F32),
                    shape(own_rows, narrow),
                ],
                [
                    pltpu.VMEM((2, features, narrow), BF),
                    pltpu.VMEM((own_rows, features), BF),
                    pltpu.SemaphoreType.DMA((2, chunks)),
                ],
                12,
                4 * own_rows * features * narrow,
                8 * features * narrow,
                hbm=(19,),
            )
            held, same, opposite = lax.optimization_barrier((held, *kept[2:]))
            crossed, prepared = lax.optimization_barrier((swap_chip(held), prepared))
            mine = total([held, crossed])
            up_first = flow(opposite, 0, middle_class)
            mine, up_first, same = lax.optimization_barrier((mine, up_first, same))
        elif step == middle:
            held, late = lax.optimization_barrier((held, late))
            crossed = swap_chip(held)
            late_arrived = [flow(late, 0, far), late_mirror, flow(late_mirror, 0, far)]
            up_mine = total([held, crossed])
            up_other, late_arrived = lax.optimization_barrier((swap_core(up_mine), late_arrived))
        else:
            during = flows = ()
            if step == sections - 1:
                held, late = lax.optimization_barrier((held, late_mine))
                during = with_other_core(early_arrived)
                flows = [flow(late, 1, lambda c, end: True)]
            up_mine, up_other, during, flows = across(held, kind_of(step), kind_of(step - 1), during, flows)
            if step == sections - 1:
                early_arrived = during
                (late_mirror,) = flows
    straight = [
        send(
            mine,
            lambda copy, end, c, shift=shift, source=source: (
                ((copy + shift) % REPL, source, 1, False) if c == 0 and end == 0 else None
            ),
        )
        for shift, source in pairs
    ]
    up_arrived = [up_first] + [flow(payload, 1, middle_class) for payload in (same, up_first)]
    straight, up_arrived = lax.optimization_barrier((straight, up_arrived))
    return call(
        own_last_kernel,
        "own_last",
        [flags, cot_rows, *with_other_core(straight), *ups[0], *ups[1], *with_other_core(up_arrived)]
        + [*prepared, held_early, held_late],
        [shape(1, 3, features, narrow)],
        [
            pltpu.VMEM((own_rows, features), BF),
            pltpu.VMEM((own_rows, narrow), F32),
            pltpu.VMEM((3, features, narrow), BF),
            pltpu.SemaphoreType.DMA((3, chunks)),
        ],
        16,
        8 * own_rows * features * narrow,
        8 * features * narrow,
        out_hbm=True,
    )[0]


def solution(mesh):
    return jax.shard_map(
        body,
        mesh=mesh,
        in_specs=(P(), P(), P("pipe", None, None, None, "tensor"), P("pipe", None, None)),
        out_specs=P("pipe", None, None, "tensor"),
        check_vma=False,
    )
```

```python
import functools

import jax
import jax.numpy as jnp
from jax import lax
from jax.experimental import pallas as pl
from jax.experimental.pallas import tpu as pltpu
from jax.sharding import PartitionSpec as P

REPL = 2
EPS = 1e-06
BF = jnp.bfloat16
F32 = jnp.float32
SMEM_SPEC = pl.BlockSpec(memory_space=pltpu.SMEM)
VMEM_SPEC = pl.BlockSpec(memory_space=pltpu.VMEM)
HBM_SPEC = pl.BlockSpec(memory_space=pltpu.HBM)
MIB = 1024 * 1024
NEAR, OUTER, FIRST_CHIP, KIND, OWN, STATE = 1, 2, 3, 4, 5, 13


def chunk_of(features):
    for size in (512, 256, 128):
        if features % size == 0:
            return size
    return features


def norm_rows(rows, gain_row):
    widened = rows.astype(F32)
    root = jnp.sqrt(jnp.mean(widened * widened, axis=-1, keepdims=True) + EPS)
    unit = widened / root
    return unit, root, (unit * gain_row).astype(BF)


def dot(left, right):
    return jnp.dot(left, right, preferred_element_type=F32)


def dot_last(left, right):
    return lax.dot_general(left, right, (((1,), (1,)), ((), ())), preferred_element_type=F32)


def dot_first(left, right):
    return lax.dot_general(left, right, (((0,), (0,)), ((), ())), preferred_element_type=F32)


def is_set(flags_ref, index, value=1):
    if len(flags_ref.shape) == 1:
        return flags_ref[index] == value
    return flags_ref[index : index + 1, 0:1] == value


def gain_at(flags_ref, gains_ref, part):
    return jnp.where(is_set(flags_ref, NEAR, 1 - part), gains_ref[0:1], gains_ref[1:2])


def own_index(flags_ref, part):
    return jnp.where(flags_ref[NEAR] == 1 - part, 0, 1)


def choose(condition, first, second):
    kept = first.dtype
    return jnp.where(condition, first.astype(F32), second.astype(F32)).astype(kept)


def weight_copies(which, w_ref, w_buf, sems, size):
    features = w_buf.shape[1]
    copies = {}
    for matrix in range(3):
        for k in range(features // size):
            rows = pl.ds(k * size, size)
            copies[matrix, k] = pltpu.make_async_copy(
                w_ref.at[which, matrix, rows], w_buf.at[matrix, rows], sems.at[matrix, k]
            )
    return copies


def fill_normed(xm_ref, xo_ref, gain, normed):
    half = xm_ref.shape[0]
    normed[:half] = norm_rows(xm_ref[...], gain)[2]
    normed[half:] = norm_rows(xo_ref[...], gain)[2]


def gate_upper(copies, w_buf, normed, size):
    gate = upper = None
    for k in range(w_buf.shape[1] // size):
        cols = pl.ds(k * size, size)
        if copies:
            copies[0, k].wait()
            copies[1, k].wait()
        block = normed[:, cols]
        gate_k = dot(block, w_buf[0, cols])
        upper_k = dot(block, w_buf[1, cols])
        gate = gate_k if gate is None else gate + gate_k
        upper = upper_k if upper is None else upper + upper_k
    return gate, upper


def forward_math(copies, xm_ref, xo_ref, gain, w_buf, pm_ref, po_ref, normed):
    size = chunk_of(w_buf.shape[1])
    half = xm_ref.shape[0]
    fill_normed(xm_ref, xo_ref, gain, normed)
    gate, upper = gate_upper(copies, w_buf, normed, size)
    active = (gate * jax.nn.sigmoid(gate) * upper).astype(BF)
    for k in range(w_buf.shape[1] // size):
        cols = pl.ds(k * size, size)
        if copies:
            copies[2, k].wait()
        part = dot_last(active, w_buf[2, cols]).astype(BF)
        pm_ref[:, cols] = part[:half]
        po_ref[:, cols] = part[half:]
    return gate, upper


def first_kernel(
    flags_ref, rows_ref, gains_ref, w_ref,
    pm_ref, po_ref, gate_ref, upper_ref, w_buf, xm_ref, xo_ref, marks_ref, normed, gains_buf, sems, row_sems
):
    size = chunk_of(w_buf.shape[1])
    moves = [
        pltpu.make_async_copy(rows_ref.at[flags_ref[OWN + i]], ref, row_sems.at[i])
        for i, ref in enumerate((xm_ref, xo_ref))
    ]
    moves.append(pltpu.make_async_copy(gains_ref, gains_buf, row_sems.at[2]))
    for move in moves:
        move.start()
    for i in range(marks_ref.shape[0]):
        marks_ref[i : i + 1] = jnp.full((1, marks_ref.shape[1]), flags_ref[i], jnp.int32)
    for move in moves:
        move.wait()
    copies = weight_copies(own_index(flags_ref, 0), w_ref, w_buf, sems, size)
    for group in ((0, 1), (2,)):
        for k in range(w_buf.shape[1] // size):
            for matrix in group:
                copies[matrix, k].start()
    gain = gain_at(flags_ref, gains_buf, 0)
    gate_ref[...], upper_ref[...] = forward_math(copies, xm_ref, xo_ref, gain, w_buf, pm_ref, po_ref, normed)


def load_kernel(flags_ref, rows_ref, cot_ref, w_ref, w_buf, xs_ref, us_ref, um_ref, uo_ref, sems, row_sems):
    copies = list(weight_copies(own_index(flags_ref, 1), w_ref, w_buf, sems, w_buf.shape[1]).values())
    for i in range(xs_ref.shape[0]):
        copies.append(pltpu.make_async_copy(cot_ref.at[flags_ref[OWN + i]], us_ref.at[i], row_sems.at[0, i]))
        copies.append(pltpu.make_async_copy(rows_ref.at[flags_ref[STATE + i]], xs_ref.at[i], row_sems.at[1, i]))
    for i, ref in enumerate((um_ref, uo_ref)):
        copies.append(pltpu.make_async_copy(cot_ref.at[flags_ref[OWN + i]], ref, row_sems.at[2, i]))
    for copy in copies:
        copy.start()
    for copy in copies:
        copy.wait()


def forward_kernel(part, live, flags_ref, xm_ref, xo_ref, gains_ref, w_buf, *refs):
    *old, pm_ref, po_ref, gate_ref, upper_ref, xms_ref, xos_ref, normed = refs
    gain = gain_at(flags_ref, gains_ref, part)
    gate, upper = forward_math(None, xm_ref, xo_ref, gain, w_buf, pm_ref, po_ref, normed)
    found = (gate, upper, xm_ref[...], xo_ref[...])
    outs = (gate_ref, upper_ref, xms_ref, xos_ref)
    if old:
        is_live = is_set(flags_ref, KIND, live)
        found = [choose(is_live, a, b[...]) for a, b in zip(found, old)]
    for out, value in zip(outs, found):
        out[...] = value


def active_gradient(um_ref, uo_ref, w_buf):
    size = chunk_of(w_buf.shape[1])
    d_active = None
    for k in range(w_buf.shape[1] // size):
        cols = pl.ds(k * size, size)
        block = jnp.concatenate([um_ref[:, cols], uo_ref[:, cols]], axis=0)
        part = dot(block, w_buf[2, cols])
        d_active = part if d_active is None else d_active + part
    return d_active


def backward_math(d_active, gate, upper, w_buf, pm_ref, po_ref):
    size = chunk_of(w_buf.shape[1])
    half = pm_ref.shape[0]
    sig = jax.nn.sigmoid(gate)
    d_gate = (d_active * upper * (sig * (1.0 + gate * (1.0 - sig)))).astype(BF)
    d_upper = (d_active * (gate * sig)).astype(BF)
    for k in range(w_buf.shape[1] // size):
        cols = pl.ds(k * size, size)
        part = (dot_last(d_gate, w_buf[0, cols]) + dot_last(d_upper, w_buf[1, cols])).astype(BF)
        pm_ref[:, cols] = part[:half]
        po_ref[:, cols] = part[half:]


def cotangent_kernel(um_ref, uo_ref, w_buf, d_ref):
    d_ref[...] = active_gradient(um_ref, uo_ref, w_buf)


def turn_kernel(
    flags_ref, d_ref, xm_ref, xo_ref, oldm_ref, oldo_ref, gains_ref, w_buf, pm_ref, po_ref, latem_ref, lateo_ref, normed
):
    fill_normed(xm_ref, xo_ref, gain_at(flags_ref, gains_ref, 1), normed)
    gate, upper = gate_upper(None, w_buf, normed, chunk_of(w_buf.shape[1]))
    backward_math(d_ref[...], gate, upper, w_buf, pm_ref, po_ref)
    is_outer = is_set(flags_ref, OUTER)
    latem_ref[...] = choose(is_outer, xm_ref[...], oldm_ref[...])
    lateo_ref[...] = choose(is_outer, xo_ref[...], oldo_ref[...])


def backward_kernel(live, has_old, has_late, flags_ref, um_ref, uo_ref, gate_ref, upper_ref, w_buf, *refs):
    refs = list(refs)
    old = [refs.pop(0) for _ in range(2)] if has_old else []
    late = refs.pop(0) if has_late else None
    pm_ref, po_ref, ums_ref, uos_ref = refs[:4]
    backward_math(active_gradient(um_ref, uo_ref, w_buf), gate_ref[...], upper_ref[...], w_buf, pm_ref, po_ref)
    found = [um_ref[...], uo_ref[...]]
    if old:
        is_live = is_set(flags_ref, KIND, live)
        found = [choose(is_live, a, b[...]) for a, b in zip(found, old)]
    ums_ref[...], uos_ref[...] = found
    if has_late:
        is_near = is_set(flags_ref, NEAR)
        refs[4][...] = choose(is_near, found[0], late[...])
        refs[5][...] = choose(is_near, late[...], found[0])


def hold_kernel(part, backward, flags_ref, pm_ref, recv_ref, base_ref, *refs):
    summed = pm_ref[...].astype(F32) + recv_ref[...].astype(F32)
    if backward:
        state_ref, gains_ref, *outs = refs
        gain = gain_at(flags_ref, gains_ref, part)
        unit, root, _ = norm_rows(state_ref[...], gain)
        d_unit = summed * gain
        summed = (d_unit - unit * jnp.mean(d_unit * unit, axis=-1, keepdims=True)) / root
    else:
        outs = refs
    base = jnp.where(is_set(flags_ref, FIRST_CHIP), base_ref[...].astype(F32), 0.0)
    (out,) = outs
    out[...] = (summed + base).astype(BF)


def sides_kernel(marks_ref, early_ref, late_ref, same_ref, opposite_ref):
    is_near = is_set(marks_ref, NEAR)
    same_ref[...] = choose(is_near, early_ref[...], late_ref[...])
    opposite_ref[...] = choose(is_near, late_ref[...], early_ref[...])


def sum_kernel(first_ref, second_ref, out_ref):
    out_ref[...] = (first_ref[...].astype(F32) + second_ref[...].astype(F32)).astype(BF)


def own_first_kernel(
    flags_ref, xs_ref, em_ref, eo_ref, lm_ref, lo_ref, p0, p1, p2, p3, p4, p5, q0, q1, q2, q3, q4, q5, gains_ref, w_ref,
    turned_ref, left_ref, right_ref, active_ref, w_buf, normed, sems
):
    features = w_buf.shape[1]
    size = chunk_of(features)
    count = features // size
    copies = {}
    for k in range(count):
        rows = pl.ds(k * size, size)
        for matrix in range(2):
            copies[matrix, k] = pltpu.make_async_copy(
                w_ref.at[0, matrix, rows], w_buf.at[matrix, rows], sems.at[matrix, k]
            )
            copies[matrix, k].start()
    gain = gains_ref[0:1]
    pieces, half = xs_ref.shape[:2]
    is_near = flags_ref[NEAR] == 1
    is_outer = flags_ref[OUTER] == 1
    inputs_used = jnp.logical_and(is_near, is_outer)

    def put(piece, rows):
        normed[piece * half : (piece + 1) * half] = norm_rows(rows, gain)[2]

    @pl.when(inputs_used)
    def _():
        for piece in range(pieces):
            put(piece, xs_ref[piece])

    cases = (
        (False, True, (em_ref, eo_ref, p0, p1, p2, p3, p4, p5)),
        (False, False, (lm_ref, lo_ref, p0, p1, p2, p3, p4, p5)),
        (True, False, (lm_ref, lo_ref, q0, q1, q2, q3, q4, q5)),
    )
    for outer, near, sources in cases:

        @pl.when(jnp.logical_and(is_outer == outer, is_near == near))
        def _(sources=sources):
            for i, ref in enumerate(sources):
                put(i, ref[...])

    gate, upper = gate_upper(copies, w_buf, normed, size)
    sig = jax.nn.sigmoid(gate)
    smooth = gate * sig
    left_ref[...] = upper * (sig * (1.0 + gate * (1.0 - sig)))
    right_ref[...] = smooth
    active_ref[...] = (smooth * upper).astype(BF)
    for k in range(count):
        cols = pl.ds(k * size, size)
        turned_ref[cols] = normed[:, cols].T


def own_last_kernel(flags_ref, us_ref, *refs):
    refs = list(refs)

    def take(count):
        return [refs.pop(0) for _ in range(count)]

    direct, early, late, arrived = take(8), take(2), take(2), take(6)
    turned_ref, left_ref, right_ref, active_ref, early_ref, late_ref = take(6)
    out_ref, u_buf, d_act, out_buf, sems = take(5)
    features = turned_ref.shape[0]
    size = chunk_of(features)
    count = features // size
    pieces, half = us_ref.shape[:2]
    is_near = flags_ref[NEAR] == 1
    is_outer = flags_ref[OUTER] == 1

    def fill(sources, w_ref):
        for i in range(pieces):
            u_buf[i * half : (i + 1) * half] = sources[i][...]
        total = None
        for k in range(count):
            cols = pl.ds(k * size, size)
            part = dot(u_buf[:, cols], w_ref[2, cols])
            total = part if total is None else total + part
        d_act[...] = total

    cases = (
        (True, True, direct, early_ref),
        (True, False, [us_ref.at[i] for i in range(pieces)], late_ref),
        (False, True, early + arrived, early_ref),
        (False, False, late + arrived, late_ref),
    )
    for outer, near, sources, w_ref in cases:

        @pl.when(jnp.logical_and(is_outer == outer, is_near == near))
        def _(sources=sources, w_ref=w_ref):
            fill(sources, w_ref)

    copies = []

    def send(matrix, k):
        rows = pl.ds(k * size, size)
        copy = pltpu.make_async_copy(out_buf.at[matrix, rows], out_ref.at[0, matrix, rows], sems.at[matrix, k])
        copy.start()
        copies.append(copy)

    active = active_ref[...]
    d_active = d_act[...]
    for k in range(count):
        cols = pl.ds(k * size, size)
        out_buf[2, cols] = dot_first(u_buf[:, cols], active).astype(BF)
        send(2, k)
    d_gate = (d_active * left_ref[...]).astype(BF)
    d_upper = (d_active * right_ref[...]).astype(BF)
    for k in range(count):
        cols = pl.ds(k * size, size)
        turned = turned_ref[cols]
        out_buf[0, cols] = dot(turned, d_gate).astype(BF)
        send(0, k)
        out_buf[1, cols] = dot(turned, d_upper).astype(BF)
        send(1, k)
    for copy in copies:
        copy.wait()


def call(kernel, name, operands, outs, scratch, limit, flops, moved, hbm=(), out_hbm=False, smem=(0,)):
    specs = [
        SMEM_SPEC if i in smem else HBM_SPEC if i in hbm else VMEM_SPEC for i in range(len(operands))
    ]
    out_spec = HBM_SPEC if out_hbm else VMEM_SPEC
    results = pl.pallas_call(
        kernel,
        out_shape=outs,
        in_specs=specs,
        out_specs=[out_spec] * len(outs),
        scratch_shapes=scratch,
        cost_estimate=pl.CostEstimate(flops=flops, bytes_accessed=moved, transcendentals=0),
        compiler_params=pltpu.CompilerParams(vmem_limit_bytes=limit * MIB),
        name=name,
    )(*operands)
    return list(results)


def body(inputs, cotangent, section_weights, section_gains):
    sections = lax.axis_size("pipe") // REPL
    ranks = lax.axis_size("tensor")
    pipe = lax.axis_index("pipe")
    tensor = lax.axis_index("tensor")
    position = pipe % sections
    replica = pipe // sections
    middle = sections // 2
    near = position < middle
    side = jnp.where(near, 0, 1)
    kind = jnp.where(near, position, sections - 1 - position)
    core = tensor % 2
    chip = tensor // 2
    rows, features = inputs.shape[2:]
    narrow = section_weights.shape[-1]
    chunks = features // chunk_of(features)
    weights = pltpu.with_memory_space_constraint(section_weights[0], pltpu.HBM)
    blocks = pltpu.with_memory_space_constraint(inputs.reshape(-1, rows, features), pltpu.HBM)
    cot_blocks = pltpu.with_memory_space_constraint(cotangent.reshape(-1, rows, features), pltpu.HBM)
    gains = section_gains[0]
    core_swap = [(i, i ^ 1) for i in range(ranks)]
    chip_swap = [(i, (i + 2) % ranks) for i in range(ranks)]

    def spot(across, end, batch):
        return (((replica + across) % REPL) * 2 + end) * 2 + batch

    pairs = ((0, 0), (0, 1), (1, 0), (1, 1))
    pairs_of = ((1, 0), (0, 1), (1, 1))
    own = [spot(across, side ^ turn, batch) for batch in (core, 1 - core) for across, turn in pairs]
    own = [own[i] for i in (0, 4, 1, 2, 3, 5, 6, 7)]
    state = [spot(across, end, batch) for batch in (core, 1 - core) for across, end in pairs]
    flags = [side, near, kind == 0, chip == 0, kind] + own + state
    flags = jnp.stack([jnp.asarray(flag).astype(jnp.int32) for flag in flags])

    def swap_core(block):
        return lax.ppermute(block, "tensor", core_swap)

    def swap_chip(block):
        return lax.ppermute(block, "tensor", chip_swap)

    def place(copy, end, c, rank):
        at = c if end == 0 else sections - 1 - c
        return (copy * sections + at) * ranks + rank

    def send(block, route):
        moves = []
        for copy in range(REPL):
            for end in range(2):
                for c in range(middle):
                    source = route(copy, end, c)
                    if source is None:
                        continue
                    for rank in range(ranks):
                        came = (rank + 2) % ranks if source[3] else rank
                        moves.append((place(*source[:3], came), place(copy, end, c, rank)))
        return lax.ppermute(block, ("pipe", "tensor"), moves)

    def hop(block, source, target, other):
        return send(block, lambda copy, end, c: (copy, end, source, other) if c == target else None)

    def flow(payload, which, wanted):
        turn, shift = pairs_of[which]

        def route(copy, end, c):
            return ((copy + shift) % REPL, end ^ turn, c, False) if wanted(c, end) else None

        return send(payload, route)

    def with_other_core(arrived):
        return arrived + [swap_core(block) for block in arrived]

    def shape(*extent, dtype=BF):
        return jax.ShapeDtypeStruct(extent, dtype)

    row = shape(rows, features)
    pieces = shape(4 * REPL, rows, features)
    gate_shape = shape(2 * rows, narrow, dtype=F32)
    held_shape = pltpu.VMEM((3, features, narrow), BF)
    normed_scratch = pltpu.VMEM((2 * rows, features), BF)
    layer_flops = 12 * rows * features * narrow
    layer_bytes = 6 * features * narrow
    row_bytes = 2 * rows * features

    def layer(kernel, name, operands, outs):
        return call(kernel, name, operands, outs, [normed_scratch], 8, layer_flops, layer_bytes, smem=())

    def hold(part, backward, operands):
        kernel = functools.partial(hold_kernel, part, backward)
        return call(kernel, "hold", [marks] + operands, [row], [], 4, 0, 4 * row_bytes, smem=())[0]

    def total(terms):
        return call(sum_kernel, "total", terms, [row], [], 4, 0, 3 * row_bytes, smem=())[0]

    def kind_of(step):
        return min(step, sections - 1 - step)

    def across(held, source, target, during, later=()):
        straight, crossed = hop(held, source, target, False), hop(held, source, target, True)
        straight, crossed, during = lax.optimization_barrier((straight, crossed, during))
        mine = total([straight, crossed])
        other, later = lax.optimization_barrier((swap_core(mine), later))
        return mine, other, during, later

    def outer_far(c, end):
        return c == 0 and end == 1

    def middle_class(c, end):
        return c > 0

    pm, po, gate, upper, held_early, mine, other, marks = call(
        first_kernel,
        "first_layer",
        [flags, blocks, pltpu.with_memory_space_constraint(gains, pltpu.HBM), weights],
        [row, row, gate_shape, gate_shape, held_shape, row, row, shape(8, 128, dtype=jnp.int32)],
        [
            normed_scratch,
            pltpu.VMEM(gains.shape, F32),
            pltpu.SemaphoreType.DMA((3, chunks)),
            pltpu.SemaphoreType.DMA((3,)),
        ],
        8,
        layer_flops,
        layer_bytes,
        hbm=(1, 2, 3),
    )
    saved = [(gate, upper, mine, other), None]
    loaded = call(
        load_kernel,
        "load_late",
        [flags, blocks, cot_blocks, weights],
        [held_shape, pieces, pieces, row, row],
        [pltpu.SemaphoreType.DMA((3, 1)), pltpu.SemaphoreType.DMA((3, 4 * REPL))],
        4,
        0,
        2 * layer_bytes,
        hbm=(1, 2, 3),
    )
    for step in range(sections - 1):
        part = 0 if step < middle else 1
        if step > 0:
            old = list(saved[part] or ())
            pm, po, *saved[part] = layer(
                functools.partial(forward_kernel, part, kind_of(step)),
                "forward_layer",
                [marks, mine, other, gains, held_late if part else held_early] + old,
                [row, row, gate_shape, gate_shape, row, row],
            )
        held = hold(part, False, [pm, swap_core(po), mine])
        during = ()
        if step == 0:
            during = loaded
        if step == middle:
            during = call(
                cotangent_kernel,
                "cotangent",
                [up_mine, up_other, held_late],
                [gate_shape],
                [],
                4,
                layer_flops // 3,
                layer_bytes // 3,
                smem=(),
            )
        if step == middle - 1:
            mine = total([held, swap_chip(held)])
            other = swap_core(mine)
        else:
            mine, other, during, _ = across(held, kind_of(step), kind_of(step + 1), during)
        if step == 0:
            held_late, input_rows, cot_rows, up_mine, up_other = during
        if step == middle:
            (d_active,) = during

    early_rows = saved[0][2:]
    sides = call(sides_kernel, "sides", [marks, saved[0][2], saved[1][2]], [row, row], [], 4, 0, 0, smem=())
    mine, (same, opposite) = lax.optimization_barrier((mine, sides))
    state_flows = [flow((opposite, same, opposite)[which], which, middle_class) for which in range(3)]
    gates = [saved[0][:2], saved[1][:2]]
    pm, po, late_mine, late_other = layer(
        turn_kernel,
        "turn_layer",
        [marks, d_active, mine, other, *saved[1][2:], gains, held_late],
        [row] * 4,
    )
    state_mine = [early_rows[0], late_mine]
    ups = [None, (up_mine, up_other)]
    own_rows = 4 * REPL * rows
    for step in range(sections - 1, 0, -1):
        part = 0 if step < middle else 1
        if step < sections - 1:
            old = list(ups[part] or ())
            extra = [ups[1][0]] if step == 1 else []
            pm, po, *kept = layer(
                functools.partial(backward_kernel, kind_of(step), bool(old), bool(extra)),
                "backward_layer",
                [marks, up_mine, up_other, *gates[part], held_late if part else held_early] + old + extra,
                [row] * (6 if extra else 4),
            )
            ups[part] = kept[:2]
        held = hold(part, True, [pm, swap_core(po), up_mine, state_mine[part], gains])
        if step == 1:
            prepared = call(
                own_first_kernel,
                "own_first",
                [flags, input_rows, *early_rows, late_mine, late_other, *middle_arrived]
                + with_other_core(outer_flows)
                + [gains, weights],
                [
                    shape(features, own_rows),
                    shape(own_rows, narrow, dtype=F32),
                    shape(own_rows, narrow, dtype=F32),
                    shape(own_rows, narrow),
                ],
                [
                    pltpu.VMEM((2, features, narrow), BF),
                    pltpu.VMEM((own_rows, features), BF),
                    pltpu.SemaphoreType.DMA((2, chunks)),
                ],
                12,
                4 * own_rows * features * narrow,
                8 * features * narrow,
                hbm=(19,),
            )
            held, same, opposite = lax.optimization_barrier((held, *kept[2:]))
            crossed, prepared = lax.optimization_barrier((swap_chip(held), prepared))
            mine = total([held, crossed])
            up_first = flow(opposite, 0, middle_class)
            mine, up_first, same = lax.optimization_barrier((mine, up_first, same))
        elif step == middle:
            held, late = lax.optimization_barrier((held, late_mine))
            up_mine = total([held, swap_chip(held)])
            outer_flows = [flow(late, which, outer_far) for which in range(3)]
            up_other, outer_flows = lax.optimization_barrier((swap_core(up_mine), outer_flows))
        else:
            later = ()
            if step == sections - 1:
                later = with_other_core(state_flows)
            up_mine, up_other, _, later = across(held, kind_of(step), kind_of(step - 1), (), later)
            if step == sections - 1:
                middle_arrived = later
    straight = [
        send(
            mine,
            lambda copy, end, c, shift=shift, source=source: (
                ((copy + shift) % REPL, source, 1, False) if c == 0 and end == 0 else None
            ),
        )
        for shift, source in pairs
    ]
    up_arrived = [up_first] + [flow(payload, 1, middle_class) for payload in (same, up_first)]
    straight, up_arrived = lax.optimization_barrier((straight, up_arrived))
    return call(
        own_last_kernel,
        "own_last",
        [flags, cot_rows, *with_other_core(straight), *ups[0], *ups[1], *with_other_core(up_arrived)]
        + [*prepared, held_early, held_late],
        [shape(1, 3, features, narrow)],
        [
            pltpu.VMEM((own_rows, features), BF),
            pltpu.VMEM((own_rows, narrow), F32),
            pltpu.VMEM((3, features, narrow), BF),
            pltpu.SemaphoreType.DMA((3, chunks)),
        ],
        16,
        8 * own_rows * features * narrow,
        8 * features * narrow,
        out_hbm=True,
    )[0]


def solution(mesh):
    return jax.shard_map(
        body,
        mesh=mesh,
        in_specs=(P(), P(), P("pipe", None, None, None, "tensor"), P("pipe", None, None)),
        out_specs=P("pipe", None, None, "tensor"),
        check_vma=False,
    )
```

```python
import functools

import jax
import jax.numpy as jnp
from jax import lax
from jax.experimental import pallas as pl
from jax.experimental.pallas import tpu as pltpu
from jax.sharding import PartitionSpec as P

REPL = 2
EPS = 1e-06
BF = jnp.bfloat16
F32 = jnp.float32
SMEM_SPEC = pl.BlockSpec(memory_space=pltpu.SMEM)
VMEM_SPEC = pl.BlockSpec(memory_space=pltpu.VMEM)
HBM_SPEC = pl.BlockSpec(memory_space=pltpu.HBM)
MIB = 1024 * 1024
NEAR, OUTER, FIRST_CHIP, KIND, OWN, STATE = 1, 2, 3, 4, 5, 13


def chunk_of(features):
    for size in (512, 256, 128):
        if features % size == 0:
            return size
    return features


def norm_rows(rows, gain_row):
    widened = rows.astype(F32)
    root = jnp.sqrt(jnp.mean(widened * widened, axis=-1, keepdims=True) + EPS)
    unit = widened / root
    return unit, root, (unit * gain_row).astype(BF)


def dot(left, right):
    return jnp.dot(left, right, preferred_element_type=F32)


def dot_last(left, right):
    return lax.dot_general(left, right, (((1,), (1,)), ((), ())), preferred_element_type=F32)


def dot_first(left, right):
    return lax.dot_general(left, right, (((0,), (0,)), ((), ())), preferred_element_type=F32)


def is_set(flags_ref, index, value=1):
    if len(flags_ref.shape) == 1:
        return flags_ref[index] == value
    return flags_ref[index : index + 1, 0:1] == value


def gain_at(flags_ref, gains_ref, part):
    return jnp.where(is_set(flags_ref, NEAR, 1 - part), gains_ref[0:1], gains_ref[1:2])


def own_index(flags_ref, part):
    return jnp.where(flags_ref[NEAR] == 1 - part, 0, 1)


def choose(condition, first, second):
    kept = first.dtype
    return jnp.where(condition, first.astype(F32), second.astype(F32)).astype(kept)


def weight_copies(which, w_ref, w_buf, sems, size):
    features = w_buf.shape[1]
    copies = {}
    for matrix in range(3):
        for k in range(features // size):
            rows = pl.ds(k * size, size)
            copies[matrix, k] = pltpu.make_async_copy(
                w_ref.at[which, matrix, rows], w_buf.at[matrix, rows], sems.at[matrix, k]
            )
    return copies


def fill_normed(xm_ref, xo_ref, gain, normed):
    half = xm_ref.shape[0]
    normed[:half] = norm_rows(xm_ref[...], gain)[2]
    normed[half:] = norm_rows(xo_ref[...], gain)[2]


def gate_upper(copies, w_buf, normed, size):
    gate = upper = None
    for k in range(w_buf.shape[1] // size):
        cols = pl.ds(k * size, size)
        if copies:
            copies[0, k].wait()
            copies[1, k].wait()
        block = normed[:, cols]
        gate_k = dot(block, w_buf[0, cols])
        upper_k = dot(block, w_buf[1, cols])
        gate = gate_k if gate is None else gate + gate_k
        upper = upper_k if upper is None else upper + upper_k
    return gate, upper


def forward_math(copies, xm_ref, xo_ref, gain, w_buf, pm_ref, po_ref, normed):
    size = chunk_of(w_buf.shape[1])
    half = xm_ref.shape[0]
    fill_normed(xm_ref, xo_ref, gain, normed)
    gate, upper = gate_upper(copies, w_buf, normed, size)
    active = (gate * jax.nn.sigmoid(gate) * upper).astype(BF)
    for k in range(w_buf.shape[1] // size):
        cols = pl.ds(k * size, size)
        if copies:
            copies[2, k].wait()
        part = dot_last(active, w_buf[2, cols]).astype(BF)
        pm_ref[:, cols] = part[:half]
        po_ref[:, cols] = part[half:]
    return gate, upper


def first_kernel(
    flags_ref, rows_ref, gains_ref, w_ref,
    pm_ref, po_ref, gate_ref, upper_ref, w_buf, xm_ref, xo_ref, marks_ref, normed, gains_buf, sems, row_sems
):
    size = chunk_of(w_buf.shape[1])
    moves = [
        pltpu.make_async_copy(rows_ref.at[flags_ref[OWN + i]], ref, row_sems.at[i])
        for i, ref in enumerate((xm_ref, xo_ref))
    ]
    moves.append(pltpu.make_async_copy(gains_ref, gains_buf, row_sems.at[2]))
    for move in moves:
        move.start()
    for i in range(marks_ref.shape[0]):
        marks_ref[i : i + 1] = jnp.full((1, marks_ref.shape[1]), flags_ref[i], jnp.int32)
    for move in moves:
        move.wait()
    copies = weight_copies(own_index(flags_ref, 0), w_ref, w_buf, sems, size)
    for group in ((0, 1), (2,)):
        for k in range(w_buf.shape[1] // size):
            for matrix in group:
                copies[matrix, k].start()
    gain = gain_at(flags_ref, gains_buf, 0)
    gate_ref[...], upper_ref[...] = forward_math(copies, xm_ref, xo_ref, gain, w_buf, pm_ref, po_ref, normed)


def load_kernel(flags_ref, rows_ref, cot_ref, w_ref, w_buf, xs_ref, us_ref, um_ref, uo_ref, sems, row_sems):
    copies = list(weight_copies(own_index(flags_ref, 1), w_ref, w_buf, sems, w_buf.shape[1]).values())
    for i in range(xs_ref.shape[0]):
        copies.append(pltpu.make_async_copy(cot_ref.at[flags_ref[OWN + i]], us_ref.at[i], row_sems.at[0, i]))
        copies.append(pltpu.make_async_copy(rows_ref.at[flags_ref[STATE + i]], xs_ref.at[i], row_sems.at[1, i]))
    for i, ref in enumerate((um_ref, uo_ref)):
        copies.append(pltpu.make_async_copy(cot_ref.at[flags_ref[OWN + i]], ref, row_sems.at[2, i]))
    for copy in copies:
        copy.start()
    for copy in copies:
        copy.wait()


def forward_kernel(part, live, flags_ref, xm_ref, xo_ref, gains_ref, w_buf, *refs):
    *old, pm_ref, po_ref, gate_ref, upper_ref, xms_ref, xos_ref, normed = refs
    gain = gain_at(flags_ref, gains_ref, part)
    gate, upper = forward_math(None, xm_ref, xo_ref, gain, w_buf, pm_ref, po_ref, normed)
    found = (gate, upper, xm_ref[...], xo_ref[...])
    outs = (gate_ref, upper_ref, xms_ref, xos_ref)
    if old:
        is_live = is_set(flags_ref, KIND, live)
        found = [choose(is_live, a, b[...]) for a, b in zip(found, old)]
    for out, value in zip(outs, found):
        out[...] = value


def active_gradient(um_ref, uo_ref, w_buf):
    size = chunk_of(w_buf.shape[1])
    d_active = None
    for k in range(w_buf.shape[1] // size):
        cols = pl.ds(k * size, size)
        block = jnp.concatenate([um_ref[:, cols], uo_ref[:, cols]], axis=0)
        part = dot(block, w_buf[2, cols])
        d_active = part if d_active is None else d_active + part
    return d_active


def backward_math(d_active, gate, upper, w_buf, pm_ref, po_ref):
    size = chunk_of(w_buf.shape[1])
    half = pm_ref.shape[0]
    sig = jax.nn.sigmoid(gate)
    d_gate = (d_active * upper * (sig * (1.0 + gate * (1.0 - sig)))).astype(BF)
    d_upper = (d_active * (gate * sig)).astype(BF)
    for k in range(w_buf.shape[1] // size):
        cols = pl.ds(k * size, size)
        part = (dot_last(d_gate, w_buf[0, cols]) + dot_last(d_upper, w_buf[1, cols])).astype(BF)
        pm_ref[:, cols] = part[:half]
        po_ref[:, cols] = part[half:]


def cotangent_kernel(um_ref, uo_ref, w_buf, d_ref):
    d_ref[...] = active_gradient(um_ref, uo_ref, w_buf)


def turn_kernel(
    flags_ref, d_ref, xm_ref, xo_ref, oldm_ref, oldo_ref, gains_ref, w_buf, pm_ref, po_ref, latem_ref, lateo_ref, normed
):
    fill_normed(xm_ref, xo_ref, gain_at(flags_ref, gains_ref, 1), normed)
    gate, upper = gate_upper(None, w_buf, normed, chunk_of(w_buf.shape[1]))
    backward_math(d_ref[...], gate, upper, w_buf, pm_ref, po_ref)
    is_outer = is_set(flags_ref, OUTER)
    latem_ref[...] = choose(is_outer, xm_ref[...], oldm_ref[...])
    lateo_ref[...] = choose(is_outer, xo_ref[...], oldo_ref[...])


def backward_kernel(live, has_old, has_late, flags_ref, um_ref, uo_ref, gate_ref, upper_ref, w_buf, *refs):
    refs = list(refs)
    old = [refs.pop(0) for _ in range(2)] if has_old else []
    late = refs.pop(0) if has_late else None
    pm_ref, po_ref, ums_ref, uos_ref = refs[:4]
    backward_math(active_gradient(um_ref, uo_ref, w_buf), gate_ref[...], upper_ref[...], w_buf, pm_ref, po_ref)
    found = [um_ref[...], uo_ref[...]]
    if old:
        is_live = is_set(flags_ref, KIND, live)
        found = [choose(is_live, a, b[...]) for a, b in zip(found, old)]
    ums_ref[...], uos_ref[...] = found
    if has_late:
        is_near = is_set(flags_ref, NEAR)
        refs[4][...] = choose(is_near, found[0], late[...])
        refs[5][...] = choose(is_near, late[...], found[0])


def hold_kernel(part, backward, flags_ref, pm_ref, recv_ref, base_ref, *refs):
    summed = pm_ref[...].astype(F32) + recv_ref[...].astype(F32)
    if backward:
        state_ref, gains_ref, *outs = refs
        gain = gain_at(flags_ref, gains_ref, part)
        unit, root, _ = norm_rows(state_ref[...], gain)
        d_unit = summed * gain
        summed = (d_unit - unit * jnp.mean(d_unit * unit, axis=-1, keepdims=True)) / root
    else:
        outs = refs
    base = jnp.where(is_set(flags_ref, FIRST_CHIP), base_ref[...].astype(F32), 0.0)
    (out,) = outs
    out[...] = (summed + base).astype(BF)


def sides_kernel(marks_ref, early_ref, late_ref, same_ref, opposite_ref):
    is_near = is_set(marks_ref, NEAR)
    same_ref[...] = choose(is_near, early_ref[...], late_ref[...])
    opposite_ref[...] = choose(is_near, late_ref[...], early_ref[...])


def stack_kernel(first_ref, second_ref, out_ref):
    rows = first_ref.shape[0]
    out_ref[:rows] = first_ref[...]
    out_ref[rows:] = second_ref[...]


def fill_rows(target, sources, change=None):
    start = 0
    for source in sources:
        rows = source[...]
        target[start : start + rows.shape[0]] = change(rows) if change else rows
        start += rows.shape[0]


def sum_kernel(first_ref, second_ref, out_ref):
    out_ref[...] = (first_ref[...].astype(F32) + second_ref[...].astype(F32)).astype(BF)


def own_first_kernel(
    flags_ref, xs_ref, em_ref, eo_ref, lm_ref, lo_ref, p0, p1, p2, p3, q0, q1, q2, q3, gains_ref, w_ref,
    turned_ref, left_ref, right_ref, active_ref, w_buf, normed, sems
):
    features = w_buf.shape[1]
    size = chunk_of(features)
    count = features // size
    copies = {}
    for k in range(count):
        rows = pl.ds(k * size, size)
        for matrix in range(2):
            copies[matrix, k] = pltpu.make_async_copy(
                w_ref.at[0, matrix, rows], w_buf.at[matrix, rows], sems.at[matrix, k]
            )
            copies[matrix, k].start()
    gain = gains_ref[0:1]
    pieces, half = xs_ref.shape[:2]
    is_near = flags_ref[NEAR] == 1
    is_outer = flags_ref[OUTER] == 1
    inputs_used = jnp.logical_and(is_near, is_outer)

    def put(piece, rows):
        normed[piece * half : (piece + 1) * half] = norm_rows(rows, gain)[2]

    @pl.when(inputs_used)
    def _():
        for piece in range(pieces):
            put(piece, xs_ref[piece])

    cases = (
        (False, True, (em_ref, eo_ref, p0, p1, p2, p3)),
        (False, False, (lm_ref, lo_ref, p0, p1, p2, p3)),
        (True, False, (lm_ref, lo_ref, q0, q1, q2, q3)),
    )
    for outer, near, sources in cases:

        @pl.when(jnp.logical_and(is_outer == outer, is_near == near))
        def _(sources=sources):
            fill_rows(normed, sources, lambda rows: norm_rows(rows, gain)[2])

    gate, upper = gate_upper(copies, w_buf, normed, size)
    sig = jax.nn.sigmoid(gate)
    smooth = gate * sig
    left_ref[...] = upper * (sig * (1.0 + gate * (1.0 - sig)))
    right_ref[...] = smooth
    active_ref[...] = (smooth * upper).astype(BF)
    for k in range(count):
        cols = pl.ds(k * size, size)
        turned_ref[cols] = normed[:, cols].T


def own_last_kernel(flags_ref, us_ref, *refs):
    refs = list(refs)

    def take(count):
        return [refs.pop(0) for _ in range(count)]

    direct, early, late, arrived = take(8), take(2), take(2), take(4)
    turned_ref, left_ref, right_ref, active_ref, early_ref, late_ref = take(6)
    out_ref, u_buf, d_act, out_buf, sems = take(5)
    features = turned_ref.shape[0]
    size = chunk_of(features)
    count = features // size
    pieces, half = us_ref.shape[:2]
    is_near = flags_ref[NEAR] == 1
    is_outer = flags_ref[OUTER] == 1

    def fill(sources, w_ref):
        fill_rows(u_buf, sources)
        total = None
        for k in range(count):
            cols = pl.ds(k * size, size)
            part = dot(u_buf[:, cols], w_ref[2, cols])
            total = part if total is None else total + part
        d_act[...] = total

    cases = (
        (True, True, direct, early_ref),
        (True, False, [us_ref.at[i] for i in range(pieces)], late_ref),
        (False, True, early + arrived, early_ref),
        (False, False, late + arrived, late_ref),
    )
    for outer, near, sources, w_ref in cases:

        @pl.when(jnp.logical_and(is_outer == outer, is_near == near))
        def _(sources=sources, w_ref=w_ref):
            fill(sources, w_ref)

    copies = []

    def send(matrix, k):
        rows = pl.ds(k * size, size)
        copy = pltpu.make_async_copy(out_buf.at[matrix, rows], out_ref.at[0, matrix, rows], sems.at[matrix, k])
        copy.start()
        copies.append(copy)

    active = active_ref[...]
    d_active = d_act[...]
    for k in range(count):
        cols = pl.ds(k * size, size)
        out_buf[2, cols] = dot_first(u_buf[:, cols], active).astype(BF)
        send(2, k)
    d_gate = (d_active * left_ref[...]).astype(BF)
    d_upper = (d_active * right_ref[...]).astype(BF)
    for k in range(count):
        cols = pl.ds(k * size, size)
        turned = turned_ref[cols]
        out_buf[0, cols] = dot(turned, d_gate).astype(BF)
        send(0, k)
        out_buf[1, cols] = dot(turned, d_upper).astype(BF)
        send(1, k)
    for copy in copies:
        copy.wait()


def call(kernel, name, operands, outs, scratch, limit, flops, moved, hbm=(), out_hbm=False, smem=(0,)):
    specs = [
        SMEM_SPEC if i in smem else HBM_SPEC if i in hbm else VMEM_SPEC for i in range(len(operands))
    ]
    out_spec = HBM_SPEC if out_hbm else VMEM_SPEC
    results = pl.pallas_call(
        kernel,
        out_shape=outs,
        in_specs=specs,
        out_specs=[out_spec] * len(outs),
        scratch_shapes=scratch,
        cost_estimate=pl.CostEstimate(flops=flops, bytes_accessed=moved, transcendentals=0),
        compiler_params=pltpu.CompilerParams(vmem_limit_bytes=limit * MIB),
        name=name,
    )(*operands)
    return list(results)


def body(inputs, cotangent, section_weights, section_gains):
    sections = lax.axis_size("pipe") // REPL
    ranks = lax.axis_size("tensor")
    pipe = lax.axis_index("pipe")
    tensor = lax.axis_index("tensor")
    position = pipe % sections
    replica = pipe // sections
    middle = sections // 2
    near = position < middle
    side = jnp.where(near, 0, 1)
    kind = jnp.where(near, position, sections - 1 - position)
    core = tensor % 2
    chip = tensor // 2
    rows, features = inputs.shape[2:]
    narrow = section_weights.shape[-1]
    chunks = features // chunk_of(features)
    weights = pltpu.with_memory_space_constraint(section_weights[0], pltpu.HBM)
    blocks = pltpu.with_memory_space_constraint(inputs.reshape(-1, rows, features), pltpu.HBM)
    cot_blocks = pltpu.with_memory_space_constraint(cotangent.reshape(-1, rows, features), pltpu.HBM)
    gains = section_gains[0]
    core_swap = [(i, i ^ 1) for i in range(ranks)]
    chip_swap = [(i, (i + 2) % ranks) for i in range(ranks)]

    def spot(across, end, batch):
        return (((replica + across) % REPL) * 2 + end) * 2 + batch

    pairs = ((0, 0), (0, 1), (1, 0), (1, 1))
    pairs_of = ((1, 0), (0, 1), (1, 1))
    own = [spot(across, side ^ turn, batch) for batch in (core, 1 - core) for across, turn in pairs]
    own = [own[i] for i in (0, 4, 1, 2, 3, 5, 6, 7)]
    state = [spot(across, end, batch) for batch in (core, 1 - core) for across, end in pairs]
    flags = [side, near, kind == 0, chip == 0, kind] + own + state
    flags = jnp.stack([jnp.asarray(flag).astype(jnp.int32) for flag in flags])

    def swap_core(block):
        return lax.ppermute(block, "tensor", core_swap)

    def swap_chip(block):
        return lax.ppermute(block, "tensor", chip_swap)

    def place(copy, end, c, rank):
        at = c if end == 0 else sections - 1 - c
        return (copy * sections + at) * ranks + rank

    def send(block, route):
        moves = []
        for copy in range(REPL):
            for end in range(2):
                for c in range(middle):
                    source = route(copy, end, c)
                    if source is None:
                        continue
                    for rank in range(ranks):
                        came = (rank + 2) % ranks if source[3] else rank
                        moves.append((place(*source[:3], came), place(copy, end, c, rank)))
        return lax.ppermute(block, ("pipe", "tensor"), moves)

    def hop(block, source, target, other):
        return send(block, lambda copy, end, c: (copy, end, source, other) if c == target else None)

    def flow(payload, which, wanted):
        turn, shift = pairs_of[which]

        def route(copy, end, c):
            return ((copy + shift) % REPL, end ^ turn, c, False) if wanted(c, end) else None

        return send(payload, route)

    def joined(first, second):
        return call(stack_kernel, "stack", [first, second], [shape(2 * rows, features)], [], 4, 0, 0, smem=())[0]

    def with_other_core(arrived):
        return arrived + [swap_core(block) for block in arrived]

    def shape(*extent, dtype=BF):
        return jax.ShapeDtypeStruct(extent, dtype)

    row = shape(rows, features)
    pieces = shape(4 * REPL, rows, features)
    gate_shape = shape(2 * rows, narrow, dtype=F32)
    held_shape = pltpu.VMEM((3, features, narrow), BF)
    normed_scratch = pltpu.VMEM((2 * rows, features), BF)
    layer_flops = 12 * rows * features * narrow
    layer_bytes = 6 * features * narrow
    row_bytes = 2 * rows * features

    def layer(kernel, name, operands, outs):
        return call(kernel, name, operands, outs, [normed_scratch], 8, layer_flops, layer_bytes, smem=())

    def hold(part, backward, operands):
        kernel = functools.partial(hold_kernel, part, backward)
        return call(kernel, "hold", [marks] + operands, [row], [], 4, 0, 4 * row_bytes, smem=())[0]

    def total(terms):
        return call(sum_kernel, "total", terms, [row], [], 4, 0, 3 * row_bytes, smem=())[0]

    def kind_of(step):
        return min(step, sections - 1 - step)

    def across(held, source, target, during, later=()):
        straight, crossed = hop(held, source, target, False), hop(held, source, target, True)
        straight, crossed, during = lax.optimization_barrier((straight, crossed, during))
        mine = total([straight, crossed])
        other, later = lax.optimization_barrier((swap_core(mine), later))
        return mine, other, during, later

    def outer_far(c, end):
        return c == 0 and end == 1

    def middle_class(c, end):
        return c > 0

    pm, po, gate, upper, held_early, mine, other, marks = call(
        first_kernel,
        "first_layer",
        [flags, blocks, pltpu.with_memory_space_constraint(gains, pltpu.HBM), weights],
        [row, row, gate_shape, gate_shape, held_shape, row, row, shape(8, 128, dtype=jnp.int32)],
        [
            normed_scratch,
            pltpu.VMEM(gains.shape, F32),
            pltpu.SemaphoreType.DMA((3, chunks)),
            pltpu.SemaphoreType.DMA((3,)),
        ],
        8,
        layer_flops,
        layer_bytes,
        hbm=(1, 2, 3),
    )
    saved = [(gate, upper, mine, other), None]
    loaded = call(
        load_kernel,
        "load_late",
        [flags, blocks, cot_blocks, weights],
        [held_shape, pieces, pieces, row, row],
        [pltpu.SemaphoreType.DMA((3, 1)), pltpu.SemaphoreType.DMA((3, 4 * REPL))],
        4,
        0,
        2 * layer_bytes,
        hbm=(1, 2, 3),
    )
    for step in range(sections - 1):
        part = 0 if step < middle else 1
        if step > 0:
            old = list(saved[part] or ())
            pm, po, *saved[part] = layer(
                functools.partial(forward_kernel, part, kind_of(step)),
                "forward_layer",
                [marks, mine, other, gains, held_late if part else held_early] + old,
                [row, row, gate_shape, gate_shape, row, row],
            )
        held = hold(part, False, [pm, swap_core(po), mine])
        during = ()
        if step == 0:
            during = loaded
        if step == middle:
            during = call(
                cotangent_kernel,
                "cotangent",
                [up_mine, up_other, held_late],
                [gate_shape],
                [],
                4,
                layer_flops // 3,
                layer_bytes // 3,
                smem=(),
            )
        if step == middle - 1:
            mine = total([held, swap_chip(held)])
            other = swap_core(mine)
        else:
            mine, other, during, _ = across(held, kind_of(step), kind_of(step + 1), during)
        if step == 0:
            held_late, input_rows, cot_rows, up_mine, up_other = during
        if step == middle:
            (d_active,) = during

    early_rows = saved[0][2:]
    sides = call(sides_kernel, "sides", [marks, saved[0][2], saved[1][2]], [row, row], [], 4, 0, 0, smem=())
    mine, (same, opposite) = lax.optimization_barrier((mine, sides))
    state_first = flow(opposite, 0, middle_class)
    state_second = flow(joined(same, state_first), 1, middle_class)
    gates = [saved[0][:2], saved[1][:2]]
    pm, po, late_mine, late_other = layer(
        turn_kernel,
        "turn_layer",
        [marks, d_active, mine, other, *saved[1][2:], gains, held_late],
        [row] * 4,
    )
    state_mine = [early_rows[0], late_mine]
    ups = [None, (up_mine, up_other)]
    own_rows = 4 * REPL * rows
    for step in range(sections - 1, 0, -1):
        part = 0 if step < middle else 1
        if step < sections - 1:
            old = list(ups[part] or ())
            extra = [ups[1][0]] if step == 1 else []
            pm, po, *kept = layer(
                functools.partial(backward_kernel, kind_of(step), bool(old), bool(extra)),
                "backward_layer",
                [marks, up_mine, up_other, *gates[part], held_late if part else held_early] + old + extra,
                [row] * (6 if extra else 4),
            )
            ups[part] = kept[:2]
        held = hold(part, True, [pm, swap_core(po), up_mine, state_mine[part], gains])
        if step == 1:
            prepared = call(
                own_first_kernel,
                "own_first",
                [flags, input_rows, *early_rows, late_mine, late_other, *middle_arrived]
                + with_other_core(outer_flows)
                + [gains, weights],
                [
                    shape(features, own_rows),
                    shape(own_rows, narrow, dtype=F32),
                    shape(own_rows, narrow, dtype=F32),
                    shape(own_rows, narrow),
                ],
                [
                    pltpu.VMEM((2, features, narrow), BF),
                    pltpu.VMEM((own_rows, features), BF),
                    pltpu.SemaphoreType.DMA((2, chunks)),
                ],
                12,
                4 * own_rows * features * narrow,
                8 * features * narrow,
                hbm=(15,),
            )
            held, same, opposite = lax.optimization_barrier((held, *kept[2:]))
            crossed, prepared = lax.optimization_barrier((swap_chip(held), prepared))
            mine = total([held, crossed])
            up_first = flow(opposite, 0, middle_class)
            mine, up_first, same = lax.optimization_barrier((mine, up_first, same))
        elif step == middle:
            held, late = lax.optimization_barrier((held, late_mine))
            up_mine = total([held, swap_chip(held)])
            up_other = swap_core(up_mine)
            outer_first = flow(late, 0, outer_far)
            outer_flows = [outer_first, flow(joined(late, outer_first), 1, outer_far)]
        else:
            later = ()
            if step == sections - 1:
                later = [state_first, state_second]
            up_mine, up_other, _, later = across(held, kind_of(step), kind_of(step - 1), (), later)
            if step == sections - 1:
                middle_arrived = with_other_core(later)
    straight = [
        send(
            mine,
            lambda copy, end, c, shift=shift, source=source: (
                ((copy + shift) % REPL, source, 1, False) if c == 0 and end == 0 else None
            ),
        )
        for shift, source in pairs
    ]
    up_arrived = [up_first, flow(joined(same, up_first), 1, middle_class)]
    straight, up_arrived = lax.optimization_barrier((straight, up_arrived))
    return call(
        own_last_kernel,
        "own_last",
        [flags, cot_rows, *with_other_core(straight), *ups[0], *ups[1], *with_other_core(up_arrived)]
        + [*prepared, held_early, held_late],
        [shape(1, 3, features, narrow)],
        [
            pltpu.VMEM((own_rows, features), BF),
            pltpu.VMEM((own_rows, narrow), F32),
            pltpu.VMEM((3, features, narrow), BF),
            pltpu.SemaphoreType.DMA((3, chunks)),
        ],
        16,
        8 * own_rows * features * narrow,
        8 * features * narrow,
        out_hbm=True,
    )[0]


def solution(mesh):
    return jax.shard_map(
        body,
        mesh=mesh,
        in_specs=(P(), P(), P("pipe", None, None, None, "tensor"), P("pipe", None, None)),
        out_specs=P("pipe", None, None, "tensor"),
        check_vma=False,
    )
```

```python
import functools

import jax
import jax.numpy as jnp
from jax import lax
from jax.experimental import pallas as pl
from jax.experimental.pallas import tpu as pltpu
from jax.sharding import PartitionSpec as P

REPL = 2
EPS = 1e-06
BF = jnp.bfloat16
F32 = jnp.float32
SMEM_SPEC = pl.BlockSpec(memory_space=pltpu.SMEM)
VMEM_SPEC = pl.BlockSpec(memory_space=pltpu.VMEM)
HBM_SPEC = pl.BlockSpec(memory_space=pltpu.HBM)
MIB = 1024 * 1024
NEAR, OUTER, FIRST_CHIP, KIND, OWN, STATE = 1, 2, 3, 4, 5, 13


def chunk_of(features):
    for size in (512, 256, 128):
        if features % size == 0:
            return size
    return features


def norm_rows(rows, gain_row):
    widened = rows.astype(F32)
    root = jnp.sqrt(jnp.mean(widened * widened, axis=-1, keepdims=True) + EPS)
    unit = widened / root
    return unit, root, (unit * gain_row).astype(BF)


def dot(left, right):
    return jnp.dot(left, right, preferred_element_type=F32)


def dot_last(left, right):
    return lax.dot_general(left, right, (((1,), (1,)), ((), ())), preferred_element_type=F32)


def dot_first(left, right):
    return lax.dot_general(left, right, (((0,), (0,)), ((), ())), preferred_element_type=F32)


def is_set(flags_ref, index, value=1):
    if len(flags_ref.shape) == 1:
        return flags_ref[index] == value
    return flags_ref[index : index + 1, 0:1] == value


def gain_at(flags_ref, gains_ref, part):
    return jnp.where(is_set(flags_ref, NEAR, 1 - part), gains_ref[0:1], gains_ref[1:2])


def own_index(flags_ref, part):
    return jnp.where(flags_ref[NEAR] == 1 - part, 0, 1)


def choose(condition, first, second):
    kept = first.dtype
    return jnp.where(condition, first.astype(F32), second.astype(F32)).astype(kept)


def weight_copies(which, w_ref, w_buf, sems, size):
    features = w_buf.shape[1]
    copies = {}
    for matrix in range(3):
        for k in range(features // size):
            rows = pl.ds(k * size, size)
            copies[matrix, k] = pltpu.make_async_copy(
                w_ref.at[which, matrix, rows], w_buf.at[matrix, rows], sems.at[matrix, k]
            )
    return copies


def fill_normed(xm_ref, xo_ref, gain, normed):
    half = xm_ref.shape[0]
    normed[:half] = norm_rows(xm_ref[...], gain)[2]
    normed[half:] = norm_rows(xo_ref[...], gain)[2]


def gate_upper(copies, w_buf, normed, size):
    gate = upper = None
    for k in range(w_buf.shape[1] // size):
        cols = pl.ds(k * size, size)
        if copies:
            copies[0, k].wait()
            copies[1, k].wait()
        block = normed[:, cols]
        gate_k = dot(block, w_buf[0, cols])
        upper_k = dot(block, w_buf[1, cols])
        gate = gate_k if gate is None else gate + gate_k
        upper = upper_k if upper is None else upper + upper_k
    return gate, upper


def forward_math(copies, xm_ref, xo_ref, gain, w_buf, pm_ref, po_ref, normed):
    size = chunk_of(w_buf.shape[1])
    half = xm_ref.shape[0]
    fill_normed(xm_ref, xo_ref, gain, normed)
    gate, upper = gate_upper(copies, w_buf, normed, size)
    active = (gate * jax.nn.sigmoid(gate) * upper).astype(BF)
    for k in range(w_buf.shape[1] // size):
        cols = pl.ds(k * size, size)
        if copies:
            copies[2, k].wait()
        part = dot_last(active, w_buf[2, cols]).astype(BF)
        pm_ref[:, cols] = part[:half]
        po_ref[:, cols] = part[half:]
    return gate, upper


def first_kernel(
    flags_ref, rows_ref, gains_ref, w_ref,
    pm_ref, po_ref, gate_ref, upper_ref, w_buf, xm_ref, xo_ref, marks_ref, normed, gains_buf, sems, row_sems
):
    size = chunk_of(w_buf.shape[1])
    moves = [
        pltpu.make_async_copy(rows_ref.at[flags_ref[OWN + i]], ref, row_sems.at[i])
        for i, ref in enumerate((xm_ref, xo_ref))
    ]
    moves.append(pltpu.make_async_copy(gains_ref, gains_buf, row_sems.at[2]))
    for move in moves:
        move.start()
    for i in range(marks_ref.shape[0]):
        marks_ref[i : i + 1] = jnp.full((1, marks_ref.shape[1]), flags_ref[i], jnp.int32)
    for move in moves:
        move.wait()
    copies = weight_copies(own_index(flags_ref, 0), w_ref, w_buf, sems, size)
    for group in ((0, 1), (2,)):
        for k in range(w_buf.shape[1] // size):
            for matrix in group:
                copies[matrix, k].start()
    gain = gain_at(flags_ref, gains_buf, 0)
    gate_ref[...], upper_ref[...] = forward_math(copies, xm_ref, xo_ref, gain, w_buf, pm_ref, po_ref, normed)


def load_kernel(flags_ref, rows_ref, cot_ref, w_ref, w_buf, xs_ref, us_ref, um_ref, uo_ref, sems, row_sems):
    copies = list(weight_copies(own_index(flags_ref, 1), w_ref, w_buf, sems, w_buf.shape[1]).values())
    for i in range(xs_ref.shape[0]):
        copies.append(pltpu.make_async_copy(cot_ref.at[flags_ref[OWN + i]], us_ref.at[i], row_sems.at[0, i]))
        copies.append(pltpu.make_async_copy(rows_ref.at[flags_ref[STATE + i]], xs_ref.at[i], row_sems.at[1, i]))
    for i, ref in enumerate((um_ref, uo_ref)):
        copies.append(pltpu.make_async_copy(cot_ref.at[flags_ref[OWN + i]], ref, row_sems.at[2, i]))
    for copy in copies:
        copy.start()
    for copy in copies:
        copy.wait()


def forward_kernel(part, live, flags_ref, xm_ref, xo_ref, gains_ref, w_buf, *refs):
    *old, pm_ref, po_ref, gate_ref, upper_ref, xms_ref, xos_ref, normed = refs
    gain = gain_at(flags_ref, gains_ref, part)
    gate, upper = forward_math(None, xm_ref, xo_ref, gain, w_buf, pm_ref, po_ref, normed)
    found = (gate, upper, xm_ref[...], xo_ref[...])
    outs = (gate_ref, upper_ref, xms_ref, xos_ref)
    if old:
        is_live = is_set(flags_ref, KIND, live)
        found = [choose(is_live, a, b[...]) for a, b in zip(found, old)]
    for out, value in zip(outs, found):
        out[...] = value


def active_gradient(um_ref, uo_ref, w_buf):
    size = chunk_of(w_buf.shape[1])
    d_active = None
    for k in range(w_buf.shape[1] // size):
        cols = pl.ds(k * size, size)
        block = jnp.concatenate([um_ref[:, cols], uo_ref[:, cols]], axis=0)
        part = dot(block, w_buf[2, cols])
        d_active = part if d_active is None else d_active + part
    return d_active


def backward_math(d_active, gate, upper, w_buf, pm_ref, po_ref):
    size = chunk_of(w_buf.shape[1])
    half = pm_ref.shape[0]
    sig = jax.nn.sigmoid(gate)
    d_gate = (d_active * upper * (sig * (1.0 + gate * (1.0 - sig)))).astype(BF)
    d_upper = (d_active * (gate * sig)).astype(BF)
    for k in range(w_buf.shape[1] // size):
        cols = pl.ds(k * size, size)
        part = (dot_last(d_gate, w_buf[0, cols]) + dot_last(d_upper, w_buf[1, cols])).astype(BF)
        pm_ref[:, cols] = part[:half]
        po_ref[:, cols] = part[half:]


def cotangent_kernel(um_ref, uo_ref, w_buf, d_ref):
    d_ref[...] = active_gradient(um_ref, uo_ref, w_buf)


def turn_kernel(
    flags_ref, d_ref, xm_ref, xo_ref, oldm_ref, oldo_ref, gains_ref, w_buf, pm_ref, po_ref, latem_ref, lateo_ref, normed
):
    fill_normed(xm_ref, xo_ref, gain_at(flags_ref, gains_ref, 1), normed)
    gate, upper = gate_upper(None, w_buf, normed, chunk_of(w_buf.shape[1]))
    backward_math(d_ref[...], gate, upper, w_buf, pm_ref, po_ref)
    is_outer = is_set(flags_ref, OUTER)
    latem_ref[...] = choose(is_outer, xm_ref[...], oldm_ref[...])
    lateo_ref[...] = choose(is_outer, xo_ref[...], oldo_ref[...])


def backward_kernel(live, has_old, has_late, flags_ref, um_ref, uo_ref, gate_ref, upper_ref, w_buf, *refs):
    refs = list(refs)
    old = [refs.pop(0) for _ in range(2)] if has_old else []
    late = refs.pop(0) if has_late else None
    pm_ref, po_ref, ums_ref, uos_ref = refs[:4]
    backward_math(active_gradient(um_ref, uo_ref, w_buf), gate_ref[...], upper_ref[...], w_buf, pm_ref, po_ref)
    found = [um_ref[...], uo_ref[...]]
    if old:
        is_live = is_set(flags_ref, KIND, live)
        found = [choose(is_live, a, b[...]) for a, b in zip(found, old)]
    ums_ref[...], uos_ref[...] = found
    if has_late:
        refs[4][...] = choose(is_set(flags_ref, OUTER), late[...], found[0])


def hold_kernel(part, backward, flags_ref, pm_ref, recv_ref, base_ref, *refs):
    summed = pm_ref[...].astype(F32) + recv_ref[...].astype(F32)
    if backward:
        state_ref, gains_ref, *outs = refs
        gain = gain_at(flags_ref, gains_ref, part)
        unit, root, _ = norm_rows(state_ref[...], gain)
        d_unit = summed * gain
        summed = (d_unit - unit * jnp.mean(d_unit * unit, axis=-1, keepdims=True)) / root
    else:
        outs = refs
    base = jnp.where(is_set(flags_ref, FIRST_CHIP), base_ref[...].astype(F32), 0.0)
    (out,) = outs
    out[...] = (summed + base).astype(BF)


def sides_kernel(marks_ref, early_ref, late_ref, same_ref, opposite_ref):
    is_near = is_set(marks_ref, NEAR)
    same_ref[...] = choose(is_near, early_ref[...], late_ref[...])
    opposite_ref[...] = choose(is_near, late_ref[...], early_ref[...])


def stack_kernel(*refs):
    *sources, out_ref = refs
    rows = sources[0].shape[0]
    for i, source in enumerate(sources):
        out_ref[i * rows : (i + 1) * rows] = source[...]


def fill_rows(target, sources, change=None):
    start = 0
    for source in sources:
        rows = source[...]
        target[start : start + rows.shape[0]] = change(rows) if change else rows
        start += rows.shape[0]


def sum_kernel(first_ref, second_ref, out_ref):
    out_ref[...] = (first_ref[...].astype(F32) + second_ref[...].astype(F32)).astype(BF)


def own_first_kernel(
    flags_ref, xs_ref, em_ref, eo_ref, lm_ref, lo_ref, p0, p1, p2, p3, q0, q1, q2, q3, gains_ref, w_ref,
    turned_ref, left_ref, right_ref, active_ref, w_buf, normed, sems
):
    features = w_buf.shape[1]
    size = chunk_of(features)
    count = features // size
    copies = {}
    for k in range(count):
        rows = pl.ds(k * size, size)
        for matrix in range(2):
            copies[matrix, k] = pltpu.make_async_copy(
                w_ref.at[0, matrix, rows], w_buf.at[matrix, rows], sems.at[matrix, k]
            )
            copies[matrix, k].start()
    gain = gains_ref[0:1]
    pieces, half = xs_ref.shape[:2]
    is_near = flags_ref[NEAR] == 1
    is_outer = flags_ref[OUTER] == 1
    inputs_used = jnp.logical_and(is_near, is_outer)

    def put(piece, rows):
        normed[piece * half : (piece + 1) * half] = norm_rows(rows, gain)[2]

    @pl.when(inputs_used)
    def _():
        for piece in range(pieces):
            put(piece, xs_ref[piece])

    cases = (
        (False, True, (em_ref, eo_ref, p0, p1, p2, p3)),
        (False, False, (lm_ref, lo_ref, p0, p1, p2, p3)),
        (True, False, (lm_ref, lo_ref, q0, q1, q2, q3)),
    )
    for outer, near, sources in cases:

        @pl.when(jnp.logical_and(is_outer == outer, is_near == near))
        def _(sources=sources):
            fill_rows(normed, sources, lambda rows: norm_rows(rows, gain)[2])

    gate, upper = gate_upper(copies, w_buf, normed, size)
    sig = jax.nn.sigmoid(gate)
    smooth = gate * sig
    left_ref[...] = upper * (sig * (1.0 + gate * (1.0 - sig)))
    right_ref[...] = smooth
    active_ref[...] = (smooth * upper).astype(BF)
    for k in range(count):
        cols = pl.ds(k * size, size)
        turned_ref[cols] = normed[:, cols].T


def own_last_kernel(flags_ref, us_ref, *refs):
    refs = list(refs)

    def take(count):
        return [refs.pop(0) for _ in range(count)]

    direct, early, late, arrived = take(2), take(2), take(2), take(8)
    turned_ref, left_ref, right_ref, active_ref, early_ref, late_ref = take(6)
    out_ref, u_buf, d_act, out_buf, sems = take(5)
    features = turned_ref.shape[0]
    size = chunk_of(features)
    count = features // size
    pieces, half = us_ref.shape[:2]
    is_near = flags_ref[NEAR] == 1
    is_outer = flags_ref[OUTER] == 1

    def fill(sources, w_ref):
        fill_rows(u_buf, sources)
        total = None
        for k in range(count):
            cols = pl.ds(k * size, size)
            part = dot(u_buf[:, cols], w_ref[2, cols])
            total = part if total is None else total + part
        d_act[...] = total

    cases = (
        (True, True, direct, early_ref),
        (True, False, [us_ref.at[i] for i in range(pieces)], late_ref),
        (False, True, early + arrived[:4], early_ref),
        (False, False, late + arrived[4:], late_ref),
    )
    for outer, near, sources, w_ref in cases:

        @pl.when(jnp.logical_and(is_outer == outer, is_near == near))
        def _(sources=sources, w_ref=w_ref):
            fill(sources, w_ref)

    copies = []

    def send(matrix, k):
        rows = pl.ds(k * size, size)
        copy = pltpu.make_async_copy(out_buf.at[matrix, rows], out_ref.at[0, matrix, rows], sems.at[matrix, k])
        copy.start()
        copies.append(copy)

    active = active_ref[...]
    d_active = d_act[...]
    for k in range(count):
        cols = pl.ds(k * size, size)
        out_buf[2, cols] = dot_first(u_buf[:, cols], active).astype(BF)
        send(2, k)
    d_gate = (d_active * left_ref[...]).astype(BF)
    d_upper = (d_active * right_ref[...]).astype(BF)
    for k in range(count):
        cols = pl.ds(k * size, size)
        turned = turned_ref[cols]
        out_buf[0, cols] = dot(turned, d_gate).astype(BF)
        send(0, k)
        out_buf[1, cols] = dot(turned, d_upper).astype(BF)
        send(1, k)
    for copy in copies:
        copy.wait()


def call(kernel, name, operands, outs, scratch, limit, flops, moved, hbm=(), out_hbm=False, smem=(0,)):
    specs = [
        SMEM_SPEC if i in smem else HBM_SPEC if i in hbm else VMEM_SPEC for i in range(len(operands))
    ]
    out_spec = HBM_SPEC if out_hbm else VMEM_SPEC
    results = pl.pallas_call(
        kernel,
        out_shape=outs,
        in_specs=specs,
        out_specs=[out_spec] * len(outs),
        scratch_shapes=scratch,
        cost_estimate=pl.CostEstimate(flops=flops, bytes_accessed=moved, transcendentals=0),
        compiler_params=pltpu.CompilerParams(vmem_limit_bytes=limit * MIB),
        name=name,
    )(*operands)
    return list(results)


def body(inputs, cotangent, section_weights, section_gains):
    sections = lax.axis_size("pipe") // REPL
    ranks = lax.axis_size("tensor")
    pipe = lax.axis_index("pipe")
    tensor = lax.axis_index("tensor")
    position = pipe % sections
    replica = pipe // sections
    middle = sections // 2
    near = position < middle
    side = jnp.where(near, 0, 1)
    kind = jnp.where(near, position, sections - 1 - position)
    core = tensor % 2
    chip = tensor // 2
    rows, features = inputs.shape[2:]
    narrow = section_weights.shape[-1]
    chunks = features // chunk_of(features)
    weights = pltpu.with_memory_space_constraint(section_weights[0], pltpu.HBM)
    blocks = pltpu.with_memory_space_constraint(inputs.reshape(-1, rows, features), pltpu.HBM)
    cot_blocks = pltpu.with_memory_space_constraint(cotangent.reshape(-1, rows, features), pltpu.HBM)
    gains = section_gains[0]
    core_swap = [(i, i ^ 1) for i in range(ranks)]
    chip_swap = [(i, (i + 2) % ranks) for i in range(ranks)]

    def spot(across, end, batch):
        return (((replica + across) % REPL) * 2 + end) * 2 + batch

    pairs = ((0, 0), (0, 1), (1, 0), (1, 1))
    pairs_of = ((1, 0), (0, 1), (1, 1))
    own = [spot(across, side ^ turn, batch) for batch in (core, 1 - core) for across, turn in pairs]
    own = [own[i] for i in (0, 4, 1, 2, 3, 5, 6, 7)]
    state = [spot(across, end, batch) for batch in (core, 1 - core) for across, end in pairs]
    flags = [side, near, kind == 0, chip == 0, kind] + own + state
    flags = jnp.stack([jnp.asarray(flag).astype(jnp.int32) for flag in flags])

    def swap_core(block):
        return lax.ppermute(block, "tensor", core_swap)

    def swap_chip(block):
        return lax.ppermute(block, "tensor", chip_swap)

    def place(copy, end, c, rank):
        at = c if end == 0 else sections - 1 - c
        return (copy * sections + at) * ranks + rank

    def send(block, route):
        moves = []
        for copy in range(REPL):
            for end in range(2):
                for c in range(middle):
                    source = route(copy, end, c)
                    if source is None:
                        continue
                    for rank in range(ranks):
                        came = (rank + 2) % ranks if source[3] else rank
                        moves.append((place(*source[:3], came), place(copy, end, c, rank)))
        return lax.ppermute(block, ("pipe", "tensor"), moves)

    def hop(block, source, target, other):
        return send(block, lambda copy, end, c: (copy, end, source, other) if c == target else None)

    def flow(payload, which, wanted):
        turn, shift = pairs_of[which]

        def route(copy, end, c):
            return ((copy + shift) % REPL, end ^ turn, c, False) if wanted(c, end) else None

        return send(payload, route)

    def joined(*parts):
        return call(stack_kernel, "stack", list(parts), [shape(len(parts) * rows, features)], [], 4, 0, 0, smem=())[0]

    def with_other_core(arrived):
        return arrived + [swap_core(block) for block in arrived]

    def shape(*extent, dtype=BF):
        return jax.ShapeDtypeStruct(extent, dtype)

    row = shape(rows, features)
    pieces = shape(4 * REPL, rows, features)
    gate_shape = shape(2 * rows, narrow, dtype=F32)
    held_shape = pltpu.VMEM((3, features, narrow), BF)
    normed_scratch = pltpu.VMEM((2 * rows, features), BF)
    layer_flops = 12 * rows * features * narrow
    layer_bytes = 6 * features * narrow
    row_bytes = 2 * rows * features

    def layer(kernel, name, operands, outs):
        return call(kernel, name, operands, outs, [normed_scratch], 8, layer_flops, layer_bytes, smem=())

    def hold(part, backward, operands):
        kernel = functools.partial(hold_kernel, part, backward)
        return call(kernel, "hold", [marks] + operands, [row], [], 4, 0, 4 * row_bytes, smem=())[0]

    def total(terms):
        return call(sum_kernel, "total", terms, [row], [], 4, 0, 3 * row_bytes, smem=())[0]

    def kind_of(step):
        return min(step, sections - 1 - step)

    def across(held, source, target, during, later=()):
        straight, crossed = hop(held, source, target, False), hop(held, source, target, True)
        straight, crossed, during = lax.optimization_barrier((straight, crossed, during))
        mine = total([straight, crossed])
        other, later = lax.optimization_barrier((swap_core(mine), later))
        return mine, other, during, later

    def far(c, end):
        return end == 1

    def middle_near(c, end):
        return c > 0 and end == 0

    def middle_class(c, end):
        return c > 0

    pm, po, gate, upper, held_early, mine, other, marks = call(
        first_kernel,
        "first_layer",
        [flags, blocks, pltpu.with_memory_space_constraint(gains, pltpu.HBM), weights],
        [row, row, gate_shape, gate_shape, held_shape, row, row, shape(8, 128, dtype=jnp.int32)],
        [
            normed_scratch,
            pltpu.VMEM(gains.shape, F32),
            pltpu.SemaphoreType.DMA((3, chunks)),
            pltpu.SemaphoreType.DMA((3,)),
        ],
        8,
        layer_flops,
        layer_bytes,
        hbm=(1, 2, 3),
    )
    saved = [(gate, upper, mine, other), None]
    loaded = call(
        load_kernel,
        "load_late",
        [flags, blocks, cot_blocks, weights],
        [held_shape, pieces, pieces, row, row],
        [pltpu.SemaphoreType.DMA((3, 1)), pltpu.SemaphoreType.DMA((3, 4 * REPL))],
        4,
        0,
        2 * layer_bytes,
        hbm=(1, 2, 3),
    )
    for step in range(sections - 1):
        part = 0 if step < middle else 1
        if step > 0:
            old = list(saved[part] or ())
            pm, po, *saved[part] = layer(
                functools.partial(forward_kernel, part, kind_of(step)),
                "forward_layer",
                [marks, mine, other, gains, held_late if part else held_early] + old,
                [row, row, gate_shape, gate_shape, row, row],
            )
        held = hold(part, False, [pm, swap_core(po), mine])
        during = ()
        if step == 0:
            during = loaded
        if step == middle:
            during = call(
                cotangent_kernel,
                "cotangent",
                [up_mine, up_other, held_late],
                [gate_shape],
                [],
                4,
                layer_flops // 3,
                layer_bytes // 3,
                smem=(),
            )
        if step == middle - 1:
            mine = total([held, swap_chip(held)])
            other = swap_core(mine)
        else:
            mine, other, during, _ = across(held, kind_of(step), kind_of(step + 1), during)
        if step == 0:
            held_late, input_rows, cot_rows, up_mine, up_other = during
        if step == middle:
            (d_active,) = during

    early_rows = saved[0][2:]
    sides = call(sides_kernel, "sides", [marks, saved[0][2], saved[1][2]], [row, row], [], 4, 0, 0, smem=())
    mine, (same, opposite) = lax.optimization_barrier((mine, sides))
    state_first = flow(opposite, 0, middle_class)
    state_second = flow(joined(same, state_first), 1, middle_class)
    gates = [saved[0][:2], saved[1][:2]]
    pm, po, late_mine, late_other = layer(
        turn_kernel,
        "turn_layer",
        [marks, d_active, mine, other, *saved[1][2:], gains, held_late],
        [row] * 4,
    )
    state_mine = [early_rows[0], late_mine]
    ups = [None, (up_mine, up_other)]
    own_rows = 4 * REPL * rows
    for step in range(sections - 1, 0, -1):
        part = 0 if step < middle else 1
        if step < sections - 1:
            old = list(ups[part] or ())
            extra = [late_mine] if step == middle else []
            pm, po, *kept = layer(
                functools.partial(backward_kernel, kind_of(step), bool(old), bool(extra)),
                "backward_layer",
                [marks, up_mine, up_other, *gates[part], held_late if part else held_early] + old + extra,
                [row] * (5 if extra else 4),
            )
            ups[part] = kept[:2]
        held = hold(part, True, [pm, swap_core(po), up_mine, state_mine[part], gains])
        if step == 1:
            held, near_up = lax.optimization_barrier((held, ups[0][0]))
            crossed = swap_chip(held)
            near_first = flow(near_up, 0, middle_near)
            crossed, near_first = lax.optimization_barrier((crossed, near_first))
            mine = total([held, crossed])
        elif step == middle:
            held, mixed = lax.optimization_barrier((held, kept[2]))
            up_mine = total([held, swap_chip(held)])
            mixed_first = flow(mixed, 0, far)
            up_other, mixed_first, middle_arrived = lax.optimization_barrier(
                (swap_core(up_mine), mixed_first, middle_arrived)
            )
            mixed_second = flow(joined(mixed, mixed_first), 1, far)
        else:
            during = ()
            if step == sections - 1:
                during = [state_first, state_second]
            up_mine, up_other, during, _ = across(held, kind_of(step), kind_of(step - 1), during)
            if step == sections - 1:
                middle_arrived = with_other_core(during)
    _, mixed_second = lax.optimization_barrier((mine, mixed_second))
    straight = [
        send(
            mine,
            lambda copy, end, c, shift=shift, source=source: (
                ((copy + shift) % REPL, source, 1, False) if c == 0 and end == 0 else None
            ),
        )
        for shift, source in pairs
    ]
    near_arrived = with_other_core([near_first, flow(joined(near_up, near_first), 1, middle_near)])
    mixed_arrived = with_other_core([mixed_first, mixed_second])
    prepared = call(
        own_first_kernel,
        "own_first",
        [flags, input_rows, *early_rows, late_mine, late_other, *middle_arrived, *mixed_arrived, gains, weights],
        [
            shape(features, own_rows),
            shape(own_rows, narrow, dtype=F32),
            shape(own_rows, narrow, dtype=F32),
            shape(own_rows, narrow),
        ],
        [
            pltpu.VMEM((2, features, narrow), BF),
            pltpu.VMEM((own_rows, features), BF),
            pltpu.SemaphoreType.DMA((2, chunks)),
        ],
        12,
        4 * own_rows * features * narrow,
        8 * features * narrow,
        hbm=(15,),
    )
    straight, prepared = lax.optimization_barrier((straight, prepared))
    direct = with_other_core([joined(*straight)])
    return call(
        own_last_kernel,
        "own_last",
        [flags, cot_rows, *direct, *ups[0], *ups[1], *near_arrived, *mixed_arrived]
        + [*prepared, held_early, held_late],
        [shape(1, 3, features, narrow)],
        [
            pltpu.VMEM((own_rows, features), BF),
            pltpu.VMEM((own_rows, narrow), F32),
            pltpu.VMEM((3, features, narrow), BF),
            pltpu.SemaphoreType.DMA((3, chunks)),
        ],
        16,
        8 * own_rows * features * narrow,
        8 * features * narrow,
        out_hbm=True,
    )[0]


def solution(mesh):
    return jax.shard_map(
        body,
        mesh=mesh,
        in_specs=(P(), P(), P("pipe", None, None, None, "tensor"), P("pipe", None, None)),
        out_specs=P("pipe", None, None, "tensor"),
        check_vma=False,
    )
```

```python
import functools

import jax
import jax.numpy as jnp
from jax import lax
from jax.experimental import pallas as pl
from jax.experimental.pallas import tpu as pltpu
from jax.sharding import PartitionSpec as P

REPL = 2
EPS = 1e-06
BF = jnp.bfloat16
F32 = jnp.float32
SMEM_SPEC = pl.BlockSpec(memory_space=pltpu.SMEM)
VMEM_SPEC = pl.BlockSpec(memory_space=pltpu.VMEM)
HBM_SPEC = pl.BlockSpec(memory_space=pltpu.HBM)
MIB = 1024 * 1024
NEAR, OUTER, FIRST_CHIP, KIND, OWN, STATE = 1, 2, 3, 4, 5, 13


def chunk_of(features):
    for size in (512, 256, 128):
        if features % size == 0:
            return size
    return features


def norm_rows(rows, gain_row):
    widened = rows.astype(F32)
    root = jnp.sqrt(jnp.mean(widened * widened, axis=-1, keepdims=True) + EPS)
    unit = widened / root
    return unit, root, (unit * gain_row).astype(BF)


def dot(left, right):
    return jnp.dot(left, right, preferred_element_type=F32)


def dot_last(left, right):
    return lax.dot_general(left, right, (((1,), (1,)), ((), ())), preferred_element_type=F32)


def dot_first(left, right):
    return lax.dot_general(left, right, (((0,), (0,)), ((), ())), preferred_element_type=F32)


def is_set(flags_ref, index, value=1):
    if len(flags_ref.shape) == 1:
        return flags_ref[index] == value
    return flags_ref[index : index + 1, 0:1] == value


def gain_at(flags_ref, gains_ref, part):
    return jnp.where(is_set(flags_ref, NEAR, 1 - part), gains_ref[0:1], gains_ref[1:2])


def own_index(flags_ref, part):
    return jnp.where(flags_ref[NEAR] == 1 - part, 0, 1)


def choose(condition, first, second):
    kept = first.dtype
    return jnp.where(condition, first.astype(F32), second.astype(F32)).astype(kept)


def weight_copies(which, w_ref, w_buf, sems, size):
    features = w_buf.shape[1]
    copies = {}
    for matrix in range(3):
        for k in range(features // size):
            rows = pl.ds(k * size, size)
            copies[matrix, k] = pltpu.make_async_copy(
                w_ref.at[which, matrix, rows], w_buf.at[matrix, rows], sems.at[matrix, k]
            )
    return copies


def fill_normed(xm_ref, xo_ref, gain, normed):
    half = xm_ref.shape[0]
    normed[:half] = norm_rows(xm_ref[...], gain)[2]
    normed[half:] = norm_rows(xo_ref[...], gain)[2]


def gate_upper(copies, w_buf, normed, size):
    gate = upper = None
    for k in range(w_buf.shape[1] // size):
        cols = pl.ds(k * size, size)
        if copies:
            copies[0, k].wait()
            copies[1, k].wait()
        block = normed[:, cols]
        gate_k = dot(block, w_buf[0, cols])
        upper_k = dot(block, w_buf[1, cols])
        gate = gate_k if gate is None else gate + gate_k
        upper = upper_k if upper is None else upper + upper_k
    return gate, upper


def forward_math(copies, xm_ref, xo_ref, gain, w_buf, pm_ref, po_ref, normed):
    size = chunk_of(w_buf.shape[1])
    half = xm_ref.shape[0]
    fill_normed(xm_ref, xo_ref, gain, normed)
    gate, upper = gate_upper(copies, w_buf, normed, size)
    active = (gate * jax.nn.sigmoid(gate) * upper).astype(BF)
    for k in range(w_buf.shape[1] // size):
        cols = pl.ds(k * size, size)
        if copies:
            copies[2, k].wait()
        part = dot_last(active, w_buf[2, cols]).astype(BF)
        pm_ref[:, cols] = part[:half]
        po_ref[:, cols] = part[half:]
    return gate, upper


def first_kernel(
    flags_ref, rows_ref, gains_ref, w_ref,
    pm_ref, po_ref, gate_ref, upper_ref, w_buf, xm_ref, xo_ref, marks_ref, normed, gains_buf, sems, row_sems
):
    size = chunk_of(w_buf.shape[1])
    moves = [
        pltpu.make_async_copy(rows_ref.at[flags_ref[OWN + i]], ref, row_sems.at[i])
        for i, ref in enumerate((xm_ref, xo_ref))
    ]
    moves.append(pltpu.make_async_copy(gains_ref, gains_buf, row_sems.at[2]))
    for move in moves:
        move.start()
    for i in range(marks_ref.shape[0]):
        marks_ref[i : i + 1] = jnp.full((1, marks_ref.shape[1]), flags_ref[i], jnp.int32)
    for move in moves:
        move.wait()
    copies = weight_copies(own_index(flags_ref, 0), w_ref, w_buf, sems, size)
    for group in ((0, 1), (2,)):
        for k in range(w_buf.shape[1] // size):
            for matrix in group:
                copies[matrix, k].start()
    gain = gain_at(flags_ref, gains_buf, 0)
    gate_ref[...], upper_ref[...] = forward_math(copies, xm_ref, xo_ref, gain, w_buf, pm_ref, po_ref, normed)


def load_kernel(flags_ref, rows_ref, cot_ref, w_ref, w_buf, xs_ref, us_ref, um_ref, uo_ref, sems, row_sems):
    copies = list(weight_copies(own_index(flags_ref, 1), w_ref, w_buf, sems, w_buf.shape[1]).values())
    for i in range(xs_ref.shape[0]):
        copies.append(pltpu.make_async_copy(cot_ref.at[flags_ref[OWN + i]], us_ref.at[i], row_sems.at[0, i]))
        copies.append(pltpu.make_async_copy(rows_ref.at[flags_ref[STATE + i]], xs_ref.at[i], row_sems.at[1, i]))
    for i, ref in enumerate((um_ref, uo_ref)):
        copies.append(pltpu.make_async_copy(cot_ref.at[flags_ref[OWN + i]], ref, row_sems.at[2, i]))
    for copy in copies:
        copy.start()
    for copy in copies:
        copy.wait()


def forward_kernel(part, live, flags_ref, xm_ref, xo_ref, gains_ref, w_buf, *refs):
    *old, pm_ref, po_ref, gate_ref, upper_ref, xms_ref, xos_ref, normed = refs
    gain = gain_at(flags_ref, gains_ref, part)
    gate, upper = forward_math(None, xm_ref, xo_ref, gain, w_buf, pm_ref, po_ref, normed)
    found = (gate, upper, xm_ref[...], xo_ref[...])
    outs = (gate_ref, upper_ref, xms_ref, xos_ref)
    if old:
        is_live = is_set(flags_ref, KIND, live)
        found = [choose(is_live, a, b[...]) for a, b in zip(found, old)]
    for out, value in zip(outs, found):
        out[...] = value


def active_gradient(um_ref, uo_ref, w_buf):
    size = chunk_of(w_buf.shape[1])
    d_active = None
    for k in range(w_buf.shape[1] // size):
        cols = pl.ds(k * size, size)
        block = jnp.concatenate([um_ref[:, cols], uo_ref[:, cols]], axis=0)
        part = dot(block, w_buf[2, cols])
        d_active = part if d_active is None else d_active + part
    return d_active


def backward_math(d_active, gate, upper, w_buf, pm_ref, po_ref):
    size = chunk_of(w_buf.shape[1])
    half = pm_ref.shape[0]
    sig = jax.nn.sigmoid(gate)
    d_gate = (d_active * upper * (sig * (1.0 + gate * (1.0 - sig)))).astype(BF)
    d_upper = (d_active * (gate * sig)).astype(BF)
    for k in range(w_buf.shape[1] // size):
        cols = pl.ds(k * size, size)
        part = (dot_last(d_gate, w_buf[0, cols]) + dot_last(d_upper, w_buf[1, cols])).astype(BF)
        pm_ref[:, cols] = part[:half]
        po_ref[:, cols] = part[half:]


def cotangent_kernel(um_ref, uo_ref, w_buf, d_ref):
    d_ref[...] = active_gradient(um_ref, uo_ref, w_buf)


def turn_kernel(
    flags_ref, d_ref, xm_ref, xo_ref, oldm_ref, oldo_ref, gains_ref, w_buf, pm_ref, po_ref, latem_ref, lateo_ref, normed
):
    fill_normed(xm_ref, xo_ref, gain_at(flags_ref, gains_ref, 1), normed)
    gate, upper = gate_upper(None, w_buf, normed, chunk_of(w_buf.shape[1]))
    backward_math(d_ref[...], gate, upper, w_buf, pm_ref, po_ref)
    is_outer = is_set(flags_ref, OUTER)
    latem_ref[...] = choose(is_outer, xm_ref[...], oldm_ref[...])
    lateo_ref[...] = choose(is_outer, xo_ref[...], oldo_ref[...])


def backward_kernel(live, has_old, has_state, flags_ref, um_ref, uo_ref, gate_ref, upper_ref, w_buf, *refs):
    refs = list(refs)
    old = [refs.pop(0) for _ in range(2)] if has_old else []
    state = refs.pop(0) if has_state else None
    pm_ref, po_ref, ums_ref, uos_ref = refs[:4]
    backward_math(active_gradient(um_ref, uo_ref, w_buf), gate_ref[...], upper_ref[...], w_buf, pm_ref, po_ref)
    found = [um_ref[...], uo_ref[...]]
    if old:
        is_live = is_set(flags_ref, KIND, live)
        found = [choose(is_live, a, b[...]) for a, b in zip(found, old)]
    ums_ref[...], uos_ref[...] = found
    if has_state:
        po_ref[...] = choose(is_set(flags_ref, OUTER), state[...], po_ref[...])


def hold_kernel(part, backward, has_state, flags_ref, pm_ref, recv_ref, base_ref, *refs):
    summed = pm_ref[...].astype(F32) + recv_ref[...].astype(F32)
    if backward:
        state_ref, gains_ref, *outs = refs
        extra = outs.pop(0) if has_state else None
        gain = gain_at(flags_ref, gains_ref, part)
        unit, root, _ = norm_rows(state_ref[...], gain)
        d_unit = summed * gain
        summed = (d_unit - unit * jnp.mean(d_unit * unit, axis=-1, keepdims=True)) / root
    else:
        outs = refs
    base = jnp.where(is_set(flags_ref, FIRST_CHIP), base_ref[...].astype(F32), 0.0)
    (out,) = outs
    value = (summed + base).astype(BF)
    out[...] = choose(is_set(flags_ref, OUTER), extra[...], value) if has_state else value


def mix_kernel(marks_ref, mine_ref, early_ref, late_ref, same_ref, out_ref):
    is_near = is_set(marks_ref, NEAR)
    early, late = early_ref[...], late_ref[...]
    same_ref[...] = choose(is_near, early, late)
    out_ref[...] = choose(is_set(marks_ref, OUTER), mine_ref[...], choose(is_near, late, early))


def last_kernel(marks_ref, mine_ref, early_ref, late_ref, first_ref, second_ref, third_ref):
    is_near = is_set(marks_ref, NEAR)
    mine, early = mine_ref[...], early_ref[...]
    first_ref[...] = choose(is_near, mine, early)
    second_ref[...] = choose(is_near, late_ref[...], mine)
    third_ref[...] = choose(is_near, early, mine)


def outer_sum_kernel(marks_ref, first_ref, second_ref, state_ref, out_ref, sent_ref):
    value = (first_ref[...].astype(F32) + second_ref[...].astype(F32)).astype(BF)
    out_ref[...] = value
    sent_ref[...] = choose(is_set(marks_ref, OUTER), state_ref[...], value)


def stack_kernel(*refs):
    *sources, out_ref = refs
    rows = sources[0].shape[0]
    for i, source in enumerate(sources):
        out_ref[i * rows : (i + 1) * rows] = source[...]


def fill_rows(target, sources, change=None):
    start = 0
    for source in sources:
        rows = source[...]
        target[start : start + rows.shape[0]] = change(rows) if change else rows
        start += rows.shape[0]


def sum_kernel(first_ref, second_ref, out_ref):
    out_ref[...] = (first_ref[...].astype(F32) + second_ref[...].astype(F32)).astype(BF)


def own_first_kernel(
    flags_ref, xs_ref, em_ref, eo_ref, lm_ref, lo_ref, p0, p1, p2, p3, q0, q1, q2, q3, q4, q5, gains_ref, w_ref,
    turned_ref, left_ref, right_ref, active_ref, w_buf, normed, sems
):
    features = w_buf.shape[1]
    size = chunk_of(features)
    count = features // size
    copies = {}
    for k in range(count):
        rows = pl.ds(k * size, size)
        for matrix in range(2):
            copies[matrix, k] = pltpu.make_async_copy(
                w_ref.at[0, matrix, rows], w_buf.at[matrix, rows], sems.at[matrix, k]
            )
            copies[matrix, k].start()
    gain = gains_ref[0:1]
    pieces, half = xs_ref.shape[:2]
    is_near = flags_ref[NEAR] == 1
    is_outer = flags_ref[OUTER] == 1
    inputs_used = jnp.logical_and(is_near, is_outer)

    def put(piece, rows):
        normed[piece * half : (piece + 1) * half] = norm_rows(rows, gain)[2]

    @pl.when(inputs_used)
    def _():
        for piece in range(pieces):
            put(piece, xs_ref[piece])

    cases = (
        (False, True, (em_ref, eo_ref, p0, p1, p2, p3)),
        (False, False, (lm_ref, lo_ref, p0, p1, p2, p3)),
        (True, False, (lm_ref, lo_ref, q0, q1, q2, q3, q4, q5)),
    )
    for outer, near, sources in cases:

        @pl.when(jnp.logical_and(is_outer == outer, is_near == near))
        def _(sources=sources):
            fill_rows(normed, sources, lambda rows: norm_rows(rows, gain)[2])

    gate, upper = gate_upper(copies, w_buf, normed, size)
    sig = jax.nn.sigmoid(gate)
    smooth = gate * sig
    left_ref[...] = upper * (sig * (1.0 + gate * (1.0 - sig)))
    right_ref[...] = smooth
    active_ref[...] = (smooth * upper).astype(BF)
    for k in range(count):
        cols = pl.ds(k * size, size)
        turned_ref[cols] = normed[:, cols].T


def own_last_kernel(flags_ref, us_ref, *refs):
    refs = list(refs)

    def take(count):
        return [refs.pop(0) for _ in range(count)]

    direct, far_in, early, late = take(2), take(2), take(2), take(2)
    turned_ref, left_ref, right_ref, active_ref, early_ref, late_ref = take(6)
    out_ref, u_buf, d_act, out_buf, sems = take(5)
    features = turned_ref.shape[0]
    size = chunk_of(features)
    count = features // size
    pieces = us_ref.shape[0]
    is_near = flags_ref[NEAR] == 1
    is_outer = flags_ref[OUTER] == 1

    def fill(sources, w_ref):
        fill_rows(u_buf, sources)
        total = None
        for k in range(count):
            cols = pl.ds(k * size, size)
            part = dot(u_buf[:, cols], w_ref[2, cols])
            total = part if total is None else total + part
        d_act[...] = total

    half = early[0].shape[0]

    def lanes(source, *places):
        return [source.at[pl.ds(i * half, half)] for i in places]

    near_sources = early + lanes(direct[0], 0, 3, 2) + lanes(direct[1], 0, 3, 2)
    far_sources = late + lanes(direct[0], 1) + far_in[:1] + lanes(direct[1], 1) + far_in[1:]
    cases = (
        (True, True, direct, early_ref),
        (True, False, [us_ref.at[i] for i in range(pieces)], late_ref),
        (False, True, near_sources, early_ref),
        (False, False, far_sources, late_ref),
    )
    for outer, near, sources, w_ref in cases:

        @pl.when(jnp.logical_and(is_outer == outer, is_near == near))
        def _(sources=sources, w_ref=w_ref):
            fill(sources, w_ref)

    copies = []

    def send(matrix, k):
        rows = pl.ds(k * size, size)
        copy = pltpu.make_async_copy(out_buf.at[matrix, rows], out_ref.at[0, matrix, rows], sems.at[matrix, k])
        copy.start()
        copies.append(copy)

    active = active_ref[...]
    d_active = d_act[...]
    for k in range(count):
        cols = pl.ds(k * size, size)
        out_buf[2, cols] = dot_first(u_buf[:, cols], active).astype(BF)
        send(2, k)
    d_gate = (d_active * left_ref[...]).astype(BF)
    d_upper = (d_active * right_ref[...]).astype(BF)
    for k in range(count):
        cols = pl.ds(k * size, size)
        turned = turned_ref[cols]
        out_buf[0, cols] = dot(turned, d_gate).astype(BF)
        send(0, k)
        out_buf[1, cols] = dot(turned, d_upper).astype(BF)
        send(1, k)
    for copy in copies:
        copy.wait()


def call(kernel, name, operands, outs, scratch, limit, flops, moved, hbm=(), out_hbm=False, smem=(0,)):
    specs = [
        SMEM_SPEC if i in smem else HBM_SPEC if i in hbm else VMEM_SPEC for i in range(len(operands))
    ]
    out_spec = HBM_SPEC if out_hbm else VMEM_SPEC
    results = pl.pallas_call(
        kernel,
        out_shape=outs,
        in_specs=specs,
        out_specs=[out_spec] * len(outs),
        scratch_shapes=scratch,
        cost_estimate=pl.CostEstimate(flops=flops, bytes_accessed=moved, transcendentals=0),
        compiler_params=pltpu.CompilerParams(vmem_limit_bytes=limit * MIB),
        name=name,
    )(*operands)
    return list(results)


def body(inputs, cotangent, section_weights, section_gains):
    sections = lax.axis_size("pipe") // REPL
    ranks = lax.axis_size("tensor")
    pipe = lax.axis_index("pipe")
    tensor = lax.axis_index("tensor")
    position = pipe % sections
    replica = pipe // sections
    middle = sections // 2
    near = position < middle
    side = jnp.where(near, 0, 1)
    kind = jnp.where(near, position, sections - 1 - position)
    core = tensor % 2
    chip = tensor // 2
    rows, features = inputs.shape[2:]
    narrow = section_weights.shape[-1]
    chunks = features // chunk_of(features)
    weights = pltpu.with_memory_space_constraint(section_weights[0], pltpu.HBM)
    blocks = pltpu.with_memory_space_constraint(inputs.reshape(-1, rows, features), pltpu.HBM)
    cot_blocks = pltpu.with_memory_space_constraint(cotangent.reshape(-1, rows, features), pltpu.HBM)
    gains = section_gains[0]
    def spot(across, end, batch):
        return (((replica + across) % REPL) * 2 + end) * 2 + batch

    pairs = ((0, 0), (0, 1), (1, 0), (1, 1))
    pairs_of = ((1, 0), (0, 1), (1, 1))
    own = [spot(across, side ^ turn, batch) for batch in (core, 1 - core) for across, turn in pairs]
    own = [own[i] for i in (0, 4, 1, 2, 3, 5, 6, 7)]
    state = [spot(across, end, batch) for batch in (core, 1 - core) for across, end in pairs]
    flags = [side, near, kind == 0, chip == 0, kind] + own + state
    flags = jnp.stack([jnp.asarray(flag).astype(jnp.int32) for flag in flags])

    def place(copy, end, c, rank):
        at = c if end == 0 else sections - 1 - c
        return (copy * sections + at) * ranks + rank

    def moves_of(route):
        moves = []
        for copy in range(REPL):
            for end in range(2):
                for c in range(middle):
                    source = route(copy, end, c)
                    if source is None:
                        continue
                    for rank in range(ranks):
                        came = rank ^ 1 if source[3] == 1 else (rank + 2) % ranks if source[3] == 2 else rank
                        moves.append((place(*source[:3], came), place(copy, end, c, rank)))
        return moves

    def send(block, *routes):
        return lax.ppermute(block, ("pipe", "tensor"), sum((moves_of(route) for route in routes), []))

    def swap_route(how, kinds):
        return lambda copy, end, c: (copy, end, c, how) if c in kinds else None

    def swap_core(block, kinds, *routes):
        return send(block, swap_route(1, kinds), *routes)

    def swap_chip(block, kinds, *routes):
        return send(block, swap_route(2, kinds), *routes)

    def hop(block, source, target, other):
        return send(block, lambda copy, end, c: (copy, end, source, other) if c == target else None)

    def flow_route(which, wanted):
        turn, shift = pairs_of[which]
        return lambda copy, end, c: ((copy + shift) % REPL, end ^ turn, c, 0) if wanted(c, end) else None

    def flow(payload, which, wanted):
        return send(payload, flow_route(which, wanted))

    def joined(*parts):
        return call(stack_kernel, "stack", list(parts), [shape(len(parts) * rows, features)], [], 4, 0, 0, smem=())[0]

    def with_other_core(arrived):
        return arrived + [swap_core(block, range(middle)) for block in arrived]

    def shape(*extent, dtype=BF):
        return jax.ShapeDtypeStruct(extent, dtype)

    row = shape(rows, features)
    pieces = shape(4 * REPL, rows, features)
    gate_shape = shape(2 * rows, narrow, dtype=F32)
    held_shape = pltpu.VMEM((3, features, narrow), BF)
    normed_scratch = pltpu.VMEM((2 * rows, features), BF)
    layer_flops = 12 * rows * features * narrow
    layer_bytes = 6 * features * narrow
    row_bytes = 2 * rows * features

    def layer(kernel, name, operands, outs):
        return call(kernel, name, operands, outs, [normed_scratch], 8, layer_flops, layer_bytes, smem=())

    def hold(part, backward, operands, has_state=False):
        kernel = functools.partial(hold_kernel, part, backward, has_state)
        return call(kernel, "hold", [marks] + operands, [row], [], 4, 0, 4 * row_bytes, smem=())[0]

    def total(terms):
        return call(sum_kernel, "total", terms, [row], [], 4, 0, 3 * row_bytes, smem=())[0]

    def kind_of(step):
        return min(step, sections - 1 - step)

    def across(held, source, target, during):
        straight, crossed = hop(held, source, target, 0), hop(held, source, target, 2)
        straight, crossed, during = lax.optimization_barrier((straight, crossed, during))
        return total([straight, crossed]), during

    def outer_far(c, end):
        return c == 0 and end == 1

    def middle_class(c, end):
        return c > 0

    def middle_near(c, end):
        return c > 0 and end == 0

    def middle_far(c, end):
        return c > 0 and end == 1

    pm, po, gate, upper, held_early, mine, other, marks = call(
        first_kernel,
        "first_layer",
        [flags, blocks, pltpu.with_memory_space_constraint(gains, pltpu.HBM), weights],
        [row, row, gate_shape, gate_shape, held_shape, row, row, shape(8, 128, dtype=jnp.int32)],
        [
            normed_scratch,
            pltpu.VMEM(gains.shape, F32),
            pltpu.SemaphoreType.DMA((3, chunks)),
            pltpu.SemaphoreType.DMA((3,)),
        ],
        8,
        layer_flops,
        layer_bytes,
        hbm=(1, 2, 3),
    )
    saved = [(gate, upper, mine, other), None]
    loaded = call(
        load_kernel,
        "load_late",
        [flags, blocks, cot_blocks, weights],
        [held_shape, pieces, pieces, row, row],
        [pltpu.SemaphoreType.DMA((3, 1)), pltpu.SemaphoreType.DMA((3, 4 * REPL))],
        4,
        0,
        2 * layer_bytes,
        hbm=(1, 2, 3),
    )
    for step in range(sections - 1):
        part = 0 if step < middle else 1
        if step > 0:
            old = list(saved[part] or ())
            pm, po, *saved[part] = layer(
                functools.partial(forward_kernel, part, kind_of(step)),
                "forward_layer",
                [marks, mine, other, gains, held_late if part else held_early] + old,
                [row, row, gate_shape, gate_shape, row, row],
            )
        active = [kind_of(step)]
        coming = [kind_of(step + 1)]
        held = hold(part, False, [pm, swap_core(po, active), mine])
        during = ()
        if step == 0:
            during = loaded
        if step == middle:
            during = call(
                cotangent_kernel,
                "cotangent",
                [up_mine, up_other, held_late],
                [gate_shape],
                [],
                4,
                layer_flops // 3,
                layer_bytes // 3,
                smem=(),
            )
        if step == middle - 1:
            mine = total([held, swap_chip(held, active)])
        else:
            mine, during = across(held, kind_of(step), kind_of(step + 1), during)
        if step < sections - 2:
            other = swap_core(mine, coming)
        if step == 0:
            held_late, input_rows, cot_rows, up_mine, up_other = during
        if step == middle:
            (d_active,) = during

    early_rows = saved[0][2:]
    same, sent = call(mix_kernel, "mix", [marks, mine, saved[0][2], saved[1][2]], [row, row], [], 4, 0, 0, smem=())
    other = swap_core(sent, [0], flow_route(0, middle_class))
    state_first = other
    gates = [saved[0][:2], saved[1][:2]]
    pm, po, late_mine, late_other = layer(
        turn_kernel,
        "turn_layer",
        [marks, d_active, mine, other, *saved[1][2:], gains, held_late],
        [row] * 4,
    )
    state_mine = [early_rows[0], late_mine]
    ups = [None, (up_mine, up_other)]
    own_rows = 4 * REPL * rows
    for step in range(sections - 1, 0, -1):
        part = 0 if step < middle else 1
        active, coming = [kind_of(step)], [kind_of(step - 1)]
        if step < sections - 1:
            old = list(ups[part] or ())
            rides = step == middle
            pm, po, *ups[part] = layer(
                functools.partial(backward_kernel, kind_of(step), bool(old), rides),
                "backward_layer",
                [marks, up_mine, up_other, *gates[part], held_late if part else held_early]
                + old
                + ([late_mine] if rides else []),
                [row] * 4,
            )
        operands = [up_mine, state_mine[part], gains]
        if step == middle:
            outer_flows = [swap_core(po, active, flow_route(0, outer_far))]
            held = hold(part, True, [pm, outer_flows[0]] + operands + [late_mine], True)
            outer_flows.append(swap_chip(held, active, flow_route(1, outer_far)))
            up_mine, sent = call(
                outer_sum_kernel, "total", [marks, held, outer_flows[1], late_mine], [row, row], [], 4, 0, 0, smem=()
            )
            outer_flows.append(swap_core(sent, coming, flow_route(2, outer_far)))
            up_other = outer_flows[2]
            continue
        held = hold(part, True, [pm, swap_core(po, active)] + operands)
        if step == 1:
            mine = total([held, swap_chip(held, active)])
            continue
        if step == sections - 1:
            held, same, state_first = lax.optimization_barrier((held, same, state_first))
        up_mine, _ = across(held, kind_of(step), kind_of(step - 1), ())
        up_other = swap_core(up_mine, coming)
        if step == sections - 1:
            state_second = flow(joined(same, state_first), 1, middle_class)
            up_other, state_second = lax.optimization_barrier((up_other, state_second))
            middle_arrived = with_other_core([state_first, state_second])

    def last_route(shift, source):
        return lambda copy, end, c: ((copy + shift) % REPL, source, 1, 0) if c == 0 and end == 0 else None

    payloads = call(
        last_kernel, "last", [marks, mine, ups[0][0], ups[1][0]], [row] * 3, [], 4, 0, 0, smem=()
    )
    straight = [
        send(payloads[0], last_route(0, 0), flow_route(0, middle_near)),
        send(payloads[1], last_route(0, 1), flow_route(0, middle_far)),
        send(payloads[0], last_route(1, 0), flow_route(2, middle_near)),
        send(payloads[2], last_route(1, 1), flow_route(1, middle_near)),
    ]
    _, up_far = lax.optimization_barrier((mine, ups[1][0]))
    far_flows = [flow(up_far, which, middle_far) for which in (1, 2)]
    prepared = call(
        own_first_kernel,
        "own_first",
        [flags, input_rows, *early_rows, late_mine, late_other, *middle_arrived]
        + with_other_core(outer_flows)
        + [gains, weights],
        [
            shape(features, own_rows),
            shape(own_rows, narrow, dtype=F32),
            shape(own_rows, narrow, dtype=F32),
            shape(own_rows, narrow),
        ],
        [
            pltpu.VMEM((2, features, narrow), BF),
            pltpu.VMEM((own_rows, features), BF),
            pltpu.SemaphoreType.DMA((2, chunks)),
        ],
        12,
        4 * own_rows * features * narrow,
        8 * features * narrow,
        hbm=(17,),
    )
    straight, far_flows, prepared = lax.optimization_barrier((straight, far_flows, prepared))
    far_in = with_other_core([joined(*far_flows)])
    direct = with_other_core([joined(*straight)])
    return call(
        own_last_kernel,
        "own_last",
        [flags, cot_rows, *direct, *far_in, *ups[0], *ups[1]]
        + [*prepared, held_early, held_late],
        [shape(1, 3, features, narrow)],
        [
            pltpu.VMEM((own_rows, features), BF),
            pltpu.VMEM((own_rows, narrow), F32),
            pltpu.VMEM((3, features, narrow), BF),
            pltpu.SemaphoreType.DMA((3, chunks)),
        ],
        16,
        8 * own_rows * features * narrow,
        8 * features * narrow,
        out_hbm=True,
    )[0]


def solution(mesh):
    return jax.shard_map(
        body,
        mesh=mesh,
        in_specs=(P(), P(), P("pipe", None, None, None, "tensor"), P("pipe", None, None)),
        out_specs=P("pipe", None, None, "tensor"),
        check_vma=False,
    )
```

```python
import functools

import jax
import jax.numpy as jnp
from jax import lax
from jax.experimental import pallas as pl
from jax.experimental.pallas import tpu as pltpu
from jax.sharding import PartitionSpec as P

REPL = 2
EPS = 1e-06
BF = jnp.bfloat16
F32 = jnp.float32
SMEM_SPEC = pl.BlockSpec(memory_space=pltpu.SMEM)
VMEM_SPEC = pl.BlockSpec(memory_space=pltpu.VMEM)
HBM_SPEC = pl.BlockSpec(memory_space=pltpu.HBM)
MIB = 1024 * 1024
NEAR, OUTER, FIRST_CHIP, KIND, OWN, TOP, BOTTOM = 1, 2, 3, 4, 5, 13, 21


def chunk_of(features):
    for size in (512, 256, 128):
        if features % size == 0:
            return size
    return features


def norm_rows(rows, gain_row):
    widened = rows.astype(F32)
    root = jnp.sqrt(jnp.mean(widened * widened, axis=-1, keepdims=True) + EPS)
    unit = widened / root
    return unit, root, (unit * gain_row).astype(BF)


def dot(left, right):
    return jnp.dot(left, right, preferred_element_type=F32)


def dot_last(left, right):
    return lax.dot_general(left, right, (((1,), (1,)), ((), ())), preferred_element_type=F32)


def dot_first(left, right):
    return lax.dot_general(left, right, (((0,), (0,)), ((), ())), preferred_element_type=F32)


def is_set(flags_ref, index, value=1):
    if len(flags_ref.shape) == 1:
        return flags_ref[index] == value
    return flags_ref[index : index + 1, 0:1] == value


def gain_at(flags_ref, gains_ref, part):
    return jnp.where(is_set(flags_ref, NEAR, 1 - part), gains_ref[0:1], gains_ref[1:2])


def own_index(flags_ref, part):
    return jnp.where(flags_ref[NEAR] == 1 - part, 0, 1)


def choose(condition, first, second):
    kept = first.dtype
    return jnp.where(condition, first.astype(F32), second.astype(F32)).astype(kept)


def weight_copies(which, w_ref, w_buf, sems, size):
    features = w_buf.shape[1]
    copies = {}
    for matrix in range(3):
        for k in range(features // size):
            rows = pl.ds(k * size, size)
            copies[matrix, k] = pltpu.make_async_copy(
                w_ref.at[which, matrix, rows], w_buf.at[matrix, rows], sems.at[matrix, k]
            )
    return copies


def fill_normed(xm_ref, xo_ref, gain, normed):
    half = xm_ref.shape[0]
    normed[:half] = norm_rows(xm_ref[...], gain)[2]
    normed[half:] = norm_rows(xo_ref[...], gain)[2]


def gate_upper(copies, w_buf, normed, size):
    gate = upper = None
    for k in range(w_buf.shape[1] // size):
        cols = pl.ds(k * size, size)
        if copies:
            copies[0, k].wait()
            copies[1, k].wait()
        block = normed[:, cols]
        gate_k = dot(block, w_buf[0, cols])
        upper_k = dot(block, w_buf[1, cols])
        gate = gate_k if gate is None else gate + gate_k
        upper = upper_k if upper is None else upper + upper_k
    return gate, upper


def forward_math(copies, xm_ref, xo_ref, gain, w_buf, pm_ref, po_ref, normed):
    size = chunk_of(w_buf.shape[1])
    half = xm_ref.shape[0]
    fill_normed(xm_ref, xo_ref, gain, normed)
    gate, upper = gate_upper(copies, w_buf, normed, size)
    active = (gate * jax.nn.sigmoid(gate) * upper).astype(BF)
    for k in range(w_buf.shape[1] // size):
        cols = pl.ds(k * size, size)
        if copies:
            copies[2, k].wait()
        part = dot_last(active, w_buf[2, cols]).astype(BF)
        pm_ref[:, cols] = part[:half]
        po_ref[:, cols] = part[half:]
    return gate, upper


def first_kernel(
    flags_ref, rows_ref, gains_ref, w_ref,
    pm_ref, po_ref, gate_ref, upper_ref, w_buf, xm_ref, xo_ref, marks_ref, normed, gains_buf, sems, row_sems
):
    size = chunk_of(w_buf.shape[1])
    moves = [
        pltpu.make_async_copy(rows_ref.at[flags_ref[OWN + i]], ref, row_sems.at[i])
        for i, ref in enumerate((xm_ref, xo_ref))
    ]
    moves.append(pltpu.make_async_copy(gains_ref, gains_buf, row_sems.at[2]))
    for move in moves:
        move.start()
    for i in range(marks_ref.shape[0]):
        marks_ref[i : i + 1] = jnp.full((1, marks_ref.shape[1]), flags_ref[i], jnp.int32)
    for move in moves:
        move.wait()
    copies = weight_copies(own_index(flags_ref, 0), w_ref, w_buf, sems, size)
    for group in ((0, 1), (2,)):
        for k in range(w_buf.shape[1] // size):
            for matrix in group:
                copies[matrix, k].start()
    gain = gain_at(flags_ref, gains_buf, 0)
    gate_ref[...], upper_ref[...] = forward_math(copies, xm_ref, xo_ref, gain, w_buf, pm_ref, po_ref, normed)


def load_kernel(flags_ref, rows_ref, cot_ref, w_ref, w_buf, xs_ref, us_ref, um_ref, uo_ref, sems, row_sems):
    copies = list(weight_copies(own_index(flags_ref, 1), w_ref, w_buf, sems, w_buf.shape[1]).values())
    pieces, rows = xs_ref.shape[:2]
    group = rows // 2
    for i in range(pieces):
        spot = flags_ref[OWN + i]
        copies.append(pltpu.make_async_copy(cot_ref.at[spot], us_ref.at[i], row_sems.at[0, i]))
        for half, base in enumerate((TOP, BOTTOM)):
            part = pl.ds(half * group, group)
            copies.append(
                pltpu.make_async_copy(
                    rows_ref.at[flags_ref[base + i], part], xs_ref.at[i, part], row_sems.at[1 + half, i]
                )
            )
    for i, ref in enumerate((um_ref, uo_ref)):
        copies.append(pltpu.make_async_copy(cot_ref.at[flags_ref[OWN + i]], ref, row_sems.at[3, i]))
    for copy in copies:
        copy.start()
    for copy in copies:
        copy.wait()


def forward_kernel(part, live, flags_ref, xm_ref, xo_ref, gains_ref, w_buf, *refs):
    *old, pm_ref, po_ref, gate_ref, upper_ref, xms_ref, xos_ref, normed = refs
    gain = gain_at(flags_ref, gains_ref, part)
    gate, upper = forward_math(None, xm_ref, xo_ref, gain, w_buf, pm_ref, po_ref, normed)
    found = (gate, upper, xm_ref[...], xo_ref[...])
    outs = (gate_ref, upper_ref, xms_ref, xos_ref)
    if old:
        is_live = is_set(flags_ref, KIND, live)
        found = [choose(is_live, a, b[...]) for a, b in zip(found, old)]
    for out, value in zip(outs, found):
        out[...] = value


def active_gradient(um_ref, uo_ref, w_buf):
    size = chunk_of(w_buf.shape[1])
    d_active = None
    for k in range(w_buf.shape[1] // size):
        cols = pl.ds(k * size, size)
        block = jnp.concatenate([um_ref[:, cols], uo_ref[:, cols]], axis=0)
        part = dot(block, w_buf[2, cols])
        d_active = part if d_active is None else d_active + part
    return d_active


def backward_math(d_active, gate, upper, w_buf, pm_ref, po_ref):
    size = chunk_of(w_buf.shape[1])
    half = pm_ref.shape[0]
    sig = jax.nn.sigmoid(gate)
    d_gate = (d_active * upper * (sig * (1.0 + gate * (1.0 - sig)))).astype(BF)
    d_upper = (d_active * (gate * sig)).astype(BF)
    for k in range(w_buf.shape[1] // size):
        cols = pl.ds(k * size, size)
        part = (dot_last(d_gate, w_buf[0, cols]) + dot_last(d_upper, w_buf[1, cols])).astype(BF)
        pm_ref[:, cols] = part[:half]
        po_ref[:, cols] = part[half:]


def cotangent_kernel(um_ref, uo_ref, w_buf, d_ref):
    d_ref[...] = active_gradient(um_ref, uo_ref, w_buf)


def turn_kernel(
    flags_ref, d_ref, xm_ref, xo_ref, oldm_ref, oldo_ref, gains_ref, w_buf, pm_ref, po_ref, latem_ref, lateo_ref, normed
):
    fill_normed(xm_ref, xo_ref, gain_at(flags_ref, gains_ref, 1), normed)
    gate, upper = gate_upper(None, w_buf, normed, chunk_of(w_buf.shape[1]))
    backward_math(d_ref[...], gate, upper, w_buf, pm_ref, po_ref)
    is_outer = is_set(flags_ref, OUTER)
    latem_ref[...] = choose(is_outer, xm_ref[...], oldm_ref[...])
    lateo_ref[...] = choose(is_outer, xo_ref[...], oldo_ref[...])


def backward_kernel(live, has_old, has_late, flags_ref, um_ref, uo_ref, gate_ref, upper_ref, w_buf, *refs):
    refs = list(refs)
    old = [refs.pop(0) for _ in range(2)] if has_old else []
    late = refs.pop(0) if has_late else None
    pm_ref, po_ref, ums_ref, uos_ref = refs[:4]
    backward_math(active_gradient(um_ref, uo_ref, w_buf), gate_ref[...], upper_ref[...], w_buf, pm_ref, po_ref)
    found = [um_ref[...], uo_ref[...]]
    if old:
        is_live = is_set(flags_ref, KIND, live)
        found = [choose(is_live, a, b[...]) for a, b in zip(found, old)]
    ums_ref[...], uos_ref[...] = found
    if has_late:
        is_near = is_set(flags_ref, NEAR)
        refs[4][...] = choose(is_near, found[0], late[...])
        refs[5][...] = choose(is_near, late[...], found[0])


def hold_kernel(part, backward, flags_ref, pm_ref, recv_ref, base_ref, *refs):
    summed = pm_ref[...].astype(F32) + recv_ref[...].astype(F32)
    if backward:
        state_ref, gains_ref, *outs = refs
        gain = gain_at(flags_ref, gains_ref, part)
        unit, root, _ = norm_rows(state_ref[...], gain)
        d_unit = summed * gain
        summed = (d_unit - unit * jnp.mean(d_unit * unit, axis=-1, keepdims=True)) / root
    else:
        outs = refs
    base = jnp.where(is_set(flags_ref, FIRST_CHIP), base_ref[...].astype(F32), 0.0)
    value = (summed + base).astype(BF)
    rows = value.shape[0] // len(outs)
    for i, out in enumerate(outs):
        out[...] = value[i * rows : (i + 1) * rows]


def sum_kernel(*refs):
    *terms, out = refs
    count = len(terms) // 2
    rows = out.shape[0] // count
    for i in range(count):
        total = terms[i][...].astype(F32) + terms[count + i][...].astype(F32)
        out[i * rows : (i + 1) * rows] = total.astype(BF)


def own_first_kernel(
    flags_ref, xs_ref, em_ref, eo_ref, lm_ref, lo_ref, p0, p1, p2, p3, p4, p5, q0, q1, q2, q3, q4, q5, gains_ref, w_ref,
    turned_ref, left_ref, right_ref, active_ref, w_buf, normed, sems
):
    features = w_buf.shape[1]
    size = chunk_of(features)
    count = features // size
    copies = {}
    for k in range(count):
        rows = pl.ds(k * size, size)
        for matrix in range(2):
            copies[matrix, k] = pltpu.make_async_copy(
                w_ref.at[0, matrix, rows], w_buf.at[matrix, rows], sems.at[matrix, k]
            )
            copies[matrix, k].start()
    gain = gains_ref[0:1]
    pieces, half = xs_ref.shape[:2]
    is_near = flags_ref[NEAR] == 1
    is_outer = flags_ref[OUTER] == 1
    inputs_used = jnp.logical_and(is_near, is_outer)

    def put(piece, rows):
        normed[piece * half : (piece + 1) * half] = norm_rows(rows, gain)[2]

    @pl.when(inputs_used)
    def _():
        for piece in range(pieces):
            put(piece, xs_ref[piece])

    @pl.when(jnp.logical_and(is_near, jnp.logical_not(is_outer)))
    def _():
        for i, ref in enumerate((em_ref, eo_ref, p0, p1, p2, p3, p4, p5)):
            put(i, ref[...])

    @pl.when(jnp.logical_not(is_near))
    def _():
        for i, ref in enumerate((lm_ref, lo_ref, q0, q1, q2, q3, q4, q5)):
            put(i, ref[...])

    gate, upper = gate_upper(copies, w_buf, normed, size)
    sig = jax.nn.sigmoid(gate)
    smooth = gate * sig
    left_ref[...] = upper * (sig * (1.0 + gate * (1.0 - sig)))
    right_ref[...] = smooth
    active_ref[...] = (smooth * upper).astype(BF)
    for k in range(count):
        cols = pl.ds(k * size, size)
        turned_ref[cols] = normed[:, cols].T


def own_last_kernel(flags_ref, us_ref, *refs):
    refs = list(refs)

    def take(count):
        return [refs.pop(0) for _ in range(count)]

    direct, early, late, arrived = take(8), take(2), take(2), take(6)
    turned_ref, left_ref, right_ref, active_ref, early_ref, late_ref = take(6)
    out_ref, u_buf, d_act, out_buf, sems = take(5)
    features = turned_ref.shape[0]
    size = chunk_of(features)
    count = features // size
    pieces, half = us_ref.shape[:2]
    is_near = flags_ref[NEAR] == 1
    is_outer = flags_ref[OUTER] == 1

    def fill(sources, w_ref):
        for i in range(pieces):
            u_buf[i * half : (i + 1) * half] = sources[i][...]
        total = None
        for k in range(count):
            cols = pl.ds(k * size, size)
            part = dot(u_buf[:, cols], w_ref[2, cols])
            total = part if total is None else total + part
        d_act[...] = total

    cases = (
        (True, True, direct, early_ref),
        (True, False, [us_ref.at[i] for i in range(pieces)], late_ref),
        (False, True, early + arrived, early_ref),
        (False, False, late + arrived, late_ref),
    )
    for outer, near, sources, w_ref in cases:

        @pl.when(jnp.logical_and(is_outer == outer, is_near == near))
        def _(sources=sources, w_ref=w_ref):
            fill(sources, w_ref)

    copies = []

    def send(matrix, k):
        rows = pl.ds(k * size, size)
        copy = pltpu.make_async_copy(out_buf.at[matrix, rows], out_ref.at[0, matrix, rows], sems.at[matrix, k])
        copy.start()
        copies.append(copy)

    active = active_ref[...]
    d_active = d_act[...]
    for k in range(count):
        cols = pl.ds(k * size, size)
        out_buf[2, cols] = dot_first(u_buf[:, cols], active).astype(BF)
        send(2, k)
    d_gate = (d_active * left_ref[...]).astype(BF)
    d_upper = (d_active * right_ref[...]).astype(BF)
    for k in range(count):
        cols = pl.ds(k * size, size)
        turned = turned_ref[cols]
        out_buf[0, cols] = dot(turned, d_gate).astype(BF)
        send(0, k)
        out_buf[1, cols] = dot(turned, d_upper).astype(BF)
        send(1, k)
    for copy in copies:
        copy.wait()


def call(kernel, name, operands, outs, scratch, limit, flops, moved, hbm=(), out_hbm=False, smem=(0,)):
    specs = [
        SMEM_SPEC if i in smem else HBM_SPEC if i in hbm else VMEM_SPEC for i in range(len(operands))
    ]
    out_spec = HBM_SPEC if out_hbm else VMEM_SPEC
    results = pl.pallas_call(
        kernel,
        out_shape=outs,
        in_specs=specs,
        out_specs=[out_spec] * len(outs),
        scratch_shapes=scratch,
        cost_estimate=pl.CostEstimate(flops=flops, bytes_accessed=moved, transcendentals=0),
        compiler_params=pltpu.CompilerParams(vmem_limit_bytes=limit * MIB),
        name=name,
    )(*operands)
    return list(results)


def body(inputs, cotangent, section_weights, section_gains):
    sections = lax.axis_size("pipe") // REPL
    ranks = lax.axis_size("tensor")
    pipe = lax.axis_index("pipe")
    tensor = lax.axis_index("tensor")
    position = pipe % sections
    replica = pipe // sections
    middle = sections // 2
    near = position < middle
    side = jnp.where(near, 0, 1)
    kind = jnp.where(near, position, sections - 1 - position)
    core = tensor % 2
    chip = tensor // 2
    rows, features = inputs.shape[2:]
    narrow = section_weights.shape[-1]
    group = rows // 2
    chunks = features // chunk_of(features)
    weights = pltpu.with_memory_space_constraint(section_weights[0], pltpu.HBM)
    blocks = pltpu.with_memory_space_constraint(inputs.reshape(-1, rows, features), pltpu.HBM)
    cot_blocks = pltpu.with_memory_space_constraint(cotangent.reshape(-1, rows, features), pltpu.HBM)
    gains = section_gains[0]
    core_swap = [(i, i ^ 1) for i in range(ranks)]
    chip_swap = [(i, (i + 2) % ranks) for i in range(ranks)]

    def spot(across, end, batch):
        return (((replica + across) % REPL) * 2 + end) * 2 + batch

    pairs = ((0, 0), (0, 1), (1, 0), (1, 1))
    own = [spot(across, side ^ turn, batch) for batch in (core, 1 - core) for across, turn in pairs]
    own = [own[i] for i in (0, 4, 1, 2, 3, 5, 6, 7)]
    top = [spot(across, end, batch) for batch in (core, 1 - core) for across, end in pairs]
    bottom = [spot(across, 1 - end, batch) for batch in (core, 1 - core) for across, end in pairs]
    flags = [side, near, kind == 0, chip == 0, kind] + own + top + bottom
    flags = jnp.stack([jnp.asarray(flag).astype(jnp.int32) for flag in flags])

    def swap_core(block):
        return lax.ppermute(block, "tensor", core_swap)

    def swap_chip(block):
        return lax.ppermute(block, "tensor", chip_swap)

    def place(copy, end, c, rank):
        at = c if end == 0 else sections - 1 - c
        return (copy * sections + at) * ranks + rank

    def completed(moves):
        total_devices = REPL * sections * ranks
        per_copy = sections * ranks
        target = dict(moves)
        back = {end: start for start, end in moves}
        sources = [i for i in range(total_devices) if i not in target]
        ends = {i for i in range(total_devices) if i not in back}
        rules = (
            lambda i: i,
            lambda i: back.get(i) if back.get(i, -1) // per_copy == i // per_copy else None,
            lambda i: next((j for j in sorted(ends) if j // per_copy == i // per_copy and j % ranks == i % ranks), None),
            lambda i: min(ends),
        )
        for rule in rules:
            for i in sources:
                if i not in target and rule(i) in ends:
                    target[i] = rule(i)
                    ends.remove(target[i])
        return sorted(target.items())

    def send(block, route):
        moves = []
        for copy in range(REPL):
            for end in range(2):
                for c in range(middle):
                    source = route(copy, end, c)
                    if source is None:
                        continue
                    for rank in range(ranks):
                        came = (rank + 2) % ranks if source[3] else rank
                        moves.append((place(*source[:3], came), place(copy, end, c, rank)))
        return lax.ppermute(block, ("pipe", "tensor"), completed(moves))

    def hop(block, source, target, turn, other):
        return send(block, lambda copy, end, c: (copy, end ^ turn, source, other) if c == target else None)

    def collect(same, opposite, wanted):
        def part(payload, turn, across):
            return send(
                payload,
                lambda copy, end, c: ((copy + across) % REPL, end ^ turn, c, False) if wanted(c, end) else None,
            )

        return [part(opposite, 1, 0), part(same, 0, 1), part(opposite, 1, 1)]

    def with_other_core(arrived):
        return arrived + [swap_core(block) for block in arrived]

    def shape(*extent, dtype=BF):
        return jax.ShapeDtypeStruct(extent, dtype)

    row = shape(rows, features)
    piece = shape(group, features)
    pieces = shape(4 * REPL, rows, features)
    gate_shape = shape(2 * rows, narrow, dtype=F32)
    held_shape = pltpu.VMEM((3, features, narrow), BF)
    normed_scratch = pltpu.VMEM((2 * rows, features), BF)
    layer_flops = 12 * rows * features * narrow
    layer_bytes = 6 * features * narrow
    row_bytes = 2 * rows * features

    def layer(kernel, name, operands, outs):
        return call(kernel, name, operands, outs, [normed_scratch], 8, layer_flops, layer_bytes, smem=())

    def hold(part, backward, split, operands):
        outs = [piece, piece] if split else [row]
        kernel = functools.partial(hold_kernel, part, backward)
        return call(kernel, "hold", [marks] + operands, outs, [], 4, 0, 4 * row_bytes, smem=())

    def total(terms):
        return call(sum_kernel, "total", terms, [row], [], 4, 0, 3 * row_bytes, smem=())[0]

    def kind_of(step):
        return min(step, sections - 1 - step)

    def across(held, source, target, during):
        straight = [hop(held[turn], source, target, turn, False) for turn in range(2)]
        crossed = [hop(held[turn], source, target, turn, True) for turn in range(2)]
        straight, crossed, during = lax.optimization_barrier((straight, crossed, during))
        mine = total(straight + crossed)
        return mine, swap_core(mine), during

    pm, po, gate, upper, held_early, mine, other, marks = call(
        first_kernel,
        "first_layer",
        [flags, blocks, pltpu.with_memory_space_constraint(gains, pltpu.HBM), weights],
        [row, row, gate_shape, gate_shape, held_shape, row, row, shape(8, 128, dtype=jnp.int32)],
        [
            normed_scratch,
            pltpu.VMEM(gains.shape, F32),
            pltpu.SemaphoreType.DMA((3, chunks)),
            pltpu.SemaphoreType.DMA((3,)),
        ],
        8,
        layer_flops,
        layer_bytes,
        hbm=(1, 2, 3),
    )
    saved = [(gate, upper, mine, other), None]
    loaded = call(
        load_kernel,
        "load_late",
        [flags, blocks, cot_blocks, weights],
        [held_shape, pieces, pieces, row, row],
        [pltpu.SemaphoreType.DMA((3, 1)), pltpu.SemaphoreType.DMA((4, 4 * REPL))],
        4,
        0,
        2 * layer_bytes,
        hbm=(1, 2, 3),
    )
    for step in range(sections - 1):
        part = 0 if step < middle else 1
        if step > 0:
            old = list(saved[part] or ())
            pm, po, *saved[part] = layer(
                functools.partial(forward_kernel, part, kind_of(step)),
                "forward_layer",
                [marks, mine, other, gains, held_late if part else held_early] + old,
                [row, row, gate_shape, gate_shape, row, row],
            )
        same_kind = step == middle - 1
        held = hold(part, False, not same_kind, [pm, swap_core(po), mine])
        during = ()
        if step == 0:
            during = loaded
        if step == middle:
            during = call(
                cotangent_kernel,
                "cotangent",
                [up_mine, up_other, held_late],
                [gate_shape],
                [],
                4,
                layer_flops // 3,
                layer_bytes // 3,
                smem=(),
            ) + with_other_core(early_arrived)
        if same_kind:
            block, early_mine = lax.optimization_barrier((held[0], saved[0][2]))
            mine = total([block, swap_chip(block)])
            early_arrived = collect(early_mine, early_mine, lambda c, end: c > 0 and end == 0)
            other, early_arrived = lax.optimization_barrier((swap_core(mine), early_arrived))
        else:
            mine, other, during = across(held, kind_of(step), kind_of(step + 1), during)
        if step == 0:
            held_late, input_rows, cot_rows, up_mine, up_other = during
        if step == middle:
            d_active, *early_arrived = during

    early_rows = saved[0][2:]
    gates = [saved[0][:2], saved[1][:2]]
    pm, po, late_mine, late_other = layer(
        turn_kernel,
        "turn_layer",
        [marks, d_active, mine, other, *saved[1][2:], gains, held_late],
        [row] * 4,
    )
    state_mine = [early_rows[0], late_mine]
    ups = [None, (up_mine, up_other)]
    own_rows = 4 * REPL * rows
    for step in range(sections - 1, 0, -1):
        part = 0 if step < middle else 1
        if step < sections - 1:
            old = list(ups[part] or ())
            extra = [ups[1][0]] if step == 1 else []
            pm, po, *kept = layer(
                functools.partial(backward_kernel, kind_of(step), bool(old), bool(extra)),
                "backward_layer",
                [marks, up_mine, up_other, *gates[part], held_late if part else held_early] + old + extra,
                [row] * (6 if extra else 4),
            )
            ups[part] = kept[:2]
        local = step == middle or step == 1
        operands = [pm, swap_core(po), up_mine, state_mine[part], gains]
        held = hold(part, True, not local, operands)
        if step == 1:
            prepared = call(
                own_first_kernel,
                "own_first",
                [flags, input_rows, *early_rows, late_mine, late_other, *early_arrived]
                + with_other_core(late_arrived)
                + [gains, weights],
                [
                    shape(features, own_rows),
                    shape(own_rows, narrow, dtype=F32),
                    shape(own_rows, narrow, dtype=F32),
                    shape(own_rows, narrow),
                ],
                [
                    pltpu.VMEM((2, features, narrow), BF),
                    pltpu.VMEM((own_rows, features), BF),
                    pltpu.SemaphoreType.DMA((2, chunks)),
                ],
                12,
                4 * own_rows * features * narrow,
                8 * features * narrow,
                hbm=(19,),
            )
            block, same, opposite = lax.optimization_barrier((held[0], *kept[2:]))
            crossed, prepared = lax.optimization_barrier((swap_chip(block), prepared))
            mine = total([block, crossed])
            up_arrived = collect(same, opposite, lambda c, end: c > 0)
        elif step == middle:
            block, late = lax.optimization_barrier((held[0], late_mine))
            up_mine = total([block, swap_chip(block)])
            late_arrived = collect(late, late, lambda c, end: end == 1)
            up_other, late_arrived = lax.optimization_barrier((swap_core(up_mine), late_arrived))
        else:
            up_mine, up_other, _ = across(held, kind_of(step), kind_of(step - 1), ())
    straight = [
        send(
            mine,
            lambda copy, end, c, shift=shift, source=source: (
                ((copy + shift) % REPL, source, 1, False) if c == 0 and end == 0 else None
            ),
        )
        for shift, source in pairs
    ]
    return call(
        own_last_kernel,
        "own_last",
        [flags, cot_rows, *with_other_core(straight), *ups[0], *ups[1], *with_other_core(up_arrived)]
        + [*prepared, held_early, held_late],
        [shape(1, 3, features, narrow)],
        [
            pltpu.VMEM((own_rows, features), BF),
            pltpu.VMEM((own_rows, narrow), F32),
            pltpu.VMEM((3, features, narrow), BF),
            pltpu.SemaphoreType.DMA((3, chunks)),
        ],
        16,
        8 * own_rows * features * narrow,
        8 * features * narrow,
        out_hbm=True,
    )[0]


def solution(mesh):
    return jax.shard_map(
        body,
        mesh=mesh,
        in_specs=(P(), P(), P("pipe", None, None, None, "tensor"), P("pipe", None, None)),
        out_specs=P("pipe", None, None, "tensor"),
        check_vma=False,
    )
```

```python
import functools

import jax
import jax.numpy as jnp
from jax import lax
from jax.experimental import pallas as pl
from jax.experimental.pallas import tpu as pltpu
from jax.sharding import PartitionSpec as P

REPL = 2
EPS = 1e-06
BF = jnp.bfloat16
F32 = jnp.float32
SMEM_SPEC = pl.BlockSpec(memory_space=pltpu.SMEM)
VMEM_SPEC = pl.BlockSpec(memory_space=pltpu.VMEM)
HBM_SPEC = pl.BlockSpec(memory_space=pltpu.HBM)
MIB = 1024 * 1024
NEAR, OUTER, FIRST_CHIP, KIND, OWN, TOP, BOTTOM = 1, 2, 3, 4, 5, 13, 21


def chunk_of(features):
    for size in (512, 256, 128):
        if features % size == 0:
            return size
    return features


def norm_rows(rows, gain_row):
    widened = rows.astype(F32)
    root = jnp.sqrt(jnp.mean(widened * widened, axis=-1, keepdims=True) + EPS)
    unit = widened / root
    return unit, root, (unit * gain_row).astype(BF)


def dot(left, right):
    return jnp.dot(left, right, preferred_element_type=F32)


def dot_last(left, right):
    return lax.dot_general(left, right, (((1,), (1,)), ((), ())), preferred_element_type=F32)


def dot_first(left, right):
    return lax.dot_general(left, right, (((0,), (0,)), ((), ())), preferred_element_type=F32)


def is_set(flags_ref, index, value=1):
    if len(flags_ref.shape) == 1:
        return flags_ref[index] == value
    return flags_ref[index : index + 1, 0:1] == value


def gain_at(flags_ref, gains_ref, part):
    return jnp.where(is_set(flags_ref, NEAR, 1 - part), gains_ref[0:1], gains_ref[1:2])


def own_index(flags_ref, part):
    return jnp.where(flags_ref[NEAR] == 1 - part, 0, 1)


def choose(condition, first, second):
    kept = first.dtype
    return jnp.where(condition, first.astype(F32), second.astype(F32)).astype(kept)


def weight_copies(which, w_ref, w_buf, sems, size):
    features = w_buf.shape[1]
    copies = {}
    for matrix in range(3):
        for k in range(features // size):
            rows = pl.ds(k * size, size)
            copies[matrix, k] = pltpu.make_async_copy(
                w_ref.at[which, matrix, rows], w_buf.at[matrix, rows], sems.at[matrix, k]
            )
    return copies


def fill_normed(xm_ref, xo_ref, gain, normed):
    half = xm_ref.shape[0]
    normed[:half] = norm_rows(xm_ref[...], gain)[2]
    normed[half:] = norm_rows(xo_ref[...], gain)[2]


def gate_upper(copies, w_buf, normed, size):
    gate = upper = None
    for k in range(w_buf.shape[1] // size):
        cols = pl.ds(k * size, size)
        if copies:
            copies[0, k].wait()
            copies[1, k].wait()
        block = normed[:, cols]
        gate_k = dot(block, w_buf[0, cols])
        upper_k = dot(block, w_buf[1, cols])
        gate = gate_k if gate is None else gate + gate_k
        upper = upper_k if upper is None else upper + upper_k
    return gate, upper


def forward_math(copies, xm_ref, xo_ref, gain, w_buf, pm_ref, po_ref, normed):
    size = chunk_of(w_buf.shape[1])
    half = xm_ref.shape[0]
    fill_normed(xm_ref, xo_ref, gain, normed)
    gate, upper = gate_upper(copies, w_buf, normed, size)
    active = (gate * jax.nn.sigmoid(gate) * upper).astype(BF)
    for k in range(w_buf.shape[1] // size):
        cols = pl.ds(k * size, size)
        if copies:
            copies[2, k].wait()
        part = dot_last(active, w_buf[2, cols]).astype(BF)
        pm_ref[:, cols] = part[:half]
        po_ref[:, cols] = part[half:]
    return gate, upper


def first_kernel(
    flags_ref, rows_ref, gains_ref, w_ref,
    pm_ref, po_ref, gate_ref, upper_ref, w_buf, xm_ref, xo_ref, marks_ref, normed, gains_buf, sems, row_sems
):
    size = chunk_of(w_buf.shape[1])
    moves = [
        pltpu.make_async_copy(rows_ref.at[flags_ref[OWN + i]], ref, row_sems.at[i])
        for i, ref in enumerate((xm_ref, xo_ref))
    ]
    moves.append(pltpu.make_async_copy(gains_ref, gains_buf, row_sems.at[2]))
    for move in moves:
        move.start()
    for i in range(marks_ref.shape[0]):
        marks_ref[i : i + 1] = jnp.full((1, marks_ref.shape[1]), flags_ref[i], jnp.int32)
    for move in moves:
        move.wait()
    copies = weight_copies(own_index(flags_ref, 0), w_ref, w_buf, sems, size)
    for group in ((0, 1), (2,)):
        for k in range(w_buf.shape[1] // size):
            for matrix in group:
                copies[matrix, k].start()
    gain = gain_at(flags_ref, gains_buf, 0)
    gate_ref[...], upper_ref[...] = forward_math(copies, xm_ref, xo_ref, gain, w_buf, pm_ref, po_ref, normed)


def load_kernel(flags_ref, rows_ref, cot_ref, w_ref, w_buf, xs_ref, us_ref, um_ref, uo_ref, sems, row_sems):
    copies = list(weight_copies(own_index(flags_ref, 1), w_ref, w_buf, sems, w_buf.shape[1]).values())
    pieces, rows = xs_ref.shape[:2]
    group = rows // 2
    for i in range(pieces):
        copies.append(pltpu.make_async_copy(cot_ref.at[flags_ref[OWN + i]], us_ref.at[i], row_sems.at[0, i]))
        for half, base in enumerate((TOP, BOTTOM)):
            part = pl.ds(half * group, group)
            copies.append(
                pltpu.make_async_copy(
                    rows_ref.at[flags_ref[base + i], part], xs_ref.at[i, part], row_sems.at[1 + half, i]
                )
            )
    for i, ref in enumerate((um_ref, uo_ref)):
        copies.append(pltpu.make_async_copy(cot_ref.at[flags_ref[OWN + i]], ref, row_sems.at[3, i]))
    for copy in copies:
        copy.start()
    for copy in copies:
        copy.wait()


def forward_kernel(part, live, flags_ref, xm_ref, xo_ref, gains_ref, w_buf, *refs):
    *old, pm_ref, po_ref, gate_ref, upper_ref, xms_ref, xos_ref, normed = refs
    gain = gain_at(flags_ref, gains_ref, part)
    gate, upper = forward_math(None, xm_ref, xo_ref, gain, w_buf, pm_ref, po_ref, normed)
    found = (gate, upper, xm_ref[...], xo_ref[...])
    outs = (gate_ref, upper_ref, xms_ref, xos_ref)
    if old:
        is_live = is_set(flags_ref, KIND, live)
        found = [choose(is_live, a, b[...]) for a, b in zip(found, old)]
    for out, value in zip(outs, found):
        out[...] = value


def active_gradient(um_ref, uo_ref, w_buf):
    size = chunk_of(w_buf.shape[1])
    d_active = None
    for k in range(w_buf.shape[1] // size):
        cols = pl.ds(k * size, size)
        block = jnp.concatenate([um_ref[:, cols], uo_ref[:, cols]], axis=0)
        part = dot(block, w_buf[2, cols])
        d_active = part if d_active is None else d_active + part
    return d_active


def backward_math(d_active, gate, upper, w_buf, pm_ref, po_ref):
    size = chunk_of(w_buf.shape[1])
    half = pm_ref.shape[0]
    sig = jax.nn.sigmoid(gate)
    d_gate = (d_active * upper * (sig * (1.0 + gate * (1.0 - sig)))).astype(BF)
    d_upper = (d_active * (gate * sig)).astype(BF)
    for k in range(w_buf.shape[1] // size):
        cols = pl.ds(k * size, size)
        part = (dot_last(d_gate, w_buf[0, cols]) + dot_last(d_upper, w_buf[1, cols])).astype(BF)
        pm_ref[:, cols] = part[:half]
        po_ref[:, cols] = part[half:]


def cotangent_kernel(um_ref, uo_ref, w_buf, d_ref):
    d_ref[...] = active_gradient(um_ref, uo_ref, w_buf)


def turn_kernel(
    flags_ref, d_ref, xm_ref, xo_ref, oldm_ref, oldo_ref, gains_ref, w_buf, pm_ref, po_ref, latem_ref, lateo_ref, normed
):
    fill_normed(xm_ref, xo_ref, gain_at(flags_ref, gains_ref, 1), normed)
    gate, upper = gate_upper(None, w_buf, normed, chunk_of(w_buf.shape[1]))
    backward_math(d_ref[...], gate, upper, w_buf, pm_ref, po_ref)
    is_outer = is_set(flags_ref, OUTER)
    latem_ref[...] = choose(is_outer, xm_ref[...], oldm_ref[...])
    lateo_ref[...] = choose(is_outer, xo_ref[...], oldo_ref[...])


def backward_kernel(live, has_old, has_late, flags_ref, um_ref, uo_ref, gate_ref, upper_ref, w_buf, *refs):
    refs = list(refs)
    old = [refs.pop(0) for _ in range(2)] if has_old else []
    late = refs.pop(0) if has_late else None
    pm_ref, po_ref, ums_ref, uos_ref = refs[:4]
    backward_math(active_gradient(um_ref, uo_ref, w_buf), gate_ref[...], upper_ref[...], w_buf, pm_ref, po_ref)
    found = [um_ref[...], uo_ref[...]]
    if old:
        is_live = is_set(flags_ref, KIND, live)
        found = [choose(is_live, a, b[...]) for a, b in zip(found, old)]
    ums_ref[...], uos_ref[...] = found
    if has_late:
        refs[4][...] = choose(is_set(flags_ref, OUTER), late[...], found[0])


def hold_kernel(part, backward, flags_ref, pm_ref, recv_ref, base_ref, *refs):
    summed = pm_ref[...].astype(F32) + recv_ref[...].astype(F32)
    if backward:
        state_ref, gains_ref, *outs = refs
        gain = gain_at(flags_ref, gains_ref, part)
        unit, root, _ = norm_rows(state_ref[...], gain)
        d_unit = summed * gain
        summed = (d_unit - unit * jnp.mean(d_unit * unit, axis=-1, keepdims=True)) / root
    else:
        outs = refs
    base = jnp.where(is_set(flags_ref, FIRST_CHIP), base_ref[...].astype(F32), 0.0)
    value = (summed + base).astype(BF)
    rows = value.shape[0] // len(outs)
    for i, out in enumerate(outs):
        out[...] = value[i * rows : (i + 1) * rows]


def sides_kernel(marks_ref, early_ref, late_ref, same_ref, opposite_ref):
    is_near = is_set(marks_ref, NEAR)
    same_ref[...] = choose(is_near, early_ref[...], late_ref[...])
    opposite_ref[...] = choose(is_near, late_ref[...], early_ref[...])


def stack_kernel(*refs):
    *sources, out_ref = refs
    rows = sources[0].shape[0]
    for i, source in enumerate(sources):
        out_ref[i * rows : (i + 1) * rows] = source[...]


def fill_rows(target, sources, change=None):
    start = 0
    for source in sources:
        rows = source[...]
        target[start : start + rows.shape[0]] = change(rows) if change else rows
        start += rows.shape[0]


def last_kernel(marks_ref, mine_ref, early_ref, first_ref, second_ref):
    is_near = is_set(marks_ref, NEAR)
    mine, early = mine_ref[...], early_ref[...]
    first_ref[...] = choose(is_near, mine, early)
    second_ref[...] = choose(is_near, early, mine)


def sum_kernel(*refs):
    *terms, out = refs
    count = len(terms) // 2
    rows = out.shape[0] // count
    for i in range(count):
        total = terms[i][...].astype(F32) + terms[count + i][...].astype(F32)
        out[i * rows : (i + 1) * rows] = total.astype(BF)


def own_first_kernel(
    flags_ref, xs_ref, em_ref, eo_ref, lm_ref, lo_ref, p0, p1, p2, p3, q0, q1, q2, q3, gains_ref, w_ref,
    turned_ref, left_ref, right_ref, active_ref, w_buf, normed, sems
):
    features = w_buf.shape[1]
    size = chunk_of(features)
    count = features // size
    copies = {}
    for k in range(count):
        rows = pl.ds(k * size, size)
        for matrix in range(2):
            copies[matrix, k] = pltpu.make_async_copy(
                w_ref.at[0, matrix, rows], w_buf.at[matrix, rows], sems.at[matrix, k]
            )
            copies[matrix, k].start()
    gain = gains_ref[0:1]
    pieces, half = xs_ref.shape[:2]
    is_near = flags_ref[NEAR] == 1
    is_outer = flags_ref[OUTER] == 1
    inputs_used = jnp.logical_and(is_near, is_outer)

    def put(piece, rows):
        normed[piece * half : (piece + 1) * half] = norm_rows(rows, gain)[2]

    @pl.when(inputs_used)
    def _():
        for piece in range(pieces):
            put(piece, xs_ref[piece])

    cases = (
        (False, True, (em_ref, eo_ref, p0, p1, p2, p3)),
        (False, False, (lm_ref, lo_ref, p0, p1, p2, p3)),
        (True, False, (lm_ref, lo_ref, q0, q1, q2, q3)),
    )
    for outer, near, sources in cases:

        @pl.when(jnp.logical_and(is_outer == outer, is_near == near))
        def _(sources=sources):
            fill_rows(normed, sources, lambda rows: norm_rows(rows, gain)[2])

    gate, upper = gate_upper(copies, w_buf, normed, size)
    sig = jax.nn.sigmoid(gate)
    smooth = gate * sig
    left_ref[...] = upper * (sig * (1.0 + gate * (1.0 - sig)))
    right_ref[...] = smooth
    active_ref[...] = (smooth * upper).astype(BF)
    for k in range(count):
        cols = pl.ds(k * size, size)
        turned_ref[cols] = normed[:, cols].T


def own_last_kernel(flags_ref, us_ref, *refs):
    refs = list(refs)

    def take(count):
        return [refs.pop(0) for _ in range(count)]

    direct, early, late, arrived = take(2), take(2), take(2), take(4)
    turned_ref, left_ref, right_ref, active_ref, early_ref, late_ref = take(6)
    out_ref, u_buf, d_act, out_buf, sems = take(5)
    features = turned_ref.shape[0]
    size = chunk_of(features)
    count = features // size
    pieces, half = us_ref.shape[:2]
    is_near = flags_ref[NEAR] == 1
    is_outer = flags_ref[OUTER] == 1

    def fill(sources, w_ref):
        fill_rows(u_buf, sources)
        total = None
        for k in range(count):
            cols = pl.ds(k * size, size)
            part = dot(u_buf[:, cols], w_ref[2, cols])
            total = part if total is None else total + part
        d_act[...] = total

    half = early[0].shape[0]

    def lanes(source, *places):
        return [source.at[pl.ds(i * half, half)] for i in places]

    near_sources = early + lanes(direct[0], 0, 3, 2) + lanes(direct[1], 0, 3, 2)
    cases = (
        (True, True, direct, early_ref),
        (True, False, [us_ref.at[i] for i in range(pieces)], late_ref),
        (False, True, near_sources, early_ref),
        (False, False, late + arrived, late_ref),
    )
    for outer, near, sources, w_ref in cases:

        @pl.when(jnp.logical_and(is_outer == outer, is_near == near))
        def _(sources=sources, w_ref=w_ref):
            fill(sources, w_ref)

    copies = []

    def send(matrix, k):
        rows = pl.ds(k * size, size)
        copy = pltpu.make_async_copy(out_buf.at[matrix, rows], out_ref.at[0, matrix, rows], sems.at[matrix, k])
        copy.start()
        copies.append(copy)

    active = active_ref[...]
    d_active = d_act[...]
    for k in range(count):
        cols = pl.ds(k * size, size)
        out_buf[2, cols] = dot_first(u_buf[:, cols], active).astype(BF)
        send(2, k)
    d_gate = (d_active * left_ref[...]).astype(BF)
    d_upper = (d_active * right_ref[...]).astype(BF)
    for k in range(count):
        cols = pl.ds(k * size, size)
        turned = turned_ref[cols]
        out_buf[0, cols] = dot(turned, d_gate).astype(BF)
        send(0, k)
        out_buf[1, cols] = dot(turned, d_upper).astype(BF)
        send(1, k)
    for copy in copies:
        copy.wait()


def call(kernel, name, operands, outs, scratch, limit, flops, moved, hbm=(), out_hbm=False, smem=(0,)):
    specs = [
        SMEM_SPEC if i in smem else HBM_SPEC if i in hbm else VMEM_SPEC for i in range(len(operands))
    ]
    out_spec = HBM_SPEC if out_hbm else VMEM_SPEC
    results = pl.pallas_call(
        kernel,
        out_shape=outs,
        in_specs=specs,
        out_specs=[out_spec] * len(outs),
        scratch_shapes=scratch,
        cost_estimate=pl.CostEstimate(flops=flops, bytes_accessed=moved, transcendentals=0),
        compiler_params=pltpu.CompilerParams(vmem_limit_bytes=limit * MIB),
        name=name,
    )(*operands)
    return list(results)


def body(inputs, cotangent, section_weights, section_gains):
    sections = lax.axis_size("pipe") // REPL
    ranks = lax.axis_size("tensor")
    pipe = lax.axis_index("pipe")
    tensor = lax.axis_index("tensor")
    position = pipe % sections
    replica = pipe // sections
    middle = sections // 2
    near = position < middle
    side = jnp.where(near, 0, 1)
    kind = jnp.where(near, position, sections - 1 - position)
    core = tensor % 2
    chip = tensor // 2
    rows, features = inputs.shape[2:]
    narrow = section_weights.shape[-1]
    group = rows // 2
    chunks = features // chunk_of(features)
    weights = pltpu.with_memory_space_constraint(section_weights[0], pltpu.HBM)
    blocks = pltpu.with_memory_space_constraint(inputs.reshape(-1, rows, features), pltpu.HBM)
    cot_blocks = pltpu.with_memory_space_constraint(cotangent.reshape(-1, rows, features), pltpu.HBM)
    gains = section_gains[0]
    core_swap = [(i, i ^ 1) for i in range(ranks)]
    chip_swap = [(i, (i + 2) % ranks) for i in range(ranks)]

    def spot(across, end, batch):
        return (((replica + across) % REPL) * 2 + end) * 2 + batch

    pairs = ((0, 0), (0, 1), (1, 0), (1, 1))
    pairs_of = ((1, 0), (0, 1), (1, 1))
    own = [spot(across, side ^ turn, batch) for batch in (core, 1 - core) for across, turn in pairs]
    own = [own[i] for i in (0, 4, 1, 2, 3, 5, 6, 7)]
    top = [spot(across, end, batch) for batch in (core, 1 - core) for across, end in pairs]
    bottom = [spot(across, 1 - end, batch) for batch in (core, 1 - core) for across, end in pairs]
    flags = [side, near, kind == 0, chip == 0, kind] + own + top + bottom
    flags = jnp.stack([jnp.asarray(flag).astype(jnp.int32) for flag in flags])

    def swap_core(block):
        return lax.ppermute(block, "tensor", core_swap)

    def swap_chip(block):
        return lax.ppermute(block, "tensor", chip_swap)

    def place(copy, end, c, rank):
        at = c if end == 0 else sections - 1 - c
        return (copy * sections + at) * ranks + rank

    def completed(moves):
        per_copy = sections * ranks
        target = dict(moves)
        back = {end: start for start, end in moves}
        sources = [i for i in range(REPL * per_copy) if i not in target]
        ends = {i for i in range(REPL * per_copy) if i not in back}
        rules = (
            lambda i: i ^ 1 if i in ends else None,
            lambda i: back.get(i) if back.get(i, -1) // per_copy == i // per_copy else None,
            lambda i: next((j for j in sorted(ends) if j // per_copy == i // per_copy and j % ranks == i % ranks), None),
            lambda i: min(ends),
        )
        for rule in rules:
            for i in sources:
                if i not in target and rule(i) in ends:
                    target[i] = rule(i)
                    if rule is rules[0] and i ^ 1 not in target:
                        target[i ^ 1] = i
                        ends.remove(i)
                    ends.remove(target[i])
        return sorted(target.items())

    def send(block, *routes):
        moves = []
        for copy in range(REPL):
            for end in range(2):
                for c in range(middle):
                    for route in routes:
                        source = route(copy, end, c)
                        if source is None:
                            continue
                        for rank in range(ranks):
                            came = (rank + 2) % ranks if source[3] else rank
                            moves.append((place(*source[:3], came), place(copy, end, c, rank)))
        return lax.ppermute(block, ("pipe", "tensor"), completed(moves))

    def hop(block, source, target, turn, other):
        return send(block, lambda copy, end, c: (copy, end ^ turn, source, other) if c == target else None)

    def flow_route(which, wanted):
        turn, shift = pairs_of[which]
        return lambda copy, end, c: ((copy + shift) % REPL, end ^ turn, c, False) if wanted(c, end) else None

    def flow(payload, which, wanted):
        return send(payload, flow_route(which, wanted))

    def joined(*parts):
        return call(stack_kernel, "stack", list(parts), [shape(len(parts) * rows, features)], [], 4, 0, 0, smem=())[0]

    def with_other_core(arrived):
        return arrived + [swap_core(block) for block in arrived]

    def shape(*extent, dtype=BF):
        return jax.ShapeDtypeStruct(extent, dtype)

    row = shape(rows, features)
    pieces = shape(4 * REPL, rows, features)
    gate_shape = shape(2 * rows, narrow, dtype=F32)
    held_shape = pltpu.VMEM((3, features, narrow), BF)
    normed_scratch = pltpu.VMEM((2 * rows, features), BF)
    layer_flops = 12 * rows * features * narrow
    layer_bytes = 6 * features * narrow
    row_bytes = 2 * rows * features

    def layer(kernel, name, operands, outs):
        return call(kernel, name, operands, outs, [normed_scratch], 8, layer_flops, layer_bytes, smem=())

    def hold(part, backward, operands, split):
        kernel = functools.partial(hold_kernel, part, backward)
        outs = [shape(group, features)] * 2 if split else [row]
        found = call(kernel, "hold", [marks] + operands, outs, [], 4, 0, 4 * row_bytes, smem=())
        return found if split else found[0]

    def total(terms):
        return call(sum_kernel, "total", terms, [row], [], 4, 0, 3 * row_bytes, smem=())[0]

    def kind_of(step):
        return min(step, sections - 1 - step)

    def across(held, source, target, during, later=()):
        straight = [hop(held[turn], source, target, turn, False) for turn in range(2)]
        crossed = [hop(held[turn], source, target, turn, True) for turn in range(2)]
        straight, crossed, during = lax.optimization_barrier((straight, crossed, during))
        mine = total(straight + crossed)
        other, later = lax.optimization_barrier((swap_core(mine), later))
        return mine, other, during, later

    def far(c, end):
        return end == 1

    def middle_near(c, end):
        return c > 0 and end == 0

    def middle_class(c, end):
        return c > 0

    pm, po, gate, upper, held_early, mine, other, marks = call(
        first_kernel,
        "first_layer",
        [flags, blocks, pltpu.with_memory_space_constraint(gains, pltpu.HBM), weights],
        [row, row, gate_shape, gate_shape, held_shape, row, row, shape(8, 128, dtype=jnp.int32)],
        [
            normed_scratch,
            pltpu.VMEM(gains.shape, F32),
            pltpu.SemaphoreType.DMA((3, chunks)),
            pltpu.SemaphoreType.DMA((3,)),
        ],
        8,
        layer_flops,
        layer_bytes,
        hbm=(1, 2, 3),
    )
    saved = [(gate, upper, mine, other), None]
    loaded = call(
        load_kernel,
        "load_late",
        [flags, blocks, cot_blocks, weights],
        [held_shape, pieces, pieces, row, row],
        [pltpu.SemaphoreType.DMA((3, 1)), pltpu.SemaphoreType.DMA((4, 4 * REPL))],
        4,
        0,
        2 * layer_bytes,
        hbm=(1, 2, 3),
    )
    for step in range(sections - 1):
        part = 0 if step < middle else 1
        if step > 0:
            old = list(saved[part] or ())
            pm, po, *saved[part] = layer(
                functools.partial(forward_kernel, part, kind_of(step)),
                "forward_layer",
                [marks, mine, other, gains, held_late if part else held_early] + old,
                [row, row, gate_shape, gate_shape, row, row],
            )
        held = hold(part, False, [pm, swap_core(po), mine], step != middle - 1)
        during = ()
        if step == 0:
            during = loaded
        if step == middle:
            during = call(
                cotangent_kernel,
                "cotangent",
                [up_mine, up_other, held_late],
                [gate_shape],
                [],
                4,
                layer_flops // 3,
                layer_bytes // 3,
                smem=(),
            )
        if step == middle - 1:
            mine = total([held, swap_chip(held)])
            other = swap_core(mine)
        else:
            mine, other, during, _ = across(held, kind_of(step), kind_of(step + 1), during)
        if step == 0:
            held_late, input_rows, cot_rows, up_mine, up_other = during
        if step == middle:
            (d_active,) = during

    early_rows = saved[0][2:]
    sides = call(sides_kernel, "sides", [marks, saved[0][2], saved[1][2]], [row, row], [], 4, 0, 0, smem=())
    mine, (same, opposite) = lax.optimization_barrier((mine, sides))
    state_first = flow(opposite, 0, middle_class)
    state_second = flow(joined(same, state_first), 1, middle_class)
    gates = [saved[0][:2], saved[1][:2]]
    pm, po, late_mine, late_other = layer(
        turn_kernel,
        "turn_layer",
        [marks, d_active, mine, other, *saved[1][2:], gains, held_late],
        [row] * 4,
    )
    state_mine = [early_rows[0], late_mine]
    ups = [None, (up_mine, up_other)]
    own_rows = 4 * REPL * rows
    for step in range(sections - 1, 0, -1):
        part = 0 if step < middle else 1
        if step < sections - 1:
            old = list(ups[part] or ())
            extra = [late_mine] if step == middle else []
            pm, po, *kept = layer(
                functools.partial(backward_kernel, kind_of(step), bool(old), bool(extra)),
                "backward_layer",
                [marks, up_mine, up_other, *gates[part], held_late if part else held_early] + old + extra,
                [row] * (5 if extra else 4),
            )
            ups[part] = kept[:2]
        held = hold(part, True, [pm, swap_core(po), up_mine, state_mine[part], gains], step not in (middle, 1))
        if step == 1:
            mine = total([held, swap_chip(held)])
        elif step == middle:
            held, mixed = lax.optimization_barrier((held, kept[2]))
            up_mine = total([held, swap_chip(held)])
            mixed_first = flow(mixed, 0, far)
            up_other, mixed_first, middle_arrived = lax.optimization_barrier(
                (swap_core(up_mine), mixed_first, middle_arrived)
            )
            mixed_second = flow(joined(mixed, mixed_first), 1, far)
        else:
            later = ()
            if step == sections - 1:
                later = [state_first, state_second]
            up_mine, up_other, _, later = across(held, kind_of(step), kind_of(step - 1), (), later)
            if step == sections - 1:
                middle_arrived = with_other_core(later)
    _, mixed_second = lax.optimization_barrier((mine, mixed_second))
    def last_route(shift, source):
        return lambda copy, end, c: ((copy + shift) % REPL, source, 1, False) if c == 0 and end == 0 else None

    payloads = call(last_kernel, "last", [marks, mine, ups[0][0]], [row] * 2, [], 4, 0, 0, smem=())
    straight = [
        send(payloads[0], last_route(0, 0), flow_route(0, middle_near)),
        send(payloads[1], last_route(0, 1)),
        send(payloads[0], last_route(1, 0), flow_route(2, middle_near)),
        send(payloads[1], last_route(1, 1), flow_route(1, middle_near)),
    ]
    mixed_arrived = with_other_core([mixed_first, mixed_second])
    prepared = call(
        own_first_kernel,
        "own_first",
        [flags, input_rows, *early_rows, late_mine, late_other, *middle_arrived, *mixed_arrived, gains, weights],
        [
            shape(features, own_rows),
            shape(own_rows, narrow, dtype=F32),
            shape(own_rows, narrow, dtype=F32),
            shape(own_rows, narrow),
        ],
        [
            pltpu.VMEM((2, features, narrow), BF),
            pltpu.VMEM((own_rows, features), BF),
            pltpu.SemaphoreType.DMA((2, chunks)),
        ],
        12,
        4 * own_rows * features * narrow,
        8 * features * narrow,
        hbm=(15,),
    )
    straight, prepared = lax.optimization_barrier((straight, prepared))
    direct = with_other_core([joined(*straight)])
    return call(
        own_last_kernel,
        "own_last",
        [flags, cot_rows, *direct, *ups[0], *ups[1], *mixed_arrived]
        + [*prepared, held_early, held_late],
        [shape(1, 3, features, narrow)],
        [
            pltpu.VMEM((own_rows, features), BF),
            pltpu.VMEM((own_rows, narrow), F32),
            pltpu.VMEM((3, features, narrow), BF),
            pltpu.SemaphoreType.DMA((3, chunks)),
        ],
        16,
        8 * own_rows * features * narrow,
        8 * features * narrow,
        out_hbm=True,
    )[0]


def solution(mesh):
    return jax.shard_map(
        body,
        mesh=mesh,
        in_specs=(P(), P(), P("pipe", None, None, None, "tensor"), P("pipe", None, None)),
        out_specs=P("pipe", None, None, "tensor"),
        check_vma=False,
    )
```

```python
import functools

import jax
import jax.numpy as jnp
from jax import lax
from jax.experimental import pallas as pl
from jax.experimental.pallas import tpu as pltpu
from jax.sharding import PartitionSpec as P

REPL = 2
EPS = 1e-06
BF = jnp.bfloat16
F32 = jnp.float32
SMEM_SPEC = pl.BlockSpec(memory_space=pltpu.SMEM)
VMEM_SPEC = pl.BlockSpec(memory_space=pltpu.VMEM)
HBM_SPEC = pl.BlockSpec(memory_space=pltpu.HBM)
MIB = 1024 * 1024
NEAR, OUTER, FIRST_CHIP, KIND, OWN, TOP, BOTTOM = 1, 2, 3, 4, 5, 13, 21


def chunk_of(features):
    for size in (512, 256, 128):
        if features % size == 0:
            return size
    return features


def norm_rows(rows, gain_row):
    widened = rows.astype(F32)
    root = jnp.sqrt(jnp.mean(widened * widened, axis=-1, keepdims=True) + EPS)
    unit = widened / root
    return unit, root, (unit * gain_row).astype(BF)


def dot(left, right):
    return jnp.dot(left, right, preferred_element_type=F32)


def dot_last(left, right):
    return lax.dot_general(left, right, (((1,), (1,)), ((), ())), preferred_element_type=F32)


def dot_first(left, right):
    return lax.dot_general(left, right, (((0,), (0,)), ((), ())), preferred_element_type=F32)


def is_set(flags_ref, index, value=1):
    if len(flags_ref.shape) == 1:
        return flags_ref[index] == value
    return flags_ref[index : index + 1, 0:1] == value


def gain_at(flags_ref, gains_ref, part):
    return jnp.where(is_set(flags_ref, NEAR, 1 - part), gains_ref[0:1], gains_ref[1:2])


def own_index(flags_ref, part):
    return jnp.where(flags_ref[NEAR] == 1 - part, 0, 1)


def choose(condition, first, second):
    kept = first.dtype
    return jnp.where(condition, first.astype(F32), second.astype(F32)).astype(kept)


def weight_copies(which, w_ref, w_buf, sems, size):
    features = w_buf.shape[1]
    copies = {}
    for matrix in range(3):
        for k in range(features // size):
            rows = pl.ds(k * size, size)
            copies[matrix, k] = pltpu.make_async_copy(
                w_ref.at[which, matrix, rows], w_buf.at[matrix, rows], sems.at[matrix, k]
            )
    return copies


def fill_normed(xm_ref, xo_ref, gain, normed):
    half = xm_ref.shape[0]
    normed[:half] = norm_rows(xm_ref[...], gain)[2]
    normed[half:] = norm_rows(xo_ref[...], gain)[2]


def gate_upper(copies, w_buf, normed, size):
    gate = upper = None
    for k in range(w_buf.shape[1] // size):
        cols = pl.ds(k * size, size)
        if copies:
            copies[0, k].wait()
            copies[1, k].wait()
        block = normed[:, cols]
        gate_k = dot(block, w_buf[0, cols])
        upper_k = dot(block, w_buf[1, cols])
        gate = gate_k if gate is None else gate + gate_k
        upper = upper_k if upper is None else upper + upper_k
    return gate, upper


def forward_math(copies, xm_ref, xo_ref, gain, w_buf, pm_ref, po_ref, normed):
    size = chunk_of(w_buf.shape[1])
    half = xm_ref.shape[0]
    fill_normed(xm_ref, xo_ref, gain, normed)
    gate, upper = gate_upper(copies, w_buf, normed, size)
    active = (gate * jax.nn.sigmoid(gate) * upper).astype(BF)
    for k in range(w_buf.shape[1] // size):
        cols = pl.ds(k * size, size)
        if copies:
            copies[2, k].wait()
        part = dot_last(active, w_buf[2, cols]).astype(BF)
        pm_ref[:, cols] = part[:half]
        po_ref[:, cols] = part[half:]
    return gate, upper


def first_kernel(
    flags_ref, rows_ref, gains_ref, w_ref,
    pm_ref, po_ref, gate_ref, upper_ref, w_buf, xm_ref, xo_ref, marks_ref, normed, gains_buf, sems, row_sems
):
    size = chunk_of(w_buf.shape[1])
    moves = [
        pltpu.make_async_copy(rows_ref.at[flags_ref[OWN + i]], ref, row_sems.at[i])
        for i, ref in enumerate((xm_ref, xo_ref))
    ]
    moves.append(pltpu.make_async_copy(gains_ref, gains_buf, row_sems.at[2]))
    for move in moves:
        move.start()
    for i in range(marks_ref.shape[0]):
        marks_ref[i : i + 1] = jnp.full((1, marks_ref.shape[1]), flags_ref[i], jnp.int32)
    for move in moves:
        move.wait()
    copies = weight_copies(own_index(flags_ref, 0), w_ref, w_buf, sems, size)
    for group in ((0, 1), (2,)):
        for k in range(w_buf.shape[1] // size):
            for matrix in group:
                copies[matrix, k].start()
    gain = gain_at(flags_ref, gains_buf, 0)
    gate_ref[...], upper_ref[...] = forward_math(copies, xm_ref, xo_ref, gain, w_buf, pm_ref, po_ref, normed)


def load_kernel(flags_ref, cot_ref, w_ref, w_buf, um_ref, uo_ref, sems, row_sems):
    copies = [
        pltpu.make_async_copy(cot_ref.at[flags_ref[OWN + i]], ref, row_sems.at[i])
        for i, ref in enumerate((um_ref, uo_ref))
    ]
    copies += list(weight_copies(own_index(flags_ref, 1), w_ref, w_buf, sems, w_buf.shape[1]).values())
    for copy in copies:
        copy.start()
    for copy in copies:
        copy.wait()


def rows_kernel(flags_ref, rows_ref, cot_ref, xs_ref, us_ref, row_sems):
    copies = []
    pieces, rows = xs_ref.shape[:2]
    group = rows // 2
    for i in range(pieces):
        copies.append(pltpu.make_async_copy(cot_ref.at[flags_ref[OWN + i]], us_ref.at[i], row_sems.at[0, i]))
        for half, base in enumerate((TOP, BOTTOM)):
            part = pl.ds(half * group, group)
            copies.append(
                pltpu.make_async_copy(
                    rows_ref.at[flags_ref[base + i], part], xs_ref.at[i, part], row_sems.at[1 + half, i]
                )
            )
    for copy in copies:
        copy.start()
    for copy in copies:
        copy.wait()


def forward_kernel(part, live, flags_ref, xm_ref, xo_ref, gains_ref, w_buf, *refs):
    *old, pm_ref, po_ref, gate_ref, upper_ref, xms_ref, xos_ref, normed = refs
    gain = gain_at(flags_ref, gains_ref, part)
    gate, upper = forward_math(None, xm_ref, xo_ref, gain, w_buf, pm_ref, po_ref, normed)
    found = (gate, upper, xm_ref[...], xo_ref[...])
    outs = (gate_ref, upper_ref, xms_ref, xos_ref)
    if old:
        is_live = is_set(flags_ref, KIND, live)
        found = [choose(is_live, a, b[...]) for a, b in zip(found, old)]
    for out, value in zip(outs, found):
        out[...] = value


def active_gradient(um_ref, uo_ref, w_buf):
    size = chunk_of(w_buf.shape[1])
    d_active = None
    for k in range(w_buf.shape[1] // size):
        cols = pl.ds(k * size, size)
        block = jnp.concatenate([um_ref[:, cols], uo_ref[:, cols]], axis=0)
        part = dot(block, w_buf[2, cols])
        d_active = part if d_active is None else d_active + part
    return d_active


def backward_math(d_active, gate, upper, w_buf, pm_ref, po_ref):
    size = chunk_of(w_buf.shape[1])
    half = pm_ref.shape[0]
    sig = jax.nn.sigmoid(gate)
    d_gate = (d_active * upper * (sig * (1.0 + gate * (1.0 - sig)))).astype(BF)
    d_upper = (d_active * (gate * sig)).astype(BF)
    for k in range(w_buf.shape[1] // size):
        cols = pl.ds(k * size, size)
        part = (dot_last(d_gate, w_buf[0, cols]) + dot_last(d_upper, w_buf[1, cols])).astype(BF)
        pm_ref[:, cols] = part[:half]
        po_ref[:, cols] = part[half:]


def cotangent_kernel(um_ref, uo_ref, w_buf, d_ref):
    d_ref[...] = active_gradient(um_ref, uo_ref, w_buf)


def turn_kernel(
    flags_ref, d_ref, xm_ref, xo_ref, oldm_ref, oldo_ref, gains_ref, w_buf, pm_ref, po_ref, latem_ref, lateo_ref, normed
):
    fill_normed(xm_ref, xo_ref, gain_at(flags_ref, gains_ref, 1), normed)
    gate, upper = gate_upper(None, w_buf, normed, chunk_of(w_buf.shape[1]))
    backward_math(d_ref[...], gate, upper, w_buf, pm_ref, po_ref)
    is_outer = is_set(flags_ref, OUTER)
    latem_ref[...] = choose(is_outer, xm_ref[...], oldm_ref[...])
    lateo_ref[...] = choose(is_outer, xo_ref[...], oldo_ref[...])


def backward_kernel(live, has_old, has_late, flags_ref, um_ref, uo_ref, gate_ref, upper_ref, w_buf, *refs):
    refs = list(refs)
    old = [refs.pop(0) for _ in range(2)] if has_old else []
    late = refs.pop(0) if has_late else None
    pm_ref, po_ref, ums_ref, uos_ref = refs[:4]
    backward_math(active_gradient(um_ref, uo_ref, w_buf), gate_ref[...], upper_ref[...], w_buf, pm_ref, po_ref)
    found = [um_ref[...], uo_ref[...]]
    if old:
        is_live = is_set(flags_ref, KIND, live)
        found = [choose(is_live, a, b[...]) for a, b in zip(found, old)]
    ums_ref[...], uos_ref[...] = found
    if has_late:
        refs[4][...] = choose(is_set(flags_ref, OUTER), late[...], found[0])


def hold_kernel(part, backward, flags_ref, pm_ref, recv_ref, base_ref, *refs):
    summed = pm_ref[...].astype(F32) + recv_ref[...].astype(F32)
    if backward:
        state_ref, gains_ref, *outs = refs
        gain = gain_at(flags_ref, gains_ref, part)
        unit, root, _ = norm_rows(state_ref[...], gain)
        d_unit = summed * gain
        summed = (d_unit - unit * jnp.mean(d_unit * unit, axis=-1, keepdims=True)) / root
    else:
        outs = refs
    base = jnp.where(is_set(flags_ref, FIRST_CHIP), base_ref[...].astype(F32), 0.0)
    value = (summed + base).astype(BF)
    rows = value.shape[0] // len(outs)
    for i, out in enumerate(outs):
        out[...] = value[i * rows : (i + 1) * rows]


def sides_kernel(marks_ref, early_ref, late_ref, same_ref, opposite_ref):
    is_near = is_set(marks_ref, NEAR)
    same_ref[...] = choose(is_near, early_ref[...], late_ref[...])
    opposite_ref[...] = choose(is_near, late_ref[...], early_ref[...])


def stack_kernel(*refs):
    *sources, out_ref = refs
    rows = sources[0].shape[0]
    for i, source in enumerate(sources):
        out_ref[i * rows : (i + 1) * rows] = source[...]


def fill_rows(target, sources, change=None):
    start = 0
    for source in sources:
        rows = source[...]
        target[start : start + rows.shape[0]] = change(rows) if change else rows
        start += rows.shape[0]


def last_kernel(marks_ref, mine_ref, early_ref, first_ref, second_ref):
    is_near = is_set(marks_ref, NEAR)
    mine, early = mine_ref[...], early_ref[...]
    first_ref[...] = choose(is_near, mine, early)
    second_ref[...] = choose(is_near, early, mine)


def sum_kernel(*refs):
    *terms, out = refs
    count = len(terms) // 2
    rows = out.shape[0] // count
    for i in range(count):
        total = terms[i][...].astype(F32) + terms[count + i][...].astype(F32)
        out[i * rows : (i + 1) * rows] = total.astype(BF)


def own_first_kernel(
    flags_ref, xs_ref, em_ref, eo_ref, lm_ref, lo_ref, p0, p1, p2, p3, q0, q1, q2, q3, gains_ref, w_ref,
    turned_ref, left_ref, right_ref, active_ref, w_buf, normed, sems
):
    features = w_buf.shape[1]
    size = chunk_of(features)
    count = features // size
    copies = {}
    for k in range(count):
        rows = pl.ds(k * size, size)
        for matrix in range(2):
            copies[matrix, k] = pltpu.make_async_copy(
                w_ref.at[0, matrix, rows], w_buf.at[matrix, rows], sems.at[matrix, k]
            )
            copies[matrix, k].start()
    gain = gains_ref[0:1]
    pieces, half = xs_ref.shape[:2]
    is_near = flags_ref[NEAR] == 1
    is_outer = flags_ref[OUTER] == 1
    inputs_used = jnp.logical_and(is_near, is_outer)

    def put(piece, rows):
        normed[piece * half : (piece + 1) * half] = norm_rows(rows, gain)[2]

    @pl.when(inputs_used)
    def _():
        for piece in range(pieces):
            put(piece, xs_ref[piece])

    cases = (
        (False, True, (em_ref, eo_ref, p0, p1, p2, p3)),
        (False, False, (lm_ref, lo_ref, p0, p1, p2, p3)),
        (True, False, (lm_ref, lo_ref, q0, q1, q2, q3)),
    )
    for outer, near, sources in cases:

        @pl.when(jnp.logical_and(is_outer == outer, is_near == near))
        def _(sources=sources):
            fill_rows(normed, sources, lambda rows: norm_rows(rows, gain)[2])

    gate, upper = gate_upper(copies, w_buf, normed, size)
    sig = jax.nn.sigmoid(gate)
    smooth = gate * sig
    left_ref[...] = upper * (sig * (1.0 + gate * (1.0 - sig)))
    right_ref[...] = smooth
    active_ref[...] = (smooth * upper).astype(BF)
    for k in range(count):
        cols = pl.ds(k * size, size)
        turned_ref[cols] = normed[:, cols].T


def own_last_kernel(flags_ref, us_ref, *refs):
    refs = list(refs)

    def take(count):
        return [refs.pop(0) for _ in range(count)]

    direct, early, late, arrived = take(2), take(2), take(2), take(4)
    turned_ref, left_ref, right_ref, active_ref, early_ref, late_ref = take(6)
    out_ref, u_buf, d_act, out_buf, sems = take(5)
    features = turned_ref.shape[0]
    size = chunk_of(features)
    count = features // size
    pieces, half = us_ref.shape[:2]
    is_near = flags_ref[NEAR] == 1
    is_outer = flags_ref[OUTER] == 1

    def fill(sources, w_ref):
        fill_rows(u_buf, sources)
        total = None
        for k in range(count):
            cols = pl.ds(k * size, size)
            part = dot(u_buf[:, cols], w_ref[2, cols])
            total = part if total is None else total + part
        d_act[...] = total

    half = early[0].shape[0]

    def lanes(source, *places):
        return [source.at[pl.ds(i * half, half)] for i in places]

    near_sources = early + lanes(direct[0], 0, 3, 2) + lanes(direct[1], 0, 3, 2)
    cases = (
        (True, True, direct, early_ref),
        (True, False, [us_ref.at[i] for i in range(pieces)], late_ref),
        (False, True, near_sources, early_ref),
        (False, False, late + arrived, late_ref),
    )
    for outer, near, sources, w_ref in cases:

        @pl.when(jnp.logical_and(is_outer == outer, is_near == near))
        def _(sources=sources, w_ref=w_ref):
            fill(sources, w_ref)

    copies = []

    def send(matrix, k):
        rows = pl.ds(k * size, size)
        copy = pltpu.make_async_copy(out_buf.at[matrix, rows], out_ref.at[0, matrix, rows], sems.at[matrix, k])
        copy.start()
        copies.append(copy)

    active = active_ref[...]
    d_active = d_act[...]
    for k in range(count):
        cols = pl.ds(k * size, size)
        out_buf[2, cols] = dot_first(u_buf[:, cols], active).astype(BF)
        send(2, k)
    d_gate = (d_active * left_ref[...]).astype(BF)
    d_upper = (d_active * right_ref[...]).astype(BF)
    for k in range(count):
        cols = pl.ds(k * size, size)
        turned = turned_ref[cols]
        out_buf[0, cols] = dot(turned, d_gate).astype(BF)
        send(0, k)
        out_buf[1, cols] = dot(turned, d_upper).astype(BF)
        send(1, k)
    for copy in copies:
        copy.wait()


def call(kernel, name, operands, outs, scratch, limit, flops, moved, hbm=(), out_hbm=False, smem=(0,)):
    specs = [
        SMEM_SPEC if i in smem else HBM_SPEC if i in hbm else VMEM_SPEC for i in range(len(operands))
    ]
    out_spec = HBM_SPEC if out_hbm else VMEM_SPEC
    results = pl.pallas_call(
        kernel,
        out_shape=outs,
        in_specs=specs,
        out_specs=[out_spec] * len(outs),
        scratch_shapes=scratch,
        cost_estimate=pl.CostEstimate(flops=flops, bytes_accessed=moved, transcendentals=0),
        compiler_params=pltpu.CompilerParams(vmem_limit_bytes=limit * MIB),
        name=name,
    )(*operands)
    return list(results)


def body(inputs, cotangent, section_weights, section_gains):
    sections = lax.axis_size("pipe") // REPL
    ranks = lax.axis_size("tensor")
    pipe = lax.axis_index("pipe")
    tensor = lax.axis_index("tensor")
    position = pipe % sections
    replica = pipe // sections
    middle = sections // 2
    near = position < middle
    side = jnp.where(near, 0, 1)
    kind = jnp.where(near, position, sections - 1 - position)
    core = tensor % 2
    chip = tensor // 2
    rows, features = inputs.shape[2:]
    narrow = section_weights.shape[-1]
    group = rows // 2
    chunks = features // chunk_of(features)
    weights = pltpu.with_memory_space_constraint(section_weights[0], pltpu.HBM)
    blocks = pltpu.with_memory_space_constraint(inputs.reshape(-1, rows, features), pltpu.HBM)
    cot_blocks = pltpu.with_memory_space_constraint(cotangent.reshape(-1, rows, features), pltpu.HBM)
    gains = section_gains[0]
    core_swap = [(i, i ^ 1) for i in range(ranks)]
    chip_swap = [(i, (i + 2) % ranks) for i in range(ranks)]

    def spot(across, end, batch):
        return (((replica + across) % REPL) * 2 + end) * 2 + batch

    pairs = ((0, 0), (0, 1), (1, 0), (1, 1))
    pairs_of = ((1, 0), (0, 1), (1, 1))
    own = [spot(across, side ^ turn, batch) for batch in (core, 1 - core) for across, turn in pairs]
    own = [own[i] for i in (0, 4, 1, 2, 3, 5, 6, 7)]
    top = [spot(across, end, batch) for batch in (core, 1 - core) for across, end in pairs]
    bottom = [spot(across, 1 - end, batch) for batch in (core, 1 - core) for across, end in pairs]
    flags = [side, near, kind == 0, chip == 0, kind] + own + top + bottom
    flags = jnp.stack([jnp.asarray(flag).astype(jnp.int32) for flag in flags])

    def swap_core(block):
        return lax.ppermute(block, "tensor", core_swap)

    def swap_chip(block):
        return lax.ppermute(block, "tensor", chip_swap)

    def place(copy, end, c, rank):
        at = c if end == 0 else sections - 1 - c
        return (copy * sections + at) * ranks + rank

    def completed(moves):
        per_copy = sections * ranks
        target = dict(moves)
        back = {end: start for start, end in moves}
        sources = [i for i in range(REPL * per_copy) if i not in target]
        ends = {i for i in range(REPL * per_copy) if i not in back}
        rules = (
            lambda i: i ^ 1 if i in ends else None,
            lambda i: back.get(i) if back.get(i, -1) // per_copy == i // per_copy else None,
            lambda i: next((j for j in sorted(ends) if j // per_copy == i // per_copy and j % ranks == i % ranks), None),
            lambda i: min(ends),
        )
        for rule in rules:
            for i in sources:
                if i not in target and rule(i) in ends:
                    target[i] = rule(i)
                    if rule is rules[0] and i ^ 1 not in target:
                        target[i ^ 1] = i
                        ends.remove(i)
                    ends.remove(target[i])
        return sorted(target.items())

    def send(block, *routes, whole=True):
        moves = []
        for copy in range(REPL):
            for end in range(2):
                for c in range(middle):
                    for route in routes:
                        source = route(copy, end, c)
                        if source is None:
                            continue
                        for rank in range(ranks):
                            came = (rank + 2) % ranks if source[3] else rank
                            moves.append((place(*source[:3], came), place(copy, end, c, rank)))
        return lax.ppermute(block, ("pipe", "tensor"), completed(moves) if whole else moves)

    def hop(block, source, target, turn, other):
        return send(block, lambda copy, end, c: (copy, end ^ turn, source, other) if c == target else None)

    def flow_route(which, wanted):
        turn, shift = pairs_of[which]
        return lambda copy, end, c: ((copy + shift) % REPL, end ^ turn, c, False) if wanted(c, end) else None

    def flow(payload, which, wanted):
        return send(payload, flow_route(which, wanted))

    def joined(*parts):
        return call(stack_kernel, "stack", list(parts), [shape(len(parts) * rows, features)], [], 4, 0, 0, smem=())[0]

    def with_other_core(arrived):
        return arrived + [swap_core(block) for block in arrived]

    def shape(*extent, dtype=BF):
        return jax.ShapeDtypeStruct(extent, dtype)

    row = shape(rows, features)
    pieces = shape(4 * REPL, rows, features)
    gate_shape = shape(2 * rows, narrow, dtype=F32)
    held_shape = pltpu.VMEM((3, features, narrow), BF)
    normed_scratch = pltpu.VMEM((2 * rows, features), BF)
    layer_flops = 12 * rows * features * narrow
    layer_bytes = 6 * features * narrow
    row_bytes = 2 * rows * features

    def layer(kernel, name, operands, outs):
        return call(kernel, name, operands, outs, [normed_scratch], 8, layer_flops, layer_bytes, smem=())

    def hold(part, backward, operands, split):
        kernel = functools.partial(hold_kernel, part, backward)
        outs = [shape(group, features)] * 2 if split else [row]
        found = call(kernel, "hold", [marks] + operands, outs, [], 4, 0, 4 * row_bytes, smem=())
        return found if split else found[0]

    def total(terms):
        return call(sum_kernel, "total", terms, [row], [], 4, 0, 3 * row_bytes, smem=())[0]

    def kind_of(step):
        return min(step, sections - 1 - step)

    def across(held, source, target, during, later=()):
        straight = [hop(held[turn], source, target, turn, False) for turn in range(2)]
        crossed = [hop(held[turn], source, target, turn, True) for turn in range(2)]
        straight, crossed, during = lax.optimization_barrier((straight, crossed, during))
        mine = total(straight + crossed)
        other, later = lax.optimization_barrier((swap_core(mine), later))
        return mine, other, during, later

    def far(c, end):
        return end == 1

    def middle_near(c, end):
        return c > 0 and end == 0

    def middle_class(c, end):
        return c > 0

    pm, po, gate, upper, held_early, mine, other, marks = call(
        first_kernel,
        "first_layer",
        [flags, blocks, pltpu.with_memory_space_constraint(gains, pltpu.HBM), weights],
        [row, row, gate_shape, gate_shape, held_shape, row, row, shape(8, 128, dtype=jnp.int32)],
        [
            normed_scratch,
            pltpu.VMEM(gains.shape, F32),
            pltpu.SemaphoreType.DMA((3, chunks)),
            pltpu.SemaphoreType.DMA((3,)),
        ],
        8,
        layer_flops,
        layer_bytes,
        hbm=(1, 2, 3),
    )
    saved = [(gate, upper, mine, other), None]
    loaded = call(
        load_kernel,
        "load_late",
        [flags, cot_blocks, weights],
        [held_shape, row, row],
        [pltpu.SemaphoreType.DMA((3, 1)), pltpu.SemaphoreType.DMA((2,))],
        4,
        0,
        2 * layer_bytes,
        hbm=(1, 2),
    )
    loaded_rows = call(
        rows_kernel,
        "load_rows",
        [flags, blocks, cot_blocks],
        [pieces, pieces],
        [pltpu.SemaphoreType.DMA((3, 4 * REPL))],
        4,
        0,
        layer_bytes,
        hbm=(1, 2),
    )
    for step in range(sections - 1):
        part = 0 if step < middle else 1
        if step > 0:
            old = list(saved[part] or ())
            pm, po, *saved[part] = layer(
                functools.partial(forward_kernel, part, kind_of(step)),
                "forward_layer",
                [marks, mine, other, gains, held_late if part else held_early] + old,
                [row, row, gate_shape, gate_shape, row, row],
            )
        held = hold(part, False, [pm, swap_core(po), mine], step != middle - 1)
        during = ()
        if step == 0:
            during = loaded
        if step == middle:
            during = call(
                cotangent_kernel,
                "cotangent",
                [up_mine, up_other, held_late],
                [gate_shape],
                [],
                4,
                layer_flops // 3,
                layer_bytes // 3,
                smem=(),
            ) + loaded_rows
        if step == middle - 1:
            mine = total([held, swap_chip(held)])
            other = swap_core(mine)
        else:
            mine, other, during, _ = across(held, kind_of(step), kind_of(step + 1), during)
        if step == 0:
            held_late, up_mine, up_other = during
        if step == middle:
            d_active, input_rows, cot_rows = during

    early_rows = saved[0][2:]
    sides = call(sides_kernel, "sides", [marks, saved[0][2], saved[1][2]], [row, row], [], 4, 0, 0, smem=())
    mine, (same, opposite) = lax.optimization_barrier((mine, sides))
    state_first = flow(opposite, 0, middle_class)
    gates = [saved[0][:2], saved[1][:2]]
    pm, po, late_mine, late_other = layer(
        turn_kernel,
        "turn_layer",
        [marks, d_active, mine, other, *saved[1][2:], gains, held_late],
        [row] * 4,
    )
    state_mine = [early_rows[0], late_mine]
    ups = [None, (up_mine, up_other)]
    own_rows = 4 * REPL * rows
    for step in range(sections - 1, 0, -1):
        part = 0 if step < middle else 1
        if step < sections - 1:
            old = list(ups[part] or ())
            extra = [late_mine] if step == middle else []
            pm, po, *kept = layer(
                functools.partial(backward_kernel, kind_of(step), bool(old), bool(extra)),
                "backward_layer",
                [marks, up_mine, up_other, *gates[part], held_late if part else held_early] + old + extra,
                [row] * (5 if extra else 4),
            )
            ups[part] = kept[:2]
        held = hold(part, True, [pm, swap_core(po), up_mine, state_mine[part], gains], step not in (middle, 1))
        if step == 1:
            held, middle_arrived = lax.optimization_barrier((held, middle_arrived))
            mine = total([held, swap_chip(held)])
        elif step == middle:
            held, mixed = lax.optimization_barrier((held, kept[2]))
            up_mine = total([held, swap_chip(held)])
            mixed_first = flow(mixed, 0, far)
            up_other, mixed_first, state_second = lax.optimization_barrier(
                (swap_core(up_mine), mixed_first, state_second)
            )
            middle_arrived = with_other_core([state_first, state_second])
            mixed_second = flow(joined(mixed, mixed_first), 1, far)
        else:
            during = [state_first] if step == sections - 1 else []
            up_mine, up_other, during, _ = across(held, kind_of(step), kind_of(step - 1), during)
            if step == sections - 1:
                (state_first,) = during
                state_second = flow(joined(same, state_first), 1, middle_class)
    _, mixed_second = lax.optimization_barrier((mine, mixed_second))
    def last_route(shift, source):
        return lambda copy, end, c: ((copy + shift) % REPL, source, 1, False) if c == 0 and end == 0 else None

    payloads = call(last_kernel, "last", [marks, mine, ups[0][0]], [row] * 2, [], 4, 0, 0, smem=())
    straight = [
        send(payloads[0], last_route(0, 0), flow_route(0, middle_near), whole=False),
        send(payloads[1], last_route(0, 1), whole=False),
        send(payloads[0], last_route(1, 0), flow_route(2, middle_near), whole=False),
        send(payloads[1], last_route(1, 1), flow_route(1, middle_near), whole=False),
    ]
    mixed_arrived = with_other_core([mixed_first, mixed_second])
    prepared = call(
        own_first_kernel,
        "own_first",
        [flags, input_rows, *early_rows, late_mine, late_other, *middle_arrived, *mixed_arrived, gains, weights],
        [
            shape(features, own_rows),
            shape(own_rows, narrow, dtype=F32),
            shape(own_rows, narrow, dtype=F32),
            shape(own_rows, narrow),
        ],
        [
            pltpu.VMEM((2, features, narrow), BF),
            pltpu.VMEM((own_rows, features), BF),
            pltpu.SemaphoreType.DMA((2, chunks)),
        ],
        12,
        4 * own_rows * features * narrow,
        8 * features * narrow,
        hbm=(15,),
    )
    straight, prepared = lax.optimization_barrier((straight, prepared))
    direct = with_other_core([joined(*straight)])
    return call(
        own_last_kernel,
        "own_last",
        [flags, cot_rows, *direct, *ups[0], *ups[1], *mixed_arrived]
        + [*prepared, held_early, held_late],
        [shape(1, 3, features, narrow)],
        [
            pltpu.VMEM((own_rows, features), BF),
            pltpu.VMEM((own_rows, narrow), F32),
            pltpu.VMEM((3, features, narrow), BF),
            pltpu.SemaphoreType.DMA((3, chunks)),
        ],
        16,
        8 * own_rows * features * narrow,
        8 * features * narrow,
        out_hbm=True,
    )[0]


def solution(mesh):
    return jax.shard_map(
        body,
        mesh=mesh,
        in_specs=(P(), P(), P("pipe", None, None, None, "tensor"), P("pipe", None, None)),
        out_specs=P("pipe", None, None, "tensor"),
        check_vma=False,
    )
```

```python
import functools

import jax
import jax.numpy as jnp
from jax import lax
from jax.experimental import pallas as pl
from jax.experimental.pallas import tpu as pltpu
from jax.sharding import PartitionSpec as P

REPL = 2
EPS = 1e-06
BF = jnp.bfloat16
F32 = jnp.float32
SMEM_SPEC = pl.BlockSpec(memory_space=pltpu.SMEM)
VMEM_SPEC = pl.BlockSpec(memory_space=pltpu.VMEM)
HBM_SPEC = pl.BlockSpec(memory_space=pltpu.HBM)
MIB = 1024 * 1024
NEAR, OUTER, FIRST_CHIP, KIND, OWN, TOP, BOTTOM = 1, 2, 3, 4, 5, 13, 21


def chunk_of(features):
    for size in (512, 256, 128):
        if features % size == 0:
            return size
    return features


def norm_rows(rows, gain_row):
    widened = rows.astype(F32)
    root = jnp.sqrt(jnp.mean(widened * widened, axis=-1, keepdims=True) + EPS)
    unit = widened / root
    return unit, root, (unit * gain_row).astype(BF)


def dot(left, right):
    return jnp.dot(left, right, preferred_element_type=F32)


def dot_last(left, right):
    return lax.dot_general(left, right, (((1,), (1,)), ((), ())), preferred_element_type=F32)


def dot_first(left, right):
    return lax.dot_general(left, right, (((0,), (0,)), ((), ())), preferred_element_type=F32)


def is_set(flags_ref, index, value=1):
    if len(flags_ref.shape) == 1:
        return flags_ref[index] == value
    return flags_ref[index : index + 1, 0:1] == value


def gain_at(flags_ref, gains_ref, part):
    return jnp.where(is_set(flags_ref, NEAR, 1 - part), gains_ref[0:1], gains_ref[1:2])


def own_index(flags_ref, part):
    return jnp.where(flags_ref[NEAR] == 1 - part, 0, 1)


def choose(condition, first, second):
    kept = first.dtype
    return jnp.where(condition, first.astype(F32), second.astype(F32)).astype(kept)


def weight_copies(which, w_ref, w_buf, sems, size):
    features = w_buf.shape[1]
    copies = {}
    for matrix in range(3):
        for k in range(features // size):
            rows = pl.ds(k * size, size)
            copies[matrix, k] = pltpu.make_async_copy(
                w_ref.at[which, matrix, rows], w_buf.at[matrix, rows], sems.at[matrix, k]
            )
    return copies


def fill_normed(xm_ref, xo_ref, gain, normed):
    half = xm_ref.shape[0]
    normed[:half] = norm_rows(xm_ref[...], gain)[2]
    normed[half:] = norm_rows(xo_ref[...], gain)[2]


def gate_upper(copies, w_buf, normed, size):
    gate = upper = None
    for k in range(w_buf.shape[1] // size):
        cols = pl.ds(k * size, size)
        if copies:
            copies[0, k].wait()
            copies[1, k].wait()
        block = normed[:, cols]
        gate_k = dot(block, w_buf[0, cols])
        upper_k = dot(block, w_buf[1, cols])
        gate = gate_k if gate is None else gate + gate_k
        upper = upper_k if upper is None else upper + upper_k
    return gate, upper


def forward_math(copies, xm_ref, xo_ref, gain, w_buf, pm_ref, po_ref, normed):
    size = chunk_of(w_buf.shape[1])
    half = xm_ref.shape[0]
    fill_normed(xm_ref, xo_ref, gain, normed)
    gate, upper = gate_upper(copies, w_buf, normed, size)
    active = (gate * jax.nn.sigmoid(gate) * upper).astype(BF)
    for k in range(w_buf.shape[1] // size):
        cols = pl.ds(k * size, size)
        if copies:
            copies[2, k].wait()
        part = dot_last(active, w_buf[2, cols]).astype(BF)
        pm_ref[:, cols] = part[:half]
        po_ref[:, cols] = part[half:]
    return gate, upper


def first_kernel(
    flags_ref, rows_ref, gains_ref, w_ref,
    pm_ref, po_ref, gate_ref, upper_ref, w_buf, xm_ref, xo_ref, marks_ref, normed, gains_buf, sems, row_sems
):
    size = chunk_of(w_buf.shape[1])
    moves = [
        pltpu.make_async_copy(rows_ref.at[flags_ref[OWN + i]], ref, row_sems.at[i])
        for i, ref in enumerate((xm_ref, xo_ref))
    ]
    moves.append(pltpu.make_async_copy(gains_ref, gains_buf, row_sems.at[2]))
    for move in moves:
        move.start()
    for i in range(marks_ref.shape[0]):
        marks_ref[i : i + 1] = jnp.full((1, marks_ref.shape[1]), flags_ref[i], jnp.int32)
    for move in moves:
        move.wait()
    copies = weight_copies(own_index(flags_ref, 0), w_ref, w_buf, sems, size)
    for group in ((0, 1), (2,)):
        for k in range(w_buf.shape[1] // size):
            for matrix in group:
                copies[matrix, k].start()
    gain = gain_at(flags_ref, gains_buf, 0)
    gate_ref[...], upper_ref[...] = forward_math(copies, xm_ref, xo_ref, gain, w_buf, pm_ref, po_ref, normed)


def load_kernel(flags_ref, cot_ref, w_ref, w_buf, um_ref, uo_ref, sems, row_sems):
    copies = [
        pltpu.make_async_copy(cot_ref.at[flags_ref[OWN + i]], ref, row_sems.at[i])
        for i, ref in enumerate((um_ref, uo_ref))
    ]
    copies += list(weight_copies(own_index(flags_ref, 1), w_ref, w_buf, sems, w_buf.shape[1]).values())
    for copy in copies:
        copy.start()
    for copy in copies:
        copy.wait()


def rows_kernel(flags_ref, rows_ref, cot_ref, xs_ref, us_ref, row_sems):
    copies = []
    pieces, rows = xs_ref.shape[:2]
    group = rows // 2
    for i in range(pieces):
        copies.append(pltpu.make_async_copy(cot_ref.at[flags_ref[OWN + i]], us_ref.at[i], row_sems.at[0, i]))
        for half, base in enumerate((TOP, BOTTOM)):
            part = pl.ds(half * group, group)
            copies.append(
                pltpu.make_async_copy(
                    rows_ref.at[flags_ref[base + i], part], xs_ref.at[i, part], row_sems.at[1 + half, i]
                )
            )
    for copy in copies:
        copy.start()
    for copy in copies:
        copy.wait()


def forward_kernel(part, live, flags_ref, xm_ref, xo_ref, gains_ref, w_buf, *refs):
    *old, pm_ref, po_ref, gate_ref, upper_ref, xms_ref, xos_ref, normed = refs
    gain = gain_at(flags_ref, gains_ref, part)
    gate, upper = forward_math(None, xm_ref, xo_ref, gain, w_buf, pm_ref, po_ref, normed)
    found = (gate, upper, xm_ref[...], xo_ref[...])
    outs = (gate_ref, upper_ref, xms_ref, xos_ref)
    if old:
        is_live = is_set(flags_ref, KIND, live)
        found = [choose(is_live, a, b[...]) for a, b in zip(found, old)]
    for out, value in zip(outs, found):
        out[...] = value


def active_gradient(um_ref, uo_ref, w_buf):
    size = chunk_of(w_buf.shape[1])
    d_active = None
    for k in range(w_buf.shape[1] // size):
        cols = pl.ds(k * size, size)
        block = jnp.concatenate([um_ref[:, cols], uo_ref[:, cols]], axis=0)
        part = dot(block, w_buf[2, cols])
        d_active = part if d_active is None else d_active + part
    return d_active


def backward_math(d_active, gate, upper, w_buf, pm_ref, po_ref):
    size = chunk_of(w_buf.shape[1])
    half = pm_ref.shape[0]
    sig = jax.nn.sigmoid(gate)
    d_gate = (d_active * upper * (sig * (1.0 + gate * (1.0 - sig)))).astype(BF)
    d_upper = (d_active * (gate * sig)).astype(BF)
    for k in range(w_buf.shape[1] // size):
        cols = pl.ds(k * size, size)
        part = (dot_last(d_gate, w_buf[0, cols]) + dot_last(d_upper, w_buf[1, cols])).astype(BF)
        pm_ref[:, cols] = part[:half]
        po_ref[:, cols] = part[half:]


def cotangent_kernel(um_ref, uo_ref, w_buf, d_ref):
    d_ref[...] = active_gradient(um_ref, uo_ref, w_buf)


def turn_kernel(
    flags_ref, d_ref, xm_ref, xo_ref, oldm_ref, oldo_ref, gains_ref, w_buf, pm_ref, po_ref, latem_ref, lateo_ref, normed
):
    fill_normed(xm_ref, xo_ref, gain_at(flags_ref, gains_ref, 1), normed)
    gate, upper = gate_upper(None, w_buf, normed, chunk_of(w_buf.shape[1]))
    backward_math(d_ref[...], gate, upper, w_buf, pm_ref, po_ref)
    is_outer = is_set(flags_ref, OUTER)
    latem_ref[...] = choose(is_outer, xm_ref[...], oldm_ref[...])
    lateo_ref[...] = choose(is_outer, xo_ref[...], oldo_ref[...])


def backward_kernel(live, has_old, has_late, flags_ref, um_ref, uo_ref, gate_ref, upper_ref, w_buf, *refs):
    refs = list(refs)
    old = [refs.pop(0) for _ in range(2)] if has_old else []
    late = refs.pop(0) if has_late else None
    pm_ref, po_ref, ums_ref, uos_ref = refs[:4]
    backward_math(active_gradient(um_ref, uo_ref, w_buf), gate_ref[...], upper_ref[...], w_buf, pm_ref, po_ref)
    found = [um_ref[...], uo_ref[...]]
    if old:
        is_live = is_set(flags_ref, KIND, live)
        found = [choose(is_live, a, b[...]) for a, b in zip(found, old)]
    ums_ref[...], uos_ref[...] = found
    if has_late:
        refs[4][...] = choose(is_set(flags_ref, OUTER), late[...], found[0])


def hold_kernel(part, backward, flags_ref, pm_ref, recv_ref, base_ref, *refs):
    summed = pm_ref[...].astype(F32) + recv_ref[...].astype(F32)
    if backward:
        state_ref, gains_ref, *outs = refs
        gain = gain_at(flags_ref, gains_ref, part)
        unit, root, _ = norm_rows(state_ref[...], gain)
        d_unit = summed * gain
        summed = (d_unit - unit * jnp.mean(d_unit * unit, axis=-1, keepdims=True)) / root
    else:
        outs = refs
    base = jnp.where(is_set(flags_ref, FIRST_CHIP), base_ref[...].astype(F32), 0.0)
    value = (summed + base).astype(BF)
    rows = value.shape[0] // len(outs)
    for i, out in enumerate(outs):
        out[...] = value[i * rows : (i + 1) * rows]


def sides_kernel(marks_ref, early_ref, late_ref, same_ref, opposite_ref):
    is_near = is_set(marks_ref, NEAR)
    same_ref[...] = choose(is_near, early_ref[...], late_ref[...])
    opposite_ref[...] = choose(is_near, late_ref[...], early_ref[...])


def stack_kernel(*refs):
    *sources, out_ref = refs
    rows = sources[0].shape[0]
    for i, source in enumerate(sources):
        out_ref[i * rows : (i + 1) * rows] = source[...]


def fill_rows(target, sources, change=None):
    start = 0
    for source in sources:
        rows = source[...]
        target[start : start + rows.shape[0]] = change(rows) if change else rows
        start += rows.shape[0]


def last_kernel(marks_ref, mine_ref, early_ref, first_ref, second_ref):
    is_near = is_set(marks_ref, NEAR)
    mine, early = mine_ref[...], early_ref[...]
    first_ref[...] = choose(is_near, mine, early)
    second_ref[...] = choose(is_near, early, mine)


def sum_kernel(*refs):
    *terms, out = refs
    count = len(terms) // 2
    rows = out.shape[0] // count
    for i in range(count):
        total = terms[i][...].astype(F32) + terms[count + i][...].astype(F32)
        out[i * rows : (i + 1) * rows] = total.astype(BF)


def own_first_kernel(
    flags_ref, xs_ref, em_ref, eo_ref, lm_ref, lo_ref, p0, p1, p2, p3, q0, q1, q2, q3, gains_ref, w_ref,
    turned_ref, left_ref, right_ref, active_ref, w_buf, normed, sems
):
    features = w_buf.shape[1]
    size = chunk_of(features)
    count = features // size
    copies = {}
    for k in range(count):
        rows = pl.ds(k * size, size)
        for matrix in range(2):
            copies[matrix, k] = pltpu.make_async_copy(
                w_ref.at[0, matrix, rows], w_buf.at[matrix, rows], sems.at[matrix, k]
            )
            copies[matrix, k].start()
    gain = gains_ref[0:1]
    pieces, half = xs_ref.shape[:2]
    is_near = flags_ref[NEAR] == 1
    is_outer = flags_ref[OUTER] == 1
    inputs_used = jnp.logical_and(is_near, is_outer)

    def put(piece, rows):
        normed[piece * half : (piece + 1) * half] = norm_rows(rows, gain)[2]

    @pl.when(inputs_used)
    def _():
        for piece in range(pieces):
            put(piece, xs_ref[piece])

    cases = (
        (False, True, (em_ref, eo_ref, p0, p1, p2, p3)),
        (False, False, (lm_ref, lo_ref, p0, p1, p2, p3)),
        (True, False, (lm_ref, lo_ref, q0, q1, q2, q3)),
    )
    for outer, near, sources in cases:

        @pl.when(jnp.logical_and(is_outer == outer, is_near == near))
        def _(sources=sources):
            fill_rows(normed, sources, lambda rows: norm_rows(rows, gain)[2])

    gate, upper = gate_upper(copies, w_buf, normed, size)
    sig = jax.nn.sigmoid(gate)
    smooth = gate * sig
    left_ref[...] = upper * (sig * (1.0 + gate * (1.0 - sig)))
    right_ref[...] = smooth
    active_ref[...] = (smooth * upper).astype(BF)
    for k in range(count):
        cols = pl.ds(k * size, size)
        turned_ref[cols] = normed[:, cols].T


def own_last_kernel(flags_ref, us_ref, *refs):
    refs = list(refs)

    def take(count):
        return [refs.pop(0) for _ in range(count)]

    direct, early, late, arrived = take(2), take(2), take(2), take(4)
    turned_ref, left_ref, right_ref, active_ref, early_ref, late_ref = take(6)
    out_ref, u_buf, d_act, out_buf, sems = take(5)
    features = turned_ref.shape[0]
    size = chunk_of(features)
    count = features // size
    pieces, half = us_ref.shape[:2]
    is_near = flags_ref[NEAR] == 1
    is_outer = flags_ref[OUTER] == 1

    def fill(sources, w_ref):
        fill_rows(u_buf, sources)
        total = None
        for k in range(count):
            cols = pl.ds(k * size, size)
            part = dot(u_buf[:, cols], w_ref[2, cols])
            total = part if total is None else total + part
        d_act[...] = total

    half = early[0].shape[0]

    def lanes(source, *places):
        return [source.at[pl.ds(i * half, half)] for i in places]

    near_sources = early + lanes(direct[0], 0, 3, 2) + lanes(direct[1], 0, 3, 2)
    cases = (
        (True, True, direct, early_ref),
        (True, False, [us_ref.at[i] for i in range(pieces)], late_ref),
        (False, True, near_sources, early_ref),
        (False, False, late + arrived, late_ref),
    )
    for outer, near, sources, w_ref in cases:

        @pl.when(jnp.logical_and(is_outer == outer, is_near == near))
        def _(sources=sources, w_ref=w_ref):
            fill(sources, w_ref)

    copies = []

    def send(matrix, k):
        rows = pl.ds(k * size, size)
        copy = pltpu.make_async_copy(out_buf.at[matrix, rows], out_ref.at[0, matrix, rows], sems.at[matrix, k])
        copy.start()
        copies.append(copy)

    active = active_ref[...]
    d_active = d_act[...]
    for k in range(count):
        cols = pl.ds(k * size, size)
        out_buf[2, cols] = dot_first(u_buf[:, cols], active).astype(BF)
        send(2, k)
    d_gate = (d_active * left_ref[...]).astype(BF)
    d_upper = (d_active * right_ref[...]).astype(BF)
    for k in range(count):
        cols = pl.ds(k * size, size)
        turned = turned_ref[cols]
        out_buf[0, cols] = dot(turned, d_gate).astype(BF)
        send(0, k)
        out_buf[1, cols] = dot(turned, d_upper).astype(BF)
        send(1, k)
    for copy in copies:
        copy.wait()


def call(kernel, name, operands, outs, scratch, limit, flops, moved, hbm=(), out_hbm=False, smem=(0,)):
    specs = [
        SMEM_SPEC if i in smem else HBM_SPEC if i in hbm else VMEM_SPEC for i in range(len(operands))
    ]
    out_spec = HBM_SPEC if out_hbm else VMEM_SPEC
    results = pl.pallas_call(
        kernel,
        out_shape=outs,
        in_specs=specs,
        out_specs=[out_spec] * len(outs),
        scratch_shapes=scratch,
        cost_estimate=pl.CostEstimate(flops=flops, bytes_accessed=moved, transcendentals=0),
        compiler_params=pltpu.CompilerParams(vmem_limit_bytes=limit * MIB),
        name=name,
    )(*operands)
    return list(results)


def body(inputs, cotangent, section_weights, section_gains):
    sections = lax.axis_size("pipe") // REPL
    ranks = lax.axis_size("tensor")
    pipe = lax.axis_index("pipe")
    tensor = lax.axis_index("tensor")
    position = pipe % sections
    replica = pipe // sections
    middle = sections // 2
    near = position < middle
    side = jnp.where(near, 0, 1)
    kind = jnp.where(near, position, sections - 1 - position)
    core = tensor % 2
    chip = tensor // 2
    rows, features = inputs.shape[2:]
    narrow = section_weights.shape[-1]
    group = rows // 2
    chunks = features // chunk_of(features)
    weights = pltpu.with_memory_space_constraint(section_weights[0], pltpu.HBM)
    blocks = pltpu.with_memory_space_constraint(inputs.reshape(-1, rows, features), pltpu.HBM)
    cot_blocks = pltpu.with_memory_space_constraint(cotangent.reshape(-1, rows, features), pltpu.HBM)
    gains = section_gains[0]
    core_swap = [(i, i ^ 1) for i in range(ranks)]
    chip_swap = [(i, (i + 2) % ranks) for i in range(ranks)]

    def spot(across, end, batch):
        return (((replica + across) % REPL) * 2 + end) * 2 + batch

    pairs = ((0, 0), (0, 1), (1, 0), (1, 1))
    pairs_of = ((1, 0), (0, 1), (1, 1))
    own = [spot(across, side ^ turn, batch) for batch in (core, 1 - core) for across, turn in pairs]
    own = [own[i] for i in (0, 4, 1, 2, 3, 5, 6, 7)]
    top = [spot(across, end, batch) for batch in (core, 1 - core) for across, end in pairs]
    bottom = [spot(across, 1 - end, batch) for batch in (core, 1 - core) for across, end in pairs]
    flags = [side, near, kind == 0, chip == 0, kind] + own + top + bottom
    flags = jnp.stack([jnp.asarray(flag).astype(jnp.int32) for flag in flags])

    def swap_core(block):
        return lax.ppermute(block, "tensor", core_swap)

    def swap_chip(block):
        return lax.ppermute(block, "tensor", chip_swap)

    def place(copy, end, c, rank):
        at = c if end == 0 else sections - 1 - c
        return (copy * sections + at) * ranks + rank

    def completed(moves):
        per_copy = sections * ranks
        target = dict(moves)
        back = {end: start for start, end in moves}
        sources = [i for i in range(REPL * per_copy) if i not in target]
        ends = {i for i in range(REPL * per_copy) if i not in back}
        rules = (
            lambda i: i ^ 1 if i in ends else None,
            lambda i: back.get(i) if back.get(i, -1) // per_copy == i // per_copy else None,
            lambda i: next((j for j in sorted(ends) if j // per_copy == i // per_copy and j % ranks == i % ranks), None),
            lambda i: min(ends),
        )
        for rule in rules:
            for i in sources:
                if i not in target and rule(i) in ends:
                    target[i] = rule(i)
                    if rule is rules[0] and i ^ 1 not in target:
                        target[i ^ 1] = i
                        ends.remove(i)
                    ends.remove(target[i])
        return sorted(target.items())

    def send(block, *routes, whole=True):
        moves = []
        for copy in range(REPL):
            for end in range(2):
                for c in range(middle):
                    for route in routes:
                        source = route(copy, end, c)
                        if source is None:
                            continue
                        for rank in range(ranks):
                            came = (rank + 2) % ranks if source[3] else rank
                            moves.append((place(*source[:3], came), place(copy, end, c, rank)))
        return lax.ppermute(block, ("pipe", "tensor"), completed(moves) if whole else moves)

    def hop(block, source, target, turn, other):
        return send(block, lambda copy, end, c: (copy, end ^ turn, source, other) if c == target else None)

    def flow_route(which, wanted):
        turn, shift = pairs_of[which]
        return lambda copy, end, c: ((copy + shift) % REPL, end ^ turn, c, False) if wanted(c, end) else None

    def flow(payload, which, wanted):
        return send(payload, flow_route(which, wanted))

    def joined(*parts):
        return call(stack_kernel, "stack", list(parts), [shape(len(parts) * rows, features)], [], 4, 0, 0, smem=())[0]

    def with_other_core(arrived):
        return arrived + [swap_core(block) for block in arrived]

    def shape(*extent, dtype=BF):
        return jax.ShapeDtypeStruct(extent, dtype)

    row = shape(rows, features)
    pieces = shape(4 * REPL, rows, features)
    gate_shape = shape(2 * rows, narrow, dtype=F32)
    held_shape = pltpu.VMEM((3, features, narrow), BF)
    normed_scratch = pltpu.VMEM((2 * rows, features), BF)
    layer_flops = 12 * rows * features * narrow
    layer_bytes = 6 * features * narrow
    row_bytes = 2 * rows * features

    def layer(kernel, name, operands, outs):
        return call(kernel, name, operands, outs, [normed_scratch], 8, layer_flops, layer_bytes, smem=())

    def hold(part, backward, operands, split):
        kernel = functools.partial(hold_kernel, part, backward)
        outs = [shape(group, features)] * 2 if split else [row]
        found = call(kernel, "hold", [marks] + operands, outs, [], 4, 0, 4 * row_bytes, smem=())
        return found if split else found[0]

    def total(terms):
        return call(sum_kernel, "total", terms, [row], [], 4, 0, 3 * row_bytes, smem=())[0]

    def kind_of(step):
        return min(step, sections - 1 - step)

    def across(held, source, target, during, later=()):
        straight = [hop(held[turn], source, target, turn, False) for turn in range(2)]
        crossed = [hop(held[turn], source, target, turn, True) for turn in range(2)]
        straight, crossed, during = lax.optimization_barrier((straight, crossed, during))
        mine = total(straight + crossed)
        other, later = lax.optimization_barrier((swap_core(mine), later))
        return mine, other, during, later

    def far(c, end):
        return end == 1

    def middle_near(c, end):
        return c > 0 and end == 0

    def middle_class(c, end):
        return c > 0

    pm, po, gate, upper, held_early, mine, other, marks = call(
        first_kernel,
        "first_layer",
        [flags, blocks, pltpu.with_memory_space_constraint(gains, pltpu.HBM), weights],
        [row, row, gate_shape, gate_shape, held_shape, row, row, shape(8, 128, dtype=jnp.int32)],
        [
            normed_scratch,
            pltpu.VMEM(gains.shape, F32),
            pltpu.SemaphoreType.DMA((3, chunks)),
            pltpu.SemaphoreType.DMA((3,)),
        ],
        8,
        layer_flops,
        layer_bytes,
        hbm=(1, 2, 3),
    )
    saved = [(gate, upper, mine, other), None]
    loaded = call(
        load_kernel,
        "load_late",
        [flags, cot_blocks, weights],
        [held_shape, row, row],
        [pltpu.SemaphoreType.DMA((3, 1)), pltpu.SemaphoreType.DMA((2,))],
        4,
        0,
        2 * layer_bytes,
        hbm=(1, 2),
    )
    loaded_rows = call(
        rows_kernel,
        "load_rows",
        [flags, blocks, cot_blocks],
        [pieces, pieces],
        [pltpu.SemaphoreType.DMA((3, 4 * REPL))],
        4,
        0,
        layer_bytes,
        hbm=(1, 2),
    )
    for step in range(sections - 1):
        part = 0 if step < middle else 1
        if step > 0:
            old = list(saved[part] or ())
            pm, po, *saved[part] = layer(
                functools.partial(forward_kernel, part, kind_of(step)),
                "forward_layer",
                [marks, mine, other, gains, held_late if part else held_early] + old,
                [row, row, gate_shape, gate_shape, row, row],
            )
        held = hold(part, False, [pm, swap_core(po), mine], step != middle - 1)
        during = ()
        if step == 0:
            during = loaded
        if step == middle:
            during = call(
                cotangent_kernel,
                "cotangent",
                [up_mine, up_other, held_late],
                [gate_shape],
                [],
                4,
                layer_flops // 3,
                layer_bytes // 3,
                smem=(),
            ) + loaded_rows
        if step == middle - 1:
            mine = total([held, swap_chip(held)])
            other = swap_core(mine)
        else:
            mine, other, during, _ = across(held, kind_of(step), kind_of(step + 1), during)
        if step == 0:
            held_late, up_mine, up_other = during
        if step == middle:
            d_active, input_rows, cot_rows = during

    early_rows = saved[0][2:]
    sides = call(sides_kernel, "sides", [marks, saved[0][2], saved[1][2]], [row, row], [], 4, 0, 0, smem=())
    mine, (same, opposite) = lax.optimization_barrier((mine, sides))
    state_first = flow(opposite, 0, middle_class)
    gates = [saved[0][:2], saved[1][:2]]
    pm, po, late_mine, late_other = layer(
        turn_kernel,
        "turn_layer",
        [marks, d_active, mine, other, *saved[1][2:], gains, held_late],
        [row] * 4,
    )
    state_mine = [early_rows[0], late_mine]
    ups = [None, (up_mine, up_other)]
    own_rows = 4 * REPL * rows
    for step in range(sections - 1, 0, -1):
        part = 0 if step < middle else 1
        if step < sections - 1:
            old = list(ups[part] or ())
            extra = [late_mine] if step == middle else []
            pm, po, *kept = layer(
                functools.partial(backward_kernel, kind_of(step), bool(old), bool(extra)),
                "backward_layer",
                [marks, up_mine, up_other, *gates[part], held_late if part else held_early] + old + extra,
                [row] * (5 if extra else 4),
            )
            ups[part] = kept[:2]
        held = hold(part, True, [pm, swap_core(po), up_mine, state_mine[part], gains], step not in (middle, 1))
        if step == 1:
            held, middle_arrived = lax.optimization_barrier((held, middle_arrived))
            mine = total([held, swap_chip(held)])
        elif step == middle:
            held, mixed = lax.optimization_barrier((held, kept[2]))
            crossed, state_second = lax.optimization_barrier((swap_chip(held), state_second))
            up_mine = total([held, crossed])
            mixed_first = flow(mixed, 0, far)
            up_other, mixed_first = lax.optimization_barrier((swap_core(up_mine), mixed_first))
            middle_arrived = with_other_core([state_first, state_second])
            mixed_second = flow(joined(mixed, mixed_first), 1, far)
        else:
            during = [state_first] if step == sections - 1 else []
            up_mine, up_other, during, _ = across(held, kind_of(step), kind_of(step - 1), during)
            if step == sections - 1:
                (state_first,) = during
                state_second = flow(joined(same, state_first), 1, middle_class)
    def last_route(shift, source):
        return lambda copy, end, c: ((copy + shift) % REPL, source, 1, False) if c == 0 and end == 0 else None

    payloads = call(last_kernel, "last", [marks, mine, ups[0][0]], [row] * 2, [], 4, 0, 0, smem=())
    straight = [
        send(payloads[0], last_route(0, 0), flow_route(0, middle_near), whole=False),
        send(payloads[1], last_route(0, 1), whole=False),
        send(payloads[0], last_route(1, 0), flow_route(2, middle_near), whole=False),
        send(payloads[1], last_route(1, 1), flow_route(1, middle_near), whole=False),
    ]
    straight, mixed_second = lax.optimization_barrier((straight, mixed_second))
    mixed_arrived = with_other_core([mixed_first, mixed_second])
    prepared = call(
        own_first_kernel,
        "own_first",
        [flags, input_rows, *early_rows, late_mine, late_other, *middle_arrived, *mixed_arrived, gains, weights],
        [
            shape(features, own_rows),
            shape(own_rows, narrow, dtype=F32),
            shape(own_rows, narrow, dtype=F32),
            shape(own_rows, narrow),
        ],
        [
            pltpu.VMEM((2, features, narrow), BF),
            pltpu.VMEM((own_rows, features), BF),
            pltpu.SemaphoreType.DMA((2, chunks)),
        ],
        12,
        4 * own_rows * features * narrow,
        8 * features * narrow,
        hbm=(15,),
    )
    direct = with_other_core([joined(*straight)])
    return call(
        own_last_kernel,
        "own_last",
        [flags, cot_rows, *direct, *ups[0], *ups[1], *mixed_arrived]
        + [*prepared, held_early, held_late],
        [shape(1, 3, features, narrow)],
        [
            pltpu.VMEM((own_rows, features), BF),
            pltpu.VMEM((own_rows, narrow), F32),
            pltpu.VMEM((3, features, narrow), BF),
            pltpu.SemaphoreType.DMA((3, chunks)),
        ],
        16,
        8 * own_rows * features * narrow,
        8 * features * narrow,
        out_hbm=True,
    )[0]


def solution(mesh):
    return jax.shard_map(
        body,
        mesh=mesh,
        in_specs=(P(), P(), P("pipe", None, None, None, "tensor"), P("pipe", None, None)),
        out_specs=P("pipe", None, None, "tensor"),
        check_vma=False,
    )
```

```python
import functools

import jax
import jax.numpy as jnp
from jax import lax
from jax.experimental import pallas as pl
from jax.experimental.pallas import tpu as pltpu
from jax.sharding import PartitionSpec as P

REPL = 2
EPS = 1e-06
BF = jnp.bfloat16
F32 = jnp.float32
SMEM_SPEC = pl.BlockSpec(memory_space=pltpu.SMEM)
VMEM_SPEC = pl.BlockSpec(memory_space=pltpu.VMEM)
HBM_SPEC = pl.BlockSpec(memory_space=pltpu.HBM)
MIB = 1024 * 1024
NEAR, OUTER, FIRST_CHIP, KIND, OWN, TOP, BOTTOM = 1, 2, 3, 4, 5, 13, 21


def chunk_of(features):
    for size in (512, 256, 128):
        if features % size == 0:
            return size
    return features


def norm_rows(rows, gain_row):
    widened = rows.astype(F32)
    root = jnp.sqrt(jnp.mean(widened * widened, axis=-1, keepdims=True) + EPS)
    unit = widened / root
    return unit, root, (unit * gain_row).astype(BF)


def dot(left, right):
    return jnp.dot(left, right, preferred_element_type=F32)


def dot_last(left, right):
    return lax.dot_general(left, right, (((1,), (1,)), ((), ())), preferred_element_type=F32)


def dot_first(left, right):
    return lax.dot_general(left, right, (((0,), (0,)), ((), ())), preferred_element_type=F32)


def is_set(flags_ref, index, value=1):
    if len(flags_ref.shape) == 1:
        return flags_ref[index] == value
    return flags_ref[index : index + 1, 0:1] == value


def gain_at(flags_ref, gains_ref, part):
    return jnp.where(is_set(flags_ref, NEAR, 1 - part), gains_ref[0:1], gains_ref[1:2])


def own_index(flags_ref, part):
    return jnp.where(flags_ref[NEAR] == 1 - part, 0, 1)


def choose(condition, first, second):
    kept = first.dtype
    return jnp.where(condition, first.astype(F32), second.astype(F32)).astype(kept)


def weight_copies(which, w_ref, w_buf, sems, size):
    features = w_buf.shape[1]
    copies = {}
    for matrix in range(3):
        for k in range(features // size):
            rows = pl.ds(k * size, size)
            copies[matrix, k] = pltpu.make_async_copy(
                w_ref.at[which, matrix, rows], w_buf.at[matrix, rows], sems.at[matrix, k]
            )
    return copies


def fill_normed(xm_ref, xo_ref, gain, normed):
    half = xm_ref.shape[0]
    normed[:half] = norm_rows(xm_ref[...], gain)[2]
    normed[half:] = norm_rows(xo_ref[...], gain)[2]


def gate_upper(copies, w_buf, normed, size):
    gate = upper = None
    for k in range(w_buf.shape[1] // size):
        cols = pl.ds(k * size, size)
        if copies:
            copies[0, k].wait()
            copies[1, k].wait()
        block = normed[:, cols]
        gate_k = dot(block, w_buf[0, cols])
        upper_k = dot(block, w_buf[1, cols])
        gate = gate_k if gate is None else gate + gate_k
        upper = upper_k if upper is None else upper + upper_k
    return gate, upper


def forward_math(copies, xm_ref, xo_ref, gain, w_buf, pm_ref, po_ref, normed):
    size = chunk_of(w_buf.shape[1])
    half = xm_ref.shape[0]
    fill_normed(xm_ref, xo_ref, gain, normed)
    gate, upper = gate_upper(copies, w_buf, normed, size)
    active = (gate * jax.nn.sigmoid(gate) * upper).astype(BF)
    for k in range(w_buf.shape[1] // size):
        cols = pl.ds(k * size, size)
        if copies:
            copies[2, k].wait()
        part = dot_last(active, w_buf[2, cols]).astype(BF)
        pm_ref[:, cols] = part[:half]
        po_ref[:, cols] = part[half:]
    return gate, upper


def first_kernel(
    flags_ref, rows_ref, gains_ref, w_ref,
    pm_ref, po_ref, gate_ref, upper_ref, w_buf, xm_ref, xo_ref, marks_ref, normed, gains_buf, sems, row_sems
):
    size = chunk_of(w_buf.shape[1])
    moves = [
        pltpu.make_async_copy(rows_ref.at[flags_ref[OWN + i]], ref, row_sems.at[i])
        for i, ref in enumerate((xm_ref, xo_ref))
    ]
    moves.append(pltpu.make_async_copy(gains_ref, gains_buf, row_sems.at[2]))
    for move in moves:
        move.start()
    for i in range(marks_ref.shape[0]):
        marks_ref[i : i + 1] = jnp.full((1, marks_ref.shape[1]), flags_ref[i], jnp.int32)
    copies = weight_copies(own_index(flags_ref, 0), w_ref, w_buf, sems, size)
    ordered = [(matrix, k) for group in ((0, 1), (2,)) for k in range(w_buf.shape[1] // size) for matrix in group]
    for key in ordered[:4]:
        copies[key].start()
    for move in moves:
        move.wait()
    for key in ordered[4:]:
        copies[key].start()
    gain = gain_at(flags_ref, gains_buf, 0)
    gate_ref[...], upper_ref[...] = forward_math(copies, xm_ref, xo_ref, gain, w_buf, pm_ref, po_ref, normed)


def load_kernel(flags_ref, cot_ref, w_ref, w_buf, um_ref, uo_ref, sems, row_sems):
    copies = [
        pltpu.make_async_copy(cot_ref.at[flags_ref[OWN + i]], ref, row_sems.at[i])
        for i, ref in enumerate((um_ref, uo_ref))
    ]
    copies += list(weight_copies(own_index(flags_ref, 1), w_ref, w_buf, sems, w_buf.shape[1]).values())
    for copy in copies:
        copy.start()
    for copy in copies:
        copy.wait()


def rows_kernel(flags_ref, rows_ref, cot_ref, xs_ref, us_ref, row_sems):
    copies = []
    pieces, rows = xs_ref.shape[:2]
    group = rows // 2
    for i in range(pieces):
        copies.append(pltpu.make_async_copy(cot_ref.at[flags_ref[OWN + i]], us_ref.at[i], row_sems.at[0, i]))
        for half, base in enumerate((TOP, BOTTOM)):
            part = pl.ds(half * group, group)
            copies.append(
                pltpu.make_async_copy(
                    rows_ref.at[flags_ref[base + i], part], xs_ref.at[i, part], row_sems.at[1 + half, i]
                )
            )
    for copy in copies:
        copy.start()
    for copy in copies:
        copy.wait()


def forward_kernel(part, live, flags_ref, xm_ref, xo_ref, gains_ref, w_buf, *refs):
    *old, pm_ref, po_ref, gate_ref, upper_ref, xms_ref, xos_ref, normed = refs
    gain = gain_at(flags_ref, gains_ref, part)
    gate, upper = forward_math(None, xm_ref, xo_ref, gain, w_buf, pm_ref, po_ref, normed)
    found = (gate, upper, xm_ref[...], xo_ref[...])
    outs = (gate_ref, upper_ref, xms_ref, xos_ref)
    if old:
        is_live = is_set(flags_ref, KIND, live)
        found = [choose(is_live, a, b[...]) for a, b in zip(found, old)]
    for out, value in zip(outs, found):
        out[...] = value


def active_gradient(um_ref, uo_ref, w_buf):
    size = chunk_of(w_buf.shape[1])
    d_active = None
    for k in range(w_buf.shape[1] // size):
        cols = pl.ds(k * size, size)
        block = jnp.concatenate([um_ref[:, cols], uo_ref[:, cols]], axis=0)
        part = dot(block, w_buf[2, cols])
        d_active = part if d_active is None else d_active + part
    return d_active


def backward_math(d_active, gate, upper, w_buf, pm_ref, po_ref):
    size = chunk_of(w_buf.shape[1])
    half = pm_ref.shape[0]
    sig = jax.nn.sigmoid(gate)
    d_gate = (d_active * upper * (sig * (1.0 + gate * (1.0 - sig)))).astype(BF)
    d_upper = (d_active * (gate * sig)).astype(BF)
    for k in range(w_buf.shape[1] // size):
        cols = pl.ds(k * size, size)
        part = (dot_last(d_gate, w_buf[0, cols]) + dot_last(d_upper, w_buf[1, cols])).astype(BF)
        pm_ref[:, cols] = part[:half]
        po_ref[:, cols] = part[half:]


def cotangent_kernel(um_ref, uo_ref, w_buf, d_ref):
    d_ref[...] = active_gradient(um_ref, uo_ref, w_buf)


def turn_kernel(
    flags_ref, d_ref, xm_ref, xo_ref, oldm_ref, oldo_ref, gains_ref, w_buf, pm_ref, po_ref, latem_ref, lateo_ref, normed
):
    fill_normed(xm_ref, xo_ref, gain_at(flags_ref, gains_ref, 1), normed)
    gate, upper = gate_upper(None, w_buf, normed, chunk_of(w_buf.shape[1]))
    backward_math(d_ref[...], gate, upper, w_buf, pm_ref, po_ref)
    is_outer = is_set(flags_ref, OUTER)
    latem_ref[...] = choose(is_outer, xm_ref[...], oldm_ref[...])
    lateo_ref[...] = choose(is_outer, xo_ref[...], oldo_ref[...])


def backward_kernel(live, has_old, has_late, flags_ref, um_ref, uo_ref, gate_ref, upper_ref, w_buf, *refs):
    refs = list(refs)
    old = [refs.pop(0) for _ in range(2)] if has_old else []
    late = refs.pop(0) if has_late else None
    pm_ref, po_ref, ums_ref, uos_ref = refs[:4]
    backward_math(active_gradient(um_ref, uo_ref, w_buf), gate_ref[...], upper_ref[...], w_buf, pm_ref, po_ref)
    found = [um_ref[...], uo_ref[...]]
    if old:
        is_live = is_set(flags_ref, KIND, live)
        found = [choose(is_live, a, b[...]) for a, b in zip(found, old)]
    ums_ref[...], uos_ref[...] = found
    if has_late:
        refs[4][...] = choose(is_set(flags_ref, OUTER), late[...], found[0])


def hold_kernel(part, backward, flags_ref, pm_ref, recv_ref, base_ref, *refs):
    summed = pm_ref[...].astype(F32) + recv_ref[...].astype(F32)
    if backward:
        state_ref, gains_ref, *outs = refs
        gain = gain_at(flags_ref, gains_ref, part)
        unit, root, _ = norm_rows(state_ref[...], gain)
        d_unit = summed * gain
        summed = (d_unit - unit * jnp.mean(d_unit * unit, axis=-1, keepdims=True)) / root
    else:
        outs = refs
    base = jnp.where(is_set(flags_ref, FIRST_CHIP), base_ref[...].astype(F32), 0.0)
    value = (summed + base).astype(BF)
    rows = value.shape[0] // len(outs)
    for i, out in enumerate(outs):
        out[...] = value[i * rows : (i + 1) * rows]


def sides_kernel(marks_ref, early_ref, late_ref, same_ref, opposite_ref):
    is_near = is_set(marks_ref, NEAR)
    same_ref[...] = choose(is_near, early_ref[...], late_ref[...])
    opposite_ref[...] = choose(is_near, late_ref[...], early_ref[...])


def stack_kernel(*refs):
    *sources, out_ref = refs
    rows = sources[0].shape[0]
    for i, source in enumerate(sources):
        out_ref[i * rows : (i + 1) * rows] = source[...]


def fill_rows(target, sources, change=None):
    start = 0
    for source in sources:
        rows = source[...]
        target[start : start + rows.shape[0]] = change(rows) if change else rows
        start += rows.shape[0]


def last_kernel(marks_ref, mine_ref, early_ref, arrived_ref, first_ref, second_ref):
    is_near = is_set(marks_ref, NEAR)
    mine = mine_ref[...]
    first_ref[...] = choose(is_near, arrived_ref[...], mine)
    second_ref[...] = choose(is_near, early_ref[...], mine)


def sum_kernel(*refs):
    *terms, out = refs
    count = len(terms) // 2
    rows = out.shape[0] // count
    for i in range(count):
        total = terms[i][...].astype(F32) + terms[count + i][...].astype(F32)
        out[i * rows : (i + 1) * rows] = total.astype(BF)


def own_first_kernel(
    flags_ref, xs_ref, em_ref, eo_ref, lm_ref, lo_ref, p0, p1, p2, p3, q0, q1, q2, q3, gains_ref, w_ref,
    turned_ref, left_ref, right_ref, active_ref, w_buf, normed, sems
):
    features = w_buf.shape[1]
    size = chunk_of(features)
    count = features // size
    copies = {}
    for k in range(count):
        rows = pl.ds(k * size, size)
        for matrix in range(2):
            copies[matrix, k] = pltpu.make_async_copy(
                w_ref.at[0, matrix, rows], w_buf.at[matrix, rows], sems.at[matrix, k]
            )
            copies[matrix, k].start()
    gain = gains_ref[0:1]
    pieces, half = xs_ref.shape[:2]
    is_near = flags_ref[NEAR] == 1
    is_outer = flags_ref[OUTER] == 1
    inputs_used = jnp.logical_and(is_near, is_outer)

    def put(piece, rows):
        normed[piece * half : (piece + 1) * half] = norm_rows(rows, gain)[2]

    @pl.when(inputs_used)
    def _():
        for piece in range(pieces):
            put(piece, xs_ref[piece])

    cases = (
        (False, True, (em_ref, eo_ref, p0, p1, p2, p3)),
        (False, False, (lm_ref, lo_ref, p0, p1, p2, p3)),
        (True, False, (lm_ref, lo_ref, q0, q1, q2, q3)),
    )
    for outer, near, sources in cases:

        @pl.when(jnp.logical_and(is_outer == outer, is_near == near))
        def _(sources=sources):
            fill_rows(normed, sources, lambda rows: norm_rows(rows, gain)[2])

    gate, upper = gate_upper(copies, w_buf, normed, size)
    sig = jax.nn.sigmoid(gate)
    smooth = gate * sig
    left_ref[...] = upper * (sig * (1.0 + gate * (1.0 - sig)))
    right_ref[...] = smooth
    active_ref[...] = (smooth * upper).astype(BF)
    for k in range(count):
        cols = pl.ds(k * size, size)
        turned_ref[cols] = normed[:, cols].T


def own_last_kernel(flags_ref, us_ref, *refs):
    refs = list(refs)

    def take(count):
        return [refs.pop(0) for _ in range(count)]

    direct, near_in, early, late, arrived = take(2), take(2), take(2), take(2), take(4)
    turned_ref, left_ref, right_ref, active_ref, early_ref, late_ref = take(6)
    out_ref, u_buf, d_act, out_buf, sems = take(5)
    features = turned_ref.shape[0]
    size = chunk_of(features)
    count = features // size
    pieces, half = us_ref.shape[:2]
    is_near = flags_ref[NEAR] == 1
    is_outer = flags_ref[OUTER] == 1

    def fill(sources, w_ref):
        fill_rows(u_buf, sources)
        total = None
        for k in range(count):
            cols = pl.ds(k * size, size)
            part = dot(u_buf[:, cols], w_ref[2, cols])
            total = part if total is None else total + part
        d_act[...] = total

    half = early[0].shape[0]

    def lanes(source, *places):
        return [source.at[pl.ds(i * half, half)] for i in places]

    near_sources = early + near_in[:1] + lanes(direct[0], 3, 1) + near_in[1:] + lanes(direct[1], 3, 1)
    cases = (
        (True, True, direct, early_ref),
        (True, False, [us_ref.at[i] for i in range(pieces)], late_ref),
        (False, True, near_sources, early_ref),
        (False, False, late + arrived, late_ref),
    )
    for outer, near, sources, w_ref in cases:

        @pl.when(jnp.logical_and(is_outer == outer, is_near == near))
        def _(sources=sources, w_ref=w_ref):
            fill(sources, w_ref)

    copies = []

    def send(matrix, k):
        rows = pl.ds(k * size, size)
        copy = pltpu.make_async_copy(out_buf.at[matrix, rows], out_ref.at[0, matrix, rows], sems.at[matrix, k])
        copy.start()
        copies.append(copy)

    active = active_ref[...]
    d_active = d_act[...]
    for k in range(count):
        cols = pl.ds(k * size, size)
        out_buf[2, cols] = dot_first(u_buf[:, cols], active).astype(BF)
        send(2, k)
    d_gate = (d_active * left_ref[...]).astype(BF)
    d_upper = (d_active * right_ref[...]).astype(BF)
    for k in range(count):
        cols = pl.ds(k * size, size)
        turned = turned_ref[cols]
        out_buf[0, cols] = dot(turned, d_gate).astype(BF)
        send(0, k)
        out_buf[1, cols] = dot(turned, d_upper).astype(BF)
        send(1, k)
    for copy in copies:
        copy.wait()


def call(kernel, name, operands, outs, scratch, limit, flops, moved, hbm=(), out_hbm=False, smem=(0,)):
    specs = [
        SMEM_SPEC if i in smem else HBM_SPEC if i in hbm else VMEM_SPEC for i in range(len(operands))
    ]
    out_spec = HBM_SPEC if out_hbm else VMEM_SPEC
    results = pl.pallas_call(
        kernel,
        out_shape=outs,
        in_specs=specs,
        out_specs=[out_spec] * len(outs),
        scratch_shapes=scratch,
        cost_estimate=pl.CostEstimate(flops=flops, bytes_accessed=moved, transcendentals=0),
        compiler_params=pltpu.CompilerParams(vmem_limit_bytes=limit * MIB),
        name=name,
    )(*operands)
    return list(results)


def body(inputs, cotangent, section_weights, section_gains):
    sections = lax.axis_size("pipe") // REPL
    ranks = lax.axis_size("tensor")
    pipe = lax.axis_index("pipe")
    tensor = lax.axis_index("tensor")
    position = pipe % sections
    replica = pipe // sections
    middle = sections // 2
    near = position < middle
    side = jnp.where(near, 0, 1)
    kind = jnp.where(near, position, sections - 1 - position)
    core = tensor % 2
    chip = tensor // 2
    rows, features = inputs.shape[2:]
    narrow = section_weights.shape[-1]
    group = rows // 2
    chunks = features // chunk_of(features)
    weights = pltpu.with_memory_space_constraint(section_weights[0], pltpu.HBM)
    blocks = pltpu.with_memory_space_constraint(inputs.reshape(-1, rows, features), pltpu.HBM)
    cot_blocks = pltpu.with_memory_space_constraint(cotangent.reshape(-1, rows, features), pltpu.HBM)
    gains = section_gains[0]
    core_swap = [(i, i ^ 1) for i in range(ranks)]
    chip_swap = [(i, (i + 2) % ranks) for i in range(ranks)]

    def spot(across, end, batch):
        return (((replica + across) % REPL) * 2 + end) * 2 + batch

    pairs = ((0, 0), (0, 1), (1, 0), (1, 1))
    pairs_of = ((1, 0), (0, 1), (1, 1))
    own = [spot(across, side ^ turn, batch) for batch in (core, 1 - core) for across, turn in pairs]
    own = [own[i] for i in (0, 4, 1, 2, 3, 5, 6, 7)]
    top = [spot(across, end, batch) for batch in (core, 1 - core) for across, end in pairs]
    bottom = [spot(across, 1 - end, batch) for batch in (core, 1 - core) for across, end in pairs]
    flags = [side, near, kind == 0, chip == 0, kind] + own + top + bottom
    flags = jnp.stack([jnp.asarray(flag).astype(jnp.int32) for flag in flags])

    def swap_core(block):
        return lax.ppermute(block, "tensor", core_swap)

    def swap_chip(block):
        return lax.ppermute(block, "tensor", chip_swap)

    def place(copy, end, c, rank):
        at = c if end == 0 else sections - 1 - c
        return (copy * sections + at) * ranks + rank

    def completed(moves):
        per_copy = sections * ranks
        target = dict(moves)
        back = {end: start for start, end in moves}
        sources = [i for i in range(REPL * per_copy) if i not in target]
        ends = {i for i in range(REPL * per_copy) if i not in back}
        rules = (
            lambda i: i ^ 1 if i in ends else None,
            lambda i: back.get(i) if back.get(i, -1) // per_copy == i // per_copy else None,
            lambda i: next((j for j in sorted(ends) if j // per_copy == i // per_copy and j % ranks == i % ranks), None),
            lambda i: min(ends),
        )
        for rule in rules:
            for i in sources:
                if i not in target and rule(i) in ends:
                    target[i] = rule(i)
                    if rule is rules[0] and i ^ 1 not in target:
                        target[i ^ 1] = i
                        ends.remove(i)
                    ends.remove(target[i])
        return sorted(target.items())

    def send(block, *routes, whole=True):
        moves = []
        for copy in range(REPL):
            for end in range(2):
                for c in range(middle):
                    for route in routes:
                        source = route(copy, end, c)
                        if source is None:
                            continue
                        for rank in range(ranks):
                            came = (rank + 2) % ranks if source[3] else rank
                            moves.append((place(*source[:3], came), place(copy, end, c, rank)))
        return lax.ppermute(block, ("pipe", "tensor"), completed(moves) if whole else moves)

    def hop(block, source, target, turn, other):
        return send(block, lambda copy, end, c: (copy, end ^ turn, source, other) if c == target else None)

    def flow_route(which, wanted):
        turn, shift = pairs_of[which]
        return lambda copy, end, c: ((copy + shift) % REPL, end ^ turn, c, False) if wanted(c, end) else None

    def flow(payload, which, wanted):
        return send(payload, flow_route(which, wanted))

    def joined(*parts):
        return call(stack_kernel, "stack", list(parts), [shape(len(parts) * rows, features)], [], 4, 0, 0, smem=())[0]

    def with_other_core(arrived):
        return arrived + [swap_core(block) for block in arrived]

    def shape(*extent, dtype=BF):
        return jax.ShapeDtypeStruct(extent, dtype)

    row = shape(rows, features)
    pieces = shape(4 * REPL, rows, features)
    gate_shape = shape(2 * rows, narrow, dtype=F32)
    held_shape = pltpu.VMEM((3, features, narrow), BF)
    normed_scratch = pltpu.VMEM((2 * rows, features), BF)
    layer_flops = 12 * rows * features * narrow
    layer_bytes = 6 * features * narrow
    row_bytes = 2 * rows * features

    def layer(kernel, name, operands, outs):
        return call(kernel, name, operands, outs, [normed_scratch], 8, layer_flops, layer_bytes, smem=())

    def hold(part, backward, operands, split):
        kernel = functools.partial(hold_kernel, part, backward)
        outs = [shape(group, features)] * 2 if split else [row]
        found = call(kernel, "hold", [marks] + operands, outs, [], 4, 0, 4 * row_bytes, smem=())
        return found if split else found[0]

    def total(terms):
        return call(sum_kernel, "total", terms, [row], [], 4, 0, 3 * row_bytes, smem=())[0]

    def kind_of(step):
        return min(step, sections - 1 - step)

    def across(held, source, target, during, later=()):
        straight = [hop(held[turn], source, target, turn, False) for turn in range(2)]
        crossed = [hop(held[turn], source, target, turn, True) for turn in range(2)]
        straight, crossed, during = lax.optimization_barrier((straight, crossed, during))
        mine = total(straight + crossed)
        other, later = lax.optimization_barrier((swap_core(mine), later))
        return mine, other, during, later

    def far(c, end):
        return end == 1

    def middle_near(c, end):
        return c > 0 and end == 0

    def middle_class(c, end):
        return c > 0

    pm, po, gate, upper, held_early, mine, other, marks = call(
        first_kernel,
        "first_layer",
        [flags, blocks, pltpu.with_memory_space_constraint(gains, pltpu.HBM), weights],
        [row, row, gate_shape, gate_shape, held_shape, row, row, shape(8, 128, dtype=jnp.int32)],
        [
            normed_scratch,
            pltpu.VMEM(gains.shape, F32),
            pltpu.SemaphoreType.DMA((3, chunks)),
            pltpu.SemaphoreType.DMA((3,)),
        ],
        8,
        layer_flops,
        layer_bytes,
        hbm=(1, 2, 3),
    )
    saved = [(gate, upper, mine, other), None]
    loaded = call(
        load_kernel,
        "load_late",
        [flags, cot_blocks, weights],
        [held_shape, row, row],
        [pltpu.SemaphoreType.DMA((3, 1)), pltpu.SemaphoreType.DMA((2,))],
        4,
        0,
        2 * layer_bytes,
        hbm=(1, 2),
    )
    loaded_rows = call(
        rows_kernel,
        "load_rows",
        [flags, blocks, cot_blocks],
        [pieces, pieces],
        [pltpu.SemaphoreType.DMA((3, 4 * REPL))],
        4,
        0,
        layer_bytes,
        hbm=(1, 2),
    )
    for step in range(sections - 1):
        part = 0 if step < middle else 1
        if step > 0:
            old = list(saved[part] or ())
            pm, po, *saved[part] = layer(
                functools.partial(forward_kernel, part, kind_of(step)),
                "forward_layer",
                [marks, mine, other, gains, held_late if part else held_early] + old,
                [row, row, gate_shape, gate_shape, row, row],
            )
        held = hold(part, False, [pm, swap_core(po), mine], step != middle - 1)
        during = ()
        if step == 0:
            during = loaded
        if step == middle:
            during = call(
                cotangent_kernel,
                "cotangent",
                [up_mine, up_other, held_late],
                [gate_shape],
                [],
                4,
                layer_flops // 3,
                layer_bytes // 3,
                smem=(),
            ) + loaded_rows
        if step == middle - 1:
            mine = total([held, swap_chip(held)])
            other = swap_core(mine)
        else:
            mine, other, during, _ = across(held, kind_of(step), kind_of(step + 1), during)
        if step == 0:
            held_late, up_mine, up_other = during
        if step == middle:
            d_active, input_rows, cot_rows = during

    early_rows = saved[0][2:]
    sides = call(sides_kernel, "sides", [marks, saved[0][2], saved[1][2]], [row, row], [], 4, 0, 0, smem=())
    mine, (same, opposite) = lax.optimization_barrier((mine, sides))
    state_first = flow(opposite, 0, middle_class)
    gates = [saved[0][:2], saved[1][:2]]
    pm, po, late_mine, late_other = layer(
        turn_kernel,
        "turn_layer",
        [marks, d_active, mine, other, *saved[1][2:], gains, held_late],
        [row] * 4,
    )
    state_mine = [early_rows[0], late_mine]
    ups = [None, (up_mine, up_other)]
    own_rows = 4 * REPL * rows
    for step in range(sections - 1, 0, -1):
        part = 0 if step < middle else 1
        if step < sections - 1:
            old = list(ups[part] or ())
            extra = [late_mine] if step == middle else []
            pm, po, *kept = layer(
                functools.partial(backward_kernel, kind_of(step), bool(old), bool(extra)),
                "backward_layer",
                [marks, up_mine, up_other, *gates[part], held_late if part else held_early] + old + extra,
                [row] * (5 if extra else 4),
            )
            ups[part] = kept[:2]
        held = hold(part, True, [pm, swap_core(po), up_mine, state_mine[part], gains], step not in (middle, 1))
        if step == 1:
            held, middle_arrived = lax.optimization_barrier((held, middle_arrived))
            held, near_up = lax.optimization_barrier((held, ups[0][0]))
            crossed = swap_chip(held)
            near_first = flow(near_up, 0, middle_near)
            crossed, near_first = lax.optimization_barrier((crossed, near_first))
            mine = total([held, crossed])
        elif step == middle:
            held, mixed = lax.optimization_barrier((held, kept[2]))
            up_mine = total([held, swap_chip(held)])
            mixed_first = flow(mixed, 0, far)
            up_other, mixed_first, state_second = lax.optimization_barrier(
                (swap_core(up_mine), mixed_first, state_second)
            )
            middle_arrived = with_other_core([state_first, state_second])
            mixed_second = flow(joined(mixed, mixed_first), 1, far)
        else:
            during = [state_first] if step == sections - 1 else []
            up_mine, up_other, during, _ = across(held, kind_of(step), kind_of(step - 1), during)
            if step == sections - 1:
                (state_first,) = during
                state_second = flow(joined(same, state_first), 1, middle_class)
    _, mixed_second = lax.optimization_barrier((mine, mixed_second))
    def last_route(shift, source):
        return lambda copy, end, c: ((copy + shift) % REPL, source, 1, False) if c == 0 and end == 0 else None

    payloads = call(last_kernel, "last", [marks, mine, ups[0][0], near_first], [row] * 2, [], 4, 0, 0, smem=())
    straight = [
        send(mine, last_route(0, 0), whole=False),
        send(payloads[0], last_route(0, 1), flow_route(1, middle_near), whole=False),
        send(mine, last_route(1, 0), whole=False),
        send(payloads[1], last_route(1, 1), flow_route(1, middle_near), whole=False),
    ]
    mixed_arrived = with_other_core([mixed_first, mixed_second])
    prepared = call(
        own_first_kernel,
        "own_first",
        [flags, input_rows, *early_rows, late_mine, late_other, *middle_arrived, *mixed_arrived, gains, weights],
        [
            shape(features, own_rows),
            shape(own_rows, narrow, dtype=F32),
            shape(own_rows, narrow, dtype=F32),
            shape(own_rows, narrow),
        ],
        [
            pltpu.VMEM((2, features, narrow), BF),
            pltpu.VMEM((own_rows, features), BF),
            pltpu.SemaphoreType.DMA((2, chunks)),
        ],
        12,
        4 * own_rows * features * narrow,
        8 * features * narrow,
        hbm=(15,),
    )
    straight, prepared = lax.optimization_barrier((straight, prepared))
    direct = with_other_core([joined(*straight)])
    return call(
        own_last_kernel,
        "own_last",
        [flags, cot_rows, *direct, *with_other_core([near_first]), *ups[0], *ups[1], *mixed_arrived]
        + [*prepared, held_early, held_late],
        [shape(1, 3, features, narrow)],
        [
            pltpu.VMEM((own_rows, features), BF),
            pltpu.VMEM((own_rows, narrow), F32),
            pltpu.VMEM((3, features, narrow), BF),
            pltpu.SemaphoreType.DMA((3, chunks)),
        ],
        16,
        8 * own_rows * features * narrow,
        8 * features * narrow,
        out_hbm=True,
    )[0]


def solution(mesh):
    return jax.shard_map(
        body,
        mesh=mesh,
        in_specs=(P(), P(), P("pipe", None, None, None, "tensor"), P("pipe", None, None)),
        out_specs=P("pipe", None, None, "tensor"),
        check_vma=False,
    )
```

```python
import functools

import jax
import jax.numpy as jnp
from jax import lax
from jax.experimental import pallas as pl
from jax.experimental.pallas import tpu as pltpu
from jax.sharding import PartitionSpec as P

REPL = 2
EPS = 1e-06
BF = jnp.bfloat16
F32 = jnp.float32
SMEM_SPEC = pl.BlockSpec(memory_space=pltpu.SMEM)
VMEM_SPEC = pl.BlockSpec(memory_space=pltpu.VMEM)
HBM_SPEC = pl.BlockSpec(memory_space=pltpu.HBM)
MIB = 1024 * 1024
NEAR, OUTER, FIRST_CHIP, KIND, OWN, TOP, BOTTOM = 1, 2, 3, 4, 5, 13, 21


def chunk_of(features):
    for size in (512, 256, 128):
        if features % size == 0:
            return size
    return features


def norm_rows(rows, gain_row):
    widened = rows.astype(F32)
    root = jnp.sqrt(jnp.mean(widened * widened, axis=-1, keepdims=True) + EPS)
    unit = widened / root
    return unit, root, (unit * gain_row).astype(BF)


def dot(left, right):
    return jnp.dot(left, right, preferred_element_type=F32)


def dot_last(left, right):
    return lax.dot_general(left, right, (((1,), (1,)), ((), ())), preferred_element_type=F32)


def dot_first(left, right):
    return lax.dot_general(left, right, (((0,), (0,)), ((), ())), preferred_element_type=F32)


def is_set(flags_ref, index, value=1):
    if len(flags_ref.shape) == 1:
        return flags_ref[index] == value
    return flags_ref[index : index + 1, 0:1] == value


def gain_at(flags_ref, gains_ref, part):
    return jnp.where(is_set(flags_ref, NEAR, 1 - part), gains_ref[0:1], gains_ref[1:2])


def own_index(flags_ref, part):
    return jnp.where(flags_ref[NEAR] == 1 - part, 0, 1)


def choose(condition, first, second):
    kept = first.dtype
    return jnp.where(condition, first.astype(F32), second.astype(F32)).astype(kept)


def weight_copies(which, w_ref, w_buf, sems, size):
    features = w_buf.shape[1]
    copies = {}
    for matrix in range(3):
        for k in range(features // size):
            rows = pl.ds(k * size, size)
            copies[matrix, k] = pltpu.make_async_copy(
                w_ref.at[which, matrix, rows], w_buf.at[matrix, rows], sems.at[matrix, k]
            )
    return copies


def fill_normed(xm_ref, xo_ref, gain, normed):
    half = xm_ref.shape[0]
    normed[:half] = norm_rows(xm_ref[...], gain)[2]
    normed[half:] = norm_rows(xo_ref[...], gain)[2]


def gate_upper(copies, w_buf, normed, size):
    gate = upper = None
    for k in range(w_buf.shape[1] // size):
        cols = pl.ds(k * size, size)
        if copies:
            copies[0, k].wait()
            copies[1, k].wait()
        block = normed[:, cols]
        gate_k = dot(block, w_buf[0, cols])
        upper_k = dot(block, w_buf[1, cols])
        gate = gate_k if gate is None else gate + gate_k
        upper = upper_k if upper is None else upper + upper_k
    return gate, upper


def forward_math(copies, xm_ref, xo_ref, gain, w_buf, pm_ref, po_ref, normed):
    size = chunk_of(w_buf.shape[1])
    half = xm_ref.shape[0]
    fill_normed(xm_ref, xo_ref, gain, normed)
    gate, upper = gate_upper(copies, w_buf, normed, size)
    active = (gate * jax.nn.sigmoid(gate) * upper).astype(BF)
    for k in range(w_buf.shape[1] // size):
        cols = pl.ds(k * size, size)
        if copies:
            copies[2, k].wait()
        part = dot_last(active, w_buf[2, cols]).astype(BF)
        pm_ref[:, cols] = part[:half]
        po_ref[:, cols] = part[half:]
    return gate, upper


def first_kernel(
    flags_ref, rows_ref, gains_ref, w_ref,
    pm_ref, po_ref, gate_ref, upper_ref, w_buf, xm_ref, xo_ref, marks_ref, normed, gains_buf, sems, row_sems
):
    size = chunk_of(w_buf.shape[1])
    moves = [
        pltpu.make_async_copy(rows_ref.at[flags_ref[OWN + i]], ref, row_sems.at[i])
        for i, ref in enumerate((xm_ref, xo_ref))
    ]
    moves.append(pltpu.make_async_copy(gains_ref, gains_buf, row_sems.at[2]))
    for move in moves:
        move.start()
    for i in range(marks_ref.shape[0]):
        marks_ref[i : i + 1] = jnp.full((1, marks_ref.shape[1]), flags_ref[i], jnp.int32)
    copies = weight_copies(own_index(flags_ref, 0), w_ref, w_buf, sems, size)
    ordered = [(matrix, k) for group in ((0, 1), (2,)) for k in range(w_buf.shape[1] // size) for matrix in group]
    for key in ordered[:4]:
        copies[key].start()
    for move in moves:
        move.wait()
    for key in ordered[4:]:
        copies[key].start()
    gain = gain_at(flags_ref, gains_buf, 0)
    gate_ref[...], upper_ref[...] = forward_math(copies, xm_ref, xo_ref, gain, w_buf, pm_ref, po_ref, normed)


def load_kernel(flags_ref, cot_ref, w_ref, w_buf, um_ref, uo_ref, sems, row_sems):
    copies = [
        pltpu.make_async_copy(cot_ref.at[flags_ref[OWN + i]], ref, row_sems.at[i])
        for i, ref in enumerate((um_ref, uo_ref))
    ]
    copies += list(weight_copies(own_index(flags_ref, 1), w_ref, w_buf, sems, w_buf.shape[1]).values())
    for copy in copies:
        copy.start()
    for copy in copies:
        copy.wait()


def rows_kernel(flags_ref, rows_ref, cot_ref, xs_ref, us_ref, row_sems):
    copies = []
    pieces, rows = xs_ref.shape[:2]
    group = rows // 2
    for i in range(pieces):
        copies.append(pltpu.make_async_copy(cot_ref.at[flags_ref[OWN + i]], us_ref.at[i], row_sems.at[0, i]))
        for half, base in enumerate((TOP, BOTTOM)):
            part = pl.ds(half * group, group)
            copies.append(
                pltpu.make_async_copy(
                    rows_ref.at[flags_ref[base + i], part], xs_ref.at[i, part], row_sems.at[1 + half, i]
                )
            )
    for copy in copies:
        copy.start()
    for copy in copies:
        copy.wait()


def forward_kernel(part, live, flags_ref, xm_ref, xo_ref, gains_ref, w_buf, *refs):
    *old, pm_ref, po_ref, gate_ref, upper_ref, xms_ref, xos_ref, normed = refs
    gain = gain_at(flags_ref, gains_ref, part)
    gate, upper = forward_math(None, xm_ref, xo_ref, gain, w_buf, pm_ref, po_ref, normed)
    found = (gate, upper, xm_ref[...], xo_ref[...])
    outs = (gate_ref, upper_ref, xms_ref, xos_ref)
    if old:
        is_live = is_set(flags_ref, KIND, live)
        found = [choose(is_live, a, b[...]) for a, b in zip(found, old)]
    for out, value in zip(outs, found):
        out[...] = value


def active_gradient(um_ref, uo_ref, w_buf):
    size = chunk_of(w_buf.shape[1])
    d_active = None
    for k in range(w_buf.shape[1] // size):
        cols = pl.ds(k * size, size)
        block = jnp.concatenate([um_ref[:, cols], uo_ref[:, cols]], axis=0)
        part = dot(block, w_buf[2, cols])
        d_active = part if d_active is None else d_active + part
    return d_active


def backward_math(d_active, gate, upper, w_buf, pm_ref, po_ref):
    size = chunk_of(w_buf.shape[1])
    half = pm_ref.shape[0]
    sig = jax.nn.sigmoid(gate)
    d_gate = (d_active * upper * (sig * (1.0 + gate * (1.0 - sig)))).astype(BF)
    d_upper = (d_active * (gate * sig)).astype(BF)
    for k in range(w_buf.shape[1] // size):
        cols = pl.ds(k * size, size)
        part = (dot_last(d_gate, w_buf[0, cols]) + dot_last(d_upper, w_buf[1, cols])).astype(BF)
        pm_ref[:, cols] = part[:half]
        po_ref[:, cols] = part[half:]


def cotangent_kernel(um_ref, uo_ref, w_buf, d_ref):
    d_ref[...] = active_gradient(um_ref, uo_ref, w_buf)


def turn_kernel(
    flags_ref, d_ref, xm_ref, xo_ref, oldm_ref, oldo_ref, gains_ref, w_buf, pm_ref, po_ref, latem_ref, lateo_ref, normed
):
    fill_normed(xm_ref, xo_ref, gain_at(flags_ref, gains_ref, 1), normed)
    gate, upper = gate_upper(None, w_buf, normed, chunk_of(w_buf.shape[1]))
    backward_math(d_ref[...], gate, upper, w_buf, pm_ref, po_ref)
    is_outer = is_set(flags_ref, OUTER)
    latem_ref[...] = choose(is_outer, xm_ref[...], oldm_ref[...])
    lateo_ref[...] = choose(is_outer, xo_ref[...], oldo_ref[...])


def backward_kernel(live, has_old, has_late, flags_ref, um_ref, uo_ref, gate_ref, upper_ref, w_buf, *refs):
    refs = list(refs)
    old = [refs.pop(0) for _ in range(2)] if has_old else []
    late = refs.pop(0) if has_late else None
    pm_ref, po_ref, ums_ref, uos_ref = refs[:4]
    backward_math(active_gradient(um_ref, uo_ref, w_buf), gate_ref[...], upper_ref[...], w_buf, pm_ref, po_ref)
    found = [um_ref[...], uo_ref[...]]
    if old:
        is_live = is_set(flags_ref, KIND, live)
        found = [choose(is_live, a, b[...]) for a, b in zip(found, old)]
    ums_ref[...], uos_ref[...] = found
    if has_late:
        refs[4][...] = choose(is_set(flags_ref, OUTER), late[...], found[0])


def hold_kernel(part, backward, flags_ref, pm_ref, recv_ref, base_ref, *refs):
    summed = pm_ref[...].astype(F32) + recv_ref[...].astype(F32)
    if backward:
        state_ref, gains_ref, *outs = refs
        gain = gain_at(flags_ref, gains_ref, part)
        unit, root, _ = norm_rows(state_ref[...], gain)
        d_unit = summed * gain
        summed = (d_unit - unit * jnp.mean(d_unit * unit, axis=-1, keepdims=True)) / root
    else:
        outs = refs
    base = jnp.where(is_set(flags_ref, FIRST_CHIP), base_ref[...].astype(F32), 0.0)
    value = (summed + base).astype(BF)
    rows = value.shape[0] // len(outs)
    for i, out in enumerate(outs):
        out[...] = value[i * rows : (i + 1) * rows]


def sides_kernel(marks_ref, early_ref, late_ref, same_ref, opposite_ref):
    is_near = is_set(marks_ref, NEAR)
    same_ref[...] = choose(is_near, early_ref[...], late_ref[...])
    opposite_ref[...] = choose(is_near, late_ref[...], early_ref[...])


def stack_kernel(*refs):
    *sources, out_ref = refs
    rows = sources[0].shape[0]
    for i, source in enumerate(sources):
        out_ref[i * rows : (i + 1) * rows] = source[...]


def fill_rows(target, sources, change=None):
    start = 0
    for source in sources:
        rows = source[...]
        target[start : start + rows.shape[0]] = change(rows) if change else rows
        start += rows.shape[0]


def last_kernel(marks_ref, mine_ref, early_ref, arrived_ref, first_ref, second_ref):
    is_near = is_set(marks_ref, NEAR)
    mine = mine_ref[...]
    first_ref[...] = choose(is_near, arrived_ref[...], mine)
    second_ref[...] = choose(is_near, early_ref[...], mine)


def sum_kernel(*refs):
    *terms, out = refs
    count = len(terms) // 2
    rows = out.shape[0] // count
    for i in range(count):
        total = terms[i][...].astype(F32) + terms[count + i][...].astype(F32)
        out[i * rows : (i + 1) * rows] = total.astype(BF)


def own_first_kernel(
    flags_ref, xs_ref, em_ref, eo_ref, lm_ref, lo_ref, p0, p1, p2, p3, q0, q1, q2, q3, gains_ref, w_ref,
    turned_ref, left_ref, right_ref, active_ref, w_buf, normed, sems
):
    features = w_buf.shape[1]
    size = chunk_of(features)
    count = features // size
    copies = {}
    for k in range(count):
        rows = pl.ds(k * size, size)
        for matrix in range(2):
            copies[matrix, k] = pltpu.make_async_copy(
                w_ref.at[0, matrix, rows], w_buf.at[matrix, rows], sems.at[matrix, k]
            )
            copies[matrix, k].start()
    gain = gains_ref[0:1]
    pieces, half = xs_ref.shape[:2]
    is_near = flags_ref[NEAR] == 1
    is_outer = flags_ref[OUTER] == 1
    inputs_used = jnp.logical_and(is_near, is_outer)

    def put(piece, rows):
        normed[piece * half : (piece + 1) * half] = norm_rows(rows, gain)[2]

    @pl.when(inputs_used)
    def _():
        for piece in range(pieces):
            put(piece, xs_ref[piece])

    cases = (
        (False, True, (em_ref, eo_ref, p0, p1, p2, p3)),
        (False, False, (lm_ref, lo_ref, p0, p1, p2, p3)),
        (True, False, (lm_ref, lo_ref, q0, q1, q2, q3)),
    )
    for outer, near, sources in cases:

        @pl.when(jnp.logical_and(is_outer == outer, is_near == near))
        def _(sources=sources):
            fill_rows(normed, sources, lambda rows: norm_rows(rows, gain)[2])

    gate, upper = gate_upper(copies, w_buf, normed, size)
    sig = jax.nn.sigmoid(gate)
    smooth = gate * sig
    left_ref[...] = upper * (sig * (1.0 + gate * (1.0 - sig)))
    right_ref[...] = smooth
    active_ref[...] = (smooth * upper).astype(BF)
    for k in range(count):
        cols = pl.ds(k * size, size)
        turned_ref[cols] = normed[:, cols].T


def own_last_kernel(flags_ref, us_ref, *refs):
    refs = list(refs)

    def take(count):
        return [refs.pop(0) for _ in range(count)]

    direct, near_in, early, late, arrived = take(2), take(2), take(2), take(2), take(4)
    turned_ref, left_ref, right_ref, active_ref, early_ref, late_ref = take(6)
    out_ref, u_buf, d_act, out_buf, sems = take(5)
    features = turned_ref.shape[0]
    size = chunk_of(features)
    count = features // size
    pieces, half = us_ref.shape[:2]
    is_near = flags_ref[NEAR] == 1
    is_outer = flags_ref[OUTER] == 1

    def fill(sources, w_ref):
        fill_rows(u_buf, sources)
        total = None
        for k in range(count):
            cols = pl.ds(k * size, size)
            part = dot(u_buf[:, cols], w_ref[2, cols])
            total = part if total is None else total + part
        d_act[...] = total

    half = early[0].shape[0]

    def lanes(source, *places):
        return [source.at[pl.ds(i * half, half)] for i in places]

    near_sources = early + near_in[:1] + lanes(direct[0], 3, 1) + near_in[1:] + lanes(direct[1], 3, 1)
    cases = (
        (True, True, direct, early_ref),
        (True, False, [us_ref.at[i] for i in range(pieces)], late_ref),
        (False, True, near_sources, early_ref),
        (False, False, late + arrived, late_ref),
    )
    for outer, near, sources, w_ref in cases:

        @pl.when(jnp.logical_and(is_outer == outer, is_near == near))
        def _(sources=sources, w_ref=w_ref):
            fill(sources, w_ref)

    copies = []

    def send(matrix, k):
        rows = pl.ds(k * size, size)
        copy = pltpu.make_async_copy(out_buf.at[matrix, rows], out_ref.at[0, matrix, rows], sems.at[matrix, k])
        copy.start()
        copies.append(copy)

    active = active_ref[...]
    d_active = d_act[...]
    for k in range(count):
        cols = pl.ds(k * size, size)
        out_buf[2, cols] = dot_first(u_buf[:, cols], active).astype(BF)
        send(2, k)
    d_gate = (d_active * left_ref[...]).astype(BF)
    d_upper = (d_active * right_ref[...]).astype(BF)
    for k in range(count):
        cols = pl.ds(k * size, size)
        turned = turned_ref[cols]
        out_buf[0, cols] = dot(turned, d_gate).astype(BF)
        send(0, k)
        out_buf[1, cols] = dot(turned, d_upper).astype(BF)
        send(1, k)
    for copy in copies:
        copy.wait()


def call(kernel, name, operands, outs, scratch, limit, flops, moved, hbm=(), out_hbm=False, smem=(0,)):
    specs = [
        SMEM_SPEC if i in smem else HBM_SPEC if i in hbm else VMEM_SPEC for i in range(len(operands))
    ]
    out_spec = HBM_SPEC if out_hbm else VMEM_SPEC
    results = pl.pallas_call(
        kernel,
        out_shape=outs,
        in_specs=specs,
        out_specs=[out_spec] * len(outs),
        scratch_shapes=scratch,
        cost_estimate=pl.CostEstimate(flops=flops, bytes_accessed=moved, transcendentals=0),
        compiler_params=pltpu.CompilerParams(vmem_limit_bytes=limit * MIB),
        name=name,
    )(*operands)
    return list(results)


def body(inputs, cotangent, section_weights, section_gains):
    sections = lax.axis_size("pipe") // REPL
    ranks = lax.axis_size("tensor")
    pipe = lax.axis_index("pipe")
    tensor = lax.axis_index("tensor")
    position = pipe % sections
    replica = pipe // sections
    middle = sections // 2
    near = position < middle
    side = jnp.where(near, 0, 1)
    kind = jnp.where(near, position, sections - 1 - position)
    core = tensor % 2
    chip = tensor // 2
    rows, features = inputs.shape[2:]
    narrow = section_weights.shape[-1]
    group = rows // 2
    chunks = features // chunk_of(features)
    weights = pltpu.with_memory_space_constraint(section_weights[0], pltpu.HBM)
    blocks = pltpu.with_memory_space_constraint(inputs.reshape(-1, rows, features), pltpu.HBM)
    cot_blocks = pltpu.with_memory_space_constraint(cotangent.reshape(-1, rows, features), pltpu.HBM)
    gains = section_gains[0]
    core_swap = [(i, i ^ 1) for i in range(ranks)]
    chip_swap = [(i, (i + 2) % ranks) for i in range(ranks)]

    def spot(across, end, batch):
        return (((replica + across) % REPL) * 2 + end) * 2 + batch

    pairs = ((0, 0), (0, 1), (1, 0), (1, 1))
    pairs_of = ((1, 0), (0, 1), (1, 1))
    own = [spot(across, side ^ turn, batch) for batch in (core, 1 - core) for across, turn in pairs]
    own = [own[i] for i in (0, 4, 1, 2, 3, 5, 6, 7)]
    top = [spot(across, end, batch) for batch in (core, 1 - core) for across, end in pairs]
    bottom = [spot(across, 1 - end, batch) for batch in (core, 1 - core) for across, end in pairs]
    flags = [side, near, kind == 0, chip == 0, kind] + own + top + bottom
    flags = jnp.stack([jnp.asarray(flag).astype(jnp.int32) for flag in flags])

    def swap_core(block):
        return lax.ppermute(block, "tensor", core_swap)

    def swap_chip(block):
        return lax.ppermute(block, "tensor", chip_swap)

    def place(copy, end, c, rank):
        at = c if end == 0 else sections - 1 - c
        return (copy * sections + at) * ranks + rank

    def completed(moves):
        per_copy = sections * ranks
        target = dict(moves)
        back = {end: start for start, end in moves}
        sources = [i for i in range(REPL * per_copy) if i not in target]
        ends = {i for i in range(REPL * per_copy) if i not in back}
        rules = (
            lambda i: i ^ 1 if i in ends else None,
            lambda i: back.get(i) if back.get(i, -1) // per_copy == i // per_copy else None,
            lambda i: next((j for j in sorted(ends) if j // per_copy == i // per_copy and j % ranks == i % ranks), None),
            lambda i: min(ends),
        )
        for rule in rules:
            for i in sources:
                if i not in target and rule(i) in ends:
                    target[i] = rule(i)
                    if rule is rules[0] and i ^ 1 not in target:
                        target[i ^ 1] = i
                        ends.remove(i)
                    ends.remove(target[i])
        return sorted(target.items())

    def send(block, *routes, whole=True):
        moves = []
        for copy in range(REPL):
            for end in range(2):
                for c in range(middle):
                    for route in routes:
                        source = route(copy, end, c)
                        if source is None:
                            continue
                        for rank in range(ranks):
                            came = (rank + 2) % ranks if source[3] else rank
                            moves.append((place(*source[:3], came), place(copy, end, c, rank)))
        return lax.ppermute(block, ("pipe", "tensor"), completed(moves) if whole else moves)

    def hop(block, source, target, turn, other):
        return send(block, lambda copy, end, c: (copy, end ^ turn, source, other) if c == target else None)

    def flow_route(which, wanted):
        turn, shift = pairs_of[which]
        return lambda copy, end, c: ((copy + shift) % REPL, end ^ turn, c, False) if wanted(c, end) else None

    def flow(payload, which, wanted):
        return send(payload, flow_route(which, wanted))

    def joined(*parts):
        return call(stack_kernel, "stack", list(parts), [shape(len(parts) * rows, features)], [], 4, 0, 0, smem=())[0]

    def with_other_core(arrived):
        return arrived + [swap_core(block) for block in arrived]

    def shape(*extent, dtype=BF):
        return jax.ShapeDtypeStruct(extent, dtype)

    row = shape(rows, features)
    pieces = shape(4 * REPL, rows, features)
    gate_shape = shape(2 * rows, narrow, dtype=F32)
    held_shape = pltpu.VMEM((3, features, narrow), BF)
    normed_scratch = pltpu.VMEM((2 * rows, features), BF)
    layer_flops = 12 * rows * features * narrow
    layer_bytes = 6 * features * narrow
    row_bytes = 2 * rows * features

    def layer(kernel, name, operands, outs):
        return call(kernel, name, operands, outs, [normed_scratch], 8, layer_flops, layer_bytes, smem=())

    def hold(part, backward, operands, split):
        kernel = functools.partial(hold_kernel, part, backward)
        outs = [shape(group, features)] * 2 if split else [row]
        found = call(kernel, "hold", [marks] + operands, outs, [], 4, 0, 4 * row_bytes, smem=())
        return found if split else found[0]

    def total(terms):
        return call(sum_kernel, "total", terms, [row], [], 4, 0, 3 * row_bytes, smem=())[0]

    def kind_of(step):
        return min(step, sections - 1 - step)

    def across(held, source, target, during, later=()):
        straight = [hop(held[turn], source, target, turn, False) for turn in range(2)]
        crossed = [hop(held[turn], source, target, turn, True) for turn in range(2)]
        straight, crossed, during = lax.optimization_barrier((straight, crossed, during))
        mine = total(straight + crossed)
        other, later = lax.optimization_barrier((swap_core(mine), later))
        return mine, other, during, later

    def far(c, end):
        return end == 1

    def middle_near(c, end):
        return c > 0 and end == 0

    def middle_class(c, end):
        return c > 0

    pm, po, gate, upper, held_early, mine, other, marks = call(
        first_kernel,
        "first_layer",
        [flags, blocks, pltpu.with_memory_space_constraint(gains, pltpu.HBM), weights],
        [row, row, gate_shape, gate_shape, held_shape, row, row, shape(8, 128, dtype=jnp.int32)],
        [
            normed_scratch,
            pltpu.VMEM(gains.shape, F32),
            pltpu.SemaphoreType.DMA((3, chunks)),
            pltpu.SemaphoreType.DMA((3,)),
        ],
        8,
        layer_flops,
        layer_bytes,
        hbm=(1, 2, 3),
    )
    saved = [(gate, upper, mine, other), None]
    loaded = call(
        load_kernel,
        "load_late",
        [flags, cot_blocks, weights],
        [held_shape, row, row],
        [pltpu.SemaphoreType.DMA((3, 1)), pltpu.SemaphoreType.DMA((2,))],
        4,
        0,
        2 * layer_bytes,
        hbm=(1, 2),
    )
    loaded_rows = call(
        rows_kernel,
        "load_rows",
        [flags, blocks, cot_blocks],
        [pieces, pieces],
        [pltpu.SemaphoreType.DMA((3, 4 * REPL))],
        4,
        0,
        layer_bytes,
        hbm=(1, 2),
    )
    for step in range(sections - 1):
        part = 0 if step < middle else 1
        if step > 0:
            old = list(saved[part] or ())
            pm, po, *saved[part] = layer(
                functools.partial(forward_kernel, part, kind_of(step)),
                "forward_layer",
                [marks, mine, other, gains, held_late if part else held_early] + old,
                [row, row, gate_shape, gate_shape, row, row],
            )
        held = hold(part, False, [pm, swap_core(po), mine], step != middle - 1)
        during = ()
        if step == 0:
            during = loaded
        if step == middle:
            during = call(
                cotangent_kernel,
                "cotangent",
                [up_mine, up_other, held_late],
                [gate_shape],
                [],
                4,
                layer_flops // 3,
                layer_bytes // 3,
                smem=(),
            ) + loaded_rows
        if step == middle - 1:
            mine = total([held, swap_chip(held)])
            other = swap_core(mine)
        else:
            mine, other, during, _ = across(held, kind_of(step), kind_of(step + 1), during)
        if step == 0:
            held_late, up_mine, up_other = during
        if step == middle:
            d_active, input_rows, cot_rows = during

    early_rows = saved[0][2:]
    sides = call(sides_kernel, "sides", [marks, saved[0][2], saved[1][2]], [row, row], [], 4, 0, 0, smem=())
    mine, (same, opposite) = lax.optimization_barrier((mine, sides))
    state_first = flow(opposite, 0, middle_class)
    gates = [saved[0][:2], saved[1][:2]]
    pm, po, late_mine, late_other = layer(
        turn_kernel,
        "turn_layer",
        [marks, d_active, mine, other, *saved[1][2:], gains, held_late],
        [row] * 4,
    )
    state_mine = [early_rows[0], late_mine]
    ups = [None, (up_mine, up_other)]
    own_rows = 4 * REPL * rows
    for step in range(sections - 1, 0, -1):
        part = 0 if step < middle else 1
        if step < sections - 1:
            old = list(ups[part] or ())
            extra = [late_mine] if step == middle else []
            pm, po, *kept = layer(
                functools.partial(backward_kernel, kind_of(step), bool(old), bool(extra)),
                "backward_layer",
                [marks, up_mine, up_other, *gates[part], held_late if part else held_early] + old + extra,
                [row] * (5 if extra else 4),
            )
            ups[part] = kept[:2]
        held = hold(part, True, [pm, swap_core(po), up_mine, state_mine[part], gains], step not in (middle, 1))
        if step == 1:
            held, middle_arrived = lax.optimization_barrier((held, middle_arrived))
            held, near_up = lax.optimization_barrier((held, ups[0][0]))
            crossed = swap_chip(held)
            near_first = flow(near_up, 0, middle_near)
            crossed, near_first = lax.optimization_barrier((crossed, near_first))
            mine = total([held, crossed])
        elif step == middle:
            held, mixed = lax.optimization_barrier((held, kept[2]))
            up_mine = total([held, swap_chip(held)])
            mixed_first = flow(mixed, 0, far)
            up_other, mixed_first, state_second = lax.optimization_barrier(
                (swap_core(up_mine), mixed_first, state_second)
            )
            middle_arrived = with_other_core([state_first, state_second])
            mixed_second = flow(joined(mixed, mixed_first), 1, far)
        else:
            during = [state_first] if step == sections - 1 else []
            up_mine, up_other, during, _ = across(held, kind_of(step), kind_of(step - 1), during)
            if step == sections - 1:
                (state_first,) = during
                state_second = flow(joined(same, state_first), 1, middle_class)
    _, mixed_second = lax.optimization_barrier((mine, mixed_second))
    def last_route(shift, source):
        return lambda copy, end, c: ((copy + shift) % REPL, source, 1, False) if c == 0 and end == 0 else None

    payloads = call(last_kernel, "last", [marks, mine, ups[0][0], near_first], [row] * 2, [], 4, 0, 0, smem=())
    mine, payloads = lax.optimization_barrier((mine, payloads))
    straight = [
        send(mine, last_route(0, 0), whole=False),
        send(payloads[0], last_route(0, 1), flow_route(1, middle_near), whole=False),
        send(mine, last_route(1, 0), whole=False),
        send(payloads[1], last_route(1, 1), flow_route(1, middle_near), whole=False),
    ]
    mixed_arrived = with_other_core([mixed_first, mixed_second])
    prepared = call(
        own_first_kernel,
        "own_first",
        [flags, input_rows, *early_rows, late_mine, late_other, *middle_arrived, *mixed_arrived, gains, weights],
        [
            shape(features, own_rows),
            shape(own_rows, narrow, dtype=F32),
            shape(own_rows, narrow, dtype=F32),
            shape(own_rows, narrow),
        ],
        [
            pltpu.VMEM((2, features, narrow), BF),
            pltpu.VMEM((own_rows, features), BF),
            pltpu.SemaphoreType.DMA((2, chunks)),
        ],
        12,
        4 * own_rows * features * narrow,
        8 * features * narrow,
        hbm=(15,),
    )
    straight, prepared = lax.optimization_barrier((straight, prepared))
    direct = with_other_core([joined(*straight)])
    return call(
        own_last_kernel,
        "own_last",
        [flags, cot_rows, *direct, *with_other_core([near_first]), *ups[0], *ups[1], *mixed_arrived]
        + [*prepared, held_early, held_late],
        [shape(1, 3, features, narrow)],
        [
            pltpu.VMEM((own_rows, features), BF),
            pltpu.VMEM((own_rows, narrow), F32),
            pltpu.VMEM((3, features, narrow), BF),
            pltpu.SemaphoreType.DMA((3, chunks)),
        ],
        16,
        8 * own_rows * features * narrow,
        8 * features * narrow,
        out_hbm=True,
    )[0]


def solution(mesh):
    return jax.shard_map(
        body,
        mesh=mesh,
        in_specs=(P(), P(), P("pipe", None, None, None, "tensor"), P("pipe", None, None)),
        out_specs=P("pipe", None, None, "tensor"),
        check_vma=False,
    )
```
